32 devices in a mesh: seq: 8 (over z, x), seg: 4 (over y, core).
Axes of the slice: x: 2, y: 2, z: 4, core: 2. Of those that a mesh axis runs over, the one named last changes fastest.
Arguments:
- tokens: bfloat16 [4, 2048, 1024], P('seg', 'seq'), may hold values from -6 to 6
- starts: int32 [4, 4], P('seg'), may hold values from 0 to 2047, as said below
- norm_gain: bfloat16 [1024], P(('seq', 'seg')), may hold values from 0.099609375 to 1.8984375
- ema_delta: bfloat16 [1024, 16], P(('seq', 'seg'))
- ema_alpha: bfloat16 [1024, 16], P(('seq', 'seg'))
- ema_beta: bfloat16 [1024, 16], P(('seq', 'seg')), may hold values from -4 to 4
- ema_eta: bfloat16 [1024, 16], P(('seq', 'seg')), may hold values from -1 to 1
- ema_omega: bfloat16 [1024], P(('seq', 'seg')), may hold values from -4 to 4
- mix_weight: bfloat16 [1024, 4224], P('seq', 'seg'), may hold values from -0.1875 to 0.1875
- value_weight: bfloat16 [1024, 2048], P('seq', 'seg'), may hold values from -0.1875 to 0.1875
- qk_affine: bfloat16 [512], P(('seq', 'seg')), may hold values from -4 to 4
- out_weight: bfloat16 [2048, 1024], P('seq', 'seg'), may hold values from -0.25 to 0.25
- ffn_gain: bfloat16 [1024], P(('seq', 'seg')), may hold values from 0.099609375 to 1.8984375
- ffn_in: bfloat16 [1024, 4096], P('seq', 'seg'), may hold values from -0.1875 to 0.1875
- ffn_out: bfloat16 [4096, 1024], P('seq', 'seg'), may hold values from -0.09375 to 0.09375
- cotangent: bfloat16 [4, 2048, 1024], P('seg', 'seq'), may hold values from -6 to 6
Outputs:
- layer_out: bfloat16 [4, 2048, 1024], P('seg', 'seq')
- grad_tokens: bfloat16 [4, 2048, 1024], P('seg', 'seq')
- grad_norm_gain: float32 [1024], P(('seq', 'seg'))
- grad_ema_delta: float32 [1024, 16], P(('seq', 'seg'))
- grad_ema_alpha: float32 [1024, 16], P(('seq', 'seg'))
- grad_ema_beta: float32 [1024, 16], P(('seq', 'seg'))
- grad_ema_eta: float32 [1024, 16], P(('seq', 'seg'))
- grad_ema_omega: float32 [1024], P(('seq', 'seg'))
- grad_mix_weight: float32 [1024, 4224], P('seq', 'seg')
- grad_value_weight: float32 [1024, 2048], P('seq', 'seg')
- grad_qk_affine: float32 [512], P(('seq', 'seg'))
- grad_out_weight: float32 [2048, 1024], P('seq', 'seg')
- grad_ffn_gain: float32 [1024], P(('seq', 'seg'))
- grad_ffn_in: float32 [1024, 4096], P('seq', 'seg')
- grad_ffn_out: float32 [4096, 1024], P('seq', 'seg')
The draws below stay inside these ranges and needn't reach their ends.
Inputs may be any that keep to these rules, and one draw needn't show every extreme that they name: Each row begins with 0 and never falls; document k of a segment runs from starts[k] to the next entry, the last one to the end of the segment.
All inputs are finite; a program needn't handle non-finite values.
Results may differ from the reference program's by a relative error of at most 0.02.
Values may be sent and summed in bfloat16 or wider, within the bound.
A program may use at most 512 MiB of HBM per device.

```python
import jax
import jax.numpy as jnp
from jax import lax

D = 1024
Z = 128
V = 2048
H = 16
FF = 4096
STRETCH = 128
LENGTH = 2048
DOCS = 4
SEG_DEV = 1
ROWS = 256
SEGMENTS = 4


def ema_logits(key, slow_lo, slow_hi, fast_share):
    pick_key = jax.random.fold_in(key, 201)
    rate_key = jax.random.fold_in(key, 202)
    fast_key = jax.random.fold_in(key, 203)
    decay_key = jax.random.fold_in(key, 204)
    slow_rate = jnp.exp(jax.random.uniform(rate_key, (D, H), jnp.float32, jnp.log(slow_lo), jnp.log(slow_hi)))
    fast_rate = jnp.exp(jax.random.uniform(fast_key, (D, H), jnp.float32, jnp.log(1.0 / 50.0), jnp.log(1.0 / 30.0)))
    rate_all = jnp.where(jax.random.uniform(pick_key, (D, H), jnp.float32) < fast_share, fast_rate, slow_rate)
    decay_logit = jax.random.uniform(decay_key, (D, H), jnp.float32, 0.0, 3.0)
    inflow = -jnp.expm1(-rate_all) / jax.nn.sigmoid(decay_logit)
    damp_logit = jnp.log(inflow) - jnp.log1p(-inflow)
    return (damp_logit, decay_logit)


def draw_ema_delta(key, part):
    pair_drawn = ema_logits(key, 1.0 / (4.0 * LENGTH), 1.0 / 30.0, 0.25)
    return pair_drawn[0].astype(jnp.bfloat16)


def draw_ema_alpha(key, part):
    pair_drawn = ema_logits(key, 1.0 / (4.0 * LENGTH), 1.0 / 30.0, 0.25)
    return pair_drawn[1].astype(jnp.bfloat16)


def draw_starts(key, part):
    key = jax.random.fold_in(key, 7)
    key_list = jax.random.split(key, 5)
    long_index = jax.random.randint(key_list[0], (SEGMENTS, 1), 0, DOCS)
    chosen = jax.random.randint(key_list[1], (SEGMENTS // SEG_DEV,), 0, SEG_DEV)
    chosen = jnp.repeat(chosen, SEG_DEV) == jnp.arange(SEGMENTS) % SEG_DEV
    early = jnp.sort(jax.random.randint(key_list[2], (SEGMENTS, DOCS - 1), 1, ROWS), axis=1)
    late = jnp.sort(jax.random.randint(key_list[3], (SEGMENTS, DOCS - 1), LENGTH - ROWS + 1, LENGTH), axis=1)
    anywhere = jnp.sort(jax.random.randint(key_list[4], (SEGMENTS, DOCS - 1), 1, LENGTH), axis=1)
    order_idx = jnp.arange(DOCS - 1)[None, :]
    spanning = jnp.where(order_idx < long_index, early, late)
    cuts_all = jnp.where(chosen[:, None], spanning, anywhere)
    return jnp.concatenate([jnp.zeros((SEGMENTS, 1), jnp.int32), cuts_all.astype(jnp.int32)], axis=1)


def shard_levels(rng, shape, shards, smallest, largest):
    def one(position, blocks):
        steps = jax.random.uniform(jax.random.fold_in(jax.random.fold_in(rng, 6), position), (blocks,), jnp.float32, smallest / len(shards), largest / len(shards))
        return jnp.repeat(jnp.exp(steps), shape[position] // blocks).reshape((-1,) + (1,) * (len(shape) - position - 1))

    level = one(*shards[0])
    for cut in shards[1:]:
        level = level * one(*cut)
    return level


def normal_values(own_key, shape, width, limit, cuts=(), kind=jnp.bfloat16):
    drawn = jax.random.normal(own_key, shape, jnp.float32) * width
    if len(cuts) > 0:
        drawn = shard_levels(own_key, shape, cuts, -0.22, 0.18) * drawn
    return jnp.clip(drawn, min=-limit, max=limit).astype(kind)


def setup_inputs(seed: int = 0) -> dict:
    streams_of = jax.random.split(jax.random.key(seed), 17)
    tokens = normal_values(streams_of[0], (SEGMENTS, LENGTH, D), 1.0, 6.0, ((0, 4), (1, 8)))
    starts = draw_starts(jax.random.fold_in(streams_of[16], 71), 0)
    norm_gain = jnp.clip(1.0 + 0.18 * jax.random.normal(streams_of[2], (D,), jnp.float32), 0.099609375, 1.8984375).astype(jnp.bfloat16)
    ema_delta = draw_ema_delta(jax.random.fold_in(streams_of[16], 71), 0)
    ema_alpha = draw_ema_alpha(jax.random.fold_in(streams_of[16], 71), 0)
    ema_beta = normal_values(streams_of[5], (D, H), 1.0, 4.0, ((0, 32),))
    ema_eta = normal_values(streams_of[6], (D, H), 0.25, 1.0, ((0, 32),))
    ema_omega = normal_values(streams_of[7], (D,), 1.0, 4.0, ((0, 32),))
    mix_weight = normal_values(streams_of[8], (D, 2 * D + Z + V), D ** -0.5, 0.1875, ((0, 8), (1, 4)))
    value_weight = normal_values(streams_of[9], (D, V), D ** -0.5, 0.1875, ((0, 8), (1, 4)))
    qk_affine = normal_values(streams_of[10], (4 * Z,), 1.0, 4.0, ((0, 32),))
    out_weight = normal_values(streams_of[11], (V, D), (V // 4) ** -0.5, 0.25, ((0, 8), (1, 4)))
    ffn_gain = jnp.clip(1.0 + 0.18 * jax.random.normal(streams_of[12], (D,), jnp.float32), 0.099609375, 1.8984375).astype(jnp.bfloat16)
    ffn_in = normal_values(streams_of[13], (D, FF), D ** -0.5, 0.1875, ((0, 8), (1, 4)))
    ffn_out = normal_values(streams_of[14], (FF, D), FF ** -0.5, 0.09375, ((0, 8), (1, 4)))
    cotangent = normal_values(streams_of[15], (SEGMENTS, LENGTH, D), 1.0, 6.0, ((0, 4), (1, 8)))
    return {"tokens": tokens, "starts": starts, "norm_gain": norm_gain, "ema_delta": ema_delta, "ema_alpha": ema_alpha, "ema_beta": ema_beta, "ema_eta": ema_eta, "ema_omega": ema_omega, "mix_weight": mix_weight, "value_weight": value_weight, "qk_affine": qk_affine, "out_weight": out_weight, "ffn_gain": ffn_gain, "ffn_in": ffn_in, "ffn_out": ffn_out, "cotangent": cotangent}


@jax.custom_vjp
def low(v):
    return lax.optimization_barrier(v.astype(jnp.bfloat16)).astype(jnp.float32)

@jax.custom_vjp
def low_back(v):
    return v

def low_keep(v):
    return (low(v), None)

def low_pass(kept, grad):
    return (grad,)

def back_keep(v):
    return (v, None)

def back_low(kept, grad):
    return (low(grad),)
low.defvjp(low_keep, low_pass)
low_back.defvjp(back_keep, back_low)
epsilon = 1e-05
highest = lax.Precision.HIGHEST

def rms_norm(values, gain):
    inverse = lax.rsqrt(lax.optimization_barrier(jnp.mean(values * values, axis=-1, keepdims=True)) + epsilon)
    return values * inverse * gain

def ema_apply(inputs, documents, damp_logit, decay_logit, inflow_gain, outflow_gain, omega_gain, block_len):
    seg_count, length, channels = inputs.shape
    damping = jax.nn.sigmoid(damp_logit)
    log_keep = jnp.log1p(-damping * jax.nn.sigmoid(decay_logit))
    inflow = damping * inflow_gain
    offsets = jnp.arange(block_len)
    steps_f = offsets.astype(inputs.dtype)
    powers = jnp.exp(steps_f[:, None, None] * log_keep[None])
    kernel = lax.optimization_barrier(jnp.sum(powers * (inflow * outflow_gain)[None], axis=2))
    carry_out = jnp.exp((steps_f + 1.0)[:, None, None] * log_keep[None]) * outflow_gain[None]
    feed_pow = jnp.exp((block_len - 1.0 - steps_f)[:, None, None] * log_keep[None]) * inflow[None]
    full_keep = jnp.exp(block_len * log_keep)
    lag_steps = offsets[:, None] - offsets[None, :]
    lower_tri = lag_steps >= 0
    selector = (jnp.maximum(lag_steps, 0)[:, :, None] == offsets[None, None, :]).astype(inputs.dtype)
    toeplitz = jnp.dot(selector.reshape(block_len * block_len, block_len), kernel, precision=highest).reshape(block_len, block_len, channels)
    blocks = length // block_len
    pieces = inputs.reshape(seg_count, blocks, block_len, channels).transpose(1, 0, 2, 3)
    labels = documents.reshape(seg_count, blocks, block_len).transpose(1, 0, 2)
    before = jnp.concatenate([jnp.zeros((1, seg_count), jnp.int32), labels[:-1, :, -1]], axis=0)

    def advance(carry_state, block_item):
        values, block_docs, earlier = block_item
        same_doc = ((block_docs[:, :, None] == block_docs[:, None, :]) & lower_tri[None]).astype(values.dtype)
        inside = jnp.einsum('isc,nis,nsc->nic', toeplitz, same_doc, values, precision=highest)
        alive_rows = (block_docs == earlier[:, None]).astype(values.dtype)
        carried = alive_rows[:, :, None] * jnp.einsum('ich,nch->nic', carry_out, carry_state, precision=highest)
        tail_mask = (block_docs == block_docs[:, -1:]).astype(values.dtype)
        fresh_state = jnp.einsum('ns,nsc,sch->nch', tail_mask, values, feed_pow, precision=highest)
        next_state = alive_rows[:, -1][:, None, None] * full_keep[None] * carry_state + fresh_state
        return (next_state, inside + carried)
    start_state = jnp.zeros((seg_count, channels, log_keep.shape[1]), inputs.dtype)
    _, outputs = lax.scan(advance, start_state, (pieces, labels, before))
    return outputs.transpose(1, 0, 2, 3).reshape(seg_count, length, channels) + omega_gain * inputs

def segment_forward(tokens, starts, params):
    norm_gain, ema_delta, ema_alpha, ema_beta, ema_eta, ema_omega, mix_weight, value_weight, qk_affine, out_weight, ffn_gain, ffn_in, ffn_out = params
    positions = jnp.arange(LENGTH, dtype=jnp.int32)
    documents = lax.optimization_barrier(jnp.sum((starts[None, :] <= positions[:, None]).astype(jnp.int32), axis=1))
    normed = low(rms_norm(tokens, norm_gain))
    ema_input = low_back(normed)
    mixed = ema_apply(ema_input[None], documents[None], ema_delta, ema_alpha, ema_beta, ema_eta, ema_omega, STRETCH)[0]
    active = low_back(low(jax.nn.silu(mixed)))
    projected = low_back(jnp.dot(active, mix_weight, precision=highest))
    update = jax.nn.sigmoid(projected[:, :D])
    gate_rows = jax.nn.silu(projected[:, D:D + Z + V])
    shared = gate_rows[:, :Z]
    reset_gate = gate_rows[:, Z:]
    candidate = projected[:, D + Z + V:]
    values = low(jax.nn.silu(low_back(jnp.dot(normed, value_weight, precision=highest))))
    affine = qk_affine.reshape(4, Z)
    query_rows = low(Z ** (-0.5) * (shared * affine[0] + affine[1]))
    key_rows = low(shared * affine[2] + affine[3])
    blocks = LENGTH // STRETCH
    block_docs = documents.reshape(blocks, STRETCH)
    offsets = jnp.arange(STRETCH)
    allowed = (block_docs[:, :, None] == block_docs[:, None, :]) & (offsets[:, None] >= offsets[None, :])[None]
    scores = low_back(jnp.einsum('cid,cjd->cij', query_rows.reshape(blocks, STRETCH, Z), key_rows.reshape(blocks, STRETCH, Z), precision=highest))
    probs = jax.nn.softmax(jnp.where(allowed, scores, -1e+30), axis=-1)
    attended = low_back(jnp.einsum('cij,cjv->civ', low(probs), values.reshape(blocks, STRETCH, V), precision=highest)).reshape(LENGTH, V)
    hidden_in = low(attended * reset_gate)
    hidden_pre = low_back(candidate + jnp.dot(hidden_in, out_weight, precision=highest))
    out_one = tokens + update * (jax.nn.silu(hidden_pre) - tokens)
    normed_two = low(rms_norm(out_one, ffn_gain))
    ffn_hidden = low_back(jnp.dot(normed_two, ffn_in, precision=highest))
    return out_one + jnp.dot(low(jax.nn.silu(ffn_hidden)), ffn_out, precision=highest)

def forward_all(tokens, starts, params):

    def one_segment(seg_item):
        return segment_forward(seg_item[0], seg_item[1], params)
    return lax.map(jax.checkpoint(one_segment), (tokens, starts))

def reference(tokens, starts, norm_gain, ema_delta, ema_alpha, ema_beta, ema_eta, ema_omega, mix_weight, value_weight, qk_affine, out_weight, ffn_gain, ffn_in, ffn_out, cotangent):
    params = (norm_gain.astype(jnp.float32), ema_delta.astype(jnp.float32), ema_alpha.astype(jnp.float32), ema_beta.astype(jnp.float32), ema_eta.astype(jnp.float32), ema_omega.astype(jnp.float32), mix_weight.astype(jnp.float32), value_weight.astype(jnp.float32), qk_affine.astype(jnp.float32), out_weight.astype(jnp.float32), ffn_gain.astype(jnp.float32), ffn_in.astype(jnp.float32), ffn_out.astype(jnp.float32))

    def whole_layer(inputs, *weight_list):
        return forward_all(inputs, starts, weight_list)
    outputs, pullback = jax.vjp(whole_layer, tokens.astype(jnp.float32), *params)
    gradients = pullback(cotangent.astype(jnp.float32))
    return (outputs.astype(jnp.bfloat16), gradients[0].astype(jnp.bfloat16), gradients[1], gradients[2], gradients[3], gradients[4], gradients[5], gradients[6], gradients[7], gradients[8], gradients[9], gradients[10], gradients[11], gradients[12], gradients[13])
```

```python
import functools
import math

import jax
import jax.numpy as jnp
import numpy as np
from jax import lax
from jax.experimental import pallas as pl
from jax.experimental.pallas import tpu as pltpu
from jax.sharding import PartitionSpec as P

STRETCH = 128
epsilon = 1e-05

MESH = pl.DeviceIdType.MESH
ANY = pl.BlockSpec(memory_space=pl.ANY)


class Grid:
    def __init__(self, nq, ng):
        self.nq, self.ng = nq, ng
        self.nz = math.gcd(nq, 4)
        self.nx = nq // self.nz
        self.nc = math.gcd(ng, 2)
        self.ny = ng // self.nc

    def here(self):
        s, g = lax.axis_index("seq"), lax.axis_index("seg")
        return s // self.nx, lax.rem(s, self.nx), g // self.nc, lax.rem(g, self.nc)

    def peer(self, axis, d):
        z, x, y, c = self.here()
        if axis == "z":
            z = lax.rem(z + d, self.nz)
        if axis == "x":
            x = lax.rem(x + d, self.nx)
        if axis == "y":
            y = lax.rem(y + d, self.ny)
        if axis == "c":
            c = lax.rem(c + d, self.nc)
        return z, x, y, c

    def size(self, axis):
        return {"z": self.nz, "x": self.nx, "y": self.ny, "c": self.nc}[axis]

    def device(self, place):
        z, x, y, c = place
        return {"seq": z * self.nx + x, "seg": y * self.nc + c}

    def peers(self, axes):
        return [self.peer(a, d) for a in axes for d in range(1, self.size(a))]


def enter(grid, peers):
    barrier = pltpu.get_barrier_semaphore()
    for place in peers:
        pl.semaphore_signal(barrier, inc=1, device_id=grid.device(place), device_id_type=MESH)
    pl.semaphore_wait(barrier, len(peers))


class Sems:
    def __init__(self, send, recv):
        self.send, self.recv, self.used = send, recv, 0

    def take(self):
        i = self.used
        self.used += 1
        return self.send.at[i], self.recv.at[i]


def gather_kernel(grid, shapes, count, *refs):
    n = len(shapes)
    shards, wholes = refs[:n], refs[n : 2 * n]
    own_sem, send, recv = refs[2 * n :]
    sems = Sems(send, recv)
    z, x, y, c = grid.here()
    enter(grid, grid.peers("zxyc"))
    pending = []

    def push(src, dst, axis, d, arrives):
        s, r = sems.take()
        copy = pltpu.make_async_remote_copy(
            src, dst, s, r, device_id=grid.device(grid.peer(axis, d)), device_id_type=MESH
        )
        copy.start()
        pending.append(copy)
        there = pltpu.make_async_remote_copy(
            arrives, arrives, s, r, device_id=grid.device(grid.peer(axis, d)), device_id_type=MESH
        )
        return there.wait_recv

    def back(axis, d):
        place = grid.peer(axis, grid.size(axis) - d)
        return dict(zip("zxyc", place))

    owns = []
    for i in range(n):
        copy = pltpu.make_async_copy(shards[i], wholes[i].at[y, c, z, x], own_sem.at[i])
        copy.start()
        owns.append(copy)

    chunks = [(i, q) for i in range(n) for q in range(shapes[i][0] // 2)]
    halves = (0, 1)
    core_waits = []

    def core(view):
        core_waits.extend(
            push(view(c), view(c), "c", d, view(back("c", d)["c"])) for d in range(1, grid.nc)
        )

    def stage_z(i, h):
        w = wholes[i]
        return [
            push(shards[i].at[h], w.at[y, c, z, x, h], "z", d, w.at[y, c, back("z", d)["z"], x, h])
            for d in range(1, grid.nz)
        ]

    def stage_two(i, h):
        w = wholes[i]
        core(lambda cc: w.at[y, cc, :, x, h])
        src = w.at[y, c, :, x, h]
        if h % 2 == 0:
            return [push(src, src, "x", d, w.at[y, c, :, back("x", d)["x"], h]) for d in range(1, grid.nx)]
        return [push(src, src, "y", d, w.at[back("y", d)["y"], c, :, x, h]) for d in range(1, grid.ny)]

    def stage_three(i, h):
        w = wholes[i]
        if h % 2 == 0:
            for d in range(1, grid.nx):
                core(lambda cc: w.at[y, cc, :, back("x", d)["x"], h])
            src = w.at[y, c, :, :, h]
            return [push(src, src, "y", d, w.at[back("y", d)["y"], c, :, :, h]) for d in range(1, grid.ny)]
        for d in range(1, grid.ny):
            core(lambda cc: w.at[back("y", d)["y"], cc, :, x, h])
        src = w.at[:, c, :, x, h]
        return [push(src, src, "x", d, w.at[:, c, :, back("x", d)["x"], h]) for d in range(1, grid.nx)]

    def stage_last(i, h):
        w = wholes[i]
        if h % 2 == 0:
            for d in range(1, grid.ny):
                core(lambda cc: w.at[back("y", d)["y"], cc, :, :, h])
        else:
            for d in range(1, grid.nx):
                core(lambda cc: w.at[:, cc, :, back("x", d)["x"], h])

    def finish(waits):
        for wait in waits:
            wait()

    got_z, got_two, got_three = {}, {}, {}
    ahead = 2
    total = len(chunks)
    for t in range(total + 3 + ahead):
        k = t
        if k < total:
            i, q = chunks[k]
            for h in halves:
                got_z[k, h] = stage_z(i, 2 * q + h)
        k = t - ahead
        if 0 <= k < total:
            i, q = chunks[k]
            if q == 0:
                owns[i].wait()
            for h in halves:
                finish(got_z[k, h])
                got_two[k, h] = stage_two(i, 2 * q + h)
        k = t - ahead - 1
        if 0 <= k < total:
            i, q = chunks[k]
            for h in halves:
                finish(got_two[k, h])
                got_three[k, h] = stage_three(i, 2 * q + h)
        k = t - ahead - 2
        if 0 <= k < total:
            i, q = chunks[k]
            for h in halves:
                finish(got_three[k, h])
                stage_last(i, 2 * q + h)
    finish(core_waits)
    for copy in pending:
        copy.wait_send()
    assert sems.used <= count, sems.used


def gather_all(grid, shards, cuts, collective_id):
    shapes, args, outs = [], [], []
    for w, q in zip(shards, cuts):
        k, n = w.shape
        shapes.append((2 * q, k // (2 * q), n))
        args.append(w.reshape(shapes[-1]))
        outs.append(jax.ShapeDtypeStruct((grid.ny, grid.nc, grid.nz, grid.nx) + shapes[-1], w.dtype))
    per = (grid.nz - 1) + (grid.nx - 1) + (grid.ny - 1) + (grid.nc - 1) * (grid.nx + grid.ny)
    count = sum(s[0] for s in shapes) * per
    wholes = pl.pallas_call(
        functools.partial(gather_kernel, grid, shapes, count),
        out_shape=outs,
        in_specs=[ANY] * len(args),
        out_specs=[ANY] * len(args),
        scratch_shapes=[
            pltpu.SemaphoreType.DMA((len(args),)),
            pltpu.SemaphoreType.DMA((count,)),
            pltpu.SemaphoreType.DMA((count,)),
        ],
        compiler_params=pltpu.CompilerParams(collective_id=collective_id, has_side_effects=True),
    )(*args)
    return [w.reshape(grid.ng, -1, w.shape[-1]) for w in wholes]


def scatter_kernel(grid, shapes, count, *refs):
    n = len(shapes)
    nz, nx, ny, nc = grid.nz, grid.nx, grid.ny, grid.nc
    nq, ng = grid.nq, grid.ng
    small, refs = refs[0], refs[1:]
    terms, sums = refs[:n], refs[n : 2 * n]
    small_sum, small_seq, small_seg, s_send, s_recv = refs[2 * n : 2 * n + 5]
    scratch = refs[2 * n + 5 :]
    own = [scratch[7 * i] for i in range(n)]
    one = [scratch[7 * i + 1] for i in range(n)]
    two_a = [scratch[7 * i + 2] for i in range(n)]
    two_b = [scratch[7 * i + 3] for i in range(n)]
    three_a = [scratch[7 * i + 4] for i in range(n)]
    three_b = [scratch[7 * i + 5] for i in range(n)]
    four = [scratch[7 * i + 6] for i in range(n)]
    own_sem, send, recv = scratch[7 * n :]
    sems = Sems(send, recv)
    z, x, y, c = grid.here()
    sq, sg = lax.axis_index("seq"), lax.axis_index("seg")
    seq_peer = [{"seq": lax.rem(sq + d, nq), "seg": sg} for d in range(1, nq)]
    seg_peer = [{"seq": sq, "seg": lax.rem(sg + d, ng)} for d in range(1, ng)]
    barrier = pltpu.get_barrier_semaphore()
    for place in seq_peer + seg_peer:
        pl.semaphore_signal(barrier, inc=1, device_id=place, device_id_type=MESH)
    pl.semaphore_wait(barrier, nq + ng - 2)
    pending = []

    small_copies = []
    for d in range(1, nq):
        small_copies.append(pltpu.make_async_remote_copy(
            small.at[lax.rem(sq + d, nq)], small_seq.at[d - 1], s_send.at[d - 1], s_recv.at[d - 1],
            device_id=seq_peer[d - 1], device_id_type=MESH))
        small_copies[-1].start()

    def small_middle():
        total = small[sq]
        for d in range(1, nq):
            small_copies[d - 1].wait_recv()
            total += small_seq[d - 1]
        small_sum[...] = total
        for d in range(1, ng):
            small_copies.append(pltpu.make_async_remote_copy(
                small_sum, small_seg.at[d - 1], s_send.at[nq + d - 2], s_recv.at[nq + d - 2],
                device_id=seg_peer[d - 1], device_id_type=MESH))
            small_copies[-1].start()

    def small_end():
        total = small_sum[...]
        for d in range(1, ng):
            small_copies[nq + d - 2].wait_recv()
            total += small_seg[d - 1]
        for copy in small_copies:
            copy.wait_send()
        small_sum[...] = total

    def push(src, dst, axis, d):
        s, r = sems.take()
        copy = pltpu.make_async_remote_copy(
            src, dst, s, r, device_id=grid.device(grid.peer(axis, d)), device_id_type=MESH
        )
        copy.start()
        pending.append(copy)
        return copy.wait_recv

    def to(axis, d):
        return dict(zip("zxyc", grid.peer(axis, d)))[axis]

    def finish(waits):
        for wait in waits:
            wait()

    assert nc == 2

    def stage_one(i, q, h):
        return [push(terms[i].at[:, to("c", 1), :, :, 2 * q + h], one[i].at[q, h], "c", 1)]

    def load_own(i, q, h):
        load = pltpu.make_async_copy(terms[i].at[:, c, :, :, 2 * q + h], own[i].at[h], own_sem.at[i, h])
        load.start()
        return [load.wait]

    def stage_two(i, q, h):
        mine = one[i].at[q, h]

        @pl.loop(0, ny * nz)
        def _(ab):
            a, b = ab // nz, lax.rem(ab, nz)
            for e in range(nx):
                mine[a, b, e] += own[i][h, a, b, e]

        if h == 0:
            return [push(mine.at[to("y", d)], two_a[i].at[q, d - 1], "y", d) for d in range(1, ny)]
        return [push(mine.at[:, :, to("x", d)], two_b[i].at[q, d - 1], "x", d) for d in range(1, nx)]

    def stage_three(i, q, h):
        mine = one[i].at[q, h]
        if h == 0:

            @pl.loop(0, nz)
            def _(b):
                for e in range(nx):
                    total = mine[y, b, e]
                    for d in range(ny - 1):
                        total += two_a[i][q, d, b, e]
                    mine[y, b, e] = total

            return [push(mine.at[y, :, to("x", d)], three_a[i].at[q, d - 1], "x", d) for d in range(1, nx)]

        @pl.loop(0, nz)
        def _(b):
            for a in range(ny):
                total = mine[a, b, x]
                for d in range(nx - 1):
                    total += two_b[i][q, d, a, b]
                mine[a, b, x] = total

        return [push(mine.at[to("y", d), :, x], three_b[i].at[q, d - 1], "y", d) for d in range(1, ny)]

    def stage_four(i, q, h):
        mine = one[i].at[q, h]
        came = three_a[i] if h == 0 else three_b[i]

        @pl.loop(0, nz)
        def _(b):
            total = mine[y, b, x]
            for d in range((nx if h == 0 else ny) - 1):
                total += came[q, d, b]
            mine[y, b, x] = total

        return [push(mine.at[y, to("z", d), x], four[i].at[q, h, d - 1], "z", d) for d in range(1, nz)]

    def stage_last(i, q, h):
        total = one[i][q, h, y, z, x].astype(jnp.float32)
        for d in range(nz - 1):
            total += four[i][q, h, d].astype(jnp.float32)
        sums[i][2 * q + h] = total

    stages = [stage_one, stage_two, stage_three, stage_four, stage_last]
    chunks = [(i, q) for i in range(n) for q in range(shapes[i][0] // 2)]
    waits = {}
    for t in range(len(chunks) + len(stages) - 1):
        if t == 1:
            small_middle()
        for j, stage in enumerate(stages):
            if 0 <= t - j < len(chunks):
                i, q = chunks[t - j]
                for h in (0, 1):
                    if j:
                        finish(waits[i, q, h])
                    waits[i, q, h] = stage(i, q, h)
            if j == 1 and t < len(chunks):
                i, q = chunks[t]
                for h in (0, 1):
                    waits[i, q, h] += load_own(i, q, h)
    small_end()
    for copy in pending:
        copy.wait_send()
    assert sems.used <= count, sems.used


def scatter_all(grid, small, terms, cuts, collective_id, vmem):
    nz, nx, ny, nc = grid.nz, grid.nx, grid.ny, grid.nc
    shapes, args, outs, scratch = [], [], [], []
    for t, q in zip(terms, cuts):
        _, rows, n = t.shape
        kh = rows // grid.nq // (2 * q)
        shapes.append((2 * q, kh, n))
        args.append(t.reshape(ny, nc, nz, nx, 2 * q, kh, n))
        outs.append(jax.ShapeDtypeStruct((2 * q, kh, n), jnp.float32))
        b = t.dtype
        scratch += [
            pltpu.VMEM((2, ny, nz, nx, kh, n), b),
            pltpu.VMEM((q, 2, ny, nz, nx, kh, n), b),
            pltpu.VMEM((q, max(ny - 1, 1), nz, nx, kh, n), b),
            pltpu.VMEM((q, max(nx - 1, 1), ny, nz, kh, n), b),
            pltpu.VMEM((q, max(nx - 1, 1), nz, kh, n), b),
            pltpu.VMEM((q, max(ny - 1, 1), nz, kh, n), b),
            pltpu.VMEM((q, 2, max(nz - 1, 1), kh, n), b),
        ]
    per = (nc - 1) + (nx - 1) + (ny - 1) + (nz - 1)
    count = per * sum(s[0] for s in shapes)
    sums = pl.pallas_call(
        functools.partial(scatter_kernel, grid, shapes, count),
        out_shape=outs + [jax.ShapeDtypeStruct(small.shape[1:], small.dtype)],
        in_specs=[pl.BlockSpec(memory_space=pltpu.VMEM)] + [ANY] * len(args),
        out_specs=[pl.BlockSpec(memory_space=pltpu.VMEM)] * (len(args) + 1),
        scratch_shapes=[
            pltpu.VMEM((grid.nq - 1,) + small.shape[1:], small.dtype),
            pltpu.VMEM((grid.ng - 1,) + small.shape[1:], small.dtype),
            pltpu.SemaphoreType.DMA((grid.nq + grid.ng - 2,)),
            pltpu.SemaphoreType.DMA((grid.nq + grid.ng - 2,)),
        ]
        + scratch
        + [
            pltpu.SemaphoreType.DMA((len(args), 2)),
            pltpu.SemaphoreType.DMA((count,)),
            pltpu.SemaphoreType.DMA((count,)),
        ],
        compiler_params=pltpu.CompilerParams(
            collective_id=collective_id, has_side_effects=True, vmem_limit_bytes=vmem
        ),
    )(small, *args)
    return sums[-1], [s.reshape(-1, s.shape[-1]) for s in sums[:-1]]


def block_of(e, nq, blocks):
    return e * blocks // nq


def mix_kernel(grid, width, dims, *refs):
    (tok, tile, alive, spans, normed_out, active_out, x_out, mixed_out, carry_out, par_out, aff_out,
     tiles, table, bound, sends_t, recv_t, sends_b, recv_b) = refs
    nq, ng = grid.nq, grid.ng
    rows = tok.shape[0]
    blocks = width // 128
    s, g = lax.axis_index("seq"), lax.axis_index("seg")
    seq_peer = [{"seq": lax.rem(s + d, nq), "seg": g} for d in range(1, nq)]
    seg_peer = [{"seq": s, "seg": lax.rem(g + d, ng)} for d in range(1, ng)]
    barrier = pltpu.get_barrier_semaphore()
    for place in seq_peer + seg_peer:
        pl.semaphore_signal(barrier, inc=1, device_id=place, device_id_type=MESH)
    pl.semaphore_wait(barrier, nq + ng - 2)

    copies = []
    for d in range(1, ng):
        copies.append(pltpu.make_async_remote_copy(
            tile, tiles.at[d - 1], sends_t.at[d - 1], recv_t.at[d - 1],
            device_id=seg_peer[d - 1], device_id_type=MESH))
        copies[-1].start()
    for copy in copies:
        copy.wait_recv()
    lanes = tile[...]
    for d in range(1, ng):
        lanes += tiles[d - 1]
    table[s] = lanes
    for d in range(1, nq):
        copies.append(pltpu.make_async_remote_copy(
            table.at[s], table.at[s], sends_t.at[ng + d - 2], recv_t.at[ng + d - 2],
            device_id=seq_peer[d - 1], device_id_type=MESH))
        copies[-1].start()
    for d in range(1, nq):
        came = table.at[lax.rem(s + nq - d, nq)]
        pltpu.make_async_remote_copy(
            came, came, sends_t.at[ng + d - 2], recv_t.at[ng + d - 2],
            device_id=seq_peer[d - 1], device_id_type=MESH).wait_recv()
    count = 4 * dims + 3
    for b in range(blocks):
        mine = [e for e in range(nq) if block_of(e, nq, blocks) == b]
        whole = table[mine[0], 0:count]
        for e in mine[1:]:
            whole += table[e, 0:count]
        par_out[:, b, :] = whole
    aff = table[0, count : count + 4]
    for e in range(1, nq):
        aff += table[e, count : count + 4]
    aff_out[...] = aff

    gain = [par_out[4 * dims, b : b + 1, :] for b in range(blocks)]
    step_rows = 32

    @pl.loop(0, rows // step_rows)
    def _(i):
        at = pl.ds(pl.multiple_of(i * step_rows, step_rows), step_rows)
        v = tok[at, :].astype(jnp.float32)
        r = lax.rsqrt(jnp.mean(v * v, axis=1, keepdims=True) + epsilon)
        for b in range(blocks):
            lane = slice(b * 128, b * 128 + 128)
            n = (v[:, lane] * r * gain[b]).astype(jnp.bfloat16)
            normed_out[at, lane] = n
            x_out[pl.ds(i * step_rows * blocks + b, step_rows, stride=blocks), :] = n.astype(jnp.float32)

    damping = [jax.nn.sigmoid(par_out[j]) for j in range(dims)]
    keep = [1.0 - damping[j] * jax.nn.sigmoid(par_out[dims + j]) for j in range(dims)]
    weight = [damping[j] * par_out[2 * dims + j] * par_out[3 * dims + j] for j in range(dims)]
    omega = par_out[4 * dims + 1]

    def row(ref, p):
        return ref[pl.ds(pl.multiple_of(p * blocks, blocks), blocks), :]

    def first_pass(p, state):
        x, a = row(x_out, p), alive[pl.ds(p, 1), :]
        return tuple(keep[j] * (state[j] * a) + x for j in range(dims))

    zero = tuple(jnp.zeros((blocks, 128), jnp.float32) for _ in range(dims))
    ends = lax.fori_loop(0, rows, first_pass, zero, unroll=4)
    for j in range(dims):
        bound[s, j] = ends[j]
    out = []
    for d in range(1, nq):
        out.append(pltpu.make_async_remote_copy(
            bound.at[s], bound.at[s], sends_b.at[d - 1], recv_b.at[d - 1],
            device_id=seq_peer[d - 1], device_id_type=MESH))
        out[-1].start()
    for d in range(1, nq):
        came = bound.at[lax.rem(s + nq - d, nq)]
        pltpu.make_async_remote_copy(
            came, came, sends_b.at[d - 1], recv_b.at[d - 1],
            device_id=seq_peer[d - 1], device_id_type=MESH).wait_recv()
    for j in range(dims):
        through = power(keep[j], rows)
        state = jnp.zeros((blocks, 128), jnp.float32)
        for e in range(nq - 1):
            later = through * spans[e : e + 1, :] * state + bound[e, j]
            state = jnp.where(e < s, later, state)
        carry_out[j] = state

    def second_pass(p, state):
        x, a = row(x_out, p), alive[pl.ds(p, 1), :]
        state = tuple(keep[j] * (state[j] * a) + x for j in range(dims))
        sums = [omega * x] + [weight[j] * state[j] for j in range(dims)]
        while len(sums) > 1:
            sums = [sum(sums[k : k + 2][1:], sums[k]) for k in range(0, len(sums), 2)]
        mixed_out[pl.ds(pl.multiple_of(p * blocks, blocks), blocks), :] = sums[0]
        return state

    lax.fori_loop(0, rows, second_pass, tuple(carry_out[j] for j in range(dims)), unroll=4)
    for b in range(blocks):
        m = mixed_out[pl.ds(b, rows, stride=blocks), :]
        active_out[:, b * 128 : b * 128 + 128] = (m * jax.nn.sigmoid(m)).astype(jnp.bfloat16)
    for copy in copies + out:
        copy.wait_send()


def power(v, n):
    result = None
    while n:
        if n & 1:
            result = v if result is None else result * v
        n >>= 1
        if n:
            v = v * v
    return result


def mix_forward(grid, tok, tile, alive, spans, dims, collective_id):
    rows, width = tok.shape
    nq, ng = grid.nq, grid.ng
    blocks = width // 128
    f = jnp.float32
    vm = pl.BlockSpec(memory_space=pltpu.VMEM)
    return pl.pallas_call(
        functools.partial(mix_kernel, grid, width, dims),
        out_shape=[
            jax.ShapeDtypeStruct((rows, width), jnp.bfloat16),
            jax.ShapeDtypeStruct((rows, width), jnp.bfloat16),
            jax.ShapeDtypeStruct((rows * blocks, 128), f),
            jax.ShapeDtypeStruct((rows * blocks, 128), f),
            jax.ShapeDtypeStruct((dims, blocks, 128), f),
            jax.ShapeDtypeStruct((4 * dims + 3, blocks, 128), f),
            jax.ShapeDtypeStruct((4, 128), f),
        ],
        in_specs=[vm] * 4,
        out_specs=[vm] * 7,
        scratch_shapes=[
            pltpu.VMEM((ng - 1,) + tile.shape, f),
            pltpu.VMEM((nq,) + tile.shape, f),
            pltpu.VMEM((nq, dims, blocks, 128), f),
            pltpu.SemaphoreType.DMA((nq + ng - 2,)),
            pltpu.SemaphoreType.DMA((nq + ng - 2,)),
            pltpu.SemaphoreType.DMA((nq - 1,)),
            pltpu.SemaphoreType.DMA((nq - 1,)),
        ],
        compiler_params=pltpu.CompilerParams(
            collective_id=collective_id, has_side_effects=True, vmem_limit_bytes=40 << 20
        ),
    )(tok, tile, alive, spans)


def mix_back_kernel(grid, dims, *refs):
    (gact, x_in, mixed, carry, par, alive, spans, gin_out, m_out, k_out, om_out,
     g_rows, gin_rows, before, bound, sends_b, recv_b) = refs
    nq = grid.nq
    rows, width = gact.shape
    blocks = width // 128
    s, g = lax.axis_index("seq"), lax.axis_index("seg")
    seq_peer = [{"seq": lax.rem(s + d, nq), "seg": g} for d in range(1, nq)]
    barrier = pltpu.get_barrier_semaphore()
    for place in seq_peer:
        pl.semaphore_signal(barrier, inc=1, device_id=place, device_id_type=MESH)
    pl.semaphore_wait(barrier, nq - 1)
    for b in range(blocks):
        g_rows[pl.ds(b, rows, stride=blocks), :] = gact[:, b * 128 : b * 128 + 128].astype(jnp.float32)

    @pl.loop(0, rows * blocks // 64)
    def _(i):
        at = pl.ds(pl.multiple_of(i * 64, 64), 64)
        g_rows[at, :] = g_rows[at, :] * silu_slope(mixed[at, :])

    damping = [jax.nn.sigmoid(par[j]) for j in range(dims)]
    keep = [1.0 - damping[j] * jax.nn.sigmoid(par[dims + j]) for j in range(dims)]
    weight = [damping[j] * par[2 * dims + j] * par[3 * dims + j] for j in range(dims)]
    omega = par[4 * dims + 1]

    def row(ref, p):
        return ref[pl.ds(pl.multiple_of(p * blocks, blocks), blocks), :]

    def first_pass(i, flow):
        p = rows - 1 - i
        gp, a = row(g_rows, p), alive[pl.ds(p, 1), :]
        return tuple(keep[j] * (a * (gp + flow[j])) for j in range(dims))

    zero = jnp.zeros((blocks, 128), jnp.float32)
    ends = lax.fori_loop(0, rows, first_pass, (zero,) * dims, unroll=4)
    for j in range(dims):
        bound[s, j] = ends[j]
    out = []
    for d in range(1, nq):
        out.append(pltpu.make_async_remote_copy(
            bound.at[s], bound.at[s], sends_b.at[d - 1], recv_b.at[d - 1],
            device_id=seq_peer[d - 1], device_id_type=MESH))
        out[-1].start()
    for d in range(1, nq):
        came = bound.at[lax.rem(s + nq - d, nq)]
        pltpu.make_async_remote_copy(
            came, came, sends_b.at[d - 1], recv_b.at[d - 1],
            device_id=seq_peer[d - 1], device_id_type=MESH).wait_recv()
    flow_in = []
    for j in range(dims):
        through = power(keep[j], rows)
        flow = zero
        for e in range(nq - 1, 0, -1):
            later = through * spans[e : e + 1, :] * flow + bound[e, j]
            flow = jnp.where(e > s, later, flow)
        flow_in.append(flow)

    few = before.shape[1]
    for j0 in range(0, dims, few):
        js = range(j0, j0 + few)

        def ahead(p, state):
            x, a = row(x_in, p), alive[pl.ds(p, 1), :]
            for t in range(few):
                before[p, t] = state[t]
            return tuple(keep[j] * (state[t] * a) + x for t, j in enumerate(js))

        lax.fori_loop(0, rows, ahead, tuple(carry[j] for j in js), unroll=4)

        def back(i, held):
            flow, m_sum, k_sum, om_sum = held
            p = rows - 1 - i
            at = pl.ds(pl.multiple_of(p * blocks, blocks), blocks)
            gp, x, a = g_rows[at, :], x_in[at, :], alive[pl.ds(p, 1), :]
            total = omega * gp if j0 == 0 else gin_rows[at, :]
            if j0 == 0:
                om_sum = om_sum + gp * x
            new_flow, new_m, new_k = [], [], []
            for t, j in enumerate(js):
                c = gp + flow[t]
                ac = a * c
                total = total + weight[j] * c
                new_flow.append(keep[j] * ac)
                new_m.append(m_sum[t] + c * x)
                new_k.append(k_sum[t] + ac * before[p, t])
            gin_rows[at, :] = total
            return tuple(new_flow), tuple(new_m), tuple(new_k), om_sum

        zeros = (zero,) * few
        _, m_sum, k_sum, om_sum = lax.fori_loop(
            0, rows, back, (tuple(flow_in[j] for j in js), zeros, zeros, zero), unroll=4
        )
        for t, j in enumerate(js):
            m_out[j] = m_sum[t]
            k_out[j] = k_sum[t]
        if j0 == 0:
            om_out[...] = om_sum
    for b in range(blocks):
        gin_out[:, b * 128 : b * 128 + 128] = gin_rows[pl.ds(b, rows, stride=blocks), :].astype(jnp.bfloat16)
    for copy in out:
        copy.wait_send()


def mix_backward(grid, gact, x_in, mixed, carry, par, alive, spans, collective_id):
    rows, width = gact.shape
    nq = grid.nq
    blocks, dims, few = width // 128, carry.shape[0], 4
    f = jnp.float32
    vm = pl.BlockSpec(memory_space=pltpu.VMEM)
    return pl.pallas_call(
        functools.partial(mix_back_kernel, grid, dims),
        out_shape=[
            jax.ShapeDtypeStruct((rows, width), jnp.bfloat16),
            jax.ShapeDtypeStruct((dims, blocks, 128), f),
            jax.ShapeDtypeStruct((dims, blocks, 128), f),
            jax.ShapeDtypeStruct((blocks, 128), f),
        ],
        in_specs=[vm] * 7,
        out_specs=[vm] * 4,
        scratch_shapes=[
            pltpu.VMEM((rows * blocks, 128), f),
            pltpu.VMEM((rows * blocks, 128), f),
            pltpu.VMEM((rows, few, blocks, 128), f),
            pltpu.VMEM((nq, dims, blocks, 128), f),
            pltpu.SemaphoreType.DMA((nq - 1,)),
            pltpu.SemaphoreType.DMA((nq - 1,)),
        ],
        compiler_params=pltpu.CompilerParams(
            collective_id=collective_id, has_side_effects=True, vmem_limit_bytes=40 << 20
        ),
    )(gact, x_in, mixed, carry, par, alive, spans)


def rms_forward(values, gain):
    inverse = lax.rsqrt(jnp.mean(values * values, axis=-1, keepdims=True) + epsilon)
    return (values * inverse * gain, inverse)


def rms_backward(grad_out, values, inverse, gain):
    scaled = grad_out * gain
    projection = jnp.mean(scaled * values, axis=-1, keepdims=True)
    grad_in = inverse * (scaled - values * inverse * inverse * projection)
    return (grad_in, jnp.sum(grad_out * values * inverse, axis=0))


def silu_slope(values):
    sigma_v = jax.nn.sigmoid(values)
    return sigma_v * (1.0 + values * (1.0 - sigma_v))


def times(left, pieces):
    return jnp.concatenate(
        [jnp.dot(left, pieces[i], preferred_element_type=jnp.float32) for i in range(pieces.shape[0])], axis=1
    )


def against(left, pieces):
    n = pieces.shape[2]
    return sum(
        lax.dot_general(
            left[:, i * n : i * n + n], pieces[i], (((1,), (1,)), ((), ())), preferred_element_type=jnp.float32
        )
        for i in range(pieces.shape[0])
    )


def over_rows(left, right, count):
    n = right.shape[1] // count
    return jnp.stack(
        [
            lax.dot_general(
                left, right[:, i * n : i * n + n], (((0,), (0,)), ((), ())), preferred_element_type=jnp.float32
            ).astype(jnp.bfloat16)
            for i in range(count)
        ]
    )


def masked_scores(query_blk, key_blk, allowed):
    raw_scores = jnp.einsum("cid,cjd->cij", query_blk, key_blk, preferred_element_type=jnp.float32)
    return jnp.where(allowed, raw_scores, -1e30)


def body(
    tokens,
    starts,
    norm_gain,
    ema_delta,
    ema_alpha,
    ema_beta,
    ema_eta,
    ema_omega,
    mix_weight,
    value_weight,
    qk_affine,
    out_weight,
    ffn_gain,
    ffn_in,
    ffn_out,
    cotangent,
):
    seg_count, row_count, model_width = tokens.shape
    nq, ng = lax.axis_size("seq"), lax.axis_size("seg")
    grid = Grid(nq, ng)
    seq_index, seg_index = lax.axis_index("seq"), lax.axis_index("seg")
    seq_length = row_count * nq
    dims = ema_delta.shape[1]
    zdim = qk_affine.shape[0] * nq * ng // 4
    vdim = value_weight.shape[1] * ng
    token_count = seg_count * row_count
    blocks = model_width // 128

    index = seq_index * ng + seg_index
    mine = norm_gain.shape[0]
    columns = jnp.concatenate(
        [ema_delta.T, ema_alpha.T, ema_beta.T, ema_eta.T, norm_gain[None], ema_omega[None], ffn_gain[None]], axis=0
    ).astype(jnp.float32)
    count = columns.shape[0]
    tile = jnp.zeros((-(-(count + 4) // 8) * 8, 128), jnp.float32)
    tile = lax.dynamic_update_slice(tile, columns, (0, lax.rem(index * mine, 128)))
    part = qk_affine.shape[0]
    tile = lax.dynamic_update_slice(
        tile, qk_affine.astype(jnp.float32)[None], (count + index * part // 128, lax.rem(index * part, 128))
    )

    places = jnp.arange(seq_length, dtype=jnp.int32)
    goes_on = 1.0 - jnp.any(starts[0][None, :] == places[:, None], axis=1).astype(jnp.float32)
    spans = jnp.broadcast_to(jnp.min(goes_on.reshape(nq, row_count), axis=1)[:, None], (nq, 128))
    alive = lax.dynamic_slice_in_dim(goes_on, seq_index * row_count, row_count, 0)
    alive = jnp.broadcast_to(alive[:, None], (row_count, 128))

    tokens_flat = tokens.reshape(token_count, model_width).astype(jnp.float32)
    normed_b, active, x_rows, mixed_rows, carry, par, affine = mix_forward(
        grid, tokens.reshape(token_count, model_width), tile, alive, spans, dims, 0
    )
    mix_full, value_full, out_full, ffn_in_full, ffn_out_full = gather_all(
        grid, [mix_weight, value_weight, out_weight, ffn_in, ffn_out], [4, 2, 2, 4, 4], 1
    )
    gain_one = par[4 * dims].reshape(-1)
    gain_two = par[4 * dims + 2].reshape(-1)
    inverse_one = lax.rsqrt(jnp.mean(tokens_flat * tokens_flat, axis=-1, keepdims=True) + epsilon)

    projected = times(active, mix_full)
    update = jax.nn.sigmoid(projected[:, :model_width])
    gate_pre = projected[:, model_width : model_width + zdim + vdim]
    gate_rows = jax.nn.silu(gate_pre)
    shared = gate_rows[:, :zdim]
    reset_gate = gate_rows[:, zdim:]
    candidate = projected[:, model_width + zdim + vdim :]
    value_pre = times(normed_b, value_full)
    values_b = jax.nn.silu(value_pre).astype(jnp.bfloat16)
    scale_q = zdim ** (-0.5)
    query_b = (scale_q * (shared * affine[0] + affine[1])).astype(jnp.bfloat16)
    key_b = (shared * affine[2] + affine[3]).astype(jnp.bfloat16)
    positions_rows = seq_index * row_count + jnp.arange(row_count, dtype=jnp.int32)
    docs_rows = jnp.sum((starts[:, None, :] <= positions_rows[None, :, None]).astype(jnp.int32), axis=2)
    block_count = token_count // STRETCH
    block_docs = docs_rows.reshape(block_count, STRETCH)
    offsets = jnp.arange(STRETCH)
    allowed = (block_docs[:, :, None] == block_docs[:, None, :]) & (offsets[:, None] >= offsets[None, :])[None]
    query_blk = query_b.reshape(block_count, STRETCH, zdim)
    key_blk = key_b.reshape(block_count, STRETCH, zdim)
    value_blk = values_b.reshape(block_count, STRETCH, vdim)
    scores = masked_scores(query_blk, key_blk, allowed)
    row_top = jnp.max(scores, axis=2, keepdims=True)
    expo_scores = jnp.exp(scores - row_top)
    row_total = jnp.sum(expo_scores, axis=2, keepdims=True)
    probs = expo_scores / row_total
    probs_b = probs.astype(jnp.bfloat16)
    attended = jnp.einsum("cij,cjv->civ", probs_b, value_blk, preferred_element_type=jnp.float32).reshape(
        token_count, vdim
    )
    hidden_in = (attended * reset_gate).astype(jnp.bfloat16)
    hidden_pre = candidate + times(hidden_in, out_full)
    hidden_act = jax.nn.silu(hidden_pre)
    out_one = tokens_flat + update * (hidden_act - tokens_flat)
    normed_two, inverse_two = rms_forward(out_one, gain_two)
    normed_two_b = normed_two.astype(jnp.bfloat16)
    ffn_hidden = times(normed_two_b, ffn_in_full)
    ffn_act = jax.nn.silu(ffn_hidden).astype(jnp.bfloat16)
    result = (out_one + times(ffn_act, ffn_out_full)).astype(jnp.bfloat16)

    grad_y_b = cotangent.reshape(token_count, model_width)
    grad_ffn_out = over_rows(ffn_act, grad_y_b, ng)
    grad_act = against(grad_y_b, ffn_out_full)
    grad_hidden_b = (grad_act * silu_slope(ffn_hidden)).astype(jnp.bfloat16)
    grad_ffn_in = over_rows(normed_two_b, grad_hidden_b, ng)
    grad_normed_two = against(grad_hidden_b, ffn_in_full)
    grad_norm_two, grad_gain_two = rms_backward(grad_normed_two, out_one, inverse_two, gain_two)
    grad_out_one = grad_y_b.astype(jnp.float32) + grad_norm_two
    grad_update = grad_out_one * (hidden_act - tokens_flat)
    grad_tokens_flat = grad_out_one * (1.0 - update)
    grad_hpre_b = (grad_out_one * update * silu_slope(hidden_pre)).astype(jnp.bfloat16)
    grad_out_weight = over_rows(hidden_in, grad_hpre_b, ng)
    grad_hidden_in = against(grad_hpre_b, out_full)
    grad_att_b = (grad_hidden_in * reset_gate).astype(jnp.bfloat16)
    grad_reset = grad_hidden_in * attended
    grad_att_blk = grad_att_b.reshape(block_count, STRETCH, vdim)
    grad_probs = jnp.einsum("civ,cjv->cij", grad_att_blk, value_blk, preferred_element_type=jnp.float32)
    weighted = jnp.sum(probs * grad_probs, axis=2, keepdims=True)
    grad_scores_b = (probs * (grad_probs - weighted)).astype(jnp.bfloat16)
    grad_query = jnp.einsum("cij,cjd->cid", grad_scores_b, key_blk, preferred_element_type=jnp.float32).reshape(
        token_count, zdim
    )
    grad_key = jnp.einsum("cij,cid->cjd", grad_scores_b, query_blk, preferred_element_type=jnp.float32).reshape(
        token_count, zdim
    )
    grad_values = jnp.einsum("cij,civ->cjv", probs_b, grad_att_blk, preferred_element_type=jnp.float32).reshape(
        token_count, vdim
    )
    grad_qs = grad_query * scale_q
    grad_shared = grad_qs * affine[0] + grad_key * affine[2]
    grad_affine = jnp.stack(
        [
            jnp.sum(grad_qs * shared, axis=0),
            jnp.sum(grad_qs, axis=0),
            jnp.sum(grad_key * shared, axis=0),
            jnp.sum(grad_key, axis=0),
        ]
    )
    grad_gate_pre = jnp.concatenate([grad_shared, grad_reset], axis=1) * silu_slope(gate_pre)
    grad_upre = grad_update * update * (1.0 - update)
    grad_proj_b = jnp.concatenate(
        [grad_upre.astype(jnp.bfloat16), grad_gate_pre.astype(jnp.bfloat16), grad_hpre_b], axis=1
    )
    grad_mix = over_rows(active, grad_proj_b, ng)
    grad_active_b = against(grad_proj_b, mix_full).astype(jnp.bfloat16)
    grad_ema_in, m_part, k_part, omega_part = mix_backward(
        grid, grad_active_b, x_rows, mixed_rows, carry, par, alive, spans, 2
    )
    grad_vpre_b = (grad_values * silu_slope(value_pre)).astype(jnp.bfloat16)
    grad_value = over_rows(normed_b, grad_vpre_b, ng)
    grad_normed = against(grad_vpre_b, value_full) + grad_ema_in.astype(jnp.float32)
    grad_norm_one, grad_gain_one = rms_backward(grad_normed, tokens_flat, inverse_one, gain_one)
    grad_tokens = (grad_tokens_flat + grad_norm_one).astype(jnp.bfloat16)

    small = jnp.concatenate(
        [m_part, k_part, omega_part[None], grad_gain_one.reshape(1, blocks, 128), grad_gain_two.reshape(1, blocks, 128)],
        axis=0,
    ).transpose(1, 0, 2)
    if nq != blocks:
        small = jnp.take(small, np.arange(nq) * blocks // nq, axis=0)
    small = jnp.concatenate([small, jnp.broadcast_to(grad_affine[None], (nq, 4, 128))], axis=1)
    small = jnp.pad(small, ((0, 0), (0, -small.shape[1] % 8), (0, 0)))
    sums, (g_mix, g_value, g_out, g_ffn_in, g_ffn_out) = scatter_all(
        grid, small, [grad_mix, grad_value, grad_out_weight, grad_ffn_in, grad_ffn_out], [4, 2, 2, 4, 4], 3, 60 << 20
    )
    return (
        result.reshape(seg_count, row_count, model_width),
        grad_tokens.reshape(seg_count, row_count, model_width),
        *small_outputs(sums, index, dims, ema_delta, ema_alpha, ema_beta, ema_eta, mine, part, g_mix, g_value, g_out, g_ffn_in, g_ffn_out),
    )


def small_outputs(sums, index, dims, ema_delta, ema_alpha, ema_beta, ema_eta, mine, part, g_mix, g_value, g_out, g_ffn_in, g_ffn_out):
    own = lax.dynamic_slice_in_dim(sums, lax.rem(index * mine, 128), mine, 1)
    m_sum, k_sum = own[:dims].T, own[dims : 2 * dims].T
    vectors = own[2 * dims : 2 * dims + 3]
    delta, alpha, beta, eta = (v.astype(jnp.float32) for v in (ema_delta, ema_alpha, ema_beta, ema_eta))
    damping, decay = jax.nn.sigmoid(delta), jax.nn.sigmoid(alpha)
    g_keep = damping * beta * eta * k_sum
    grad_eta = damping * beta * m_sum
    grad_beta = damping * eta * m_sum
    grad_alpha = -g_keep * damping * decay * (1.0 - decay)
    grad_delta = (beta * eta * m_sum - g_keep * decay) * damping * (1.0 - damping)
    grad_affine = lax.dynamic_slice(
        sums, (2 * dims + 3 + index * part // 128, lax.rem(index * part, 128)), (1, part)
    ).reshape(-1)
    return (vectors[1], grad_delta, grad_alpha, grad_beta, grad_eta, vectors[0],
            g_mix, g_value, grad_affine, g_out, vectors[2], g_ffn_in, g_ffn_out)


def solution(mesh):
    placed = (
        P("seg", "seq", None),
        P("seg", None),
        P(("seq", "seg")),
        P(("seq", "seg"), None),
        P(("seq", "seg"), None),
        P(("seq", "seg"), None),
        P(("seq", "seg"), None),
        P(("seq", "seg")),
        P("seq", "seg"),
        P("seq", "seg"),
        P(("seq", "seg")),
        P("seq", "seg"),
        P(("seq", "seg")),
        P("seq", "seg"),
        P("seq", "seg"),
        P("seg", "seq", None),
    )
    return jax.shard_map(
        body,
        mesh=mesh,
        in_specs=placed,
        out_specs=(P("seg", "seq", None),) * 2 + placed[2:15],
        check_vma=False,
    )
```

```python
import functools
import math

import jax
import jax.numpy as jnp
import numpy as np
from jax import lax
from jax.experimental import pallas as pl
from jax.experimental.pallas import tpu as pltpu
from jax.sharding import PartitionSpec as P

STRETCH = 128
epsilon = 1e-05
GATHER_CUTS = (4, 4, 4, 4, 8)
SCATTER_CUTS = (4, 4, 2, 4, 2)

MESH = pl.DeviceIdType.MESH
ANY = pl.BlockSpec(memory_space=pl.ANY)


class Grid:
    def __init__(self, nq, ng):
        self.nq, self.ng = nq, ng
        self.nz = math.gcd(nq, 4)
        self.nx = nq // self.nz
        self.nc = math.gcd(ng, 2)
        self.ny = ng // self.nc

    def here(self):
        s, g = lax.axis_index("seq"), lax.axis_index("seg")
        return s // self.nx, lax.rem(s, self.nx), g // self.nc, lax.rem(g, self.nc)

    def peer(self, axis, d):
        z, x, y, c = self.here()
        if axis == "z":
            z = lax.rem(z + d, self.nz)
        if axis == "x":
            x = lax.rem(x + d, self.nx)
        if axis == "y":
            y = lax.rem(y + d, self.ny)
        if axis == "c":
            c = lax.rem(c + d, self.nc)
        return z, x, y, c

    def size(self, axis):
        return {"z": self.nz, "x": self.nx, "y": self.ny, "c": self.nc}[axis]

    def device(self, place):
        z, x, y, c = place
        return {"seq": z * self.nx + x, "seg": y * self.nc + c}

    def peers(self, axes):
        return [self.peer(a, d) for a in axes for d in range(1, self.size(a))]


def enter(grid, peers):
    barrier = pltpu.get_barrier_semaphore()
    for place in peers:
        pl.semaphore_signal(barrier, inc=1, device_id=grid.device(place), device_id_type=MESH)
    pl.semaphore_wait(barrier, len(peers))


class Sems:
    def __init__(self, send, recv):
        self.send, self.recv, self.used = send, recv, 0

    def take(self):
        i = self.used
        self.used += 1
        return self.send.at[i], self.recv.at[i]


def gather_steps(grid, shapes, shards, wholes, own_sem, sems):
    n = len(shapes)
    z, x, y, c = grid.here()
    pending = []

    def push(src, dst, axis, d, arrives):
        s, r = sems.take()
        device = grid.device(grid.peer(axis, d))
        copy = pltpu.make_async_remote_copy(src, dst, s, r, device_id=device, device_id_type=MESH)
        copy.start()
        pending.append(copy)
        there = pltpu.make_async_remote_copy(arrives, arrives, s, r, device_id=device, device_id_type=MESH)
        return there.wait_recv

    def back(axis, d):
        return dict(zip("zxyc", grid.peer(axis, grid.size(axis) - d)))[axis]

    owns = []
    chunks = [(i, q) for i in range(n) for q in range(shapes[i][0] // 2)]
    core_waits = {}

    def core(k, view):
        core_waits.setdefault(k, []).extend(
            push(view(c), view(c), "c", d, view(back("c", d))) for d in range(1, grid.nc)
        )

    def stage_z(k, i, h):
        w = wholes[i]
        return [
            push(shards[i].at[h], w.at[y, c, z, x, h], "z", d, w.at[y, c, back("z", d), x, h])
            for d in range(1, grid.nz)
        ]

    def stage_two(k, i, h):
        w = wholes[i]
        src = w.at[y, c, :, x, h]
        if h % 2 == 0:
            waits = [push(src, src, "x", d, w.at[y, c, :, back("x", d), h]) for d in range(1, grid.nx)]
        else:
            waits = [push(src, src, "y", d, w.at[back("y", d), c, :, x, h]) for d in range(1, grid.ny)]
        core(k, lambda cc: w.at[y, cc, :, x, h])
        return waits

    def stage_three(k, i, h):
        w = wholes[i]
        if h % 2 == 0:
            src = w.at[y, c, :, :, h]
            waits = [push(src, src, "y", d, w.at[back("y", d), c, :, :, h]) for d in range(1, grid.ny)]
            for d in range(1, grid.nx):
                core(k, lambda cc: w.at[y, cc, :, back("x", d), h])
            return waits
        src = w.at[:, c, :, x, h]
        waits = [push(src, src, "x", d, w.at[:, c, :, back("x", d), h]) for d in range(1, grid.nx)]
        for d in range(1, grid.ny):
            core(k, lambda cc: w.at[back("y", d), cc, :, x, h])
        return waits

    def stage_last(k, i, h):
        w = wholes[i]
        if h % 2 == 0:
            for d in range(1, grid.ny):
                core(k, lambda cc: w.at[back("y", d), cc, :, :, h])
        else:
            for d in range(1, grid.nx):
                core(k, lambda cc: w.at[:, cc, :, back("x", d), h])

    def finish(waits):
        for wait in waits:
            wait()

    got = {}
    total = len(chunks)
    for t in range(-1, total + 3):
        if t == 0:
            for i in range(n):
                copy = pltpu.make_async_copy(shards[i], wholes[i].at[y, c, z, x], own_sem.at[i])
                copy.start()
                owns.append(copy)
        if 0 <= t < total:
            i, q = chunks[t]
            if q == 0:
                owns[i].wait()
            for h in (0, 1):
                finish(got[t, h])
                got[t, h] = stage_two(t, i, 2 * q + h)
        if t + 1 < total:
            i, q = chunks[t + 1]
            for h in (0, 1):
                got[t + 1, h] = stage_z(t + 1, i, 2 * q + h)
        k = t - 1
        if 0 <= k < total:
            i, q = chunks[k]
            for h in (0, 1):
                finish(got[k, h])
                got[k, h] = stage_three(k, i, 2 * q + h)
        k = t - 2
        if 0 <= k < total:
            i, q = chunks[k]
            for h in (0, 1):
                finish(got[k, h])
                stage_last(k, i, 2 * q + h)
        k = t - 3
        done = []
        if 0 <= k < total:
            finish(core_waits[k])
            i, q = chunks[k]
            if q + 1 == shapes[i][0] // 2:
                done = [i]
        if t == total + 2:
            for copy in pending:
                copy.wait_send()
        yield done


def gather_plan(grid, shards, cuts):
    shapes, args, outs = [], [], []
    for w, q in zip(shards, cuts):
        k, n = w.shape
        q = max(1, min(q, k // 32))
        shapes.append((2 * q, k // (2 * q), n))
        args.append(w.reshape(shapes[-1]))
        outs.append(jax.ShapeDtypeStruct((grid.ny, grid.nc, grid.nz, grid.nx) + shapes[-1], w.dtype))
    per = (grid.nz - 1) + (grid.nx - 1) + (grid.ny - 1) + (grid.nc - 1) * (grid.nx + grid.ny)
    count = sum(s[0] for s in shapes) * per
    return shapes, args, outs, count


def scatter_steps(grid, shapes, terms, sums, scratch, own_sem, sems):
    n = len(shapes)
    nz, nx, ny, nc = grid.nz, grid.nx, grid.ny, grid.nc
    own = [scratch[7 * i] for i in range(n)]
    one = [scratch[7 * i + 1] for i in range(n)]
    two_a = [scratch[7 * i + 2] for i in range(n)]
    two_b = [scratch[7 * i + 3] for i in range(n)]
    three_a = [scratch[7 * i + 4] for i in range(n)]
    three_b = [scratch[7 * i + 5] for i in range(n)]
    four = [scratch[7 * i + 6] for i in range(n)]
    z, x, y, c = grid.here()
    pending = []

    def push(src, dst, axis, d):
        s, r = sems.take()
        copy = pltpu.make_async_remote_copy(
            src, dst, s, r, device_id=grid.device(grid.peer(axis, d)), device_id_type=MESH
        )
        copy.start()
        pending.append(copy)
        return copy.wait_recv

    def to(axis, d):
        return dict(zip("zxyc", grid.peer(axis, d)))[axis]

    def finish(waits):
        for wait in waits:
            wait()

    assert nc == 2

    def stage_one(i, q, h):
        return [push(terms[i].at[:, to("c", 1), :, :, 2 * q + h], one[i].at[q, h], "c", 1)]

    def load_own(i, q, h):
        load = pltpu.make_async_copy(terms[i].at[:, c, :, :, 2 * q + h], own[i].at[h], own_sem.at[i, h])
        load.start()
        return [load.wait]

    def stage_two(i, q, h):
        mine = one[i].at[q, h]

        @pl.loop(0, ny * nz)
        def _(ab):
            a, b = ab // nz, lax.rem(ab, nz)
            for e in range(nx):
                mine[a, b, e] += own[i][h, a, b, e]

        if h == 0:
            return [push(mine.at[to("y", d)], two_a[i].at[q, d - 1], "y", d) for d in range(1, ny)]
        return [push(mine.at[:, :, to("x", d)], two_b[i].at[q, d - 1], "x", d) for d in range(1, nx)]

    def stage_three(i, q, h):
        mine = one[i].at[q, h]
        if h == 0:

            @pl.loop(0, nz)
            def _(b):
                for e in range(nx):
                    total = mine[y, b, e]
                    for d in range(ny - 1):
                        total += two_a[i][q, d, b, e]
                    mine[y, b, e] = total

            return [push(mine.at[y, :, to("x", d)], three_a[i].at[q, d - 1], "x", d) for d in range(1, nx)]

        @pl.loop(0, nz)
        def _(b):
            for a in range(ny):
                total = mine[a, b, x]
                for d in range(nx - 1):
                    total += two_b[i][q, d, a, b]
                mine[a, b, x] = total

        return [push(mine.at[to("y", d), :, x], three_b[i].at[q, d - 1], "y", d) for d in range(1, ny)]

    def stage_four(i, q, h):
        mine = one[i].at[q, h]
        came = three_a[i] if h == 0 else three_b[i]

        @pl.loop(0, nz)
        def _(b):
            total = mine[y, b, x]
            for d in range((nx if h == 0 else ny) - 1):
                total += came[q, d, b]
            mine[y, b, x] = total

        return [push(mine.at[y, to("z", d), x], four[i].at[q, h, d - 1], "z", d) for d in range(1, nz)]

    def stage_last(i, q, h):
        total = one[i][q, h, y, z, x].astype(jnp.float32)
        for d in range(nz - 1):
            total += four[i][q, h, d].astype(jnp.float32)
        sums[i][2 * q + h] = total

    stages = [stage_one, stage_two, stage_three, stage_four, stage_last]
    chunks = [(i, q) for i in range(n) for q in range(shapes[i][0] // 2)]
    waits = {}
    for t in range(len(chunks) + len(stages) - 1):
        for j, stage in enumerate(stages):
            if 0 <= t - j < len(chunks):
                i, q = chunks[t - j]
                for h in (0, 1):
                    if j:
                        finish(waits[i, q, h])
                    waits[i, q, h] = stage(i, q, h)
            if j == 1 and t < len(chunks):
                i, q = chunks[t]
                for h in (0, 1):
                    waits[i, q, h] += load_own(i, q, h)
        if t == len(chunks) + len(stages) - 2:
            for copy in pending:
                copy.wait_send()
        yield


class SmallSum:
    def __init__(self, grid, small, total, seq_in, seg_in, send, recv):
        self.grid, self.small, self.total = grid, small, total
        self.seq_in, self.seg_in, self.send, self.recv = seq_in, seg_in, send, recv
        self.seq_peer, self.seg_peer = small_peers(grid)
        self.copies = []

    def push(self, src, dst, device):
        i = len(self.copies)
        copy = pltpu.make_async_remote_copy(
            src, dst, self.send.at[i], self.recv.at[i], device_id=device, device_id_type=MESH
        )
        copy.start()
        self.copies.append(copy)

    def start(self):
        nq, sq = self.grid.nq, lax.axis_index("seq")
        for d in range(1, nq):
            self.push(self.small.at[lax.rem(sq + d, nq)], self.seq_in.at[d - 1], self.seq_peer[d - 1])

    def middle(self):
        nq, ng = self.grid.nq, self.grid.ng
        total = self.small[lax.axis_index("seq")]
        for d in range(1, nq):
            self.copies[d - 1].wait_recv()
            total += self.seq_in[d - 1]
        self.total[...] = total
        for d in range(1, ng):
            self.push(self.total, self.seg_in.at[d - 1], self.seg_peer[d - 1])

    def end(self):
        nq, ng = self.grid.nq, self.grid.ng
        total = self.total[...]
        for d in range(1, ng):
            self.copies[nq + d - 2].wait_recv()
            total += self.seg_in[d - 1]
        for copy in self.copies:
            copy.wait_send()
        self.total[...] = total


def small_peers(grid):
    nq, ng = grid.nq, grid.ng
    s, g = lax.axis_index("seq"), lax.axis_index("seg")
    return (
        [{"seq": lax.rem(s + d, nq), "seg": g} for d in range(1, nq)],
        [{"seq": s, "seg": lax.rem(g + d, ng)} for d in range(1, ng)],
    )


def meet(peers):
    barrier = pltpu.get_barrier_semaphore()
    for place in peers:
        pl.semaphore_signal(barrier, inc=1, device_id=place, device_id_type=MESH)
    pl.semaphore_wait(barrier, len(peers))


def scatter_plan(grid, terms, cuts):
    nz, nx, ny = grid.nz, grid.nx, grid.ny
    shapes, args, outs, scratch = [], [], [], []
    for t, q in zip(terms, cuts):
        _, rows, n = t.shape
        if n < 128:
            rows, n = rows * n // 128, 128
        k = rows // grid.nq
        q = max(1, min(q, k // 32))
        kh = k // (2 * q)
        shapes.append((2 * q, kh, n))
        args.append(t.reshape(ny, grid.nc, nz, nx, 2 * q, kh, n))
        outs.append(jax.ShapeDtypeStruct((2 * q, kh, n), jnp.float32))
        b = t.dtype
        scratch += [
            pltpu.VMEM((2, ny, nz, nx, kh, n), b),
            pltpu.VMEM((q, 2, ny, nz, nx, kh, n), b),
            pltpu.VMEM((q, max(ny - 1, 1), nz, nx, kh, n), b),
            pltpu.VMEM((q, max(nx - 1, 1), ny, nz, kh, n), b),
            pltpu.VMEM((q, max(nx - 1, 1), nz, kh, n), b),
            pltpu.VMEM((q, max(ny - 1, 1), nz, kh, n), b),
            pltpu.VMEM((q, 2, max(nz - 1, 1), kh, n), b),
        ]
    per = (grid.nc - 1) + (nx - 1) + (ny - 1) + (nz - 1)
    count = per * sum(s[0] for s in shapes)
    return shapes, args, outs, scratch, count


def block_of(e, nq, blocks):
    return e * blocks // nq


def mix_kernel(grid, width, dims, shapes, *refs):
    n = len(shapes)
    shards, refs = refs[:n], refs[n:]
    tok, tile, alive, spans, mask, *refs = refs
    wholes, refs = refs[:n], refs[n:]
    (normed_out, active_out, x_out, mixed_out, carry_out, par_out, aff_out, probs_out, out_one_out, two_out, layer_out,
     proj_hbm, value_hbm, att_hbm, hin_hbm, hpre_hbm, ffn_hbm, act_hbm,
     proj, value_pre, att, hin, hpre, ffn_pre, act, values,
     tiles, table, bound, sends_t, recv_t, sends_b, recv_b, own_sem, flush_sem, load_sem, send, recv,
     *slots) = refs
    nq, ng = grid.nq, grid.ng
    rows = tok.shape[0]
    blocks = width // 128
    s = lax.axis_index("seq")
    seq_peer, seg_peer = small_peers(grid)
    meet(seq_peer + seg_peer)
    steps = gather_steps(grid, shapes, shards, wholes, own_sem, Sems(send, recv))

    done = set()

    def pump(count=1):
        for _ in range(count):
            done.update(next(steps, ()))

    copies = []
    for d in range(1, ng):
        copies.append(pltpu.make_async_remote_copy(
            tile, tiles.at[d - 1], sends_t.at[d - 1], recv_t.at[d - 1],
            device_id=seg_peer[d - 1], device_id_type=MESH))
        copies[-1].start()
    pump()
    for copy in copies:
        copy.wait_recv()
    lanes = tile[...]
    for d in range(1, ng):
        lanes += tiles[d - 1]
    table[s] = lanes
    for d in range(1, nq):
        copies.append(pltpu.make_async_remote_copy(
            table.at[s], table.at[s], sends_t.at[ng + d - 2], recv_t.at[ng + d - 2],
            device_id=seq_peer[d - 1], device_id_type=MESH))
        copies[-1].start()
    for d in range(1, nq):
        came = table.at[lax.rem(s + nq - d, nq)]
        pltpu.make_async_remote_copy(
            came, came, sends_t.at[ng + d - 2], recv_t.at[ng + d - 2],
            device_id=seq_peer[d - 1], device_id_type=MESH).wait_recv()
    count = 4 * dims + 3
    for b in range(blocks):
        mine = [e for e in range(nq) if block_of(e, nq, blocks) == b]
        whole = table[mine[0], 0:count]
        for e in mine[1:]:
            whole += table[e, 0:count]
        par_out[:, b, :] = whole
    aff = table[0, count : count + 4]
    for e in range(1, nq):
        aff += table[e, count : count + 4]
    aff_out[...] = aff

    pump()

    gain = [par_out[4 * dims, b : b + 1, :] for b in range(blocks)]
    step_rows = 32

    @pl.loop(0, rows // step_rows)
    def _(i):
        at = pl.ds(pl.multiple_of(i * step_rows, step_rows), step_rows)
        v = tok[at, :].astype(jnp.float32)
        r = lax.rsqrt(jnp.mean(v * v, axis=1, keepdims=True) + epsilon)
        for b in range(blocks):
            lane = slice(b * 128, b * 128 + 128)
            n = (v[:, lane] * r * gain[b]).astype(jnp.bfloat16)
            normed_out[at, lane] = n
            x_out[pl.ds(i * step_rows * blocks + b, step_rows, stride=blocks), :] = n.astype(jnp.float32)

    damping = [jax.nn.sigmoid(par_out[j]) for j in range(dims)]
    keep = [1.0 - damping[j] * jax.nn.sigmoid(par_out[dims + j]) for j in range(dims)]
    weight = [damping[j] * par_out[2 * dims + j] * par_out[3 * dims + j] for j in range(dims)]
    omega = par_out[4 * dims + 1]

    def row(ref, p):
        return ref[pl.ds(pl.multiple_of(p * blocks, blocks), blocks), :]

    def first_pass(p, state):
        x, a = row(x_out, p), alive[pl.ds(p, 1), :]
        return tuple(keep[j] * (state[j] * a) + x for j in range(dims))

    zero = tuple(jnp.zeros((blocks, 128), jnp.float32) for _ in range(dims))
    ends = lax.fori_loop(0, rows, first_pass, zero, unroll=4)
    for j in range(dims):
        bound[s, j] = ends[j]
    out = []
    for d in range(1, nq):
        out.append(pltpu.make_async_remote_copy(
            bound.at[s], bound.at[s], sends_b.at[d - 1], recv_b.at[d - 1],
            device_id=seq_peer[d - 1], device_id_type=MESH))
        out[-1].start()
    pump()
    for d in range(1, nq):
        came = bound.at[lax.rem(s + nq - d, nq)]
        pltpu.make_async_remote_copy(
            came, came, sends_b.at[d - 1], recv_b.at[d - 1],
            device_id=seq_peer[d - 1], device_id_type=MESH).wait_recv()
    for j in range(dims):
        through = power(keep[j], rows)
        state = jnp.zeros((blocks, 128), jnp.float32)
        for e in range(nq - 1):
            later = through * spans[e : e + 1, :] * state + bound[e, j]
            state = jnp.where(e < s, later, state)
        carry_out[j] = state

    def second_pass(p, state):
        x, a = row(x_out, p), alive[pl.ds(p, 1), :]
        state = tuple(keep[j] * (state[j] * a) + x for j in range(dims))
        sums = [omega * x] + [weight[j] * state[j] for j in range(dims)]
        while len(sums) > 1:
            sums = [sum(sums[k : k + 2][1:], sums[k]) for k in range(0, len(sums), 2)]
        mixed_out[pl.ds(pl.multiple_of(p * blocks, blocks), blocks), :] = sums[0]
        return state

    state = tuple(carry_out[j] for j in range(dims))
    for half in range(2):
        state = lax.fori_loop(half * rows // 2, (half + 1) * rows // 2, second_pass, state, unroll=4)
        pump()
    for b in range(blocks):
        m = mixed_out[pl.ds(b, rows, stride=blocks), :]
        active_out[:, b * 128 : b * 128 + 128] = (m * jax.nn.sigmoid(m)).astype(jnp.bfloat16)
    for copy in copies + out:
        copy.wait_send()

    flushes = []

    def flush(ref, hbm):
        copy = pltpu.make_async_copy(ref, hbm, flush_sem.at[len(flushes)])
        copy.start()
        flushes.append(copy)

    def pieces(i):
        while i not in done:
            pump()

        def fetch(g):
            return pltpu.make_async_copy(
                wholes[i].at[g // grid.nc, g % grid.nc], slots[i].at[g % 2], load_sem.at[i, g % 2]
            )

        fetch(0).start()
        for g in range(grid.ng):
            if g + 1 < grid.ng:
                fetch(g + 1).start()
            fetch(g).wait()
            piece = slots[i][g % 2]
            wide = piece.shape[-1]
            yield g, slice(g * wide, g * wide + wide), piece.reshape(-1, wide)
            if g % 2:
                pump()

    block_rows = 32
    zdim = aff_out.shape[1]
    vdim = value_pre.shape[1]
    first_gate, first_reset, first_cand = width, width + zdim, width + zdim + vdim
    dot = functools.partial(jnp.dot, preferred_element_type=jnp.float32)

    def by_rows(count=rows, each=block_rows):
        def wrap(f):
            pl.loop(0, count // each)(lambda i: f(pl.ds(pl.multiple_of(i * each, each), each)))

        return wrap

    for g, cols, piece in pieces(0):
        proj[:, cols] = dot(active_out[...], piece)
    flush(proj, proj_hbm)

    scale_q = zdim**-0.5
    near = []
    for r in range(rows // STRETCH):
        at = slice(r * STRETCH, r * STRETCH + STRETCH)
        gate = proj[at, first_gate:first_reset]
        shared = gate * jax.nn.sigmoid(gate)
        query = (scale_q * (shared * aff_out[0:1] + aff_out[1:2])).astype(jnp.bfloat16)
        key = (shared * aff_out[2:3] + aff_out[3:4]).astype(jnp.bfloat16)
        scores = lax.dot_general(query, key, (((1,), (1,)), ((), ())), preferred_element_type=jnp.float32)
        scores = jnp.where(mask[at, :] > 0.0, scores, -1e30)
        expo = jnp.exp(scores - jnp.max(scores, axis=1, keepdims=True))
        probs = expo / jnp.sum(expo, axis=1, keepdims=True)
        probs_out[at, :] = probs
        near.append(probs.astype(jnp.bfloat16))

    for g, cols, piece in pieces(1):
        pre = dot(normed_out[...], piece)
        value_pre[:, cols] = pre
        values[:, cols] = (pre * jax.nn.sigmoid(pre)).astype(jnp.bfloat16)
    flush(value_pre, value_hbm)
    for r in range(rows // STRETCH):
        at = slice(r * STRETCH, r * STRETCH + STRETCH)
        att[at, :] = dot(near[r], values[at, :])

    @by_rows()
    def _(at):
        gate = proj[at, first_reset:first_cand]
        hin[at, :] = (att[at, :] * (gate * jax.nn.sigmoid(gate))).astype(jnp.bfloat16)

    flush(att, att_hbm)
    flush(hin, hin_hbm)

    for g, cols, piece in pieces(2):
        hpre[:, cols] = proj[:, first_cand + cols.start : first_cand + cols.stop] + dot(hin[...], piece)
    flush(hpre, hpre_hbm)

    gain_two = [par_out[4 * dims + 2, b : b + 1, :] for b in range(blocks)]

    @by_rows()
    def _(at):
        v = tok[at, :].astype(jnp.float32)
        h = hpre[at, :]
        one = v + jax.nn.sigmoid(proj[at, 0:width]) * (h * jax.nn.sigmoid(h) - v)
        out_one_out[at, :] = one
        r = lax.rsqrt(jnp.mean(one * one, axis=1, keepdims=True) + epsilon)
        for b in range(blocks):
            lane = slice(b * 128, b * 128 + 128)
            two_out[at, lane] = (one[:, lane] * r * gain_two[b]).astype(jnp.bfloat16)

    for g, cols, piece in pieces(3):
        pre = dot(two_out[...], piece)
        ffn_pre[:, cols] = pre
        act[:, cols] = (pre * jax.nn.sigmoid(pre)).astype(jnp.bfloat16)
    flush(ffn_pre, ffn_hbm)
    flush(act, act_hbm)
    for g, cols, piece in pieces(4):
        layer_out[:, cols] = (out_one_out[:, cols] + dot(act[...], piece)).astype(jnp.bfloat16)
    for _ in steps:
        pass
    for copy in flushes:
        copy.wait()


def power(v, n):
    result = None
    while n:
        if n & 1:
            result = v if result is None else result * v
        n >>= 1
        if n:
            v = v * v
    return result


def mix_forward(grid, weights, cuts, tok, tile, alive, spans, mask, dims, collective_id):
    rows, width = tok.shape
    nq, ng = grid.nq, grid.ng
    blocks = width // 128
    f = jnp.float32
    vm = pl.BlockSpec(memory_space=pltpu.VMEM)
    shapes, shards, outs, count = gather_plan(grid, weights, cuts)
    n = len(shards)
    vdim, fdim, proj_dim = weights[1].shape[1] * ng, weights[3].shape[1] * ng, weights[0].shape[1] * ng
    low = jnp.bfloat16
    kept = [
        ((rows, proj_dim), f),
        ((rows, vdim), f),
        ((rows, vdim), f),
        ((rows, vdim), low),
        ((rows, width), f),
        ((rows, fdim), f),
        ((rows, fdim), low),
    ]
    local = [
        ((rows, width), low),
        ((rows, width), low),
        ((rows * blocks, 128), f),
        ((rows * blocks, 128), f),
        ((dims, blocks, 128), f),
        ((4 * dims + 3, blocks, 128), f),
        ((4, 128), f),
        ((rows, STRETCH), f),
        ((rows, width), f),
        ((rows, width), low),
        ((rows, width), low),
    ]
    result = pl.pallas_call(
        functools.partial(mix_kernel, grid, width, dims, shapes),
        out_shape=outs + [jax.ShapeDtypeStruct(*v) for v in local + kept],
        in_specs=[ANY] * n + [vm] * 5,
        out_specs=[ANY] * n + [vm] * len(local) + [ANY] * len(kept),
        scratch_shapes=[pltpu.VMEM(*v) for v in kept]
        + [
            pltpu.VMEM((rows, vdim), low),
            pltpu.VMEM((ng - 1,) + tile.shape, f),
            pltpu.VMEM((nq,) + tile.shape, f),
            pltpu.VMEM((nq, dims, blocks, 128), f),
            pltpu.SemaphoreType.DMA((nq + ng - 2,)),
            pltpu.SemaphoreType.DMA((nq + ng - 2,)),
            pltpu.SemaphoreType.DMA((nq - 1,)),
            pltpu.SemaphoreType.DMA((nq - 1,)),
            pltpu.SemaphoreType.DMA((n,)),
            pltpu.SemaphoreType.DMA((len(kept),)),
            pltpu.SemaphoreType.DMA((n, 2)),
            pltpu.SemaphoreType.DMA((count,)),
            pltpu.SemaphoreType.DMA((count,)),
        ]
        + [pltpu.VMEM((2,) + o.shape[2:], o.dtype) for o in outs],
        compiler_params=pltpu.CompilerParams(
            collective_id=collective_id, has_side_effects=True, vmem_limit_bytes=60 << 20
        ),
    )(*shards, tok, tile, alive, spans, mask)
    return [w.reshape(ng, -1, w.shape[-1]) for w in result[:n]], result[n:]


def mix_back_kernel(grid, dims, shapes, *refs):
    n = len(shapes)
    terms, refs = refs[:n], refs[n:]
    gact, x_in, mixed, carry, par, alive, spans, tok, pre, direct, small_in, *refs = refs
    sums, refs = refs[:n], refs[n:]
    (gtok_out, small_out,
     g_rows, gin_rows, before, bound, m_all, k_all, small, seq_in, seg_in,
     sends_b, recv_b, s_send, s_recv, own_sem, send, recv, *scratch) = refs
    nq = grid.nq
    rows, width = gact.shape
    blocks = width // 128
    s = lax.axis_index("seq")
    seq_peer, seg_peer = small_peers(grid)
    meet(seq_peer + seg_peer)
    steps = scatter_steps(grid, shapes, terms, sums, scratch, own_sem, Sems(send, recv))
    little = SmallSum(grid, small, small_out, seq_in, seg_in, s_send, s_recv)

    def pump(count=1):
        for _ in range(count):
            next(steps, None)

    pump()
    for b in range(blocks):
        g_rows[pl.ds(b, rows, stride=blocks), :] = gact[:, b * 128 : b * 128 + 128].astype(jnp.float32)

    @pl.loop(0, rows * blocks // 64)
    def _(i):
        at = pl.ds(pl.multiple_of(i * 64, 64), 64)
        g_rows[at, :] = g_rows[at, :] * silu_slope(mixed[at, :])

    damping = [jax.nn.sigmoid(par[j]) for j in range(dims)]
    keep = [1.0 - damping[j] * jax.nn.sigmoid(par[dims + j]) for j in range(dims)]
    weight = [damping[j] * par[2 * dims + j] * par[3 * dims + j] for j in range(dims)]
    omega = par[4 * dims + 1]

    def row(ref, p):
        return ref[pl.ds(pl.multiple_of(p * blocks, blocks), blocks), :]

    def first_pass(i, flow):
        p = rows - 1 - i
        gp, a = row(g_rows, p), alive[pl.ds(p, 1), :]
        return tuple(keep[j] * (a * (gp + flow[j])) for j in range(dims))

    zero = jnp.zeros((blocks, 128), jnp.float32)
    ends = lax.fori_loop(0, rows, first_pass, (zero,) * dims, unroll=4)
    for j in range(dims):
        bound[s, j] = ends[j]
    out = []
    for d in range(1, nq):
        out.append(pltpu.make_async_remote_copy(
            bound.at[s], bound.at[s], sends_b.at[d - 1], recv_b.at[d - 1],
            device_id=seq_peer[d - 1], device_id_type=MESH))
        out[-1].start()
    pump()
    for d in range(1, nq):
        came = bound.at[lax.rem(s + nq - d, nq)]
        pltpu.make_async_remote_copy(
            came, came, sends_b.at[d - 1], recv_b.at[d - 1],
            device_id=seq_peer[d - 1], device_id_type=MESH).wait_recv()
    flow_in = []
    for j in range(dims):
        through = power(keep[j], rows)
        flow = zero
        for e in range(nq - 1, 0, -1):
            later = through * spans[e : e + 1, :] * flow + bound[e, j]
            flow = jnp.where(e > s, later, flow)
        flow_in.append(flow)

    few = before.shape[1]
    for j0 in range(0, dims, few):
        js = range(j0, j0 + few)

        def ahead(p, state):
            x, a = row(x_in, p), alive[pl.ds(p, 1), :]
            for t in range(few):
                before[p, t] = state[t]
            return tuple(keep[j] * (state[t] * a) + x for t, j in enumerate(js))

        lax.fori_loop(0, rows, ahead, tuple(carry[j] for j in js), unroll=4)
        if j0:
            pump()

        def back(i, held):
            flow, m_sum, k_sum, om_sum = held
            p = rows - 1 - i
            at = pl.ds(pl.multiple_of(p * blocks, blocks), blocks)
            gp, x, a = g_rows[at, :], x_in[at, :], alive[pl.ds(p, 1), :]
            total = omega * gp if j0 == 0 else gin_rows[at, :]
            if j0 == 0:
                om_sum = om_sum + gp * x
            new_flow, new_m, new_k = [], [], []
            for t, j in enumerate(js):
                c = gp + flow[t]
                ac = a * c
                total = total + weight[j] * c
                new_flow.append(keep[j] * ac)
                new_m.append(m_sum[t] + c * x)
                new_k.append(k_sum[t] + ac * before[p, t])
            gin_rows[at, :] = total
            return tuple(new_flow), tuple(new_m), tuple(new_k), om_sum

        zeros = (zero,) * few
        _, m_sum, k_sum, om_sum = lax.fori_loop(
            0, rows, back, (tuple(flow_in[j] for j in js), zeros, zeros, zero), unroll=4
        )
        for t, j in enumerate(js):
            m_all[j] = m_sum[t]
            k_all[j] = k_sum[t]
        if j0 == 0:
            m_all[dims] = om_sum
        pump()

    gain = [par[4 * dims, b : b + 1, :] for b in range(blocks)]
    lanes = [slice(b * 128, b * 128 + 128) for b in range(blocks)]
    step_rows = 32

    def norm_back(i, gains):
        at = pl.ds(pl.multiple_of(i * step_rows, step_rows), step_rows)
        v = tok[at, :].astype(jnp.float32)
        r = lax.rsqrt(jnp.mean(v * v, axis=1, keepdims=True) + epsilon)
        gy = []
        for b in range(blocks):
            came = gin_rows[pl.ds(i * step_rows * blocks + b, step_rows, stride=blocks), :]
            gy.append(pre[at, lanes[b]] + came.astype(jnp.bfloat16).astype(jnp.float32))
        scaled = [gy[b] * gain[b] for b in range(blocks)]
        dots = sum(jnp.sum(scaled[b] * v[:, lanes[b]], axis=1, keepdims=True) for b in range(blocks))
        pull = r * r * (dots / width)
        new = []
        for b in range(blocks):
            vb = v[:, lanes[b]]
            gx = r * (scaled[b] - vb * pull)
            gtok_out[at, lanes[b]] = (direct[at, lanes[b]] + gx).astype(jnp.bfloat16)
            new.append(gains[b] + jnp.sum(gy[b] * (vb * r), axis=0, keepdims=True))
        return tuple(new)

    gains = lax.fori_loop(
        0, rows // step_rows, norm_back, tuple(jnp.zeros((1, 128), jnp.float32) for _ in range(blocks))
    )
    for e in range(nq):
        b = block_of(e, nq, blocks)
        small[e] = small_in[e]
        small[e, 0:dims] = m_all[0:dims, b, :]
        small[e, dims : 2 * dims] = k_all[:, b, :]
        small[e, 2 * dims : 2 * dims + 1] = m_all[dims, b : b + 1, :]
        small[e, 2 * dims + 1 : 2 * dims + 2] = gains[b]
    little.start()
    pump()
    little.middle()
    for copy in out:
        copy.wait_send()
    for _ in steps:
        pass
    little.end()


def mix_backward(grid, terms, cuts, gact, x_in, mixed, carry, par, alive, spans, tok, pre, direct, small, collective_id):
    rows, width = gact.shape
    nq, ng = grid.nq, grid.ng
    blocks, dims, few = width // 128, carry.shape[0], 4
    f = jnp.float32
    vm = pl.BlockSpec(memory_space=pltpu.VMEM)
    shapes, parts, outs, scratch, count = scatter_plan(grid, terms, cuts)
    n = len(parts)
    result = pl.pallas_call(
        functools.partial(mix_back_kernel, grid, dims, shapes),
        out_shape=outs
        + [jax.ShapeDtypeStruct((rows, width), jnp.bfloat16), jax.ShapeDtypeStruct(small.shape[1:], f)],
        in_specs=[ANY] * n + [vm] * 11,
        out_specs=[vm] * (n + 2),
        scratch_shapes=[
            pltpu.VMEM((rows * blocks, 128), f),
            pltpu.VMEM((rows * blocks, 128), f),
            pltpu.VMEM((rows, few, blocks, 128), f),
            pltpu.VMEM((nq, dims, blocks, 128), f),
            pltpu.VMEM((dims + 1, blocks, 128), f),
            pltpu.VMEM((dims, blocks, 128), f),
            pltpu.VMEM(small.shape, f),
            pltpu.VMEM((nq - 1,) + small.shape[1:], f),
            pltpu.VMEM((ng - 1,) + small.shape[1:], f),
            pltpu.SemaphoreType.DMA((nq - 1,)),
            pltpu.SemaphoreType.DMA((nq - 1,)),
            pltpu.SemaphoreType.DMA((nq + ng - 2,)),
            pltpu.SemaphoreType.DMA((nq + ng - 2,)),
            pltpu.SemaphoreType.DMA((n, 2)),
            pltpu.SemaphoreType.DMA((count,)),
            pltpu.SemaphoreType.DMA((count,)),
        ]
        + scratch,
        compiler_params=pltpu.CompilerParams(
            collective_id=collective_id, has_side_effects=True, vmem_limit_bytes=62 << 20
        ),
    )(*parts, gact, x_in, mixed, carry, par, alive, spans, tok, pre, direct, small)
    return [v.reshape(-1, t.shape[-1]) for v, t in zip(result, terms)], result[n], result[n + 1]


def rms_forward(values, gain):
    inverse = lax.rsqrt(jnp.mean(values * values, axis=-1, keepdims=True) + epsilon)
    return (values * inverse * gain, inverse)


def rms_backward(grad_out, values, inverse, gain):
    scaled = grad_out * gain
    projection = jnp.mean(scaled * values, axis=-1, keepdims=True)
    grad_in = inverse * (scaled - values * inverse * inverse * projection)
    return (grad_in, jnp.sum(grad_out * values * inverse, axis=0))


def silu_slope(values):
    sigma_v = jax.nn.sigmoid(values)
    return sigma_v * (1.0 + values * (1.0 - sigma_v))


def times(left, pieces):
    return jnp.concatenate(
        [jnp.dot(left, pieces[i], preferred_element_type=jnp.float32) for i in range(pieces.shape[0])], axis=1
    )


def against(left, pieces):
    n = pieces.shape[2]
    return sum(
        lax.dot_general(
            left[:, i * n : i * n + n], pieces[i], (((1,), (1,)), ((), ())), preferred_element_type=jnp.float32
        )
        for i in range(pieces.shape[0])
    )


def over_rows(left, right, count):
    n = right.shape[1] // count
    return jnp.stack(
        [
            lax.dot_general(
                left, right[:, i * n : i * n + n], (((0,), (0,)), ((), ())), preferred_element_type=jnp.float32
            ).astype(jnp.bfloat16)
            for i in range(count)
        ]
    )


def masked_scores(query_blk, key_blk, allowed):
    raw_scores = jnp.einsum("cid,cjd->cij", query_blk, key_blk, preferred_element_type=jnp.float32)
    return jnp.where(allowed, raw_scores, -1e30)


def body(
    tokens,
    starts,
    norm_gain,
    ema_delta,
    ema_alpha,
    ema_beta,
    ema_eta,
    ema_omega,
    mix_weight,
    value_weight,
    qk_affine,
    out_weight,
    ffn_gain,
    ffn_in,
    ffn_out,
    cotangent,
):
    seg_count, row_count, model_width = tokens.shape
    nq, ng = lax.axis_size("seq"), lax.axis_size("seg")
    grid = Grid(nq, ng)
    seq_index, seg_index = lax.axis_index("seq"), lax.axis_index("seg")
    seq_length = row_count * nq
    dims = ema_delta.shape[1]
    zdim = qk_affine.shape[0] * nq * ng // 4
    vdim = value_weight.shape[1] * ng
    token_count = seg_count * row_count
    blocks = model_width // 128

    index = seq_index * ng + seg_index
    mine = norm_gain.shape[0]
    columns = jnp.concatenate(
        [ema_delta.T, ema_alpha.T, ema_beta.T, ema_eta.T, norm_gain[None], ema_omega[None], ffn_gain[None]], axis=0
    ).astype(jnp.float32)
    count = columns.shape[0]
    tile = jnp.zeros((-(-(count + 4) // 8) * 8, 128), jnp.float32)
    tile = lax.dynamic_update_slice(tile, columns, (0, lax.rem(index * mine, 128)))
    part = qk_affine.shape[0]
    tile = lax.dynamic_update_slice(
        tile, qk_affine.astype(jnp.float32)[None], (count + index * part // 128, lax.rem(index * part, 128))
    )

    places = jnp.arange(seq_length, dtype=jnp.int32)
    goes_on = 1.0 - jnp.any(starts[0][None, :] == places[:, None], axis=1).astype(jnp.float32)
    spans = jnp.broadcast_to(jnp.min(goes_on.reshape(nq, row_count), axis=1)[:, None], (nq, 128))
    alive = lax.dynamic_slice_in_dim(goes_on, seq_index * row_count, row_count, 0)
    alive = jnp.broadcast_to(alive[:, None], (row_count, 128))

    tokens_flat = tokens.reshape(token_count, model_width).astype(jnp.float32)
    positions_rows = seq_index * row_count + jnp.arange(row_count, dtype=jnp.int32)
    docs_rows = jnp.sum((starts[:, None, :] <= positions_rows[None, :, None]).astype(jnp.int32), axis=2)
    block_count = token_count // STRETCH
    block_docs = docs_rows.reshape(block_count, STRETCH)
    offsets = jnp.arange(STRETCH)
    allowed = (block_docs[:, :, None] == block_docs[:, None, :]) & (offsets[:, None] >= offsets[None, :])[None]
    mask = allowed.astype(jnp.float32).reshape(token_count, STRETCH)
    tokens_low = tokens.reshape(token_count, model_width)
    weights, forward = mix_forward(
        grid, [mix_weight, value_weight, out_weight, ffn_in, ffn_out], GATHER_CUTS, tokens_low, tile, alive, spans, mask, dims, 0
    )
    mix_full, value_full, out_full, ffn_in_full, ffn_out_full = weights
    (normed_b, active, x_rows, mixed_rows, carry, par, affine, probs, out_one, normed_two_b, result,
     projected, value_pre, attended, hidden_in, hidden_pre, ffn_hidden, ffn_act) = forward
    gain_two = par[4 * dims + 2].reshape(-1)
    update = jax.nn.sigmoid(projected[:, :model_width])
    gate_pre = projected[:, model_width : model_width + zdim + vdim]
    gate_rows = jax.nn.silu(gate_pre)
    shared = gate_rows[:, :zdim]
    reset_gate = gate_rows[:, zdim:]
    values_b = jax.nn.silu(value_pre).astype(jnp.bfloat16)
    scale_q = zdim ** (-0.5)
    query_b = (scale_q * (shared * affine[0] + affine[1])).astype(jnp.bfloat16)
    key_b = (shared * affine[2] + affine[3]).astype(jnp.bfloat16)
    query_blk = query_b.reshape(block_count, STRETCH, zdim)
    key_blk = key_b.reshape(block_count, STRETCH, zdim)
    value_blk = values_b.reshape(block_count, STRETCH, vdim)
    probs = probs.reshape(block_count, STRETCH, STRETCH)
    probs_b = probs.astype(jnp.bfloat16)
    hidden_act = jax.nn.silu(hidden_pre)
    inverse_two = lax.rsqrt(jnp.mean(out_one * out_one, axis=-1, keepdims=True) + epsilon)

    grad_y_b = cotangent.reshape(token_count, model_width)
    grad_ffn_out = over_rows(ffn_act, grad_y_b, ng)
    grad_act = against(grad_y_b, ffn_out_full)
    grad_hidden_b = (grad_act * silu_slope(ffn_hidden)).astype(jnp.bfloat16)
    grad_ffn_in = over_rows(normed_two_b, grad_hidden_b, ng)
    grad_normed_two = against(grad_hidden_b, ffn_in_full)
    grad_norm_two, grad_gain_two = rms_backward(grad_normed_two, out_one, inverse_two, gain_two)
    grad_out_one = grad_y_b.astype(jnp.float32) + grad_norm_two
    grad_update = grad_out_one * (hidden_act - tokens_flat)
    grad_tokens_flat = grad_out_one * (1.0 - update)
    grad_hpre_b = (grad_out_one * update * silu_slope(hidden_pre)).astype(jnp.bfloat16)
    grad_out_weight = over_rows(hidden_in, grad_hpre_b, ng)
    grad_hidden_in = against(grad_hpre_b, out_full)
    grad_att_b = (grad_hidden_in * reset_gate).astype(jnp.bfloat16)
    grad_reset = grad_hidden_in * attended
    grad_att_blk = grad_att_b.reshape(block_count, STRETCH, vdim)
    grad_probs = jnp.einsum("civ,cjv->cij", grad_att_blk, value_blk, preferred_element_type=jnp.float32)
    weighted = jnp.sum(probs * grad_probs, axis=2, keepdims=True)
    grad_scores_b = (probs * (grad_probs - weighted)).astype(jnp.bfloat16)
    grad_query = jnp.einsum("cij,cjd->cid", grad_scores_b, key_blk, preferred_element_type=jnp.float32).reshape(
        token_count, zdim
    )
    grad_key = jnp.einsum("cij,cid->cjd", grad_scores_b, query_blk, preferred_element_type=jnp.float32).reshape(
        token_count, zdim
    )
    grad_values = jnp.einsum("cij,civ->cjv", probs_b, grad_att_blk, preferred_element_type=jnp.float32).reshape(
        token_count, vdim
    )
    grad_qs = grad_query * scale_q
    grad_shared = grad_qs * affine[0] + grad_key * affine[2]
    grad_affine = jnp.stack(
        [
            jnp.sum(grad_qs * shared, axis=0),
            jnp.sum(grad_qs, axis=0),
            jnp.sum(grad_key * shared, axis=0),
            jnp.sum(grad_key, axis=0),
        ]
    )
    grad_gate_pre = jnp.concatenate([grad_shared, grad_reset], axis=1) * silu_slope(gate_pre)
    grad_upre = grad_update * update * (1.0 - update)
    grad_proj_b = jnp.concatenate(
        [grad_upre.astype(jnp.bfloat16), grad_gate_pre.astype(jnp.bfloat16), grad_hpre_b], axis=1
    )
    grad_mix = over_rows(active, grad_proj_b, ng)
    grad_active_b = against(grad_proj_b, mix_full).astype(jnp.bfloat16)
    grad_vpre_b = (grad_values * silu_slope(value_pre)).astype(jnp.bfloat16)
    grad_value = over_rows(normed_b, grad_vpre_b, ng)
    grad_normed = against(grad_vpre_b, value_full)

    small = jnp.concatenate(
        [jnp.zeros((blocks, 2 * dims + 2, 128), jnp.float32), grad_gain_two.reshape(blocks, 1, 128)], axis=1
    )
    if nq != blocks:
        small = jnp.take(small, np.arange(nq) * blocks // nq, axis=0)
    small = jnp.concatenate([small, jnp.broadcast_to(grad_affine[None], (nq, 4, 128))], axis=1)
    small = jnp.pad(small, ((0, 0), (0, -small.shape[1] % 8), (0, 0)))
    (g_ffn_out, g_ffn_in, g_out, g_mix, g_value), grad_tokens, sums = mix_backward(
        grid, [grad_ffn_out, grad_ffn_in, grad_out_weight, grad_mix, grad_value], SCATTER_CUTS, grad_active_b, x_rows,
        mixed_rows, carry, par, alive, spans, tokens_low, grad_normed, grad_tokens_flat, small, 1
    )
    return (
        result.reshape(seg_count, row_count, model_width),
        grad_tokens.reshape(seg_count, row_count, model_width),
        *small_outputs(sums, index, dims, ema_delta, ema_alpha, ema_beta, ema_eta, mine, part, g_mix, g_value, g_out, g_ffn_in, g_ffn_out),
    )


def small_outputs(sums, index, dims, ema_delta, ema_alpha, ema_beta, ema_eta, mine, part, g_mix, g_value, g_out, g_ffn_in, g_ffn_out):
    own = lax.dynamic_slice_in_dim(sums, lax.rem(index * mine, 128), mine, 1)
    m_sum, k_sum = own[:dims].T, own[dims : 2 * dims].T
    vectors = own[2 * dims : 2 * dims + 3]
    delta, alpha, beta, eta = (v.astype(jnp.float32) for v in (ema_delta, ema_alpha, ema_beta, ema_eta))
    damping, decay = jax.nn.sigmoid(delta), jax.nn.sigmoid(alpha)
    g_keep = damping * beta * eta * k_sum
    grad_eta = damping * beta * m_sum
    grad_beta = damping * eta * m_sum
    grad_alpha = -g_keep * damping * decay * (1.0 - decay)
    grad_delta = (beta * eta * m_sum - g_keep * decay) * damping * (1.0 - damping)
    grad_affine = lax.dynamic_slice(
        sums, (2 * dims + 3 + index * part // 128, lax.rem(index * part, 128)), (1, part)
    ).reshape(-1)
    return (vectors[1], grad_delta, grad_alpha, grad_beta, grad_eta, vectors[0],
            g_mix, g_value, grad_affine, g_out, vectors[2], g_ffn_in, g_ffn_out)


def solution(mesh):
    placed = (
        P("seg", "seq", None),
        P("seg", None),
        P(("seq", "seg")),
        P(("seq", "seg"), None),
        P(("seq", "seg"), None),
        P(("seq", "seg"), None),
        P(("seq", "seg"), None),
        P(("seq", "seg")),
        P("seq", "seg"),
        P("seq", "seg"),
        P(("seq", "seg")),
        P("seq", "seg"),
        P(("seq", "seg")),
        P("seq", "seg"),
        P("seq", "seg"),
        P("seg", "seq", None),
    )
    return jax.shard_map(
        body,
        mesh=mesh,
        in_specs=placed,
        out_specs=(P("seg", "seq", None),) * 2 + placed[2:15],
        check_vma=False,
    )
```

```python
import functools
import math

import jax
import jax.numpy as jnp
import numpy as np
from jax import lax
from jax.experimental import pallas as pl
from jax.experimental.pallas import tpu as pltpu
from jax.sharding import PartitionSpec as P

STRETCH = 128
epsilon = 1e-05
GATHER_CUTS = (4, 4, 4, 4, 8)
SCATTER_CUTS = (4, 4, 2, 2, 4)

MESH = pl.DeviceIdType.MESH
ANY = pl.BlockSpec(memory_space=pl.ANY)


class Grid:
    def __init__(self, nq, ng):
        self.nq, self.ng = nq, ng
        self.nz = math.gcd(nq, 4)
        self.nx = nq // self.nz
        self.nc = math.gcd(ng, 2)
        self.ny = ng // self.nc

    def here(self):
        s, g = lax.axis_index("seq"), lax.axis_index("seg")
        return s // self.nx, lax.rem(s, self.nx), g // self.nc, lax.rem(g, self.nc)

    def peer(self, axis, d):
        z, x, y, c = self.here()
        if axis == "z":
            z = lax.rem(z + d, self.nz)
        if axis == "x":
            x = lax.rem(x + d, self.nx)
        if axis == "y":
            y = lax.rem(y + d, self.ny)
        if axis == "c":
            c = lax.rem(c + d, self.nc)
        return z, x, y, c

    def size(self, axis):
        return {"z": self.nz, "x": self.nx, "y": self.ny, "c": self.nc}[axis]

    def device(self, place):
        z, x, y, c = place
        return {"seq": z * self.nx + x, "seg": y * self.nc + c}

    def peers(self, axes):
        return [self.peer(a, d) for a in axes for d in range(1, self.size(a))]


def enter(grid, peers):
    barrier = pltpu.get_barrier_semaphore()
    for place in peers:
        pl.semaphore_signal(barrier, inc=1, device_id=grid.device(place), device_id_type=MESH)
    pl.semaphore_wait(barrier, len(peers))


class Sems:
    def __init__(self, send, recv):
        self.send, self.recv, self.used = send, recv, 0

    def take_index(self):
        self.used += 1
        return self.used - 1

    def take(self):
        i = self.take_index()
        return self.send.at[i], self.recv.at[i]


def gather_steps(grid, shapes, shards, wholes, own_sem, sems):
    n = len(shapes)
    z, x, y, c = grid.here()
    pending = []

    def push(src, dst, axis, d, arrives):
        s, r = sems.take()
        device = grid.device(grid.peer(axis, d))
        copy = pltpu.make_async_remote_copy(src, dst, s, r, device_id=device, device_id_type=MESH)
        copy.start()
        pending.append(copy)
        there = pltpu.make_async_remote_copy(arrives, arrives, s, r, device_id=device, device_id_type=MESH)
        return there.wait_recv

    def back(axis, d):
        return dict(zip("zxyc", grid.peer(axis, grid.size(axis) - d)))[axis]

    owns = []
    chunks = [(i, q) for i in range(n) for q in range(shapes[i][0] // 2)]
    core_waits = {}

    def core(k, view):
        core_waits.setdefault(k, []).extend(
            push(view(c), view(c), "c", d, view(back("c", d))) for d in range(1, grid.nc)
        )

    def stage_z(k, i, h):
        w = wholes[i]
        return [
            push(shards[i].at[h], w.at[y, c, z, x, h], "z", d, w.at[y, c, back("z", d), x, h])
            for d in range(1, grid.nz)
        ]

    def stage_two(k, i, h):
        w = wholes[i]
        src = w.at[y, c, :, x, h]
        if h % 2 == 0:
            waits = [push(src, src, "x", d, w.at[y, c, :, back("x", d), h]) for d in range(1, grid.nx)]
        else:
            waits = [push(src, src, "y", d, w.at[back("y", d), c, :, x, h]) for d in range(1, grid.ny)]
        core(k, lambda cc: w.at[y, cc, :, x, h])
        return waits

    def stage_three(k, i, h):
        w = wholes[i]
        if h % 2 == 0:
            src = w.at[y, c, :, :, h]
            waits = [push(src, src, "y", d, w.at[back("y", d), c, :, :, h]) for d in range(1, grid.ny)]
            for d in range(1, grid.nx):
                core(k, lambda cc: w.at[y, cc, :, back("x", d), h])
            return waits
        src = w.at[:, c, :, x, h]
        waits = [push(src, src, "x", d, w.at[:, c, :, back("x", d), h]) for d in range(1, grid.nx)]
        for d in range(1, grid.ny):
            core(k, lambda cc: w.at[back("y", d), cc, :, x, h])
        return waits

    def stage_last(k, i, h):
        w = wholes[i]
        if h % 2 == 0:
            for d in range(1, grid.ny):
                core(k, lambda cc: w.at[back("y", d), cc, :, :, h])
        else:
            for d in range(1, grid.nx):
                core(k, lambda cc: w.at[:, cc, :, back("x", d), h])

    def finish(waits):
        for wait in waits:
            wait()

    got = {}
    total = len(chunks)
    for t in range(-1, total + 3):
        if t == 0:
            for i in range(n):
                copy = pltpu.make_async_copy(shards[i], wholes[i].at[y, c, z, x], own_sem.at[i])
                copy.start()
                owns.append(copy)
        if 0 <= t < total:
            i, q = chunks[t]
            if q == 0:
                owns[i].wait()
            for h in (0, 1):
                finish(got[t, h])
                got[t, h] = stage_two(t, i, 2 * q + h)
        if t + 1 < total:
            i, q = chunks[t + 1]
            for h in (0, 1):
                got[t + 1, h] = stage_z(t + 1, i, 2 * q + h)
        k = t - 1
        if 0 <= k < total:
            i, q = chunks[k]
            for h in (0, 1):
                finish(got[k, h])
                got[k, h] = stage_three(k, i, 2 * q + h)
        k = t - 2
        if 0 <= k < total:
            i, q = chunks[k]
            for h in (0, 1):
                finish(got[k, h])
                stage_last(k, i, 2 * q + h)
        k = t - 3
        done = []
        if 0 <= k < total:
            finish(core_waits[k])
            i, q = chunks[k]
            if q + 1 == shapes[i][0] // 2:
                done = [i]
        if t == total + 2:
            for copy in pending:
                copy.wait_send()
        yield done


def gather_plan(grid, shards, cuts):
    shapes, args, outs = [], [], []
    for w, q in zip(shards, cuts):
        k, n = w.shape
        q = max(1, min(q, k // 32))
        shapes.append((2 * q, k // (2 * q), n))
        args.append(w.reshape(shapes[-1]))
        outs.append(jax.ShapeDtypeStruct((grid.ny, grid.nc, grid.nz, grid.nx) + shapes[-1], w.dtype))
    per = (grid.nz - 1) + (grid.nx - 1) + (grid.ny - 1) + (grid.nc - 1) * (grid.nx + grid.ny)
    count = sum(s[0] for s in shapes) * per
    return shapes, args, outs, count


def scatter_steps(grid, shapes, terms, sums, scratch, own_sem, sems, ready=None):
    n = len(shapes)
    nz, nx, ny, nc = grid.nz, grid.nx, grid.ny, grid.nc
    own = [scratch[7 * i] for i in range(n)]
    one = [scratch[7 * i + 1] for i in range(n)]
    two_a = [scratch[7 * i + 2] for i in range(n)]
    two_b = [scratch[7 * i + 3] for i in range(n)]
    three_a = [scratch[7 * i + 4] for i in range(n)]
    three_b = [scratch[7 * i + 5] for i in range(n)]
    four = [scratch[7 * i + 6] for i in range(n)]
    z, x, y, c = grid.here()
    pending = []
    around = {(axis, d): grid.peer(axis, d) for axis in "zxyc" for d in range(1, grid.size(axis))}
    devices = {key: grid.device(place) for key, place in around.items()}

    def push(ends, axis, d):
        k = sems.take_index()

        def copy():
            return pltpu.make_async_remote_copy(
                *ends(), sems.send.at[k], sems.recv.at[k], device_id=devices[axis, d], device_id_type=MESH
            )

        copy().start()
        pending.append(lambda: copy().wait_send())
        return lambda: copy().wait_recv()

    def to(axis, d):
        return dict(zip("zxyc", around[axis, d]))[axis]

    def finish(waits):
        for wait in waits:
            wait()

    assert nc == 2

    def stage_one(i, q, h):
        return [push(lambda: (terms[i].at[:, to("c", 1), :, :, 2 * q + h], one[i].at[q, h]), "c", 1)]

    def load_own(i, q, h):
        def load():
            return pltpu.make_async_copy(terms[i].at[:, c, :, :, 2 * q + h], own[i].at[h], own_sem.at[i, h])

        load().start()
        return [lambda: load().wait()]

    def stage_two(i, q, h):
        mine = one[i].at[q, h]

        @pl.loop(0, ny * nz)
        def _(ab):
            a, b = ab // nz, lax.rem(ab, nz)
            for e in range(nx):
                mine[a, b, e] += own[i][h, a, b, e]

        if h == 0:
            return [
                push(lambda d=d: (one[i].at[q, h, to("y", d)], two_a[i].at[q, d - 1]), "y", d) for d in range(1, ny)
            ]
        return [
            push(lambda d=d: (one[i].at[q, h, :, :, to("x", d)], two_b[i].at[q, d - 1]), "x", d) for d in range(1, nx)
        ]

    def stage_three(i, q, h):
        mine = one[i].at[q, h]
        if h == 0:

            @pl.loop(0, nz)
            def _(b):
                for e in range(nx):
                    total = mine[y, b, e]
                    for d in range(ny - 1):
                        total += two_a[i][q, d, b, e]
                    mine[y, b, e] = total

            return [
                push(lambda d=d: (one[i].at[q, h, y, :, to("x", d)], three_a[i].at[q, d - 1]), "x", d)
                for d in range(1, nx)
            ]

        @pl.loop(0, nz)
        def _(b):
            for a in range(ny):
                total = mine[a, b, x]
                for d in range(nx - 1):
                    total += two_b[i][q, d, a, b]
                mine[a, b, x] = total

        return [
            push(lambda d=d: (one[i].at[q, h, to("y", d), :, x], three_b[i].at[q, d - 1]), "y", d)
            for d in range(1, ny)
        ]

    def stage_four(i, q, h):
        mine = one[i].at[q, h]
        came = three_a[i] if h == 0 else three_b[i]

        @pl.loop(0, nz)
        def _(b):
            total = mine[y, b, x]
            for d in range((nx if h == 0 else ny) - 1):
                total += came[q, d, b]
            mine[y, b, x] = total

        return [
            push(lambda d=d: (one[i].at[q, h, y, to("z", d), x], four[i].at[q, h, d - 1]), "z", d)
            for d in range(1, nz)
        ]

    def stage_last(i, q, h):
        total = one[i][q, h, y, z, x].astype(jnp.float32)
        for d in range(nz - 1):
            total += four[i][q, h, d].astype(jnp.float32)
        sums[i][2 * q + h] = total

    stages = [stage_one, stage_two, stage_three, stage_four, stage_last]
    chunks = [(i, q) for i in range(n) for q in range(shapes[i][0] // 2)]
    waits = {}
    total = len(chunks)
    at = [0] * len(stages)
    yield
    while at[-1] < total:
        there = total if ready is None else sum(1 for i, q in chunks if i < ready())
        before = [there] + at[:-1]
        fresh = None
        for j, stage in enumerate(stages):
            if at[j] < before[j]:
                i, q = chunks[at[j]]
                for h in (0, 1):
                    if j:
                        finish(waits[i, q, h])
                    waits[i, q, h] = stage(i, q, h)
                if j == 0:
                    fresh = i, q
                at[j] += 1
            if j == 1 and fresh:
                for h in (0, 1):
                    waits[fresh[0], fresh[1], h] += load_own(*fresh, h)
        if at[-1] == total:
            finish(pending)
        yield


class SmallSum:
    def __init__(self, grid, small, total, seq_in, seg_in, send, recv):
        self.grid, self.small, self.total = grid, small, total
        self.seq_in, self.seg_in, self.send, self.recv = seq_in, seg_in, send, recv
        self.seq_peer, self.seg_peer = small_peers(grid)
        self.copies = []

    def push(self, src, dst, device):
        i = len(self.copies)
        copy = pltpu.make_async_remote_copy(
            src, dst, self.send.at[i], self.recv.at[i], device_id=device, device_id_type=MESH
        )
        copy.start()
        self.copies.append(copy)

    def start(self):
        nq, sq = self.grid.nq, lax.axis_index("seq")
        for d in range(1, nq):
            self.push(self.small.at[lax.rem(sq + d, nq)], self.seq_in.at[d - 1], self.seq_peer[d - 1])

    def middle(self):
        nq, ng = self.grid.nq, self.grid.ng
        total = self.small[lax.axis_index("seq")]
        for d in range(1, nq):
            self.copies[d - 1].wait_recv()
            total += self.seq_in[d - 1]
        self.total[...] = total
        for d in range(1, ng):
            self.push(self.total, self.seg_in.at[d - 1], self.seg_peer[d - 1])

    def end(self):
        nq, ng = self.grid.nq, self.grid.ng
        total = self.total[...]
        for d in range(1, ng):
            self.copies[nq + d - 2].wait_recv()
            total += self.seg_in[d - 1]
        for copy in self.copies:
            copy.wait_send()
        self.total[...] = total


def small_peers(grid):
    nq, ng = grid.nq, grid.ng
    s, g = lax.axis_index("seq"), lax.axis_index("seg")
    return (
        [{"seq": lax.rem(s + d, nq), "seg": g} for d in range(1, nq)],
        [{"seq": s, "seg": lax.rem(g + d, ng)} for d in range(1, ng)],
    )


def meet(peers):
    barrier = pltpu.get_barrier_semaphore()
    for place in peers:
        pl.semaphore_signal(barrier, inc=1, device_id=place, device_id_type=MESH)
    pl.semaphore_wait(barrier, len(peers))


def scatter_plan(grid, terms, cuts):
    nz, nx, ny = grid.nz, grid.nx, grid.ny
    shapes, outs, scratch = [], [], []
    for t, q in zip(terms, cuts):
        _, rows, n = t.shape
        if n < 128:
            rows, n = rows * n // 128, 128
        k = rows // grid.nq
        q = max(1, min(q, k // 32))
        kh = k // (2 * q)
        shapes.append((2 * q, kh, n))
        outs.append(jax.ShapeDtypeStruct((2 * q, kh, n), jnp.float32))
        b = t.dtype
        scratch += [
            pltpu.VMEM((2, ny, nz, nx, kh, n), b),
            pltpu.VMEM((q, 2, ny, nz, nx, kh, n), b),
            pltpu.VMEM((q, max(ny - 1, 1), nz, nx, kh, n), b),
            pltpu.VMEM((q, max(nx - 1, 1), ny, nz, kh, n), b),
            pltpu.VMEM((q, max(nx - 1, 1), nz, kh, n), b),
            pltpu.VMEM((q, max(ny - 1, 1), nz, kh, n), b),
            pltpu.VMEM((q, 2, max(nz - 1, 1), kh, n), b),
        ]
    per = (grid.nc - 1) + (nx - 1) + (ny - 1) + (nz - 1)
    count = per * sum(s[0] for s in shapes)
    return shapes, outs, scratch, count


def block_of(e, nq, blocks):
    return e * blocks // nq


def mix_kernel(grid, width, dims, shapes, *refs):
    n = len(shapes)
    shards, refs = refs[:n], refs[n:]
    tok, tile, alive, spans, mask, *refs = refs
    wholes, refs = refs[:n], refs[n:]
    (normed_out, active_out, x_out, mixed_out, carry_out, par_out, aff_out, probs_out, out_one_out, two_out, layer_out,
     proj_hbm, value_hbm, att_hbm, hin_hbm, hpre_hbm, ffn_hbm, act_hbm,
     proj, value_pre, att, hin, hpre, ffn_pre, act, values,
     tiles, table, bound, sends_t, recv_t, sends_b, recv_b, own_sem, flush_sem, load_sem, send, recv,
     *slots) = refs
    nq, ng = grid.nq, grid.ng
    rows = tok.shape[0]
    blocks = width // 128
    s = lax.axis_index("seq")
    seq_peer, seg_peer = small_peers(grid)
    meet(seq_peer + seg_peer)
    steps = gather_steps(grid, shapes, shards, wholes, own_sem, Sems(send, recv))

    done = set()

    def pump(count=1):
        for _ in range(count):
            done.update(next(steps, ()))

    copies = []
    for d in range(1, ng):
        copies.append(pltpu.make_async_remote_copy(
            tile, tiles.at[d - 1], sends_t.at[d - 1], recv_t.at[d - 1],
            device_id=seg_peer[d - 1], device_id_type=MESH))
        copies[-1].start()
    pump()
    for copy in copies:
        copy.wait_recv()
    lanes = tile[...]
    for d in range(1, ng):
        lanes += tiles[d - 1]
    table[s] = lanes
    for d in range(1, nq):
        copies.append(pltpu.make_async_remote_copy(
            table.at[s], table.at[s], sends_t.at[ng + d - 2], recv_t.at[ng + d - 2],
            device_id=seq_peer[d - 1], device_id_type=MESH))
        copies[-1].start()
    for d in range(1, nq):
        came = table.at[lax.rem(s + nq - d, nq)]
        pltpu.make_async_remote_copy(
            came, came, sends_t.at[ng + d - 2], recv_t.at[ng + d - 2],
            device_id=seq_peer[d - 1], device_id_type=MESH).wait_recv()
    count = 4 * dims + 3
    for b in range(blocks):
        mine = [e for e in range(nq) if block_of(e, nq, blocks) == b]
        whole = table[mine[0], 0:count]
        for e in mine[1:]:
            whole += table[e, 0:count]
        par_out[:, b, :] = whole
    aff = table[0, count : count + 4]
    for e in range(1, nq):
        aff += table[e, count : count + 4]
    aff_out[...] = aff

    pump()

    gain = [par_out[4 * dims, b : b + 1, :] for b in range(blocks)]
    step_rows = 32

    @pl.loop(0, rows // step_rows)
    def _(i):
        at = pl.ds(pl.multiple_of(i * step_rows, step_rows), step_rows)
        v = tok[at, :].astype(jnp.float32)
        r = lax.rsqrt(jnp.mean(v * v, axis=1, keepdims=True) + epsilon)
        for b in range(blocks):
            lane = slice(b * 128, b * 128 + 128)
            n = (v[:, lane] * r * gain[b]).astype(jnp.bfloat16)
            normed_out[at, lane] = n
            x_out[pl.ds(i * step_rows * blocks + b, step_rows, stride=blocks), :] = n.astype(jnp.float32)

    damping = [jax.nn.sigmoid(par_out[j]) for j in range(dims)]
    keep = [1.0 - damping[j] * jax.nn.sigmoid(par_out[dims + j]) for j in range(dims)]
    weight = [damping[j] * par_out[2 * dims + j] * par_out[3 * dims + j] for j in range(dims)]
    omega = par_out[4 * dims + 1]

    def row(ref, p):
        return ref[pl.ds(pl.multiple_of(p * blocks, blocks), blocks), :]

    def first_pass(p, state):
        x, a = row(x_out, p), alive[pl.ds(p, 1), :]
        return tuple(keep[j] * (state[j] * a) + x for j in range(dims))

    zero = tuple(jnp.zeros((blocks, 128), jnp.float32) for _ in range(dims))
    ends = lax.fori_loop(0, rows, first_pass, zero, unroll=4)
    for j in range(dims):
        bound[s, j] = ends[j]
    out = []
    for d in range(1, nq):
        out.append(pltpu.make_async_remote_copy(
            bound.at[s], bound.at[s], sends_b.at[d - 1], recv_b.at[d - 1],
            device_id=seq_peer[d - 1], device_id_type=MESH))
        out[-1].start()
    pump()
    for d in range(1, nq):
        came = bound.at[lax.rem(s + nq - d, nq)]
        pltpu.make_async_remote_copy(
            came, came, sends_b.at[d - 1], recv_b.at[d - 1],
            device_id=seq_peer[d - 1], device_id_type=MESH).wait_recv()
    for j in range(dims):
        through = power(keep[j], rows)
        state = jnp.zeros((blocks, 128), jnp.float32)
        for e in range(nq - 1):
            later = through * spans[e : e + 1, :] * state + bound[e, j]
            state = jnp.where(e < s, later, state)
        carry_out[j] = state

    def second_pass(p, state):
        x, a = row(x_out, p), alive[pl.ds(p, 1), :]
        state = tuple(keep[j] * (state[j] * a) + x for j in range(dims))
        sums = [omega * x] + [weight[j] * state[j] for j in range(dims)]
        while len(sums) > 1:
            sums = [sum(sums[k : k + 2][1:], sums[k]) for k in range(0, len(sums), 2)]
        mixed_out[pl.ds(pl.multiple_of(p * blocks, blocks), blocks), :] = sums[0]
        return state

    state = tuple(carry_out[j] for j in range(dims))
    for half in range(2):
        state = lax.fori_loop(half * rows // 2, (half + 1) * rows // 2, second_pass, state, unroll=4)
        pump()
    for b in range(blocks):
        m = mixed_out[pl.ds(b, rows, stride=blocks), :]
        active_out[:, b * 128 : b * 128 + 128] = (m * jax.nn.sigmoid(m)).astype(jnp.bfloat16)
    for copy in copies + out:
        copy.wait_send()

    flushes = []

    def flush(ref, hbm):
        copy = pltpu.make_async_copy(ref, hbm, flush_sem.at[len(flushes)])
        copy.start()
        flushes.append(copy)

    def pieces(i):
        while i not in done:
            pump()

        def fetch(g):
            return pltpu.make_async_copy(
                wholes[i].at[g // grid.nc, g % grid.nc], slots[i].at[g % 2], load_sem.at[i, g % 2]
            )

        fetch(0).start()
        for g in range(grid.ng):
            if g + 1 < grid.ng:
                fetch(g + 1).start()
            fetch(g).wait()
            piece = slots[i][g % 2]
            wide = piece.shape[-1]
            yield g, slice(g * wide, g * wide + wide), piece.reshape(-1, wide)
            if g % 2:
                pump()

    block_rows = 32
    zdim = aff_out.shape[1]
    vdim = value_pre.shape[1]
    first_gate, first_reset, first_cand = width, width + zdim, width + zdim + vdim
    dot = functools.partial(jnp.dot, preferred_element_type=jnp.float32)

    def by_rows(count=rows, each=block_rows):
        def wrap(f):
            pl.loop(0, count // each)(lambda i: f(pl.ds(pl.multiple_of(i * each, each), each)))

        return wrap

    for g, cols, piece in pieces(0):
        proj[:, cols] = dot(active_out[...], piece)
    flush(proj, proj_hbm)

    scale_q = zdim**-0.5
    near = []
    for r in range(rows // STRETCH):
        at = slice(r * STRETCH, r * STRETCH + STRETCH)
        gate = proj[at, first_gate:first_reset]
        shared = gate * jax.nn.sigmoid(gate)
        query = (scale_q * (shared * aff_out[0:1] + aff_out[1:2])).astype(jnp.bfloat16)
        key = (shared * aff_out[2:3] + aff_out[3:4]).astype(jnp.bfloat16)
        scores = lax.dot_general(query, key, (((1,), (1,)), ((), ())), preferred_element_type=jnp.float32)
        scores = jnp.where(mask[at, :] > 0.0, scores, -1e30)
        expo = jnp.exp(scores - jnp.max(scores, axis=1, keepdims=True))
        probs = expo / jnp.sum(expo, axis=1, keepdims=True)
        probs_out[at, :] = probs
        near.append(probs.astype(jnp.bfloat16))

    for g, cols, piece in pieces(1):
        pre = dot(normed_out[...], piece)
        value_pre[:, cols] = pre
        values[:, cols] = (pre * jax.nn.sigmoid(pre)).astype(jnp.bfloat16)
    flush(value_pre, value_hbm)
    for r in range(rows // STRETCH):
        at = slice(r * STRETCH, r * STRETCH + STRETCH)
        att[at, :] = dot(near[r], values[at, :])

    @by_rows()
    def _(at):
        gate = proj[at, first_reset:first_cand]
        hin[at, :] = (att[at, :] * (gate * jax.nn.sigmoid(gate))).astype(jnp.bfloat16)

    flush(att, att_hbm)
    flush(hin, hin_hbm)

    for g, cols, piece in pieces(2):
        hpre[:, cols] = proj[:, first_cand + cols.start : first_cand + cols.stop] + dot(hin[...], piece)
    flush(hpre, hpre_hbm)

    gain_two = [par_out[4 * dims + 2, b : b + 1, :] for b in range(blocks)]

    @by_rows()
    def _(at):
        v = tok[at, :].astype(jnp.float32)
        h = hpre[at, :]
        one = v + jax.nn.sigmoid(proj[at, 0:width]) * (h * jax.nn.sigmoid(h) - v)
        out_one_out[at, :] = one
        r = lax.rsqrt(jnp.mean(one * one, axis=1, keepdims=True) + epsilon)
        for b in range(blocks):
            lane = slice(b * 128, b * 128 + 128)
            two_out[at, lane] = (one[:, lane] * r * gain_two[b]).astype(jnp.bfloat16)

    for g, cols, piece in pieces(3):
        pre = dot(two_out[...], piece)
        ffn_pre[:, cols] = pre.astype(jnp.bfloat16)
        act[:, cols] = (pre * jax.nn.sigmoid(pre)).astype(jnp.bfloat16)
    flush(ffn_pre, ffn_hbm)
    flush(act, act_hbm)
    for g, cols, piece in pieces(4):
        layer_out[:, cols] = (out_one_out[:, cols] + dot(act[...], piece)).astype(jnp.bfloat16)
    for _ in steps:
        pass
    for copy in flushes:
        copy.wait()


def power(v, n):
    result = None
    while n:
        if n & 1:
            result = v if result is None else result * v
        n >>= 1
        if n:
            v = v * v
    return result


def mix_forward(grid, weights, cuts, tok, tile, alive, spans, mask, dims, collective_id):
    rows, width = tok.shape
    nq, ng = grid.nq, grid.ng
    blocks = width // 128
    f = jnp.float32
    vm = pl.BlockSpec(memory_space=pltpu.VMEM)
    shapes, shards, outs, count = gather_plan(grid, weights, cuts)
    n = len(shards)
    vdim, fdim, proj_dim = weights[1].shape[1] * ng, weights[3].shape[1] * ng, weights[0].shape[1] * ng
    low = jnp.bfloat16
    kept = [
        ((rows, proj_dim), f),
        ((rows, vdim), f),
        ((rows, vdim), f),
        ((rows, vdim), low),
        ((rows, width), f),
        ((rows, fdim), low),
        ((rows, fdim), low),
    ]
    local = [
        ((rows, width), low),
        ((rows, width), low),
        ((rows * blocks, 128), f),
        ((rows * blocks, 128), f),
        ((dims, blocks, 128), f),
        ((4 * dims + 3, blocks, 128), f),
        ((4, 128), f),
        ((rows, STRETCH), f),
        ((rows, width), f),
        ((rows, width), low),
        ((rows, width), low),
    ]
    result = pl.pallas_call(
        functools.partial(mix_kernel, grid, width, dims, shapes),
        out_shape=outs + [jax.ShapeDtypeStruct(*v) for v in local + kept],
        in_specs=[ANY] * n + [vm] * 5,
        out_specs=[ANY] * n + [vm] * len(local) + [ANY] * len(kept),
        scratch_shapes=[pltpu.VMEM(*v) for v in kept]
        + [
            pltpu.VMEM((rows, vdim), low),
            pltpu.VMEM((ng - 1,) + tile.shape, f),
            pltpu.VMEM((nq,) + tile.shape, f),
            pltpu.VMEM((nq, dims, blocks, 128), f),
            pltpu.SemaphoreType.DMA((nq + ng - 2,)),
            pltpu.SemaphoreType.DMA((nq + ng - 2,)),
            pltpu.SemaphoreType.DMA((nq - 1,)),
            pltpu.SemaphoreType.DMA((nq - 1,)),
            pltpu.SemaphoreType.DMA((n,)),
            pltpu.SemaphoreType.DMA((len(kept),)),
            pltpu.SemaphoreType.DMA((n, 2)),
            pltpu.SemaphoreType.DMA((count,)),
            pltpu.SemaphoreType.DMA((count,)),
        ]
        + [pltpu.VMEM((2,) + o.shape[2:], o.dtype) for o in outs],
        compiler_params=pltpu.CompilerParams(
            collective_id=collective_id, has_side_effects=True, vmem_limit_bytes=60 << 20
        ),
    )(*shards, tok, tile, alive, spans, mask)
    return result[:n], result[n:]


def scan_back(grid, dims, g_rows, x_in, mixed, carry, par, alive, spans, gin_rows, before, bound, sends_b, recv_b,
              m_all, k_all, seq_peer, s, pump):
    nq = grid.nq
    blocks = carry.shape[1]
    rows = g_rows.shape[0] // blocks

    @pl.loop(0, rows * blocks // 64)
    def _(i):
        at = pl.ds(pl.multiple_of(i * 64, 64), 64)
        g_rows[at, :] = g_rows[at, :] * silu_slope(mixed[at, :])

    damping = [jax.nn.sigmoid(par[j]) for j in range(dims)]
    keep = [1.0 - damping[j] * jax.nn.sigmoid(par[dims + j]) for j in range(dims)]
    weight = [damping[j] * par[2 * dims + j] * par[3 * dims + j] for j in range(dims)]
    omega = par[4 * dims + 1]

    def row(ref, p):
        return ref[pl.ds(pl.multiple_of(p * blocks, blocks), blocks), :]

    def first_pass(i, flow):
        p = rows - 1 - i
        gp, a = row(g_rows, p), alive[pl.ds(p, 1), :]
        return tuple(keep[j] * (a * (gp + flow[j])) for j in range(dims))

    zero = jnp.zeros((blocks, 128), jnp.float32)
    ends = lax.fori_loop(0, rows, first_pass, (zero,) * dims, unroll=4)
    for j in range(dims):
        bound[s, j] = ends[j]
    def sent(d):
        return pltpu.make_async_remote_copy(
            bound.at[s], bound.at[s], sends_b.at[d - 1], recv_b.at[d - 1],
            device_id=seq_peer[d - 1], device_id_type=MESH)

    for d in range(1, nq):
        sent(d).start()
    pump()
    for d in range(1, nq):
        came = bound.at[lax.rem(s + nq - d, nq)]
        pltpu.make_async_remote_copy(
            came, came, sends_b.at[d - 1], recv_b.at[d - 1],
            device_id=seq_peer[d - 1], device_id_type=MESH).wait_recv()
    flow_in = []
    for j in range(dims):
        through = power(keep[j], rows)
        flow = zero
        for e in range(nq - 1, 0, -1):
            later = through * spans[e : e + 1, :] * flow + bound[e, j]
            flow = jnp.where(e > s, later, flow)
        flow_in.append(flow)

    few = before.shape[1]
    for j0 in range(0, dims, few):
        js = range(j0, j0 + few)

        def ahead(p, state):
            x, a = row(x_in, p), alive[pl.ds(p, 1), :]
            for t in range(few):
                before[p, t] = state[t]
            return tuple(keep[j] * (state[t] * a) + x for t, j in enumerate(js))

        lax.fori_loop(0, rows, ahead, tuple(carry[j] for j in js), unroll=4)
        if j0:
            pump()

        def back(i, held):
            flow, m_sum, k_sum, om_sum = held
            p = rows - 1 - i
            at = pl.ds(pl.multiple_of(p * blocks, blocks), blocks)
            gp, x, a = g_rows[at, :], x_in[at, :], alive[pl.ds(p, 1), :]
            total = omega * gp if j0 == 0 else gin_rows[at, :]
            if j0 == 0:
                om_sum = om_sum + gp * x
            new_flow, new_m, new_k = [], [], []
            for t, j in enumerate(js):
                c = gp + flow[t]
                ac = a * c
                total = total + weight[j] * c
                new_flow.append(keep[j] * ac)
                new_m.append(m_sum[t] + c * x)
                new_k.append(k_sum[t] + ac * before[p, t])
            gin_rows[at, :] = total
            return tuple(new_flow), tuple(new_m), tuple(new_k), om_sum

        zeros = (zero,) * few
        _, m_sum, k_sum, om_sum = lax.fori_loop(
            0, rows, back, (tuple(flow_in[j] for j in js), zeros, zeros, zero), unroll=4
        )
        for t, j in enumerate(js):
            m_all[j] = m_sum[t]
            k_all[j] = k_sum[t]
        if j0 == 0:
            m_all[dims] = om_sum
        pump()
    for d in range(1, nq):
        sent(d).wait_send()


def norm_back(par, dims, tok, pre, direct, gin_rows, gtok_out, row_sums):
    rows, width = tok.shape
    blocks = width // 128
    gain = [par[4 * dims, b : b + 1, :] for b in range(blocks)]
    lanes = [slice(b * 128, b * 128 + 128) for b in range(blocks)]
    step_rows = 32

    def some(i, gains):
        at = pl.ds(pl.multiple_of(i * step_rows, step_rows), step_rows)
        v = tok[at, :].astype(jnp.float32)
        r = lax.rsqrt(jnp.mean(v * v, axis=1, keepdims=True) + epsilon)
        gy = []
        for b in range(blocks):
            came = gin_rows[pl.ds(i * step_rows * blocks + b, step_rows, stride=blocks), :]
            gy.append(pre[at, lanes[b]] + came.astype(jnp.bfloat16).astype(jnp.float32))
        scaled = [gy[b] * gain[b] for b in range(blocks)]
        dots = sum(jnp.sum(scaled[b] * v[:, lanes[b]], axis=1, keepdims=True) for b in range(blocks))
        pull = r * r * (dots / width)
        new = []
        for b in range(blocks):
            vb = v[:, lanes[b]]
            gx = r * (scaled[b] - vb * pull)
            gtok_out[at, lanes[b]] = (direct[at, lanes[b]] + gx).astype(jnp.bfloat16)
            new.append(gains[b] + jnp.sum(gy[b] * (vb * r), axis=0, keepdims=True))
        return tuple(new)

    gains = lax.fori_loop(
        0, rows // step_rows, some, tuple(jnp.zeros((1, 128), jnp.float32) for _ in range(blocks))
    )
    for b in range(blocks):
        row_sums[b : b + 1, :] = gains[b]


def fill_small(grid, dims, small, m_all, k_all, row_sums):
    blocks = row_sums.shape[0]
    for e in range(grid.nq):
        b = block_of(e, grid.nq, blocks)
        small[e, 0:dims] = m_all[0:dims, b, :]
        small[e, dims : 2 * dims] = k_all[:, b, :]
        small[e, 2 * dims : 2 * dims + 1] = m_all[dims, b : b + 1, :]
        small[e, 2 * dims + 1 : 2 * dims + 2] = row_sums[b : b + 1, :]


def mix_back_kernel(grid, dims, shapes, *refs):
    n = len(shapes)
    terms, refs = refs[:n], refs[n:]
    gact, x_in, mixed, carry, par, alive, spans, tok, pre, direct, small_in, *refs = refs
    sums, refs = refs[:n], refs[n:]
    (gtok_out, small_out,
     g_rows, gin_rows, before, bound, m_all, k_all, row_sums, small, seq_in, seg_in,
     sends_b, recv_b, s_send, s_recv, own_sem, send, recv, *scratch) = refs
    nq = grid.nq
    rows, width = gact.shape
    blocks = width // 128
    s = lax.axis_index("seq")
    seq_peer, seg_peer = small_peers(grid)
    meet(seq_peer + seg_peer)
    steps = scatter_steps(grid, shapes, terms, sums, scratch, own_sem, Sems(send, recv))
    little = SmallSum(grid, small, small_out, seq_in, seg_in, s_send, s_recv)

    def pump(count=1):
        for _ in range(count):
            next(steps, None)

    pump(2)
    for b in range(blocks):
        g_rows[pl.ds(b, rows, stride=blocks), :] = gact[:, b * 128 : b * 128 + 128].astype(jnp.float32)

    scan_back(
        grid, dims, g_rows, x_in, mixed, carry, par, alive, spans, gin_rows, before, bound, sends_b, recv_b,
        m_all, k_all, seq_peer, s, pump
    )
    norm_back(par, dims, tok, pre, direct, gin_rows, gtok_out, row_sums)
    for e in range(nq):
        small[e] = small_in[e]
    fill_small(grid, dims, small, m_all, k_all, row_sums)
    little.start()
    pump()
    little.middle()
    for _ in steps:
        pass
    little.end()


def mix_backward(grid, terms, cuts, gact, x_in, mixed, carry, par, alive, spans, tok, pre, direct, small, collective_id):
    rows, width = gact.shape
    nq, ng = grid.nq, grid.ng
    blocks, dims, few = width // 128, carry.shape[0], 4
    f = jnp.float32
    vm = pl.BlockSpec(memory_space=pltpu.VMEM)
    shapes, outs, scratch, count = scatter_plan(grid, terms, cuts)
    parts = [t.reshape((grid.ny, grid.nc, grid.nz, grid.nx) + v) for t, v in zip(terms, shapes)]
    n = len(parts)
    result = pl.pallas_call(
        functools.partial(mix_back_kernel, grid, dims, shapes),
        out_shape=outs
        + [jax.ShapeDtypeStruct((rows, width), jnp.bfloat16), jax.ShapeDtypeStruct(small.shape[1:], f)],
        in_specs=[ANY] * n + [vm] * 11,
        out_specs=[vm] * (n + 2),
        scratch_shapes=[
            pltpu.VMEM((rows * blocks, 128), f),
            pltpu.VMEM((rows * blocks, 128), f),
            pltpu.VMEM((rows, few, blocks, 128), f),
            pltpu.VMEM((nq, dims, blocks, 128), f),
            pltpu.VMEM((dims + 1, blocks, 128), f),
            pltpu.VMEM((dims, blocks, 128), f),
            pltpu.VMEM((blocks, 128), f),
            pltpu.VMEM(small.shape, f),
            pltpu.VMEM((nq - 1,) + small.shape[1:], f),
            pltpu.VMEM((ng - 1,) + small.shape[1:], f),
            pltpu.SemaphoreType.DMA((nq - 1,)),
            pltpu.SemaphoreType.DMA((nq - 1,)),
            pltpu.SemaphoreType.DMA((nq + ng - 2,)),
            pltpu.SemaphoreType.DMA((nq + ng - 2,)),
            pltpu.SemaphoreType.DMA((n, 2)),
            pltpu.SemaphoreType.DMA((count,)),
            pltpu.SemaphoreType.DMA((count,)),
        ]
        + scratch,
        compiler_params=pltpu.CompilerParams(
            collective_id=collective_id, has_side_effects=True, vmem_limit_bytes=62 << 20
        ),
    )(*parts, gact, x_in, mixed, carry, par, alive, spans, tok, pre, direct, small)
    return [v.reshape(-1, t.shape[-1]) for v, t in zip(result, terms)], result[n], result[n + 1]


def layer_back_kernel(grid, dims, shapes, sizes, *refs):
    n = len(shapes)
    zdim, vdim, fdim = sizes
    wholes, refs = refs[:n], refs[n:]
    (cot_hbm, act_hbm, ffn_hbm, two_hbm, one_hbm, hpre_hbm, proj_hbm, att_hbm, hin_hbm, value_hbm, probs, active_hbm,
     normed_hbm, tok_hbm, x_hbm, mixed_hbm, carry, par, aff, alive, spans, *refs) = refs
    sums, refs = refs[:n], refs[n:]
    gtok_out, small_out, *refs = refs
    terms, refs = refs[:n], refs[n:]
    (gproj, direct, pre, bound, m_all, k_all, row_sums, two_sums, aff_sums, small, seq_in, seg_in,
     sends_b, recv_b, s_send, s_recv, own_sem, load_sem, tile_sem, stage_sem, send, recv, *scratch) = refs
    nq, ng, nc, nz = grid.nq, grid.ng, grid.nc, grid.nz
    rows, width = direct.shape
    blocks = width // 128
    low, f = jnp.bfloat16, jnp.float32
    s = lax.axis_index("seq")
    seq_peer, seg_peer = small_peers(grid)
    meet(seq_peer + seg_peer)
    ready = [0]
    steps = scatter_steps(grid, shapes, terms, sums, scratch, own_sem, Sems(send, recv), lambda: ready[0])
    little = SmallSum(grid, small, small_out, seq_in, seg_in, s_send, s_recv)
    loads = [0]

    def pump(count=1):
        for _ in range(count):
            next(steps, None)

    pump()
    dot = functools.partial(jnp.dot, preferred_element_type=f)

    def dot_nt(a, b):
        return lax.dot_general(a, b, (((1,), (1,)), ((), ())), preferred_element_type=f)

    def dot_tn(a, b):
        return lax.dot_general(a, b, (((0,), (0,)), ((), ())), preferred_element_type=f)

    def fetch(src, dst):
        copy = pltpu.make_async_copy(src, dst, load_sem.at[loads[0]])
        loads[0] += 1
        copy.start()
        return copy.wait

    def by_rows(each=32):
        def wrap(some):
            pl.loop(0, rows // each)(lambda i: some(pl.ds(pl.multiple_of(i * each, each), each)))

        return wrap

    def wide(i):
        return shapes[i][-1]

    def tile_shape(i):
        return (2, grid.ny, nc, grid.nx) + shapes[i]

    def depth(i):
        return grid.nx * shapes[i][0] * shapes[i][1]

    def against(i, tiles, part):
        def get(zt):
            return pltpu.make_async_copy(wholes[i].at[:, :, zt], tiles.at[zt % 2], tile_sem.at[zt % 2])

        get(0).start()
        for zt in range(nz):
            if zt + 1 < nz:
                get(zt + 1).start()
            get(zt).wait()
            total = None
            for g in range(ng):
                term = dot_nt(part(g), tiles[zt % 2, g // nc, g % nc].reshape(depth(i), wide(i)))
                total = term if total is None else total + term
            yield slice(zt * depth(i), zt * depth(i) + depth(i)), total

    def grads(i, left, stage, part):
        copies = []
        slots = stage.shape[0]
        for g in range(ng):
            right = part(g)
            for zt in range(nz):
                k = len(copies)
                if k >= slots:
                    copies[k - slots].wait()
                d = depth(i)
                term = dot(left[zt * d : zt * d + d, :], right)
                stage[k % slots] = term.astype(low).reshape(stage.shape[1:])
                copies.append(
                    pltpu.make_async_copy(stage.at[k % slots], terms[i].at[g // nc, g % nc, zt], stage_sem.at[k % slots])
                )
                copies[k].start()
        for copy in copies[-slots:]:
            copy.wait()
        ready[0] = i + 1

    def turned(src, dst):
        for a in range(0, src.shape[1], 256):
            b = min(a + 256, src.shape[1])
            dst[a:b, :] = src[:, a:b].T

    def vm(*shape, kind=low):
        return pltpu.VMEM(shape, kind)

    def stage_of(i, slots=4):
        return pltpu.VMEM((slots, grid.nx) + shapes[i], low)

    def cut(ref, i):
        return lambda g: ref[:, g * wide(i) : (g + 1) * wide(i)]

    first_gate, first_reset, first_cand = width, width + zdim, width + zdim + vdim
    out_i, in_i, att_i, value_i, mix_i = range(5)

    def ffn_back(cot, hold, norm_grad):
        fetch(cot_hbm, cot)()

        def second(pre_act, left, stage, tiles):
            wait_act, wait_pre = fetch(act_hbm, hold), fetch(ffn_hbm, pre_act)
            wait_act()
            turned(hold, left)
            grads(out_i, left, stage, cut(cot, out_i))
            pump()
            wait_pre()
            for cols, grad in against(out_i, tiles, cut(cot, out_i)):
                v = pre_act[:, cols].astype(f)
                hold[:, cols] = (grad * silu_slope(v)).astype(low)
            pump()

        pl.run_scoped(second, vm(rows, fdim), vm(fdim, rows), stage_of(out_i), pltpu.VMEM(tile_shape(out_i), low))

        def first(two, left, stage, tiles):
            fetch(two_hbm, two)()
            turned(two, left)
            grads(in_i, left, stage, cut(hold, in_i))
            pump()
            for cols, grad in against(in_i, tiles, cut(hold, in_i)):
                norm_grad[:, cols] = grad

        pl.run_scoped(first, vm(rows, width), vm(width, rows), stage_of(in_i), pltpu.VMEM(tile_shape(in_i), low))

        def middle(one, hpre, upd, tok):
            for wait in [fetch(one_hbm, one), fetch(hpre_hbm, hpre), fetch(proj_hbm.at[:, 0:width], upd), fetch(tok_hbm, tok)]:
                wait()
            two_sums[...] = jnp.zeros_like(two_sums)

            @by_rows(16)
            def _(at):
                v, x, h, c = one[at, :], tok[at, :].astype(f), hpre[at, :], cot[at, :].astype(f)
                gain = jnp.concatenate([par[4 * dims + 2, b : b + 1, :] for b in range(blocks)], axis=1)
                r = lax.rsqrt(jnp.mean(v * v, axis=1, keepdims=True) + epsilon)
                gy = norm_grad[at, :]
                scaled = gy * gain
                pull = r * r * jnp.mean(scaled * v, axis=1, keepdims=True)
                grad_one = c + r * (scaled - v * pull)
                two_sums[...] += jnp.sum(gy * (v * r), axis=0, keepdims=True)
                u = jax.nn.sigmoid(upd[at, :])
                sig = jax.nn.sigmoid(h)
                direct[at, :] = grad_one * (1.0 - u)
                gproj[at, first_cand:] = (grad_one * u * (sig * (1.0 + h * (1.0 - sig)))).astype(low)
                gproj[at, 0:width] = (grad_one * (h * sig - x) * (u * (1.0 - u))).astype(low)

        pl.run_scoped(
            middle, vm(rows, width, kind=f), vm(rows, width, kind=f), vm(rows, width, kind=f), vm(rows, width)
        )

    pl.run_scoped(ffn_back, vm(rows, width), vm(rows, fdim), vm(rows, width, kind=f))
    pump()

    def attention_back(grad_hin):
        def out_back(hin, left, stage, tiles):
            fetch(hin_hbm, hin)()
            turned(hin, left)

            def part(g):
                return gproj[:, first_cand + g * wide(att_i) : first_cand + (g + 1) * wide(att_i)]

            grads(att_i, left, stage, part)
            pump()
            for cols, grad in against(att_i, tiles, part):
                grad_hin[:, cols] = grad

        pl.run_scoped(out_back, vm(rows, vdim), vm(vdim, rows), stage_of(att_i), pltpu.VMEM(tile_shape(att_i), low))

        def inner(value_pre, grad_pre):
            def blocks_back(att, gate, shared_pre, grad_att, values):
                waits = [
                    fetch(att_hbm, att),
                    fetch(proj_hbm.at[:, first_reset:first_cand], gate),
                    fetch(proj_hbm.at[:, first_gate:first_reset], shared_pre),
                    fetch(value_hbm, value_pre),
                ]
                for wait in waits:
                    wait()

                @by_rows(16)
                def _(at):
                    v, g, p = gate[at, :], grad_hin[at, :], value_pre[at, :]
                    sig = jax.nn.sigmoid(v)
                    grad_att[at, :] = (g * (v * sig)).astype(low)
                    gproj[at, first_reset:first_cand] = (g * att[at, :] * (sig * (1.0 + v * (1.0 - sig)))).astype(low)
                    values[at, :] = (p * jax.nn.sigmoid(p)).astype(low)

                aff_total = [jnp.zeros((1, zdim), f)] * 4
                scale_q = zdim**-0.5
                for r in range(rows // STRETCH):
                    at = slice(r * STRETCH, r * STRETCH + STRETCH)
                    v = shared_pre[at, :]
                    shared = v * jax.nn.sigmoid(v)
                    query = (scale_q * (shared * aff[0:1] + aff[1:2])).astype(low)
                    key = (shared * aff[2:3] + aff[3:4]).astype(low)
                    prob, ga = probs[at, :], grad_att[at, :]
                    grad_prob = dot_nt(ga, values[at, :])
                    weighted = jnp.sum(prob * grad_prob, axis=1, keepdims=True)
                    grad_score = (prob * (grad_prob - weighted)).astype(low)
                    grad_query = dot(grad_score, key) * scale_q
                    grad_key = dot_tn(grad_score, query)
                    grad_shared = grad_query * aff[0:1] + grad_key * aff[2:3]
                    gproj[at, first_gate:first_reset] = (grad_shared * silu_slope(v)).astype(low)
                    for k, t in enumerate([grad_query * shared, grad_query, grad_key * shared, grad_key]):
                        aff_total[k] = aff_total[k] + jnp.sum(t, axis=0, keepdims=True)
                    grad_hin[at, :] = dot_tn(prob.astype(low), ga)
                for k in range(4):
                    aff_sums[k : k + 1, :] = aff_total[k]

                @by_rows(16)
                def _(at):
                    grad_pre[at, :] = (grad_hin[at, :] * silu_slope(value_pre[at, :])).astype(low)

            pl.run_scoped(
                blocks_back, vm(rows, vdim, kind=f), vm(rows, vdim, kind=f), vm(rows, zdim, kind=f),
                vm(rows, vdim), vm(rows, vdim)
            )
            pump()

            def value_back(normed, left, stage, tiles):
                fetch(normed_hbm, normed)()
                turned(normed, left)
                grads(value_i, left, stage, cut(grad_pre, value_i))
                for cols, grad in against(value_i, tiles, cut(grad_pre, value_i)):
                    pre[:, cols] = grad

            pl.run_scoped(
                value_back, vm(rows, width), vm(width, rows), stage_of(value_i), pltpu.VMEM(tile_shape(value_i), low)
            )

        pl.run_scoped(inner, vm(rows, vdim, kind=f), vm(rows, vdim))

    pl.run_scoped(attention_back, vm(rows, vdim, kind=f))
    pump()

    def mix_back(g_rows, gin_rows):
        def mix_weight_back(active, left, stage, tiles):
            fetch(active_hbm, active)()
            turned(active, left)
            grads(mix_i, left, stage, cut(gproj, mix_i))
            pump()
            for cols, grad in against(mix_i, tiles, cut(gproj, mix_i)):
                grad = grad.astype(low).astype(f)
                for b in range(cols.start // 128, cols.stop // 128):
                    lane = b * 128 - cols.start
                    g_rows[pl.ds(b, rows, stride=blocks), :] = grad[:, lane : lane + 128]

        pl.run_scoped(
            mix_weight_back, vm(rows, width), vm(width, rows), stage_of(mix_i), pltpu.VMEM(tile_shape(mix_i), low)
        )

        def scan(x_in, mixed, before):
            waits = [fetch(x_hbm, x_in), fetch(mixed_hbm, mixed)]
            for wait in waits:
                wait()
            scan_back(
                grid, dims, g_rows, x_in, mixed, carry, par, alive, spans, gin_rows, before, bound, sends_b, recv_b,
                m_all, k_all, seq_peer, s, pump
            )

        pl.run_scoped(
            scan, vm(rows * blocks, 128, kind=f), vm(rows * blocks, 128, kind=f), vm(rows, 4, blocks, 128, kind=f)
        )

        def last(tok):
            fetch(tok_hbm, tok)()
            norm_back(par, dims, tok, pre, direct, gin_rows, gtok_out, row_sums)

        pl.run_scoped(last, vm(rows, width))

    pl.run_scoped(mix_back, vm(rows * blocks, 128, kind=f), vm(rows * blocks, 128, kind=f))
    small[...] = jnp.zeros_like(small)
    fill_small(grid, dims, small, m_all, k_all, row_sums)
    for e in range(nq):
        b = block_of(e, nq, blocks)
        small[e, 2 * dims + 2 : 2 * dims + 3] = two_sums[:, b * 128 : b * 128 + 128]
        small[e, 2 * dims + 3 : 2 * dims + 7] = aff_sums[...]
    little.start()
    pump()
    little.middle()
    for _ in steps:
        pass
    little.end()


def layer_backward(grid, wholes, cuts, kept, probs, carry, par, aff, alive, spans, sizes, collective_id):
    nq, ng = grid.nq, grid.ng
    dims, blocks = carry.shape[0], carry.shape[1]
    zdim, vdim, fdim = sizes
    width = blocks * 128
    rows = probs.shape[0]
    f = jnp.float32
    vm = pl.BlockSpec(memory_space=pltpu.VMEM)
    n = len(wholes)
    like = [jax.ShapeDtypeStruct((ng, w.size // ng // w.shape[-1], w.shape[-1]), w.dtype) for w in wholes]
    shapes, outs, scratch, count = scatter_plan(grid, like, cuts)
    whole_shapes = [jax.ShapeDtypeStruct(w.shape[:4] + s, w.dtype) for w, s in zip(wholes, shapes)]
    low = [w.reshape(v.shape) for w, v in zip(wholes, whole_shapes)]
    small_shape = (-(-(2 * dims + 7) // 8) * 8, 128)
    result = pl.pallas_call(
        functools.partial(layer_back_kernel, grid, dims, shapes, sizes),
        out_shape=outs
        + [jax.ShapeDtypeStruct((rows, width), jnp.bfloat16), jax.ShapeDtypeStruct(small_shape, f)]
        + whole_shapes,
        in_specs=[ANY] * n + [ANY] * 10 + [vm] + [ANY] * 5 + [vm] * 5,
        out_specs=[vm] * (n + 2) + [ANY] * n,
        scratch_shapes=[
            pltpu.VMEM((rows, width * 2 + zdim + vdim), jnp.bfloat16),
            pltpu.VMEM((rows, width), f),
            pltpu.VMEM((rows, width), f),
            pltpu.VMEM((nq, dims, blocks, 128), f),
            pltpu.VMEM((dims + 1, blocks, 128), f),
            pltpu.VMEM((dims, blocks, 128), f),
            pltpu.VMEM((blocks, 128), f),
            pltpu.VMEM((1, width), f),
            pltpu.VMEM((4, zdim), f),
            pltpu.VMEM((nq,) + small_shape, f),
            pltpu.VMEM((nq - 1,) + small_shape, f),
            pltpu.VMEM((ng - 1,) + small_shape, f),
            pltpu.SemaphoreType.DMA((nq - 1,)),
            pltpu.SemaphoreType.DMA((nq - 1,)),
            pltpu.SemaphoreType.DMA((nq + ng - 2,)),
            pltpu.SemaphoreType.DMA((nq + ng - 2,)),
            pltpu.SemaphoreType.DMA((n, 2)),
            pltpu.SemaphoreType.DMA((24,)),
            pltpu.SemaphoreType.DMA((2,)),
            pltpu.SemaphoreType.DMA((4,)),
            pltpu.SemaphoreType.DMA((count,)),
            pltpu.SemaphoreType.DMA((count,)),
        ]
        + scratch,
        compiler_params=pltpu.CompilerParams(
            collective_id=collective_id, has_side_effects=True, vmem_limit_bytes=63 << 20
        ),
    )(*low, *kept[:10], probs, *kept[10:], carry, par, aff, alive, spans)
    return [v.reshape(-1, t.shape[-1]) for v, t in zip(result, like)], result[n], result[n + 1]


def rms_forward(values, gain):
    inverse = lax.rsqrt(jnp.mean(values * values, axis=-1, keepdims=True) + epsilon)
    return (values * inverse * gain, inverse)


def rms_backward(grad_out, values, inverse, gain):
    scaled = grad_out * gain
    projection = jnp.mean(scaled * values, axis=-1, keepdims=True)
    grad_in = inverse * (scaled - values * inverse * inverse * projection)
    return (grad_in, jnp.sum(grad_out * values * inverse, axis=0))


def silu_slope(values):
    sigma_v = jax.nn.sigmoid(values)
    return sigma_v * (1.0 + values * (1.0 - sigma_v))


def times(left, pieces):
    return jnp.concatenate(
        [jnp.dot(left, pieces[i], preferred_element_type=jnp.float32) for i in range(pieces.shape[0])], axis=1
    )


def against(left, pieces):
    n = pieces.shape[2]
    return sum(
        lax.dot_general(
            left[:, i * n : i * n + n], pieces[i], (((1,), (1,)), ((), ())), preferred_element_type=jnp.float32
        )
        for i in range(pieces.shape[0])
    )


def over_rows(left, right, count):
    n = right.shape[1] // count
    return jnp.stack(
        [
            lax.dot_general(
                left, right[:, i * n : i * n + n], (((0,), (0,)), ((), ())), preferred_element_type=jnp.float32
            ).astype(jnp.bfloat16)
            for i in range(count)
        ]
    )


def masked_scores(query_blk, key_blk, allowed):
    raw_scores = jnp.einsum("cid,cjd->cij", query_blk, key_blk, preferred_element_type=jnp.float32)
    return jnp.where(allowed, raw_scores, -1e30)


def backward_apart(grid, cotangent, tokens_low, forward, weights, alive, spans, sizes):
    (normed_b, active, x_rows, mixed_rows, carry, par, affine, probs, out_one, normed_two_b, _,
     projected, value_pre, attended, hidden_in, hidden_pre, ffn_hidden, ffn_act) = forward
    ffn_hidden = ffn_hidden.astype(jnp.float32)
    token_count, model_width = tokens_low.shape
    nq, ng = grid.nq, grid.ng
    dims, blocks = carry.shape[0], carry.shape[1]
    zdim, vdim, _ = sizes
    block_count = token_count // STRETCH
    tokens_flat = tokens_low.astype(jnp.float32)
    mix_full, value_full, out_full, ffn_in_full, ffn_out_full = (w.reshape(ng, -1, w.shape[-1]) for w in weights)
    gain_two = par[4 * dims + 2].reshape(-1)
    update = jax.nn.sigmoid(projected[:, :model_width])
    gate_pre = projected[:, model_width : model_width + zdim + vdim]
    gate_rows = jax.nn.silu(gate_pre)
    shared = gate_rows[:, :zdim]
    reset_gate = gate_rows[:, zdim:]
    values_b = jax.nn.silu(value_pre).astype(jnp.bfloat16)
    scale_q = zdim ** (-0.5)
    query_b = (scale_q * (shared * affine[0] + affine[1])).astype(jnp.bfloat16)
    key_b = (shared * affine[2] + affine[3]).astype(jnp.bfloat16)
    query_blk = query_b.reshape(block_count, STRETCH, zdim)
    key_blk = key_b.reshape(block_count, STRETCH, zdim)
    value_blk = values_b.reshape(block_count, STRETCH, vdim)
    probs = probs.reshape(block_count, STRETCH, STRETCH)
    probs_b = probs.astype(jnp.bfloat16)
    hidden_act = jax.nn.silu(hidden_pre)
    inverse_two = lax.rsqrt(jnp.mean(out_one * out_one, axis=-1, keepdims=True) + epsilon)

    grad_y_b = cotangent
    grad_ffn_out = over_rows(ffn_act, grad_y_b, ng)
    grad_act = against(grad_y_b, ffn_out_full)
    grad_hidden_b = (grad_act * silu_slope(ffn_hidden)).astype(jnp.bfloat16)
    grad_ffn_in = over_rows(normed_two_b, grad_hidden_b, ng)
    grad_normed_two = against(grad_hidden_b, ffn_in_full)
    grad_norm_two, grad_gain_two = rms_backward(grad_normed_two, out_one, inverse_two, gain_two)
    grad_out_one = grad_y_b.astype(jnp.float32) + grad_norm_two
    grad_update = grad_out_one * (hidden_act - tokens_flat)
    grad_tokens_flat = grad_out_one * (1.0 - update)
    grad_hpre_b = (grad_out_one * update * silu_slope(hidden_pre)).astype(jnp.bfloat16)
    grad_out_weight = over_rows(hidden_in, grad_hpre_b, ng)
    grad_hidden_in = against(grad_hpre_b, out_full)
    grad_att_b = (grad_hidden_in * reset_gate).astype(jnp.bfloat16)
    grad_reset = grad_hidden_in * attended
    grad_att_blk = grad_att_b.reshape(block_count, STRETCH, vdim)
    grad_probs = jnp.einsum("civ,cjv->cij", grad_att_blk, value_blk, preferred_element_type=jnp.float32)
    weighted = jnp.sum(probs * grad_probs, axis=2, keepdims=True)
    grad_scores_b = (probs * (grad_probs - weighted)).astype(jnp.bfloat16)
    grad_query = jnp.einsum("cij,cjd->cid", grad_scores_b, key_blk, preferred_element_type=jnp.float32).reshape(
        token_count, zdim
    )
    grad_key = jnp.einsum("cij,cid->cjd", grad_scores_b, query_blk, preferred_element_type=jnp.float32).reshape(
        token_count, zdim
    )
    grad_values = jnp.einsum("cij,civ->cjv", probs_b, grad_att_blk, preferred_element_type=jnp.float32).reshape(
        token_count, vdim
    )
    grad_qs = grad_query * scale_q
    grad_shared = grad_qs * affine[0] + grad_key * affine[2]
    grad_affine = jnp.stack(
        [
            jnp.sum(grad_qs * shared, axis=0),
            jnp.sum(grad_qs, axis=0),
            jnp.sum(grad_key * shared, axis=0),
            jnp.sum(grad_key, axis=0),
        ]
    )
    grad_gate_pre = jnp.concatenate([grad_shared, grad_reset], axis=1) * silu_slope(gate_pre)
    grad_upre = grad_update * update * (1.0 - update)
    grad_proj_b = jnp.concatenate(
        [grad_upre.astype(jnp.bfloat16), grad_gate_pre.astype(jnp.bfloat16), grad_hpre_b], axis=1
    )
    grad_mix = over_rows(active, grad_proj_b, ng)
    grad_active_b = against(grad_proj_b, mix_full).astype(jnp.bfloat16)
    grad_vpre_b = (grad_values * silu_slope(value_pre)).astype(jnp.bfloat16)
    grad_value = over_rows(normed_b, grad_vpre_b, ng)
    grad_normed = against(grad_vpre_b, value_full)

    small = jnp.concatenate(
        [jnp.zeros((blocks, 2 * dims + 2, 128), jnp.float32), grad_gain_two.reshape(blocks, 1, 128)], axis=1
    )
    if nq != blocks:
        small = jnp.take(small, np.arange(nq) * blocks // nq, axis=0)
    small = jnp.concatenate([small, jnp.broadcast_to(grad_affine[None], (nq, 4, 128))], axis=1)
    small = jnp.pad(small, ((0, 0), (0, -small.shape[1] % 8), (0, 0)))
    return mix_backward(
        grid, [grad_ffn_out, grad_ffn_in, grad_out_weight, grad_value, grad_mix], SCATTER_CUTS, grad_active_b, x_rows,
        mixed_rows, carry, par, alive, spans, tokens_low, grad_normed, grad_tokens_flat, small, 1
    )


def body(
    tokens,
    starts,
    norm_gain,
    ema_delta,
    ema_alpha,
    ema_beta,
    ema_eta,
    ema_omega,
    mix_weight,
    value_weight,
    qk_affine,
    out_weight,
    ffn_gain,
    ffn_in,
    ffn_out,
    cotangent,
):
    seg_count, row_count, model_width = tokens.shape
    nq, ng = lax.axis_size("seq"), lax.axis_size("seg")
    grid = Grid(nq, ng)
    seq_index, seg_index = lax.axis_index("seq"), lax.axis_index("seg")
    seq_length = row_count * nq
    dims = ema_delta.shape[1]
    zdim = qk_affine.shape[0] * nq * ng // 4
    vdim = value_weight.shape[1] * ng
    token_count = seg_count * row_count
    blocks = model_width // 128

    index = seq_index * ng + seg_index
    mine = norm_gain.shape[0]
    columns = jnp.concatenate(
        [ema_delta.T, ema_alpha.T, ema_beta.T, ema_eta.T, norm_gain[None], ema_omega[None], ffn_gain[None]], axis=0
    ).astype(jnp.float32)
    count = columns.shape[0]
    tile = jnp.zeros((-(-(count + 4) // 8) * 8, 128), jnp.float32)
    tile = lax.dynamic_update_slice(tile, columns, (0, lax.rem(index * mine, 128)))
    part = qk_affine.shape[0]
    tile = lax.dynamic_update_slice(
        tile, qk_affine.astype(jnp.float32)[None], (count + index * part // 128, lax.rem(index * part, 128))
    )

    places = jnp.arange(seq_length, dtype=jnp.int32)
    goes_on = 1.0 - jnp.any(starts[0][None, :] == places[:, None], axis=1).astype(jnp.float32)
    spans = jnp.broadcast_to(jnp.min(goes_on.reshape(nq, row_count), axis=1)[:, None], (nq, 128))
    alive = lax.dynamic_slice_in_dim(goes_on, seq_index * row_count, row_count, 0)
    alive = jnp.broadcast_to(alive[:, None], (row_count, 128))

    positions_rows = seq_index * row_count + jnp.arange(row_count, dtype=jnp.int32)
    docs_rows = jnp.sum((starts[:, None, :] <= positions_rows[None, :, None]).astype(jnp.int32), axis=2)
    block_count = token_count // STRETCH
    block_docs = docs_rows.reshape(block_count, STRETCH)
    offsets = jnp.arange(STRETCH)
    allowed = (block_docs[:, :, None] == block_docs[:, None, :]) & (offsets[:, None] >= offsets[None, :])[None]
    mask = allowed.astype(jnp.float32).reshape(token_count, STRETCH)
    tokens_low = tokens.reshape(token_count, model_width)
    weights, forward = mix_forward(
        grid, [mix_weight, value_weight, out_weight, ffn_in, ffn_out], GATHER_CUTS, tokens_low, tile, alive, spans, mask, dims, 0
    )
    mix_full, value_full, out_full, ffn_in_full, ffn_out_full = weights
    (normed_b, active, x_rows, mixed_rows, carry, par, affine, probs, out_one, normed_two_b, result,
     projected, value_pre, attended, hidden_in, hidden_pre, ffn_hidden, ffn_act) = forward
    sizes = (zdim, vdim, ffn_act.shape[1])
    cotangent_low = cotangent.reshape(token_count, model_width)
    if min(w.shape[1] for w in (mix_weight, value_weight, out_weight, ffn_in, ffn_out)) < 128:
        result_back = backward_apart(grid, cotangent_low, tokens_low, forward, weights, alive, spans, sizes)
    else:
        kept = [cotangent_low, ffn_act, ffn_hidden, normed_two_b, out_one, hidden_pre, projected, attended, hidden_in,
                value_pre, active, normed_b, tokens_low, x_rows, mixed_rows]
        order = [weights[4], weights[3], weights[2], weights[1], weights[0]]
        result_back = layer_backward(
            grid, order, SCATTER_CUTS, kept, probs, carry, par, affine, alive, spans, sizes, 1
        )
    (g_ffn_out, g_ffn_in, g_out, g_value, g_mix), grad_tokens, sums = result_back
    return (
        result.reshape(seg_count, row_count, model_width),
        grad_tokens.reshape(seg_count, row_count, model_width),
        *small_outputs(sums, index, dims, ema_delta, ema_alpha, ema_beta, ema_eta, mine, part, g_mix, g_value, g_out, g_ffn_in, g_ffn_out),
    )


def small_outputs(sums, index, dims, ema_delta, ema_alpha, ema_beta, ema_eta, mine, part, g_mix, g_value, g_out, g_ffn_in, g_ffn_out):
    own = lax.dynamic_slice_in_dim(sums, lax.rem(index * mine, 128), mine, 1)
    m_sum, k_sum = own[:dims].T, own[dims : 2 * dims].T
    vectors = own[2 * dims : 2 * dims + 3]
    delta, alpha, beta, eta = (v.astype(jnp.float32) for v in (ema_delta, ema_alpha, ema_beta, ema_eta))
    damping, decay = jax.nn.sigmoid(delta), jax.nn.sigmoid(alpha)
    g_keep = damping * beta * eta * k_sum
    grad_eta = damping * beta * m_sum
    grad_beta = damping * eta * m_sum
    grad_alpha = -g_keep * damping * decay * (1.0 - decay)
    grad_delta = (beta * eta * m_sum - g_keep * decay) * damping * (1.0 - damping)
    grad_affine = lax.dynamic_slice(
        sums, (2 * dims + 3 + index * part // 128, lax.rem(index * part, 128)), (1, part)
    ).reshape(-1)
    return (vectors[1], grad_delta, grad_alpha, grad_beta, grad_eta, vectors[0],
            g_mix, g_value, grad_affine, g_out, vectors[2], g_ffn_in, g_ffn_out)


def solution(mesh):
    placed = (
        P("seg", "seq", None),
        P("seg", None),
        P(("seq", "seg")),
        P(("seq", "seg"), None),
        P(("seq", "seg"), None),
        P(("seq", "seg"), None),
        P(("seq", "seg"), None),
        P(("seq", "seg")),
        P("seq", "seg"),
        P("seq", "seg"),
        P(("seq", "seg")),
        P("seq", "seg"),
        P(("seq", "seg")),
        P("seq", "seg"),
        P("seq", "seg"),
        P("seg", "seq", None),
    )
    return jax.shard_map(
        body,
        mesh=mesh,
        in_specs=placed,
        out_specs=(P("seg", "seq", None),) * 2 + placed[2:15],
        check_vma=False,
    )
```

```python
import functools
import math

import jax
import jax.numpy as jnp
import numpy as np
from jax import lax
from jax.experimental import pallas as pl
from jax.experimental.pallas import tpu as pltpu
from jax.sharding import PartitionSpec as P

STRETCH = 128
epsilon = 1e-05
GATHER_LAG = (1, 1, 1, 1, 1)
SCATTER_LAG = (0, 1, 1, 1, 1)
GATHER_CUTS = (4, 2, 2, 4, 4)
SCATTER_CUTS = (4, 4, 2, 2, 4)

MESH = pl.DeviceIdType.MESH
ANY = pl.BlockSpec(memory_space=pl.ANY)


class Grid:
    def __init__(self, nq, ng):
        self.nq, self.ng = nq, ng
        self.nz = math.gcd(nq, 4)
        self.nx = nq // self.nz
        self.nc = math.gcd(ng, 2)
        self.ny = ng // self.nc

    def here(self):
        s, g = lax.axis_index("seq"), lax.axis_index("seg")
        return s // self.nx, lax.rem(s, self.nx), g // self.nc, lax.rem(g, self.nc)

    def peer(self, axis, d):
        z, x, y, c = self.here()
        if axis == "z":
            z = lax.rem(z + d, self.nz)
        if axis == "x":
            x = lax.rem(x + d, self.nx)
        if axis == "y":
            y = lax.rem(y + d, self.ny)
        if axis == "c":
            c = lax.rem(c + d, self.nc)
        return z, x, y, c

    def size(self, axis):
        return {"z": self.nz, "x": self.nx, "y": self.ny, "c": self.nc}[axis]

    def device(self, place):
        z, x, y, c = place
        return {"seq": z * self.nx + x, "seg": y * self.nc + c}

    def peers(self, axes):
        return [self.peer(a, d) for a in axes for d in range(1, self.size(a))]


def enter(grid, peers):
    barrier = pltpu.get_barrier_semaphore()
    for place in peers:
        pl.semaphore_signal(barrier, inc=1, device_id=grid.device(place), device_id_type=MESH)
    pl.semaphore_wait(barrier, len(peers))


class Sems:
    def __init__(self, send, recv):
        self.send, self.recv, self.used = send, recv, 0

    def take_index(self):
        self.used += 1
        return self.used - 1

    def take(self):
        i = self.take_index()
        return self.send.at[i], self.recv.at[i]


def gather_steps(grid, shapes, shards, wholes, own_sem, sems):
    n = len(shapes)
    z, x, y, c = grid.here()
    pending = []

    def push(src, dst, axis, d, arrives):
        s, r = sems.take()
        device = grid.device(grid.peer(axis, d))
        copy = pltpu.make_async_remote_copy(src, dst, s, r, device_id=device, device_id_type=MESH)
        copy.start()
        pending.append(copy)
        there = pltpu.make_async_remote_copy(arrives, arrives, s, r, device_id=device, device_id_type=MESH)
        return there.wait_recv

    def back(axis, d):
        return dict(zip("zxyc", grid.peer(axis, grid.size(axis) - d)))[axis]

    owns = []
    chunks = [(i, q) for i in range(n) for q in range(shapes[i][0] // 2)]
    core_waits = {}

    def core(k, view):
        core_waits.setdefault(k, []).extend(
            push(view(c), view(c), "c", d, view(back("c", d))) for d in range(1, grid.nc)
        )

    def stage_z(k, i, h):
        w = wholes[i]
        return [
            push(shards[i].at[h], w.at[y, c, z, x, h], "z", d, w.at[y, c, back("z", d), x, h])
            for d in range(1, grid.nz)
        ]

    def stage_two(k, i, h):
        w = wholes[i]
        src = w.at[y, c, :, x, h]
        if h % 2 == 0:
            waits = [push(src, src, "x", d, w.at[y, c, :, back("x", d), h]) for d in range(1, grid.nx)]
        else:
            waits = [push(src, src, "y", d, w.at[back("y", d), c, :, x, h]) for d in range(1, grid.ny)]
        core(k, lambda cc: w.at[y, cc, :, x, h])
        return waits

    def stage_three(k, i, h):
        w = wholes[i]
        if h % 2 == 0:
            src = w.at[y, c, :, :, h]
            waits = [push(src, src, "y", d, w.at[back("y", d), c, :, :, h]) for d in range(1, grid.ny)]
            for d in range(1, grid.nx):
                core(k, lambda cc: w.at[y, cc, :, back("x", d), h])
            return waits
        src = w.at[:, c, :, x, h]
        waits = [push(src, src, "x", d, w.at[:, c, :, back("x", d), h]) for d in range(1, grid.nx)]
        for d in range(1, grid.ny):
            core(k, lambda cc: w.at[back("y", d), cc, :, x, h])
        return waits

    def stage_last(k, i, h):
        w = wholes[i]
        if h % 2 == 0:
            for d in range(1, grid.ny):
                core(k, lambda cc: w.at[back("y", d), cc, :, :, h])
        else:
            for d in range(1, grid.nx):
                core(k, lambda cc: w.at[:, cc, :, back("x", d), h])

    def finish(waits):
        for wait in waits:
            wait()

    got = {}
    total = len(chunks)
    at = [0] * 5

    def advance(j):
        k = at[j]
        i, q = chunks[k]
        if j == 1 and q == 0:
            owns[i].wait()
        if j == 4:
            finish(core_waits[k])
            at[j] += 1
            return [i] if q + 1 == shapes[i][0] // 2 else []
        for h in (0, 1):
            if j:
                finish(got[k, h])
            got[k, h] = (stage_z, stage_two, stage_three, stage_last)[j](k, i, 2 * q + h)
        at[j] += 1
        return []

    advance(0)
    yield []
    for i in range(n):
        copy = pltpu.make_async_copy(shards[i], wholes[i].at[y, c, z, x], own_sem.at[i])
        copy.start()
        owns.append(copy)
    while at[4] < total:
        before = list(at)
        done = []
        for j in (1, 0, 2, 3, 4):
            if j == 0:
                go = at[0] < total and at[0] - at[1] < GATHER_LAG[0]
            else:
                go = at[j] < before[j - 1] and (before[j - 1] == total or before[j - 1] - at[j] >= GATHER_LAG[j])
            if go:
                done += advance(j)
        if at[4] == total:
            for copy in pending:
                copy.wait_send()
        yield done


def gather_plan(grid, shards, cuts):
    shapes, args, outs = [], [], []
    for w, q in zip(shards, cuts):
        k, n = w.shape
        q = max(1, min(q, k // 32))
        shapes.append((2 * q, k // (2 * q), n))
        args.append(w.reshape(shapes[-1]))
        outs.append(jax.ShapeDtypeStruct((grid.ny, grid.nc, grid.nz, grid.nx) + shapes[-1], w.dtype))
    per = (grid.nz - 1) + (grid.nx - 1) + (grid.ny - 1) + (grid.nc - 1) * (grid.nx + grid.ny)
    count = sum(s[0] for s in shapes) * per
    return shapes, args, outs, count


def scatter_steps(grid, shapes, terms, sums, scratch, own_sem, sems, ready=None):
    n = len(shapes)
    nz, nx, ny, nc = grid.nz, grid.nx, grid.ny, grid.nc
    own = [scratch[7 * i] for i in range(n)]
    one = [scratch[7 * i + 1] for i in range(n)]
    two_a = [scratch[7 * i + 2] for i in range(n)]
    two_b = [scratch[7 * i + 3] for i in range(n)]
    three_a = [scratch[7 * i + 4] for i in range(n)]
    three_b = [scratch[7 * i + 5] for i in range(n)]
    four = [scratch[7 * i + 6] for i in range(n)]
    z, x, y, c = grid.here()
    pending = []
    around = {(axis, d): grid.peer(axis, d) for axis in "zxyc" for d in range(1, grid.size(axis))}
    devices = {key: grid.device(place) for key, place in around.items()}

    def push(ends, axis, d):
        k = sems.take_index()

        def copy():
            return pltpu.make_async_remote_copy(
                *ends(), sems.send.at[k], sems.recv.at[k], device_id=devices[axis, d], device_id_type=MESH
            )

        copy().start()
        pending.append(lambda: copy().wait_send())
        return lambda: copy().wait_recv()

    def to(axis, d):
        return dict(zip("zxyc", around[axis, d]))[axis]

    def finish(waits):
        for wait in waits:
            wait()

    assert nc == 2

    def stage_one(i, q, h):
        return [push(lambda: (terms[i].at[:, to("c", 1), :, :, 2 * q + h], one[i].at[q, h]), "c", 1)]

    def load_own(i, q, h):
        def load():
            return pltpu.make_async_copy(terms[i].at[:, c, :, :, 2 * q + h], own[i].at[h], own_sem.at[i, h])

        load().start()
        return [lambda: load().wait()]

    def stage_two(i, q, h):
        mine = one[i].at[q, h]

        @pl.loop(0, ny * nz)
        def _(ab):
            a, b = ab // nz, lax.rem(ab, nz)
            for e in range(nx):
                mine[a, b, e] += own[i][h, a, b, e]

        if h == 0:
            return [
                push(lambda d=d: (one[i].at[q, h, to("y", d)], two_a[i].at[q, d - 1]), "y", d) for d in range(1, ny)
            ]
        return [
            push(lambda d=d: (one[i].at[q, h, :, :, to("x", d)], two_b[i].at[q, d - 1]), "x", d) for d in range(1, nx)
        ]

    def stage_three(i, q, h):
        mine = one[i].at[q, h]
        if h == 0:

            @pl.loop(0, nz)
            def _(b):
                for e in range(nx):
                    total = mine[y, b, e]
                    for d in range(ny - 1):
                        total += two_a[i][q, d, b, e]
                    mine[y, b, e] = total

            return [
                push(lambda d=d: (one[i].at[q, h, y, :, to("x", d)], three_a[i].at[q, d - 1]), "x", d)
                for d in range(1, nx)
            ]

        @pl.loop(0, nz)
        def _(b):
            for a in range(ny):
                total = mine[a, b, x]
                for d in range(nx - 1):
                    total += two_b[i][q, d, a, b]
                mine[a, b, x] = total

        return [
            push(lambda d=d: (one[i].at[q, h, to("y", d), :, x], three_b[i].at[q, d - 1]), "y", d)
            for d in range(1, ny)
        ]

    def stage_four(i, q, h):
        mine = one[i].at[q, h]
        came = three_a[i] if h == 0 else three_b[i]

        @pl.loop(0, nz)
        def _(b):
            total = mine[y, b, x]
            for d in range((nx if h == 0 else ny) - 1):
                total += came[q, d, b]
            mine[y, b, x] = total

        return [
            push(lambda d=d: (one[i].at[q, h, y, to("z", d), x], four[i].at[q, h, d - 1]), "z", d)
            for d in range(1, nz)
        ]

    def stage_last(i, q, h):
        total = one[i][q, h, y, z, x].astype(jnp.float32)
        for d in range(nz - 1):
            total += four[i][q, h, d].astype(jnp.float32)
        sums[i][2 * q + h] = total

    stages = [stage_one, stage_two, stage_three, stage_four, stage_last]
    chunks = [(i, q) for i in range(n) for q in range(shapes[i][0] // 2)]
    waits = {}
    total = len(chunks)
    at = [0] * len(stages)
    yield
    while at[-1] < total:
        there = total if ready is None else sum(1 for i, q in chunks if i < ready())
        before = [there] + at[:-1]
        fresh = None
        for j, stage in enumerate(stages):
            lag = SCATTER_LAG[j]
            if at[j] < before[j] and (before[j] == total or j == 0 or before[j] - at[j] >= lag):
                i, q = chunks[at[j]]
                for h in (0, 1):
                    if j:
                        finish(waits[i, q, h])
                    waits[i, q, h] = stage(i, q, h)
                if j == 0:
                    fresh = i, q
                at[j] += 1
            if j == 1 and fresh:
                for h in (0, 1):
                    waits[fresh[0], fresh[1], h] += load_own(*fresh, h)
        if at[-1] == total:
            finish(pending)
        yield


class SmallSum:
    def __init__(self, grid, small, total, seq_in, seg_in, send, recv):
        self.grid, self.small, self.total = grid, small, total
        self.seq_in, self.seg_in, self.send, self.recv = seq_in, seg_in, send, recv
        self.seq_peer, self.seg_peer = small_peers(grid)
        self.copies = []

    def push(self, src, dst, device):
        i = len(self.copies)
        copy = pltpu.make_async_remote_copy(
            src, dst, self.send.at[i], self.recv.at[i], device_id=device, device_id_type=MESH
        )
        copy.start()
        self.copies.append(copy)

    def start(self):
        nq, sq = self.grid.nq, lax.axis_index("seq")
        for d in range(1, nq):
            self.push(self.small.at[lax.rem(sq + d, nq)], self.seq_in.at[d - 1], self.seq_peer[d - 1])

    def middle(self):
        nq, ng = self.grid.nq, self.grid.ng
        total = self.small[lax.axis_index("seq")]
        for d in range(1, nq):
            self.copies[d - 1].wait_recv()
            total += self.seq_in[d - 1]
        self.total[...] = total
        for d in range(1, ng):
            self.push(self.total, self.seg_in.at[d - 1], self.seg_peer[d - 1])

    def end(self):
        nq, ng = self.grid.nq, self.grid.ng
        total = self.total[...]
        for d in range(1, ng):
            self.copies[nq + d - 2].wait_recv()
            total += self.seg_in[d - 1]
        for copy in self.copies:
            copy.wait_send()
        self.total[...] = total


def small_peers(grid):
    nq, ng = grid.nq, grid.ng
    s, g = lax.axis_index("seq"), lax.axis_index("seg")
    return (
        [{"seq": lax.rem(s + d, nq), "seg": g} for d in range(1, nq)],
        [{"seq": s, "seg": lax.rem(g + d, ng)} for d in range(1, ng)],
    )


def meet(peers):
    barrier = pltpu.get_barrier_semaphore()
    for place in peers:
        pl.semaphore_signal(barrier, inc=1, device_id=place, device_id_type=MESH)
    pl.semaphore_wait(barrier, len(peers))


def scatter_plan(grid, terms, cuts):
    nz, nx, ny = grid.nz, grid.nx, grid.ny
    shapes, outs, scratch = [], [], []
    for t, q in zip(terms, cuts):
        _, rows, n = t.shape
        if n < 128:
            rows, n = rows * n // 128, 128
        k = rows // grid.nq
        q = max(1, min(q, k // 32))
        kh = k // (2 * q)
        shapes.append((2 * q, kh, n))
        outs.append(jax.ShapeDtypeStruct((2 * q, kh, n), jnp.float32))
        b = t.dtype
        scratch += [
            pltpu.VMEM((2, ny, nz, nx, kh, n), b),
            pltpu.VMEM((q, 2, ny, nz, nx, kh, n), b),
            pltpu.VMEM((q, max(ny - 1, 1), nz, nx, kh, n), b),
            pltpu.VMEM((q, max(nx - 1, 1), ny, nz, kh, n), b),
            pltpu.VMEM((q, max(nx - 1, 1), nz, kh, n), b),
            pltpu.VMEM((q, max(ny - 1, 1), nz, kh, n), b),
            pltpu.VMEM((q, 2, max(nz - 1, 1), kh, n), b),
        ]
    per = (grid.nc - 1) + (nx - 1) + (ny - 1) + (nz - 1)
    count = per * sum(s[0] for s in shapes)
    return shapes, outs, scratch, count


def block_of(e, nq, blocks):
    return e * blocks // nq


def mix_kernel(grid, width, dims, shapes, *refs):
    n = len(shapes)
    shards, refs = refs[:n], refs[n:]
    tok, tile, alive, spans, mask, *refs = refs
    wholes, refs = refs[:n], refs[n:]
    (normed_out, active_out, x_out, mixed_out, carry_out, par_out, aff_out, probs_out, out_one_out, two_out, layer_out,
     proj_hbm, value_hbm, att_hbm, hin_hbm, hpre_hbm, ffn_hbm, act_hbm,
     proj, value_pre, att, hin, hpre, ffn_pre, act, values,
     tiles, table, bound, sends_t, recv_t, sends_b, recv_b, own_sem, flush_sem, load_sem, send, recv,
     *slots) = refs
    nq, ng = grid.nq, grid.ng
    rows = tok.shape[0]
    blocks = width // 128
    s = lax.axis_index("seq")
    seq_peer, seg_peer = small_peers(grid)
    meet(seq_peer + seg_peer)
    steps = gather_steps(grid, shapes, shards, wholes, own_sem, Sems(send, recv))

    done = set()

    def pump(count=1):
        for _ in range(count):
            done.update(next(steps, ()))

    copies = []
    for d in range(1, ng):
        copies.append(pltpu.make_async_remote_copy(
            tile, tiles.at[d - 1], sends_t.at[d - 1], recv_t.at[d - 1],
            device_id=seg_peer[d - 1], device_id_type=MESH))
        copies[-1].start()
    for copy in copies:
        copy.wait_recv()
    lanes = tile[...]
    for d in range(1, ng):
        lanes += tiles[d - 1]
    table[s] = lanes
    for d in range(1, nq):
        copies.append(pltpu.make_async_remote_copy(
            table.at[s], table.at[s], sends_t.at[ng + d - 2], recv_t.at[ng + d - 2],
            device_id=seq_peer[d - 1], device_id_type=MESH))
        copies[-1].start()
    pump()
    for d in range(1, nq):
        came = table.at[lax.rem(s + nq - d, nq)]
        pltpu.make_async_remote_copy(
            came, came, sends_t.at[ng + d - 2], recv_t.at[ng + d - 2],
            device_id=seq_peer[d - 1], device_id_type=MESH).wait_recv()
    count = 4 * dims + 3
    for b in range(blocks):
        mine = [e for e in range(nq) if block_of(e, nq, blocks) == b]
        whole = table[mine[0], 0:count]
        for e in mine[1:]:
            whole += table[e, 0:count]
        par_out[:, b, :] = whole
    aff = table[0, count : count + 4]
    for e in range(1, nq):
        aff += table[e, count : count + 4]
    aff_out[...] = aff

    pump()

    gain = [par_out[4 * dims, b : b + 1, :] for b in range(blocks)]
    step_rows = 32

    @pl.loop(0, rows // step_rows)
    def _(i):
        at = pl.ds(pl.multiple_of(i * step_rows, step_rows), step_rows)
        v = tok[at, :].astype(jnp.float32)
        r = lax.rsqrt(jnp.mean(v * v, axis=1, keepdims=True) + epsilon)
        for b in range(blocks):
            lane = slice(b * 128, b * 128 + 128)
            n = (v[:, lane] * r * gain[b]).astype(jnp.bfloat16)
            normed_out[at, lane] = n
            x_out[pl.ds(i * step_rows * blocks + b, step_rows, stride=blocks), :] = n.astype(jnp.float32)

    damping = [jax.nn.sigmoid(par_out[j]) for j in range(dims)]
    keep = [1.0 - damping[j] * jax.nn.sigmoid(par_out[dims + j]) for j in range(dims)]
    weight = [damping[j] * par_out[2 * dims + j] * par_out[3 * dims + j] for j in range(dims)]
    omega = par_out[4 * dims + 1]

    def row(ref, p):
        return ref[pl.ds(pl.multiple_of(p * blocks, blocks), blocks), :]

    def first_pass(p, state):
        x, a = row(x_out, p), alive[pl.ds(p, 1), :]
        return tuple(keep[j] * (state[j] * a) + x for j in range(dims))

    zero = tuple(jnp.zeros((blocks, 128), jnp.float32) for _ in range(dims))
    pump()
    ends = zero
    for part in range(2):
        ends = lax.fori_loop(part * rows // 2, (part + 1) * rows // 2, first_pass, ends, unroll=4)
        if part == 0:
            pump()
    for j in range(dims):
        bound[s, j] = ends[j]
    out = []
    for d in range(1, nq):
        out.append(pltpu.make_async_remote_copy(
            bound.at[s], bound.at[s], sends_b.at[d - 1], recv_b.at[d - 1],
            device_id=seq_peer[d - 1], device_id_type=MESH))
        out[-1].start()
    pump(3)
    for d in range(1, nq):
        came = bound.at[lax.rem(s + nq - d, nq)]
        pltpu.make_async_remote_copy(
            came, came, sends_b.at[d - 1], recv_b.at[d - 1],
            device_id=seq_peer[d - 1], device_id_type=MESH).wait_recv()
    for j in range(dims):
        through = power(keep[j], rows)
        state = jnp.zeros((blocks, 128), jnp.float32)
        for e in range(nq - 1):
            later = through * spans[e : e + 1, :] * state + bound[e, j]
            state = jnp.where(e < s, later, state)
        carry_out[j] = state

    def second_pass(p, state):
        x, a = row(x_out, p), alive[pl.ds(p, 1), :]
        state = tuple(keep[j] * (state[j] * a) + x for j in range(dims))
        sums = [omega * x] + [weight[j] * state[j] for j in range(dims)]
        while len(sums) > 1:
            sums = [sum(sums[k : k + 2][1:], sums[k]) for k in range(0, len(sums), 2)]
        mixed_out[pl.ds(pl.multiple_of(p * blocks, blocks), blocks), :] = sums[0]
        return state

    state = tuple(carry_out[j] for j in range(dims))
    for part in range(4):
        state = lax.fori_loop(part * rows // 4, (part + 1) * rows // 4, second_pass, state, unroll=4)
        if part % 2:
            pump()
    for b in range(blocks):
        m = mixed_out[pl.ds(b, rows, stride=blocks), :]
        active_out[:, b * 128 : b * 128 + 128] = (m * jax.nn.sigmoid(m)).astype(jnp.bfloat16)
    for copy in copies + out:
        copy.wait_send()

    flushes = []

    def flush(ref, hbm):
        copy = pltpu.make_async_copy(ref, hbm, flush_sem.at[len(flushes)])
        copy.start()
        flushes.append(copy)

    def pieces(i):
        while i not in done:
            pump()

        def fetch(g):
            return pltpu.make_async_copy(
                wholes[i].at[g // grid.nc, g % grid.nc], slots[i].at[g % 2], load_sem.at[i, g % 2]
            )

        fetch(0).start()
        for g in range(grid.ng):
            if g + 1 < grid.ng:
                fetch(g + 1).start()
            fetch(g).wait()
            piece = slots[i][g % 2]
            wide = piece.shape[-1]
            yield g, slice(g * wide, g * wide + wide), piece.reshape(-1, wide)
            pump()

    block_rows = 32
    zdim = aff_out.shape[1]
    vdim = value_pre.shape[1]
    first_gate, first_reset, first_cand = width, width + zdim, width + zdim + vdim
    dot = functools.partial(jnp.dot, preferred_element_type=jnp.float32)

    def by_rows(count=rows, each=block_rows):
        def wrap(f):
            pl.loop(0, count // each)(lambda i: f(pl.ds(pl.multiple_of(i * each, each), each)))

        return wrap

    for g, cols, piece in pieces(0):
        proj[:, cols] = dot(active_out[...], piece)
    flush(proj, proj_hbm)

    scale_q = zdim**-0.5
    near = []
    for r in range(rows // STRETCH):
        at = slice(r * STRETCH, r * STRETCH + STRETCH)
        gate = proj[at, first_gate:first_reset]
        shared = gate * jax.nn.sigmoid(gate)
        query = (scale_q * (shared * aff_out[0:1] + aff_out[1:2])).astype(jnp.bfloat16)
        key = (shared * aff_out[2:3] + aff_out[3:4]).astype(jnp.bfloat16)
        scores = lax.dot_general(query, key, (((1,), (1,)), ((), ())), preferred_element_type=jnp.float32)
        scores = jnp.where(mask[at, :] > 0.0, scores, -1e30)
        expo = jnp.exp(scores - jnp.max(scores, axis=1, keepdims=True))
        probs = expo / jnp.sum(expo, axis=1, keepdims=True)
        probs_out[at, :] = probs
        near.append(probs.astype(jnp.bfloat16))

    for g, cols, piece in pieces(1):
        pre = dot(normed_out[...], piece)
        value_pre[:, cols] = pre
        values[:, cols] = (pre * jax.nn.sigmoid(pre)).astype(jnp.bfloat16)
    flush(value_pre, value_hbm)
    for r in range(rows // STRETCH):
        at = slice(r * STRETCH, r * STRETCH + STRETCH)
        att[at, :] = dot(near[r], values[at, :])

    @by_rows()
    def _(at):
        gate = proj[at, first_reset:first_cand]
        hin[at, :] = (att[at, :] * (gate * jax.nn.sigmoid(gate))).astype(jnp.bfloat16)

    flush(att, att_hbm)
    flush(hin, hin_hbm)

    for g, cols, piece in pieces(2):
        hpre[:, cols] = proj[:, first_cand + cols.start : first_cand + cols.stop] + dot(hin[...], piece)
    flush(hpre, hpre_hbm)

    gain_two = [par_out[4 * dims + 2, b : b + 1, :] for b in range(blocks)]

    @by_rows()
    def _(at):
        v = tok[at, :].astype(jnp.float32)
        h = hpre[at, :]
        one = v + jax.nn.sigmoid(proj[at, 0:width]) * (h * jax.nn.sigmoid(h) - v)
        out_one_out[at, :] = one
        r = lax.rsqrt(jnp.mean(one * one, axis=1, keepdims=True) + epsilon)
        for b in range(blocks):
            lane = slice(b * 128, b * 128 + 128)
            two_out[at, lane] = (one[:, lane] * r * gain_two[b]).astype(jnp.bfloat16)

    for g, cols, piece in pieces(3):
        pre = dot(two_out[...], piece)
        ffn_pre[:, cols] = pre
        act[:, cols] = (pre * jax.nn.sigmoid(pre)).astype(jnp.bfloat16)
    flush(ffn_pre, ffn_hbm)
    flush(act, act_hbm)
    for g, cols, piece in pieces(4):
        layer_out[:, cols] = (out_one_out[:, cols] + dot(act[...], piece)).astype(jnp.bfloat16)
    for _ in steps:
        pass
    for copy in flushes:
        copy.wait()


def power(v, n):
    result = None
    while n:
        if n & 1:
            result = v if result is None else result * v
        n >>= 1
        if n:
            v = v * v
    return result


def mix_forward(grid, weights, cuts, tok, tile, alive, spans, mask, dims, collective_id):
    rows, width = tok.shape
    nq, ng = grid.nq, grid.ng
    blocks = width // 128
    f = jnp.float32
    vm = pl.BlockSpec(memory_space=pltpu.VMEM)
    shapes, shards, outs, count = gather_plan(grid, weights, cuts)
    n = len(shards)
    vdim, fdim, proj_dim = weights[1].shape[1] * ng, weights[3].shape[1] * ng, weights[0].shape[1] * ng
    low = jnp.bfloat16
    kept = [
        ((rows, proj_dim), f),
        ((rows, vdim), f),
        ((rows, vdim), f),
        ((rows, vdim), low),
        ((rows, width), f),
        ((rows, fdim), f),
        ((rows, fdim), low),
    ]
    local = [
        ((rows, width), low),
        ((rows, width), low),
        ((rows * blocks, 128), f),
        ((rows * blocks, 128), f),
        ((dims, blocks, 128), f),
        ((4 * dims + 3, blocks, 128), f),
        ((4, 128), f),
        ((rows, STRETCH), f),
        ((rows, width), f),
        ((rows, width), low),
        ((rows, width), low),
    ]
    result = pl.pallas_call(
        functools.partial(mix_kernel, grid, width, dims, shapes),
        out_shape=outs + [jax.ShapeDtypeStruct(*v) for v in local + kept],
        in_specs=[ANY] * n + [vm] * 5,
        out_specs=[ANY] * n + [vm] * len(local) + [ANY] * len(kept),
        scratch_shapes=[pltpu.VMEM(*v) for v in kept]
        + [
            pltpu.VMEM((rows, vdim), low),
            pltpu.VMEM((ng - 1,) + tile.shape, f),
            pltpu.VMEM((nq,) + tile.shape, f),
            pltpu.VMEM((nq, dims, blocks, 128), f),
            pltpu.SemaphoreType.DMA((nq + ng - 2,)),
            pltpu.SemaphoreType.DMA((nq + ng - 2,)),
            pltpu.SemaphoreType.DMA((nq - 1,)),
            pltpu.SemaphoreType.DMA((nq - 1,)),
            pltpu.SemaphoreType.DMA((n,)),
            pltpu.SemaphoreType.DMA((len(kept),)),
            pltpu.SemaphoreType.DMA((n, 2)),
            pltpu.SemaphoreType.DMA((count,)),
            pltpu.SemaphoreType.DMA((count,)),
        ]
        + [pltpu.VMEM((2,) + o.shape[2:], o.dtype) for o in outs],
        compiler_params=pltpu.CompilerParams(
            collective_id=collective_id, has_side_effects=True, vmem_limit_bytes=60 << 20
        ),
    )(*shards, tok, tile, alive, spans, mask)
    return result[:n], result[n:]


def scan_back(grid, dims, g_rows, x_in, mixed, carry, par, alive, spans, gin_rows, before, bound, sends_b, recv_b,
              m_all, k_all, seq_peer, s, pump):
    nq = grid.nq
    blocks = carry.shape[1]
    rows = g_rows.shape[0] // blocks

    @pl.loop(0, rows * blocks // 64)
    def _(i):
        at = pl.ds(pl.multiple_of(i * 64, 64), 64)
        g_rows[at, :] = g_rows[at, :] * silu_slope(mixed[at, :])

    damping = [jax.nn.sigmoid(par[j]) for j in range(dims)]
    keep = [1.0 - damping[j] * jax.nn.sigmoid(par[dims + j]) for j in range(dims)]
    weight = [damping[j] * par[2 * dims + j] * par[3 * dims + j] for j in range(dims)]
    omega = par[4 * dims + 1]

    def row(ref, p):
        return ref[pl.ds(pl.multiple_of(p * blocks, blocks), blocks), :]

    def first_pass(i, flow):
        p = rows - 1 - i
        gp, a = row(g_rows, p), alive[pl.ds(p, 1), :]
        return tuple(keep[j] * (a * (gp + flow[j])) for j in range(dims))

    zero = jnp.zeros((blocks, 128), jnp.float32)
    ends = lax.fori_loop(0, rows, first_pass, (zero,) * dims, unroll=4)
    for j in range(dims):
        bound[s, j] = ends[j]
    def sent(d):
        return pltpu.make_async_remote_copy(
            bound.at[s], bound.at[s], sends_b.at[d - 1], recv_b.at[d - 1],
            device_id=seq_peer[d - 1], device_id_type=MESH)

    for d in range(1, nq):
        sent(d).start()
    pump()
    for d in range(1, nq):
        came = bound.at[lax.rem(s + nq - d, nq)]
        pltpu.make_async_remote_copy(
            came, came, sends_b.at[d - 1], recv_b.at[d - 1],
            device_id=seq_peer[d - 1], device_id_type=MESH).wait_recv()
    flow_in = []
    for j in range(dims):
        through = power(keep[j], rows)
        flow = zero
        for e in range(nq - 1, 0, -1):
            later = through * spans[e : e + 1, :] * flow + bound[e, j]
            flow = jnp.where(e > s, later, flow)
        flow_in.append(flow)

    few = before.shape[1]
    for j0 in range(0, dims, few):
        js = range(j0, j0 + few)

        def ahead(p, state):
            x, a = row(x_in, p), alive[pl.ds(p, 1), :]
            for t in range(few):
                before[p, t] = state[t]
            return tuple(keep[j] * (state[t] * a) + x for t, j in enumerate(js))

        lax.fori_loop(0, rows, ahead, tuple(carry[j] for j in js), unroll=4)
        if j0:
            pump()

        def back(i, held):
            flow, m_sum, k_sum, om_sum = held
            p = rows - 1 - i
            at = pl.ds(pl.multiple_of(p * blocks, blocks), blocks)
            gp, x, a = g_rows[at, :], x_in[at, :], alive[pl.ds(p, 1), :]
            total = omega * gp if j0 == 0 else gin_rows[at, :]
            if j0 == 0:
                om_sum = om_sum + gp * x
            new_flow, new_m, new_k = [], [], []
            for t, j in enumerate(js):
                c = gp + flow[t]
                ac = a * c
                total = total + weight[j] * c
                new_flow.append(keep[j] * ac)
                new_m.append(m_sum[t] + c * x)
                new_k.append(k_sum[t] + ac * before[p, t])
            gin_rows[at, :] = total
            return tuple(new_flow), tuple(new_m), tuple(new_k), om_sum

        zeros = (zero,) * few
        _, m_sum, k_sum, om_sum = lax.fori_loop(
            0, rows, back, (tuple(flow_in[j] for j in js), zeros, zeros, zero), unroll=4
        )
        for t, j in enumerate(js):
            m_all[j] = m_sum[t]
            k_all[j] = k_sum[t]
        if j0 == 0:
            m_all[dims] = om_sum
        pump()
    for d in range(1, nq):
        sent(d).wait_send()


def norm_back(par, dims, tok, pre, direct, gin_rows, gtok_out, row_sums):
    rows, width = tok.shape
    blocks = width // 128
    gain = [par[4 * dims, b : b + 1, :] for b in range(blocks)]
    lanes = [slice(b * 128, b * 128 + 128) for b in range(blocks)]
    step_rows = 32

    def some(i, gains):
        at = pl.ds(pl.multiple_of(i * step_rows, step_rows), step_rows)
        v = tok[at, :].astype(jnp.float32)
        r = lax.rsqrt(jnp.mean(v * v, axis=1, keepdims=True) + epsilon)
        gy = []
        for b in range(blocks):
            came = gin_rows[pl.ds(i * step_rows * blocks + b, step_rows, stride=blocks), :]
            gy.append(pre[at, lanes[b]] + came.astype(jnp.bfloat16).astype(jnp.float32))
        scaled = [gy[b] * gain[b] for b in range(blocks)]
        dots = sum(jnp.sum(scaled[b] * v[:, lanes[b]], axis=1, keepdims=True) for b in range(blocks))
        pull = r * r * (dots / width)
        new = []
        for b in range(blocks):
            vb = v[:, lanes[b]]
            gx = r * (scaled[b] - vb * pull)
            gtok_out[at, lanes[b]] = (direct[at, lanes[b]] + gx).astype(jnp.bfloat16)
            new.append(gains[b] + jnp.sum(gy[b] * (vb * r), axis=0, keepdims=True))
        return tuple(new)

    gains = lax.fori_loop(
        0, rows // step_rows, some, tuple(jnp.zeros((1, 128), jnp.float32) for _ in range(blocks))
    )
    for b in range(blocks):
        row_sums[b : b + 1, :] = gains[b]


def fill_small(grid, dims, small, m_all, k_all, row_sums):
    blocks = row_sums.shape[0]
    for e in range(grid.nq):
        b = block_of(e, grid.nq, blocks)
        small[e, 0:dims] = m_all[0:dims, b, :]
        small[e, dims : 2 * dims] = k_all[:, b, :]
        small[e, 2 * dims : 2 * dims + 1] = m_all[dims, b : b + 1, :]
        small[e, 2 * dims + 1 : 2 * dims + 2] = row_sums[b : b + 1, :]


def mix_back_kernel(grid, dims, shapes, *refs):
    n = len(shapes)
    terms, refs = refs[:n], refs[n:]
    gact, x_in, mixed, carry, par, alive, spans, tok, pre, direct, small_in, *refs = refs
    sums, refs = refs[:n], refs[n:]
    (gtok_out, small_out,
     g_rows, gin_rows, before, bound, m_all, k_all, row_sums, small, seq_in, seg_in,
     sends_b, recv_b, s_send, s_recv, own_sem, send, recv, *scratch) = refs
    nq = grid.nq
    rows, width = gact.shape
    blocks = width // 128
    s = lax.axis_index("seq")
    seq_peer, seg_peer = small_peers(grid)
    meet(seq_peer + seg_peer)
    steps = scatter_steps(grid, shapes, terms, sums, scratch, own_sem, Sems(send, recv))
    little = SmallSum(grid, small, small_out, seq_in, seg_in, s_send, s_recv)

    def pump(count=1):
        for _ in range(count):
            next(steps, None)

    pump(2)
    for b in range(blocks):
        g_rows[pl.ds(b, rows, stride=blocks), :] = gact[:, b * 128 : b * 128 + 128].astype(jnp.float32)

    scan_back(
        grid, dims, g_rows, x_in, mixed, carry, par, alive, spans, gin_rows, before, bound, sends_b, recv_b,
        m_all, k_all, seq_peer, s, pump
    )
    norm_back(par, dims, tok, pre, direct, gin_rows, gtok_out, row_sums)
    for e in range(nq):
        small[e] = small_in[e]
    fill_small(grid, dims, small, m_all, k_all, row_sums)
    little.start()
    pump()
    little.middle()
    for _ in steps:
        pass
    little.end()


def mix_backward(grid, terms, cuts, gact, x_in, mixed, carry, par, alive, spans, tok, pre, direct, small, collective_id):
    rows, width = gact.shape
    nq, ng = grid.nq, grid.ng
    blocks, dims, few = width // 128, carry.shape[0], 4
    f = jnp.float32
    vm = pl.BlockSpec(memory_space=pltpu.VMEM)
    shapes, outs, scratch, count = scatter_plan(grid, terms, cuts)
    parts = [t.reshape((grid.ny, grid.nc, grid.nz, grid.nx) + v) for t, v in zip(terms, shapes)]
    n = len(parts)
    result = pl.pallas_call(
        functools.partial(mix_back_kernel, grid, dims, shapes),
        out_shape=outs
        + [jax.ShapeDtypeStruct((rows, width), jnp.bfloat16), jax.ShapeDtypeStruct(small.shape[1:], f)],
        in_specs=[ANY] * n + [vm] * 11,
        out_specs=[vm] * (n + 2),
        scratch_shapes=[
            pltpu.VMEM((rows * blocks, 128), f),
            pltpu.VMEM((rows * blocks, 128), f),
            pltpu.VMEM((rows, few, blocks, 128), f),
            pltpu.VMEM((nq, dims, blocks, 128), f),
            pltpu.VMEM((dims + 1, blocks, 128), f),
            pltpu.VMEM((dims, blocks, 128), f),
            pltpu.VMEM((blocks, 128), f),
            pltpu.VMEM(small.shape, f),
            pltpu.VMEM((nq - 1,) + small.shape[1:], f),
            pltpu.VMEM((ng - 1,) + small.shape[1:], f),
            pltpu.SemaphoreType.DMA((nq - 1,)),
            pltpu.SemaphoreType.DMA((nq - 1,)),
            pltpu.SemaphoreType.DMA((nq + ng - 2,)),
            pltpu.SemaphoreType.DMA((nq + ng - 2,)),
            pltpu.SemaphoreType.DMA((n, 2)),
            pltpu.SemaphoreType.DMA((count,)),
            pltpu.SemaphoreType.DMA((count,)),
        ]
        + scratch,
        compiler_params=pltpu.CompilerParams(
            collective_id=collective_id, has_side_effects=True, vmem_limit_bytes=62 << 20
        ),
    )(*parts, gact, x_in, mixed, carry, par, alive, spans, tok, pre, direct, small)
    return [v.reshape(-1, t.shape[-1]) for v, t in zip(result, terms)], result[n], result[n + 1]


def layer_back_kernel(grid, dims, shapes, sizes, *refs):
    n = len(shapes)
    zdim, vdim, fdim = sizes
    wholes, refs = refs[:n], refs[n:]
    (cot_hbm, act_hbm, ffn_hbm, two_hbm, one_hbm, hpre_hbm, proj_hbm, att_hbm, hin_hbm, value_hbm, probs, active_hbm,
     normed_hbm, tok_hbm, x_hbm, mixed_hbm, carry, par, aff, alive, spans, *refs) = refs
    sums, refs = refs[:n], refs[n:]
    gtok_out, small_out, *refs = refs
    terms, refs = refs[:n], refs[n:]
    (gproj, direct, pre, bound, m_all, k_all, row_sums, two_sums, aff_sums, small, seq_in, seg_in,
     sends_b, recv_b, s_send, s_recv, own_sem, load_sem, tile_sem, stage_sem, send, recv, *scratch) = refs
    nq, ng, nc, nz = grid.nq, grid.ng, grid.nc, grid.nz
    rows, width = direct.shape
    blocks = width // 128
    low, f = jnp.bfloat16, jnp.float32
    s = lax.axis_index("seq")
    seq_peer, seg_peer = small_peers(grid)
    meet(seq_peer + seg_peer)
    ready = [0]
    steps = scatter_steps(grid, shapes, terms, sums, scratch, own_sem, Sems(send, recv), lambda: ready[0])
    little = SmallSum(grid, small, small_out, seq_in, seg_in, s_send, s_recv)
    loads = [0]

    def pump(count=1):
        for _ in range(count):
            next(steps, None)

    pump()
    dot = functools.partial(jnp.dot, preferred_element_type=f)

    def dot_nt(a, b):
        return lax.dot_general(a, b, (((1,), (1,)), ((), ())), preferred_element_type=f)

    def dot_tn(a, b):
        return lax.dot_general(a, b, (((0,), (0,)), ((), ())), preferred_element_type=f)

    def fetch(src, dst):
        copy = pltpu.make_async_copy(src, dst, load_sem.at[loads[0]])
        loads[0] += 1
        copy.start()
        return copy.wait

    def by_rows(each=32):
        def wrap(some):
            pl.loop(0, rows // each)(lambda i: some(pl.ds(pl.multiple_of(i * each, each), each)))

        return wrap

    def wide(i):
        return shapes[i][-1]

    def tile_shape(i):
        return (2, grid.ny, nc, grid.nx) + shapes[i]

    def depth(i):
        return grid.nx * shapes[i][0] * shapes[i][1]

    def tile(i, tiles, zt):
        return pltpu.make_async_copy(wholes[i].at[:, :, zt], tiles.at[zt % 2], tile_sem.at[zt % 2])

    def begin(i, tiles):
        for zt in range(min(2, nz)):
            tile(i, tiles, zt).start()

    def against(i, tiles, part):
        for zt in range(nz):
            tile(i, tiles, zt).wait()
            total = None
            for g in range(ng):
                term = dot_nt(part(g), tiles[zt % 2, g // nc, g % nc].reshape(depth(i), wide(i)))
                total = term if total is None else total + term
            if zt + 2 < nz:
                tile(i, tiles, zt + 2).start()
            if zt == 1:
                pump()
            yield slice(zt * depth(i), zt * depth(i) + depth(i)), total

    def grads(i, left, stage, part):
        copies = []
        slots = stage.shape[0]
        for g in range(ng):
            right = part(g)
            for zt in range(nz):
                k = len(copies)
                if k >= slots:
                    copies[k - slots].wait()
                d = depth(i)
                term = dot(left[zt * d : zt * d + d, :], right)
                stage[k % slots] = term.astype(low).reshape(stage.shape[1:])
                copies.append(
                    pltpu.make_async_copy(stage.at[k % slots], terms[i].at[g // nc, g % nc, zt], stage_sem.at[k % slots])
                )
                copies[k].start()
        for copy in copies[-slots:]:
            copy.wait()
        ready[0] = i + 1

    def turned(src, dst):
        for a in range(0, src.shape[1], 256):
            b = min(a + 256, src.shape[1])
            dst[a:b, :] = src[:, a:b].T

    def vm(*shape, kind=low):
        return pltpu.VMEM(shape, kind)

    def stage_of(i, slots=4):
        return pltpu.VMEM((slots, grid.nx) + shapes[i], low)

    def cut(ref, i):
        return lambda g: ref[:, g * wide(i) : (g + 1) * wide(i)]

    first_gate, first_reset, first_cand = width, width + zdim, width + zdim + vdim
    out_i, in_i, att_i, value_i, mix_i = range(5)

    def ffn_back(cot, hold, norm_grad, two):
        wait_cot, wait_act, wait_two = fetch(cot_hbm, cot), fetch(act_hbm, hold), fetch(two_hbm, two)

        def second(pre_act, left, stage, tiles):
            begin(out_i, tiles)
            each = depth(out_i)
            pre_waits = [fetch(ffn_hbm.at[:, k * each : (k + 1) * each], pre_act.at[k]) for k in range(2)]
            wait_act()
            turned(hold, left)
            wait_cot()
            grads(out_i, left, stage, cut(cot, out_i))
            pump()
            for k, (cols, grad) in enumerate(against(out_i, tiles, cut(cot, out_i))):
                pre_waits[k]()
                hold[:, cols] = (grad * silu_slope(pre_act[k % 2])).astype(low)
                if k + 2 < nz:
                    pre_waits.append(fetch(ffn_hbm.at[:, (k + 2) * each : (k + 3) * each], pre_act.at[k % 2]))
            pump()

        pl.run_scoped(
            second, vm(2, rows, depth(out_i), kind=f), vm(fdim, rows), stage_of(out_i), pltpu.VMEM(tile_shape(out_i), low)
        )

        def rest(one, hpre, upd, tok):
            waits = [fetch(one_hbm, one), fetch(hpre_hbm, hpre), fetch(proj_hbm.at[:, 0:width], upd), fetch(tok_hbm, tok)]

            def first(left, stage, tiles):
                begin(in_i, tiles)
                wait_two()
                turned(two, left)
                grads(in_i, left, stage, cut(hold, in_i))
                pump()
                for cols, grad in against(in_i, tiles, cut(hold, in_i)):
                    norm_grad[:, cols] = grad

            pl.run_scoped(first, vm(width, rows), stage_of(in_i), pltpu.VMEM(tile_shape(in_i), low))
            for wait in waits:
                wait()
            two_sums[...] = jnp.zeros_like(two_sums)

            @by_rows(16)
            def _(at):
                v, x, h, c = one[at, :], tok[at, :].astype(f), hpre[at, :], cot[at, :].astype(f)
                gain = jnp.concatenate([par[4 * dims + 2, b : b + 1, :] for b in range(blocks)], axis=1)
                r = lax.rsqrt(jnp.mean(v * v, axis=1, keepdims=True) + epsilon)
                gy = norm_grad[at, :]
                scaled = gy * gain
                pull = r * r * jnp.mean(scaled * v, axis=1, keepdims=True)
                grad_one = c + r * (scaled - v * pull)
                two_sums[...] += jnp.sum(gy * (v * r), axis=0, keepdims=True)
                u = jax.nn.sigmoid(upd[at, :])
                sig = jax.nn.sigmoid(h)
                direct[at, :] = grad_one * (1.0 - u)
                gproj[at, first_cand:] = (grad_one * u * (sig * (1.0 + h * (1.0 - sig)))).astype(low)
                gproj[at, 0:width] = (grad_one * (h * sig - x) * (u * (1.0 - u))).astype(low)

        pl.run_scoped(
            rest, vm(rows, width, kind=f), vm(rows, width, kind=f), vm(rows, width, kind=f), vm(rows, width)
        )

    pl.run_scoped(ffn_back, vm(rows, width), vm(rows, fdim), vm(rows, width, kind=f), vm(rows, width))
    pump()

    def attention_back(grad_hin, att, gate, shared_pre, value_pre):
        waits = [
            fetch(att_hbm, att),
            fetch(proj_hbm.at[:, first_reset:first_cand], gate),
            fetch(proj_hbm.at[:, first_gate:first_reset], shared_pre),
            fetch(value_hbm, value_pre),
        ]

        def out_back(hin, left, stage, tiles):
            wait_hin = fetch(hin_hbm, hin)
            begin(att_i, tiles)
            wait_hin()
            turned(hin, left)

            def part(g):
                return gproj[:, first_cand + g * wide(att_i) : first_cand + (g + 1) * wide(att_i)]

            grads(att_i, left, stage, part)
            pump()
            for cols, grad in against(att_i, tiles, part):
                grad_hin[:, cols] = grad

        pl.run_scoped(out_back, vm(rows, vdim), vm(vdim, rows), stage_of(att_i), pltpu.VMEM(tile_shape(att_i), low))

        def inner(grad_pre, normed, value_tiles):
            wait_normed = fetch(normed_hbm, normed)
            begin(value_i, value_tiles)

            def blocks_back(grad_att, values):
                for wait in waits:
                    wait()

                @by_rows(16)
                def _(at):
                    v, g, p = gate[at, :], grad_hin[at, :], value_pre[at, :]
                    sig = jax.nn.sigmoid(v)
                    grad_att[at, :] = (g * (v * sig)).astype(low)
                    gproj[at, first_reset:first_cand] = (g * att[at, :] * (sig * (1.0 + v * (1.0 - sig)))).astype(low)
                    values[at, :] = (p * jax.nn.sigmoid(p)).astype(low)

                aff_total = [jnp.zeros((1, zdim), f)] * 4
                scale_q = zdim**-0.5
                for r in range(rows // STRETCH):
                    at = slice(r * STRETCH, r * STRETCH + STRETCH)
                    v = shared_pre[at, :]
                    shared = v * jax.nn.sigmoid(v)
                    query = (scale_q * (shared * aff[0:1] + aff[1:2])).astype(low)
                    key = (shared * aff[2:3] + aff[3:4]).astype(low)
                    prob, ga = probs[at, :], grad_att[at, :]
                    grad_prob = dot_nt(ga, values[at, :])
                    weighted = jnp.sum(prob * grad_prob, axis=1, keepdims=True)
                    grad_score = (prob * (grad_prob - weighted)).astype(low)
                    grad_query = dot(grad_score, key) * scale_q
                    grad_key = dot_tn(grad_score, query)
                    grad_shared = grad_query * aff[0:1] + grad_key * aff[2:3]
                    gproj[at, first_gate:first_reset] = (grad_shared * silu_slope(v)).astype(low)
                    for k, t in enumerate([grad_query * shared, grad_query, grad_key * shared, grad_key]):
                        aff_total[k] = aff_total[k] + jnp.sum(t, axis=0, keepdims=True)
                    grad_hin[at, :] = dot_tn(prob.astype(low), ga)
                for k in range(4):
                    aff_sums[k : k + 1, :] = aff_total[k]

                @by_rows(16)
                def _(at):
                    grad_pre[at, :] = (grad_hin[at, :] * silu_slope(value_pre[at, :])).astype(low)

            pl.run_scoped(blocks_back, vm(rows, vdim), vm(rows, vdim))
            pump()

            def value_back(left, stage):
                wait_normed()
                turned(normed, left)
                grads(value_i, left, stage, cut(grad_pre, value_i))
                for cols, grad in against(value_i, value_tiles, cut(grad_pre, value_i)):
                    pre[:, cols] = grad

            pl.run_scoped(value_back, vm(width, rows), stage_of(value_i))

        pl.run_scoped(inner, vm(rows, vdim), vm(rows, width), pltpu.VMEM(tile_shape(value_i), low))

    pl.run_scoped(
        attention_back, vm(rows, vdim, kind=f), vm(rows, vdim, kind=f), vm(rows, vdim, kind=f), vm(rows, zdim, kind=f),
        vm(rows, vdim, kind=f)
    )
    pump()

    def mix_back(g_rows, gin_rows, x_in, mixed, tok):
        waits = [fetch(x_hbm, x_in), fetch(mixed_hbm, mixed), fetch(tok_hbm, tok)]

        def mix_weight_back(active, left, stage, tiles):
            wait_active = fetch(active_hbm, active)
            begin(mix_i, tiles)
            wait_active()
            turned(active, left)
            grads(mix_i, left, stage, cut(gproj, mix_i))
            pump()
            for cols, grad in against(mix_i, tiles, cut(gproj, mix_i)):
                grad = grad.astype(low).astype(f)
                for b in range(cols.start // 128, cols.stop // 128):
                    lane = b * 128 - cols.start
                    g_rows[pl.ds(b, rows, stride=blocks), :] = grad[:, lane : lane + 128]

        pl.run_scoped(
            mix_weight_back, vm(rows, width), vm(width, rows), stage_of(mix_i), pltpu.VMEM(tile_shape(mix_i), low)
        )

        for wait in waits:
            wait()

        def scan(before):
            scan_back(
                grid, dims, g_rows, x_in, mixed, carry, par, alive, spans, gin_rows, before, bound, sends_b, recv_b,
                m_all, k_all, seq_peer, s, pump
            )

        pl.run_scoped(scan, vm(rows, 4, blocks, 128, kind=f))
        norm_back(par, dims, tok, pre, direct, gin_rows, gtok_out, row_sums)

    pl.run_scoped(
        mix_back, vm(rows * blocks, 128, kind=f), vm(rows * blocks, 128, kind=f), vm(rows * blocks, 128, kind=f),
        vm(rows * blocks, 128, kind=f), vm(rows, width)
    )
    small[...] = jnp.zeros_like(small)
    fill_small(grid, dims, small, m_all, k_all, row_sums)
    for e in range(nq):
        b = block_of(e, nq, blocks)
        small[e, 2 * dims + 2 : 2 * dims + 3] = two_sums[:, b * 128 : b * 128 + 128]
        small[e, 2 * dims + 3 : 2 * dims + 7] = aff_sums[...]
    little.start()
    pump()
    little.middle()
    for _ in steps:
        pass
    little.end()


def layer_backward(grid, wholes, cuts, kept, probs, carry, par, aff, alive, spans, sizes, collective_id):
    nq, ng = grid.nq, grid.ng
    dims, blocks = carry.shape[0], carry.shape[1]
    zdim, vdim, fdim = sizes
    width = blocks * 128
    rows = probs.shape[0]
    f = jnp.float32
    vm = pl.BlockSpec(memory_space=pltpu.VMEM)
    n = len(wholes)
    like = [jax.ShapeDtypeStruct((ng, w.size // ng // w.shape[-1], w.shape[-1]), w.dtype) for w in wholes]
    shapes, outs, scratch, count = scatter_plan(grid, like, cuts)
    whole_shapes = [jax.ShapeDtypeStruct(w.shape[:4] + s, w.dtype) for w, s in zip(wholes, shapes)]
    low = [w.reshape(v.shape) for w, v in zip(wholes, whole_shapes)]
    small_shape = (-(-(2 * dims + 7) // 8) * 8, 128)
    result = pl.pallas_call(
        functools.partial(layer_back_kernel, grid, dims, shapes, sizes),
        out_shape=outs
        + [jax.ShapeDtypeStruct((rows, width), jnp.bfloat16), jax.ShapeDtypeStruct(small_shape, f)]
        + whole_shapes,
        in_specs=[ANY] * n + [ANY] * 10 + [vm] + [ANY] * 5 + [vm] * 5,
        out_specs=[vm] * (n + 2) + [ANY] * n,
        scratch_shapes=[
            pltpu.VMEM((rows, width * 2 + zdim + vdim), jnp.bfloat16),
            pltpu.VMEM((rows, width), f),
            pltpu.VMEM((rows, width), f),
            pltpu.VMEM((nq, dims, blocks, 128), f),
            pltpu.VMEM((dims + 1, blocks, 128), f),
            pltpu.VMEM((dims, blocks, 128), f),
            pltpu.VMEM((blocks, 128), f),
            pltpu.VMEM((1, width), f),
            pltpu.VMEM((4, zdim), f),
            pltpu.VMEM((nq,) + small_shape, f),
            pltpu.VMEM((nq - 1,) + small_shape, f),
            pltpu.VMEM((ng - 1,) + small_shape, f),
            pltpu.SemaphoreType.DMA((nq - 1,)),
            pltpu.SemaphoreType.DMA((nq - 1,)),
            pltpu.SemaphoreType.DMA((nq + ng - 2,)),
            pltpu.SemaphoreType.DMA((nq + ng - 2,)),
            pltpu.SemaphoreType.DMA((n, 2)),
            pltpu.SemaphoreType.DMA((24,)),
            pltpu.SemaphoreType.DMA((2,)),
            pltpu.SemaphoreType.DMA((4,)),
            pltpu.SemaphoreType.DMA((count,)),
            pltpu.SemaphoreType.DMA((count,)),
        ]
        + scratch,
        compiler_params=pltpu.CompilerParams(
            collective_id=collective_id, has_side_effects=True, vmem_limit_bytes=63 << 20
        ),
    )(*low, *kept[:10], probs, *kept[10:], carry, par, aff, alive, spans)
    return [v.reshape(-1, t.shape[-1]) for v, t in zip(result, like)], result[n], result[n + 1]


def rms_forward(values, gain):
    inverse = lax.rsqrt(jnp.mean(values * values, axis=-1, keepdims=True) + epsilon)
    return (values * inverse * gain, inverse)


def rms_backward(grad_out, values, inverse, gain):
    scaled = grad_out * gain
    projection = jnp.mean(scaled * values, axis=-1, keepdims=True)
    grad_in = inverse * (scaled - values * inverse * inverse * projection)
    return (grad_in, jnp.sum(grad_out * values * inverse, axis=0))


def silu_slope(values):
    sigma_v = jax.nn.sigmoid(values)
    return sigma_v * (1.0 + values * (1.0 - sigma_v))


def times(left, pieces):
    return jnp.concatenate(
        [jnp.dot(left, pieces[i], preferred_element_type=jnp.float32) for i in range(pieces.shape[0])], axis=1
    )


def against(left, pieces):
    n = pieces.shape[2]
    return sum(
        lax.dot_general(
            left[:, i * n : i * n + n], pieces[i], (((1,), (1,)), ((), ())), preferred_element_type=jnp.float32
        )
        for i in range(pieces.shape[0])
    )


def over_rows(left, right, count):
    n = right.shape[1] // count
    return jnp.stack(
        [
            lax.dot_general(
                left, right[:, i * n : i * n + n], (((0,), (0,)), ((), ())), preferred_element_type=jnp.float32
            ).astype(jnp.bfloat16)
            for i in range(count)
        ]
    )


def masked_scores(query_blk, key_blk, allowed):
    raw_scores = jnp.einsum("cid,cjd->cij", query_blk, key_blk, preferred_element_type=jnp.float32)
    return jnp.where(allowed, raw_scores, -1e30)


def backward_apart(grid, cotangent, tokens_low, forward, weights, alive, spans, sizes):
    (normed_b, active, x_rows, mixed_rows, carry, par, affine, probs, out_one, normed_two_b, _,
     projected, value_pre, attended, hidden_in, hidden_pre, ffn_hidden, ffn_act) = forward
    ffn_hidden = ffn_hidden.astype(jnp.float32)
    token_count, model_width = tokens_low.shape
    nq, ng = grid.nq, grid.ng
    dims, blocks = carry.shape[0], carry.shape[1]
    zdim, vdim, _ = sizes
    block_count = token_count // STRETCH
    tokens_flat = tokens_low.astype(jnp.float32)
    mix_full, value_full, out_full, ffn_in_full, ffn_out_full = (w.reshape(ng, -1, w.shape[-1]) for w in weights)
    gain_two = par[4 * dims + 2].reshape(-1)
    update = jax.nn.sigmoid(projected[:, :model_width])
    gate_pre = projected[:, model_width : model_width + zdim + vdim]
    gate_rows = jax.nn.silu(gate_pre)
    shared = gate_rows[:, :zdim]
    reset_gate = gate_rows[:, zdim:]
    values_b = jax.nn.silu(value_pre).astype(jnp.bfloat16)
    scale_q = zdim ** (-0.5)
    query_b = (scale_q * (shared * affine[0] + affine[1])).astype(jnp.bfloat16)
    key_b = (shared * affine[2] + affine[3]).astype(jnp.bfloat16)
    query_blk = query_b.reshape(block_count, STRETCH, zdim)
    key_blk = key_b.reshape(block_count, STRETCH, zdim)
    value_blk = values_b.reshape(block_count, STRETCH, vdim)
    probs = probs.reshape(block_count, STRETCH, STRETCH)
    probs_b = probs.astype(jnp.bfloat16)
    hidden_act = jax.nn.silu(hidden_pre)
    inverse_two = lax.rsqrt(jnp.mean(out_one * out_one, axis=-1, keepdims=True) + epsilon)

    grad_y_b = cotangent
    grad_ffn_out = over_rows(ffn_act, grad_y_b, ng)
    grad_act = against(grad_y_b, ffn_out_full)
    grad_hidden_b = (grad_act * silu_slope(ffn_hidden)).astype(jnp.bfloat16)
    grad_ffn_in = over_rows(normed_two_b, grad_hidden_b, ng)
    grad_normed_two = against(grad_hidden_b, ffn_in_full)
    grad_norm_two, grad_gain_two = rms_backward(grad_normed_two, out_one, inverse_two, gain_two)
    grad_out_one = grad_y_b.astype(jnp.float32) + grad_norm_two
    grad_update = grad_out_one * (hidden_act - tokens_flat)
    grad_tokens_flat = grad_out_one * (1.0 - update)
    grad_hpre_b = (grad_out_one * update * silu_slope(hidden_pre)).astype(jnp.bfloat16)
    grad_out_weight = over_rows(hidden_in, grad_hpre_b, ng)
    grad_hidden_in = against(grad_hpre_b, out_full)
    grad_att_b = (grad_hidden_in * reset_gate).astype(jnp.bfloat16)
    grad_reset = grad_hidden_in * attended
    grad_att_blk = grad_att_b.reshape(block_count, STRETCH, vdim)
    grad_probs = jnp.einsum("civ,cjv->cij", grad_att_blk, value_blk, preferred_element_type=jnp.float32)
    weighted = jnp.sum(probs * grad_probs, axis=2, keepdims=True)
    grad_scores_b = (probs * (grad_probs - weighted)).astype(jnp.bfloat16)
    grad_query = jnp.einsum("cij,cjd->cid", grad_scores_b, key_blk, preferred_element_type=jnp.float32).reshape(
        token_count, zdim
    )
    grad_key = jnp.einsum("cij,cid->cjd", grad_scores_b, query_blk, preferred_element_type=jnp.float32).reshape(
        token_count, zdim
    )
    grad_values = jnp.einsum("cij,civ->cjv", probs_b, grad_att_blk, preferred_element_type=jnp.float32).reshape(
        token_count, vdim
    )
    grad_qs = grad_query * scale_q
    grad_shared = grad_qs * affine[0] + grad_key * affine[2]
    grad_affine = jnp.stack(
        [
            jnp.sum(grad_qs * shared, axis=0),
            jnp.sum(grad_qs, axis=0),
            jnp.sum(grad_key * shared, axis=0),
            jnp.sum(grad_key, axis=0),
        ]
    )
    grad_gate_pre = jnp.concatenate([grad_shared, grad_reset], axis=1) * silu_slope(gate_pre)
    grad_upre = grad_update * update * (1.0 - update)
    grad_proj_b = jnp.concatenate(
        [grad_upre.astype(jnp.bfloat16), grad_gate_pre.astype(jnp.bfloat16), grad_hpre_b], axis=1
    )
    grad_mix = over_rows(active, grad_proj_b, ng)
    grad_active_b = against(grad_proj_b, mix_full).astype(jnp.bfloat16)
    grad_vpre_b = (grad_values * silu_slope(value_pre)).astype(jnp.bfloat16)
    grad_value = over_rows(normed_b, grad_vpre_b, ng)
    grad_normed = against(grad_vpre_b, value_full)

    small = jnp.concatenate(
        [jnp.zeros((blocks, 2 * dims + 2, 128), jnp.float32), grad_gain_two.reshape(blocks, 1, 128)], axis=1
    )
    if nq != blocks:
        small = jnp.take(small, np.arange(nq) * blocks // nq, axis=0)
    small = jnp.concatenate([small, jnp.broadcast_to(grad_affine[None], (nq, 4, 128))], axis=1)
    small = jnp.pad(small, ((0, 0), (0, -small.shape[1] % 8), (0, 0)))
    return mix_backward(
        grid, [grad_ffn_out, grad_ffn_in, grad_out_weight, grad_value, grad_mix], SCATTER_CUTS, grad_active_b, x_rows,
        mixed_rows, carry, par, alive, spans, tokens_low, grad_normed, grad_tokens_flat, small, 1
    )


def body(
    tokens,
    starts,
    norm_gain,
    ema_delta,
    ema_alpha,
    ema_beta,
    ema_eta,
    ema_omega,
    mix_weight,
    value_weight,
    qk_affine,
    out_weight,
    ffn_gain,
    ffn_in,
    ffn_out,
    cotangent,
):
    seg_count, row_count, model_width = tokens.shape
    nq, ng = lax.axis_size("seq"), lax.axis_size("seg")
    grid = Grid(nq, ng)
    seq_index, seg_index = lax.axis_index("seq"), lax.axis_index("seg")
    seq_length = row_count * nq
    dims = ema_delta.shape[1]
    zdim = qk_affine.shape[0] * nq * ng // 4
    vdim = value_weight.shape[1] * ng
    token_count = seg_count * row_count
    blocks = model_width // 128

    index = seq_index * ng + seg_index
    mine = norm_gain.shape[0]
    columns = jnp.concatenate(
        [ema_delta.T, ema_alpha.T, ema_beta.T, ema_eta.T, norm_gain[None], ema_omega[None], ffn_gain[None]], axis=0
    ).astype(jnp.float32)
    count = columns.shape[0]
    tile = jnp.zeros((-(-(count + 4) // 8) * 8, 128), jnp.float32)
    tile = lax.dynamic_update_slice(tile, columns, (0, lax.rem(index * mine, 128)))
    part = qk_affine.shape[0]
    tile = lax.dynamic_update_slice(
        tile, qk_affine.astype(jnp.float32)[None], (count + index * part // 128, lax.rem(index * part, 128))
    )

    places = jnp.arange(seq_length, dtype=jnp.int32)
    goes_on = 1.0 - jnp.any(starts[0][None, :] == places[:, None], axis=1).astype(jnp.float32)
    spans = jnp.broadcast_to(jnp.min(goes_on.reshape(nq, row_count), axis=1)[:, None], (nq, 128))
    alive = lax.dynamic_slice_in_dim(goes_on, seq_index * row_count, row_count, 0)
    alive = jnp.broadcast_to(alive[:, None], (row_count, 128))

    positions_rows = seq_index * row_count + jnp.arange(row_count, dtype=jnp.int32)
    docs_rows = jnp.sum((starts[:, None, :] <= positions_rows[None, :, None]).astype(jnp.int32), axis=2)
    block_count = token_count // STRETCH
    block_docs = docs_rows.reshape(block_count, STRETCH)
    offsets = jnp.arange(STRETCH)
    allowed = (block_docs[:, :, None] == block_docs[:, None, :]) & (offsets[:, None] >= offsets[None, :])[None]
    mask = allowed.astype(jnp.float32).reshape(token_count, STRETCH)
    tokens_low = tokens.reshape(token_count, model_width)
    weights, forward = mix_forward(
        grid, [mix_weight, value_weight, out_weight, ffn_in, ffn_out], GATHER_CUTS, tokens_low, tile, alive, spans, mask, dims, 0
    )
    mix_full, value_full, out_full, ffn_in_full, ffn_out_full = weights
    (normed_b, active, x_rows, mixed_rows, carry, par, affine, probs, out_one, normed_two_b, result,
     projected, value_pre, attended, hidden_in, hidden_pre, ffn_hidden, ffn_act) = forward
    sizes = (zdim, vdim, ffn_act.shape[1])
    cotangent_low = cotangent.reshape(token_count, model_width)
    if min(w.shape[1] for w in (mix_weight, value_weight, out_weight, ffn_in, ffn_out)) < 128:
        result_back = backward_apart(grid, cotangent_low, tokens_low, forward, weights, alive, spans, sizes)
    else:
        kept = [cotangent_low, ffn_act, ffn_hidden, normed_two_b, out_one, hidden_pre, projected, attended, hidden_in,
                value_pre, active, normed_b, tokens_low, x_rows, mixed_rows]
        order = [weights[4], weights[3], weights[2], weights[1], weights[0]]
        result_back = layer_backward(
            grid, order, SCATTER_CUTS, kept, probs, carry, par, affine, alive, spans, sizes, 1
        )
    (g_ffn_out, g_ffn_in, g_out, g_value, g_mix), grad_tokens, sums = result_back
    return (
        result.reshape(seg_count, row_count, model_width),
        grad_tokens.reshape(seg_count, row_count, model_width),
        *small_outputs(sums, index, dims, ema_delta, ema_alpha, ema_beta, ema_eta, mine, part, g_mix, g_value, g_out, g_ffn_in, g_ffn_out),
    )


def small_outputs(sums, index, dims, ema_delta, ema_alpha, ema_beta, ema_eta, mine, part, g_mix, g_value, g_out, g_ffn_in, g_ffn_out):
    own = lax.dynamic_slice_in_dim(sums, lax.rem(index * mine, 128), mine, 1)
    m_sum, k_sum = own[:dims].T, own[dims : 2 * dims].T
    vectors = own[2 * dims : 2 * dims + 3]
    delta, alpha, beta, eta = (v.astype(jnp.float32) for v in (ema_delta, ema_alpha, ema_beta, ema_eta))
    damping, decay = jax.nn.sigmoid(delta), jax.nn.sigmoid(alpha)
    g_keep = damping * beta * eta * k_sum
    grad_eta = damping * beta * m_sum
    grad_beta = damping * eta * m_sum
    grad_alpha = -g_keep * damping * decay * (1.0 - decay)
    grad_delta = (beta * eta * m_sum - g_keep * decay) * damping * (1.0 - damping)
    grad_affine = lax.dynamic_slice(
        sums, (2 * dims + 3 + index * part // 128, lax.rem(index * part, 128)), (1, part)
    ).reshape(-1)
    return (vectors[1], grad_delta, grad_alpha, grad_beta, grad_eta, vectors[0],
            g_mix, g_value, grad_affine, g_out, vectors[2], g_ffn_in, g_ffn_out)


def solution(mesh):
    placed = (
        P("seg", "seq", None),
        P("seg", None),
        P(("seq", "seg")),
        P(("seq", "seg"), None),
        P(("seq", "seg"), None),
        P(("seq", "seg"), None),
        P(("seq", "seg"), None),
        P(("seq", "seg")),
        P("seq", "seg"),
        P("seq", "seg"),
        P(("seq", "seg")),
        P("seq", "seg"),
        P(("seq", "seg")),
        P("seq", "seg"),
        P("seq", "seg"),
        P("seg", "seq", None),
    )
    return jax.shard_map(
        body,
        mesh=mesh,
        in_specs=placed,
        out_specs=(P("seg", "seq", None),) * 2 + placed[2:15],
        check_vma=False,
    )
```

```python
import functools
import math

import jax
import jax.numpy as jnp
import numpy as np
from jax import lax
from jax.experimental import pallas as pl
from jax.experimental.pallas import tpu as pltpu
from jax.sharding import PartitionSpec as P

STRETCH = 128
epsilon = 1e-05
GATHER_LAG = (1, 1, 1, 1, 1)
SCATTER_LAG = (0, 1, 1, 1, 1)
GATHER_CUTS = (4, 2, 2, 4, 4)
SCATTER_CUTS = (4, 4, 2, 2, 4)

MESH = pl.DeviceIdType.MESH
ANY = pl.BlockSpec(memory_space=pl.ANY)


class Grid:
    def __init__(self, nq, ng):
        self.nq, self.ng = nq, ng
        self.nz = math.gcd(nq, 4)
        self.nx = nq // self.nz
        self.nc = math.gcd(ng, 2)
        self.ny = ng // self.nc

    def here(self):
        s, g = lax.axis_index("seq"), lax.axis_index("seg")
        return s // self.nx, lax.rem(s, self.nx), g // self.nc, lax.rem(g, self.nc)

    def peer(self, axis, d):
        z, x, y, c = self.here()
        if axis == "z":
            z = lax.rem(z + d, self.nz)
        if axis == "x":
            x = lax.rem(x + d, self.nx)
        if axis == "y":
            y = lax.rem(y + d, self.ny)
        if axis == "c":
            c = lax.rem(c + d, self.nc)
        return z, x, y, c

    def size(self, axis):
        return {"z": self.nz, "x": self.nx, "y": self.ny, "c": self.nc}[axis]

    def device(self, place):
        z, x, y, c = place
        return {"seq": z * self.nx + x, "seg": y * self.nc + c}

    def peers(self, axes):
        return [self.peer(a, d) for a in axes for d in range(1, self.size(a))]


def enter(grid, peers):
    barrier = pltpu.get_barrier_semaphore()
    for place in peers:
        pl.semaphore_signal(barrier, inc=1, device_id=grid.device(place), device_id_type=MESH)
    pl.semaphore_wait(barrier, len(peers))


class Sems:
    def __init__(self, send, recv):
        self.send, self.recv, self.used = send, recv, 0

    def take_index(self):
        self.used += 1
        return self.used - 1

    def take(self):
        i = self.take_index()
        return self.send.at[i], self.recv.at[i]


def gather_steps(grid, shapes, shards, wholes, own_sem, sems):
    n = len(shapes)
    z, x, y, c = grid.here()
    pending = []

    def push(src, dst, axis, d, arrives):
        s, r = sems.take()
        device = grid.device(grid.peer(axis, d))
        copy = pltpu.make_async_remote_copy(src, dst, s, r, device_id=device, device_id_type=MESH)
        copy.start()
        pending.append(copy)
        there = pltpu.make_async_remote_copy(arrives, arrives, s, r, device_id=device, device_id_type=MESH)
        return there.wait_recv

    def back(axis, d):
        return dict(zip("zxyc", grid.peer(axis, grid.size(axis) - d)))[axis]

    owns = []
    chunks = [(i, q) for i in range(n) for q in range(shapes[i][0] // 2)]
    core_waits = {}

    def core(k, view):
        core_waits.setdefault(k, []).extend(
            push(view(c), view(c), "c", d, view(back("c", d))) for d in range(1, grid.nc)
        )

    def stage_z(k, i, h):
        w = wholes[i]
        return [
            push(shards[i].at[h], w.at[y, c, z, x, h], "z", d, w.at[y, c, back("z", d), x, h])
            for d in range(1, grid.nz)
        ]

    def stage_two(k, i, h):
        w = wholes[i]
        src = w.at[y, c, :, x, h]
        if h % 2 == 0:
            waits = [push(src, src, "x", d, w.at[y, c, :, back("x", d), h]) for d in range(1, grid.nx)]
        else:
            waits = [push(src, src, "y", d, w.at[back("y", d), c, :, x, h]) for d in range(1, grid.ny)]
        core(k, lambda cc: w.at[y, cc, :, x, h])
        return waits

    def stage_three(k, i, h):
        w = wholes[i]
        if h % 2 == 0:
            src = w.at[y, c, :, :, h]
            waits = [push(src, src, "y", d, w.at[back("y", d), c, :, :, h]) for d in range(1, grid.ny)]
            for d in range(1, grid.nx):
                core(k, lambda cc: w.at[y, cc, :, back("x", d), h])
            return waits
        src = w.at[:, c, :, x, h]
        waits = [push(src, src, "x", d, w.at[:, c, :, back("x", d), h]) for d in range(1, grid.nx)]
        for d in range(1, grid.ny):
            core(k, lambda cc: w.at[back("y", d), cc, :, x, h])
        return waits

    def stage_last(k, i, h):
        w = wholes[i]
        if h % 2 == 0:
            for d in range(1, grid.ny):
                core(k, lambda cc: w.at[back("y", d), cc, :, :, h])
        else:
            for d in range(1, grid.nx):
                core(k, lambda cc: w.at[:, cc, :, back("x", d), h])

    def finish(waits):
        for wait in waits:
            wait()

    got = {}
    total = len(chunks)
    at = [0] * 5

    def advance(j):
        k = at[j]
        i, q = chunks[k]
        if j == 1 and q == 0:
            owns[i].wait()
        if j == 4:
            finish(core_waits[k])
            at[j] += 1
            return [i] if q + 1 == shapes[i][0] // 2 else []
        for h in (0, 1):
            if j:
                finish(got[k, h])
            got[k, h] = (stage_z, stage_two, stage_three, stage_last)[j](k, i, 2 * q + h)
        at[j] += 1
        return []

    advance(0)
    yield []
    for i in range(n):
        copy = pltpu.make_async_copy(shards[i], wholes[i].at[y, c, z, x], own_sem.at[i])
        copy.start()
        owns.append(copy)
    while at[4] < total:
        before = list(at)
        done = []
        for j in (1, 0, 2, 3, 4):
            if j == 0:
                go = at[0] < total and at[0] - at[1] < GATHER_LAG[0]
            else:
                go = at[j] < before[j - 1] and (before[j - 1] == total or before[j - 1] - at[j] >= GATHER_LAG[j])
            if go:
                done += advance(j)
        if at[4] == total:
            for copy in pending:
                copy.wait_send()
        yield done


def gather_plan(grid, shards, cuts):
    shapes, args, outs = [], [], []
    for w, q in zip(shards, cuts):
        k, n = w.shape
        q = max(1, min(q, k // 32))
        shapes.append((2 * q, k // (2 * q), n))
        args.append(w.reshape(shapes[-1]))
        outs.append(jax.ShapeDtypeStruct((grid.ny, grid.nc, grid.nz, grid.nx) + shapes[-1], w.dtype))
    per = (grid.nz - 1) + (grid.nx - 1) + (grid.ny - 1) + (grid.nc - 1) * (grid.nx + grid.ny)
    count = sum(s[0] for s in shapes) * per
    return shapes, args, outs, count


def scatter_steps(grid, shapes, terms, sums, scratch, own_sem, sems, ready=None):
    n = len(shapes)
    nz, nx, ny, nc = grid.nz, grid.nx, grid.ny, grid.nc
    own = [scratch[7 * i] for i in range(n)]
    one = [scratch[7 * i + 1] for i in range(n)]
    two_a = [scratch[7 * i + 2] for i in range(n)]
    two_b = [scratch[7 * i + 3] for i in range(n)]
    three_a = [scratch[7 * i + 4] for i in range(n)]
    three_b = [scratch[7 * i + 5] for i in range(n)]
    four = [scratch[7 * i + 6] for i in range(n)]
    z, x, y, c = grid.here()
    pending = []
    around = {(axis, d): grid.peer(axis, d) for axis in "zxyc" for d in range(1, grid.size(axis))}
    devices = {key: grid.device(place) for key, place in around.items()}

    def push(ends, axis, d):
        k = sems.take_index()

        def copy():
            return pltpu.make_async_remote_copy(
                *ends(), sems.send.at[k], sems.recv.at[k], device_id=devices[axis, d], device_id_type=MESH
            )

        copy().start()
        pending.append(lambda: copy().wait_send())
        return lambda: copy().wait_recv()

    def to(axis, d):
        return dict(zip("zxyc", around[axis, d]))[axis]

    def finish(waits):
        for wait in waits:
            wait()

    assert nc == 2

    def stage_one(i, q, h):
        return [push(lambda: (terms[i].at[:, to("c", 1), :, :, 2 * q + h], one[i].at[q, h]), "c", 1)]

    def load_own(i, q, h):
        def load():
            return pltpu.make_async_copy(terms[i].at[:, c, :, :, 2 * q + h], own[i].at[h], own_sem.at[i, h])

        load().start()
        return [lambda: load().wait()]

    def stage_two(i, q, h):
        mine = one[i].at[q, h]

        @pl.loop(0, ny * nz)
        def _(ab):
            a, b = ab // nz, lax.rem(ab, nz)
            for e in range(nx):
                mine[a, b, e] += own[i][h, a, b, e]

        if h == 0:
            return [
                push(lambda d=d: (one[i].at[q, h, to("y", d)], two_a[i].at[q, d - 1]), "y", d) for d in range(1, ny)
            ]
        return [
            push(lambda d=d: (one[i].at[q, h, :, :, to("x", d)], two_b[i].at[q, d - 1]), "x", d) for d in range(1, nx)
        ]

    def stage_three(i, q, h):
        mine = one[i].at[q, h]
        if h == 0:

            @pl.loop(0, nz)
            def _(b):
                for e in range(nx):
                    total = mine[y, b, e]
                    for d in range(ny - 1):
                        total += two_a[i][q, d, b, e]
                    mine[y, b, e] = total

            return [
                push(lambda d=d: (one[i].at[q, h, y, :, to("x", d)], three_a[i].at[q, d - 1]), "x", d)
                for d in range(1, nx)
            ]

        @pl.loop(0, nz)
        def _(b):
            for a in range(ny):
                total = mine[a, b, x]
                for d in range(nx - 1):
                    total += two_b[i][q, d, a, b]
                mine[a, b, x] = total

        return [
            push(lambda d=d: (one[i].at[q, h, to("y", d), :, x], three_b[i].at[q, d - 1]), "y", d)
            for d in range(1, ny)
        ]

    def stage_four(i, q, h):
        mine = one[i].at[q, h]
        came = three_a[i] if h == 0 else three_b[i]

        @pl.loop(0, nz)
        def _(b):
            total = mine[y, b, x]
            for d in range((nx if h == 0 else ny) - 1):
                total += came[q, d, b]
            mine[y, b, x] = total

        return [
            push(lambda d=d: (one[i].at[q, h, y, to("z", d), x], four[i].at[q, h, d - 1]), "z", d)
            for d in range(1, nz)
        ]

    def stage_last(i, q, h):
        total = one[i][q, h, y, z, x].astype(jnp.float32)
        for d in range(nz - 1):
            total += four[i][q, h, d].astype(jnp.float32)
        sums[i][2 * q + h] = total

    stages = [stage_one, stage_two, stage_three, stage_four, stage_last]
    chunks = [(i, q) for i in range(n) for q in range(shapes[i][0] // 2)]
    waits = {}
    total = len(chunks)
    at = [0] * len(stages)
    yield
    while at[-1] < total:
        there = total if ready is None else sum(1 for i, q in chunks if i < ready())
        before = [there] + at[:-1]
        fresh = None
        for j, stage in enumerate(stages):
            lag = SCATTER_LAG[j]
            if at[j] < before[j] and (before[j] == total or j == 0 or before[j] - at[j] >= lag):
                i, q = chunks[at[j]]
                for h in (0, 1):
                    if j:
                        finish(waits[i, q, h])
                    waits[i, q, h] = stage(i, q, h)
                if j == 0:
                    fresh = i, q
                at[j] += 1
            if j == 1 and fresh:
                for h in (0, 1):
                    waits[fresh[0], fresh[1], h] += load_own(*fresh, h)
        if at[-1] == total:
            finish(pending)
        yield


class SmallSum:
    def __init__(self, grid, small, total, seq_in, seg_in, send, recv):
        self.grid, self.small, self.total = grid, small, total
        self.seq_in, self.seg_in, self.send, self.recv = seq_in, seg_in, send, recv
        self.seq_peer, self.seg_peer = small_peers(grid)
        self.copies = []

    def push(self, src, dst, device):
        i = len(self.copies)
        copy = pltpu.make_async_remote_copy(
            src, dst, self.send.at[i], self.recv.at[i], device_id=device, device_id_type=MESH
        )
        copy.start()
        self.copies.append(copy)

    def start(self):
        nq, sq = self.grid.nq, lax.axis_index("seq")
        for d in range(1, nq):
            self.push(self.small.at[lax.rem(sq + d, nq)], self.seq_in.at[d - 1], self.seq_peer[d - 1])

    def middle(self):
        nq, ng = self.grid.nq, self.grid.ng
        total = self.small[lax.axis_index("seq")]
        for d in range(1, nq):
            self.copies[d - 1].wait_recv()
            total += self.seq_in[d - 1]
        self.total[...] = total
        for d in range(1, ng):
            self.push(self.total, self.seg_in.at[d - 1], self.seg_peer[d - 1])

    def end(self):
        nq, ng = self.grid.nq, self.grid.ng
        total = self.total[...]
        for d in range(1, ng):
            self.copies[nq + d - 2].wait_recv()
            total += self.seg_in[d - 1]
        for copy in self.copies:
            copy.wait_send()
        self.total[...] = total


def small_peers(grid):
    nq, ng = grid.nq, grid.ng
    s, g = lax.axis_index("seq"), lax.axis_index("seg")
    return (
        [{"seq": lax.rem(s + d, nq), "seg": g} for d in range(1, nq)],
        [{"seq": s, "seg": lax.rem(g + d, ng)} for d in range(1, ng)],
    )


def meet(peers):
    barrier = pltpu.get_barrier_semaphore()
    for place in peers:
        pl.semaphore_signal(barrier, inc=1, device_id=place, device_id_type=MESH)
    pl.semaphore_wait(barrier, len(peers))


def scatter_plan(grid, terms, cuts):
    nz, nx, ny = grid.nz, grid.nx, grid.ny
    shapes, outs, scratch = [], [], []
    for t, q in zip(terms, cuts):
        _, rows, n = t.shape
        if n < 128:
            rows, n = rows * n // 128, 128
        k = rows // grid.nq
        q = max(1, min(q, k // 32))
        kh = k // (2 * q)
        shapes.append((2 * q, kh, n))
        outs.append(jax.ShapeDtypeStruct((2 * q, kh, n), jnp.float32))
        b = t.dtype
        scratch += [
            pltpu.VMEM((2, ny, nz, nx, kh, n), b),
            pltpu.VMEM((q, 2, ny, nz, nx, kh, n), b),
            pltpu.VMEM((q, max(ny - 1, 1), nz, nx, kh, n), b),
            pltpu.VMEM((q, max(nx - 1, 1), ny, nz, kh, n), b),
            pltpu.VMEM((q, max(nx - 1, 1), nz, kh, n), b),
            pltpu.VMEM((q, max(ny - 1, 1), nz, kh, n), b),
            pltpu.VMEM((q, 2, max(nz - 1, 1), kh, n), b),
        ]
    per = (grid.nc - 1) + (nx - 1) + (ny - 1) + (nz - 1)
    count = per * sum(s[0] for s in shapes)
    return shapes, outs, scratch, count


def block_of(e, nq, blocks):
    return e * blocks // nq


def place_params(grid, own, tile, count, mine, part):
    index = lax.axis_index("seq") * grid.ng + lax.axis_index("seg")
    row = lax.broadcasted_iota(jnp.int32, (mine, 128), 0)
    lane = lax.broadcasted_iota(jnp.int32, (mine, 128), 1)

    def spread(first):
        where = (lane == row + first).astype(jnp.bfloat16)
        return lax.dot_general(own[...], where, (((0,), (0,)), ((), ())), preferred_element_type=jnp.float32)

    tile[...] = jnp.zeros_like(tile)
    tile[0:count, :] = spread(lax.rem(index * mine, 128))[0:count]
    affine = spread(lax.rem(index * part, 128))[count : count + 1]
    at = lax.broadcasted_iota(jnp.int32, (4, 128), 0) == index * part // 128
    tile[count : count + 4, :] = jnp.where(at, affine, 0.0)


def place_documents(grid, starts, alive, spans, mask):
    rows = alive.shape[0]
    first = [starts[0, k] for k in range(starts.shape[1])]
    base = lax.axis_index("seq") * rows
    place = lax.broadcasted_iota(jnp.int32, (rows, 128), 0)
    column = lax.broadcasted_iota(jnp.int32, (rows, 128), 1)
    within = jnp.bitwise_and(place, STRETCH - 1)
    here, there = base + place, base + place - within + column
    goes_on = jnp.ones((rows, 128), jnp.float32)
    doc_here, doc_there = jnp.zeros((rows, 128), jnp.int32), jnp.zeros((rows, 128), jnp.int32)
    for f in first:
        goes_on = jnp.where(here == f, 0.0, goes_on)
        doc_here = doc_here + jnp.where(here >= f, 1, 0)
        doc_there = doc_there + jnp.where(there >= f, 1, 0)
    alive[...] = goes_on
    mask[...] = jnp.where((doc_here == doc_there) & (column <= within), 1.0, 0.0)
    low = lax.broadcasted_iota(jnp.int32, spans.shape, 0) * rows
    whole = jnp.ones(spans.shape, jnp.float32)
    for f in first:
        whole = jnp.where((low <= f) & (f < low + rows), 0.0, whole)
    spans[...] = whole


def mix_kernel(grid, width, dims, shapes, part, out_term, *refs):
    n = len(shapes)
    shards, refs = refs[:n], refs[n:]
    tok, own_params, starts, cot, *refs = refs
    wholes, refs = refs[:n], refs[n:]
    term_hbm = None
    if out_term:
        term_hbm, *refs = refs
    (alive, spans, carry_out, par_out, aff_out, probs_out, layer_out,
     normed_hbm, active_hbm, x_hbm, mixed_hbm, one_hbm, two_hbm, proj_hbm, value_hbm, att_hbm, hin_hbm, hpre_hbm, ffn_hbm, act_hbm,
     normed_out, active_out, x_out, mixed_out, out_one_out, two_out, proj, value_pre, att, hin, hpre, ffn_pre, act, values,
     mask, tile, tiles, table, bound, sends_t, recv_t, sends_b, recv_b, own_sem, flush_sem, load_sem, send, recv,
     *slots) = refs
    if out_term:
        *slots, turned_act, stage, stage_sem = slots
    nq, ng = grid.nq, grid.ng
    rows = tok.shape[0]
    blocks = width // 128
    s = lax.axis_index("seq")
    seq_peer, seg_peer = small_peers(grid)
    meet(seq_peer + seg_peer)
    steps = gather_steps(grid, shapes, shards, wholes, own_sem, Sems(send, recv))

    done = set()

    def pump(count=1):
        for _ in range(count):
            done.update(next(steps, ()))

    flushes = []

    def flush(ref, hbm):
        copy = pltpu.make_async_copy(ref, hbm, flush_sem.at[len(flushes)])
        copy.start()
        flushes.append(copy)

    place_params(grid, own_params, tile, 4 * dims + 3, width // (nq * ng), part)
    place_documents(grid, starts, alive, spans, mask)

    copies = []
    for d in range(1, ng):
        copies.append(pltpu.make_async_remote_copy(
            tile, tiles.at[d - 1], sends_t.at[d - 1], recv_t.at[d - 1],
            device_id=seg_peer[d - 1], device_id_type=MESH))
        copies[-1].start()
    for copy in copies:
        copy.wait_recv()
    lanes = tile[...]
    for d in range(1, ng):
        lanes += tiles[d - 1]
    table[s] = lanes
    for d in range(1, nq):
        copies.append(pltpu.make_async_remote_copy(
            table.at[s], table.at[s], sends_t.at[ng + d - 2], recv_t.at[ng + d - 2],
            device_id=seq_peer[d - 1], device_id_type=MESH))
        copies[-1].start()
    pump()
    for d in range(1, nq):
        came = table.at[lax.rem(s + nq - d, nq)]
        pltpu.make_async_remote_copy(
            came, came, sends_t.at[ng + d - 2], recv_t.at[ng + d - 2],
            device_id=seq_peer[d - 1], device_id_type=MESH).wait_recv()
    count = 4 * dims + 3
    for b in range(blocks):
        mine = [e for e in range(nq) if block_of(e, nq, blocks) == b]
        whole = table[mine[0], 0:count]
        for e in mine[1:]:
            whole += table[e, 0:count]
        par_out[:, b, :] = whole
    aff = table[0, count : count + 4]
    for e in range(1, nq):
        aff += table[e, count : count + 4]
    aff_out[...] = aff

    pump()

    gain = [par_out[4 * dims, b : b + 1, :] for b in range(blocks)]
    step_rows = 32

    @pl.loop(0, rows // step_rows)
    def _(i):
        at = pl.ds(pl.multiple_of(i * step_rows, step_rows), step_rows)
        v = tok[at, :].astype(jnp.float32)
        r = lax.rsqrt(jnp.mean(v * v, axis=1, keepdims=True) + epsilon)
        for b in range(blocks):
            lane = slice(b * 128, b * 128 + 128)
            n = (v[:, lane] * r * gain[b]).astype(jnp.bfloat16)
            normed_out[at, lane] = n
            x_out[pl.ds(i * step_rows * blocks + b, step_rows, stride=blocks), :] = n.astype(jnp.float32)

    flush(normed_out, normed_hbm)
    flush(x_out, x_hbm)
    damping = [jax.nn.sigmoid(par_out[j]) for j in range(dims)]
    keep = [1.0 - damping[j] * jax.nn.sigmoid(par_out[dims + j]) for j in range(dims)]
    weight = [damping[j] * par_out[2 * dims + j] * par_out[3 * dims + j] for j in range(dims)]
    omega = par_out[4 * dims + 1]

    def row(ref, p):
        return ref[pl.ds(pl.multiple_of(p * blocks, blocks), blocks), :]

    def first_pass(p, state):
        x, a = row(x_out, p), alive[pl.ds(p, 1), :]
        return tuple(keep[j] * (state[j] * a) + x for j in range(dims))

    zero = tuple(jnp.zeros((blocks, 128), jnp.float32) for _ in range(dims))
    pump()
    ends = zero
    for part in range(2):
        ends = lax.fori_loop(part * rows // 2, (part + 1) * rows // 2, first_pass, ends, unroll=4)
        if part == 0:
            pump()
    for j in range(dims):
        bound[s, j] = ends[j]
    out = []
    for d in range(1, nq):
        out.append(pltpu.make_async_remote_copy(
            bound.at[s], bound.at[s], sends_b.at[d - 1], recv_b.at[d - 1],
            device_id=seq_peer[d - 1], device_id_type=MESH))
        out[-1].start()
    pump(3)
    for d in range(1, nq):
        came = bound.at[lax.rem(s + nq - d, nq)]
        pltpu.make_async_remote_copy(
            came, came, sends_b.at[d - 1], recv_b.at[d - 1],
            device_id=seq_peer[d - 1], device_id_type=MESH).wait_recv()
    for j in range(dims):
        through = power(keep[j], rows)
        state = jnp.zeros((blocks, 128), jnp.float32)
        for e in range(nq - 1):
            later = through * spans[e : e + 1, :] * state + bound[e, j]
            state = jnp.where(e < s, later, state)
        carry_out[j] = state

    def second_pass(p, state):
        x, a = row(x_out, p), alive[pl.ds(p, 1), :]
        state = tuple(keep[j] * (state[j] * a) + x for j in range(dims))
        sums = [omega * x] + [weight[j] * state[j] for j in range(dims)]
        while len(sums) > 1:
            sums = [sum(sums[k : k + 2][1:], sums[k]) for k in range(0, len(sums), 2)]
        mixed_out[pl.ds(pl.multiple_of(p * blocks, blocks), blocks), :] = sums[0]
        return state

    state = tuple(carry_out[j] for j in range(dims))
    for part in range(4):
        state = lax.fori_loop(part * rows // 4, (part + 1) * rows // 4, second_pass, state, unroll=4)
        if part % 2:
            pump()
    for b in range(blocks):
        m = mixed_out[pl.ds(b, rows, stride=blocks), :]
        active_out[:, b * 128 : b * 128 + 128] = (m * jax.nn.sigmoid(m)).astype(jnp.bfloat16)
    flush(mixed_out, mixed_hbm)
    flush(active_out, active_hbm)
    for copy in copies + out:
        copy.wait_send()

    def pieces(i):
        while i not in done:
            pump()

        def fetch(g):
            return pltpu.make_async_copy(
                wholes[i].at[g // grid.nc, g % grid.nc], slots[i].at[g % 2], load_sem.at[i, g % 2]
            )

        fetch(0).start()
        for g in range(grid.ng):
            if g + 1 < grid.ng:
                fetch(g + 1).start()
            fetch(g).wait()
            piece = slots[i][g % 2]
            wide = piece.shape[-1]
            yield g, slice(g * wide, g * wide + wide), piece.reshape(-1, wide)
            if g + 1 == grid.ng:
                pump()

    block_rows = 32
    zdim = aff_out.shape[1]
    vdim = value_pre.shape[1]
    first_gate, first_reset, first_cand = width, width + zdim, width + zdim + vdim
    dot = functools.partial(jnp.dot, preferred_element_type=jnp.float32)

    def by_rows(count=rows, each=block_rows):
        def wrap(f):
            pl.loop(0, count // each)(lambda i: f(pl.ds(pl.multiple_of(i * each, each), each)))

        return wrap

    for g, cols, piece in pieces(0):
        proj[:, cols] = dot(active_out[...], piece)
    flush(proj, proj_hbm)

    scale_q = zdim**-0.5
    near = []
    for r in range(rows // STRETCH):
        at = slice(r * STRETCH, r * STRETCH + STRETCH)
        gate = proj[at, first_gate:first_reset]
        shared = gate * jax.nn.sigmoid(gate)
        query = (scale_q * (shared * aff_out[0:1] + aff_out[1:2])).astype(jnp.bfloat16)
        key = (shared * aff_out[2:3] + aff_out[3:4]).astype(jnp.bfloat16)
        scores = lax.dot_general(query, key, (((1,), (1,)), ((), ())), preferred_element_type=jnp.float32)
        scores = jnp.where(mask[at, :] > 0.0, scores, -1e30)
        expo = jnp.exp(scores - jnp.max(scores, axis=1, keepdims=True))
        probs = expo / jnp.sum(expo, axis=1, keepdims=True)
        probs_out[at, :] = probs
        near.append(probs.astype(jnp.bfloat16))

    for g, cols, piece in pieces(1):
        pre = dot(normed_out[...], piece)
        value_pre[:, cols] = pre
        values[:, cols] = (pre * jax.nn.sigmoid(pre)).astype(jnp.bfloat16)
    flush(value_pre, value_hbm)
    for r in range(rows // STRETCH):
        at = slice(r * STRETCH, r * STRETCH + STRETCH)
        att[at, :] = dot(near[r], values[at, :])

    @by_rows()
    def _(at):
        gate = proj[at, first_reset:first_cand]
        hin[at, :] = (att[at, :] * (gate * jax.nn.sigmoid(gate))).astype(jnp.bfloat16)

    flush(att, att_hbm)
    flush(hin, hin_hbm)

    for g, cols, piece in pieces(2):
        hpre[:, cols] = proj[:, first_cand + cols.start : first_cand + cols.stop] + dot(hin[...], piece)
    flush(hpre, hpre_hbm)

    gain_two = [par_out[4 * dims + 2, b : b + 1, :] for b in range(blocks)]

    @by_rows()
    def _(at):
        v = tok[at, :].astype(jnp.float32)
        h = hpre[at, :]
        one = v + jax.nn.sigmoid(proj[at, 0:width]) * (h * jax.nn.sigmoid(h) - v)
        out_one_out[at, :] = one
        r = lax.rsqrt(jnp.mean(one * one, axis=1, keepdims=True) + epsilon)
        for b in range(blocks):
            lane = slice(b * 128, b * 128 + 128)
            two_out[at, lane] = (one[:, lane] * r * gain_two[b]).astype(jnp.bfloat16)

    flush(out_one_out, one_hbm)
    flush(two_out, two_hbm)
    for g, cols, piece in pieces(3):
        pre = dot(two_out[...], piece)
        ffn_pre[:, cols] = pre
        act[:, cols] = (pre * jax.nn.sigmoid(pre)).astype(jnp.bfloat16)
    flush(ffn_pre, ffn_hbm)
    flush(act, act_hbm)

    if out_term:
        for a in range(0, act.shape[1], 256):
            turned_act[a : a + 256, :] = act[:, a : a + 256].T
        n_cols, deep = out_term[-1], act.shape[1] // grid.nz
        copies = []
        for g in range(ng):
            right = cot[:, g * n_cols : (g + 1) * n_cols]
            for zt in range(grid.nz):
                m = len(copies)
                if m >= 4:
                    copies[m - 4].wait()
                stage[m % 4] = dot(turned_act[zt * deep : (zt + 1) * deep, :], right).astype(jnp.bfloat16).reshape(stage.shape[1:])
                copies.append(
                    pltpu.make_async_copy(stage.at[m % 4], term_hbm.at[g // grid.nc, g % grid.nc, zt], stage_sem.at[m % 4])
                )
                copies[m].start()
            if g == ng // 2:
                pump()
        for copy in copies[-4:]:
            copy.wait()
    for g, cols, piece in pieces(4):
        layer_out[:, cols] = (out_one_out[:, cols] + dot(act[...], piece)).astype(jnp.bfloat16)
    for _ in steps:
        pass
    for copy in flushes:
        copy.wait()


def power(v, n):
    result = None
    while n:
        if n & 1:
            result = v if result is None else result * v
        n >>= 1
        if n:
            v = v * v
    return result


def mix_forward(grid, weights, cuts, tok, own_params, starts, cot, dims, part, out_term, collective_id):
    rows, width = tok.shape
    nq, ng = grid.nq, grid.ng
    blocks = width // 128
    f = jnp.float32
    vm = pl.BlockSpec(memory_space=pltpu.VMEM)
    shapes, shards, outs, count = gather_plan(grid, weights, cuts)
    n = len(shards)
    vdim, fdim, proj_dim = weights[1].shape[1] * ng, weights[3].shape[1] * ng, weights[0].shape[1] * ng
    low = jnp.bfloat16
    kept = [
        ((rows, width), low),
        ((rows, width), low),
        ((rows * blocks, 128), f),
        ((rows * blocks, 128), f),
        ((rows, width), f),
        ((rows, width), low),
        ((rows, proj_dim), f),
        ((rows, vdim), f),
        ((rows, vdim), f),
        ((rows, vdim), low),
        ((rows, width), f),
        ((rows, fdim), f),
        ((rows, fdim), low),
    ]
    count_rows = 4 * dims + 3
    tile_shape = (-(-(count_rows + 4) // 8) * 8, 128)
    local = [
        ((rows, 128), f),
        ((nq, 128), f),
        ((dims, blocks, 128), f),
        ((count_rows, blocks, 128), f),
        ((4, 128), f),
        ((rows, STRETCH), f),
        ((rows, width), low),
    ]
    term = [jax.ShapeDtypeStruct((grid.ny, grid.nc, grid.nz, grid.nx) + out_term, low)] if out_term else []
    held = len(term)
    turning = [
        pltpu.VMEM((fdim, rows), low),
        pltpu.VMEM((4, grid.nx) + out_term, low),
        pltpu.SemaphoreType.DMA((4,)),
    ] if out_term else []
    result = pl.pallas_call(
        functools.partial(mix_kernel, grid, width, dims, shapes, part, out_term),
        out_shape=outs + term + [jax.ShapeDtypeStruct(*v) for v in local + kept],
        in_specs=[ANY] * n + [vm] * 2 + [pl.BlockSpec(memory_space=pltpu.SMEM), vm],
        out_specs=[ANY] * (n + held) + [vm] * len(local) + [ANY] * len(kept),
        scratch_shapes=[pltpu.VMEM(*v) for v in kept]
        + [
            pltpu.VMEM((rows, vdim), low),
            pltpu.VMEM((rows, STRETCH), f),
            pltpu.VMEM(tile_shape, f),
            pltpu.VMEM((ng - 1,) + tile_shape, f),
            pltpu.VMEM((nq,) + tile_shape, f),
            pltpu.VMEM((nq, dims, blocks, 128), f),
            pltpu.SemaphoreType.DMA((nq + ng - 2,)),
            pltpu.SemaphoreType.DMA((nq + ng - 2,)),
            pltpu.SemaphoreType.DMA((nq - 1,)),
            pltpu.SemaphoreType.DMA((nq - 1,)),
            pltpu.SemaphoreType.DMA((n,)),
            pltpu.SemaphoreType.DMA((len(kept),)),
            pltpu.SemaphoreType.DMA((n, 2)),
            pltpu.SemaphoreType.DMA((count,)),
            pltpu.SemaphoreType.DMA((count,)),
        ]
        + [pltpu.VMEM((2,) + o.shape[2:], o.dtype) for o in outs]
        + turning,
        compiler_params=pltpu.CompilerParams(
            collective_id=collective_id, has_side_effects=True, vmem_limit_bytes=60 << 20
        ),
    )(*shards, tok, own_params, starts, cot)
    return result[:n], result[n : n + held], result[n + held :]


def scan_back(grid, dims, g_rows, x_in, mixed, carry, par, alive, spans, gin_rows, before, bound, sends_b, recv_b,
              m_all, k_all, seq_peer, s, pump):
    nq = grid.nq
    blocks = carry.shape[1]
    rows = g_rows.shape[0] // blocks

    @pl.loop(0, rows * blocks // 64)
    def _(i):
        at = pl.ds(pl.multiple_of(i * 64, 64), 64)
        g_rows[at, :] = g_rows[at, :] * silu_slope(mixed[at, :])

    damping = [jax.nn.sigmoid(par[j]) for j in range(dims)]
    keep = [1.0 - damping[j] * jax.nn.sigmoid(par[dims + j]) for j in range(dims)]
    weight = [damping[j] * par[2 * dims + j] * par[3 * dims + j] for j in range(dims)]
    omega = par[4 * dims + 1]

    def row(ref, p):
        return ref[pl.ds(pl.multiple_of(p * blocks, blocks), blocks), :]

    def first_pass(i, flow):
        p = rows - 1 - i
        gp, a = row(g_rows, p), alive[pl.ds(p, 1), :]
        return tuple(keep[j] * (a * (gp + flow[j])) for j in range(dims))

    zero = jnp.zeros((blocks, 128), jnp.float32)
    ends = lax.fori_loop(0, rows, first_pass, (zero,) * dims, unroll=4)
    for j in range(dims):
        bound[s, j] = ends[j]
    def sent(d):
        return pltpu.make_async_remote_copy(
            bound.at[s], bound.at[s], sends_b.at[d - 1], recv_b.at[d - 1],
            device_id=seq_peer[d - 1], device_id_type=MESH)

    for d in range(1, nq):
        sent(d).start()
    pump()
    for d in range(1, nq):
        came = bound.at[lax.rem(s + nq - d, nq)]
        pltpu.make_async_remote_copy(
            came, came, sends_b.at[d - 1], recv_b.at[d - 1],
            device_id=seq_peer[d - 1], device_id_type=MESH).wait_recv()
    flow_in = []
    for j in range(dims):
        through = power(keep[j], rows)
        flow = zero
        for e in range(nq - 1, 0, -1):
            later = through * spans[e : e + 1, :] * flow + bound[e, j]
            flow = jnp.where(e > s, later, flow)
        flow_in.append(flow)

    few = before.shape[1]
    for j0 in range(0, dims, few):
        js = range(j0, j0 + few)

        def ahead(p, state):
            x, a = row(x_in, p), alive[pl.ds(p, 1), :]
            for t in range(few):
                before[p, t] = state[t]
            return tuple(keep[j] * (state[t] * a) + x for t, j in enumerate(js))

        lax.fori_loop(0, rows, ahead, tuple(carry[j] for j in js), unroll=4)
        if j0:
            pump()

        def back(i, held):
            flow, m_sum, k_sum, om_sum = held
            p = rows - 1 - i
            at = pl.ds(pl.multiple_of(p * blocks, blocks), blocks)
            gp, x, a = g_rows[at, :], x_in[at, :], alive[pl.ds(p, 1), :]
            total = omega * gp if j0 == 0 else gin_rows[at, :]
            if j0 == 0:
                om_sum = om_sum + gp * x
            new_flow, new_m, new_k = [], [], []
            for t, j in enumerate(js):
                c = gp + flow[t]
                ac = a * c
                total = total + weight[j] * c
                new_flow.append(keep[j] * ac)
                new_m.append(m_sum[t] + c * x)
                new_k.append(k_sum[t] + ac * before[p, t])
            gin_rows[at, :] = total
            return tuple(new_flow), tuple(new_m), tuple(new_k), om_sum

        zeros = (zero,) * few
        _, m_sum, k_sum, om_sum = lax.fori_loop(
            0, rows, back, (tuple(flow_in[j] for j in js), zeros, zeros, zero), unroll=4
        )
        for t, j in enumerate(js):
            m_all[j] = m_sum[t]
            k_all[j] = k_sum[t]
        if j0 == 0:
            m_all[dims] = om_sum
        pump()
    for d in range(1, nq):
        sent(d).wait_send()


def norm_back(par, dims, tok, pre, direct, gin_rows, gtok_out, row_sums):
    rows, width = tok.shape
    blocks = width // 128
    gain = [par[4 * dims, b : b + 1, :] for b in range(blocks)]
    lanes = [slice(b * 128, b * 128 + 128) for b in range(blocks)]
    step_rows = 32

    def some(i, gains):
        at = pl.ds(pl.multiple_of(i * step_rows, step_rows), step_rows)
        v = tok[at, :].astype(jnp.float32)
        r = lax.rsqrt(jnp.mean(v * v, axis=1, keepdims=True) + epsilon)
        gy = []
        for b in range(blocks):
            came = gin_rows[pl.ds(i * step_rows * blocks + b, step_rows, stride=blocks), :]
            gy.append(pre[at, lanes[b]] + came.astype(jnp.bfloat16).astype(jnp.float32))
        scaled = [gy[b] * gain[b] for b in range(blocks)]
        dots = sum(jnp.sum(scaled[b] * v[:, lanes[b]], axis=1, keepdims=True) for b in range(blocks))
        pull = r * r * (dots / width)
        new = []
        for b in range(blocks):
            vb = v[:, lanes[b]]
            gx = r * (scaled[b] - vb * pull)
            gtok_out[at, lanes[b]] = (direct[at, lanes[b]] + gx).astype(jnp.bfloat16)
            new.append(gains[b] + jnp.sum(gy[b] * (vb * r), axis=0, keepdims=True))
        return tuple(new)

    gains = lax.fori_loop(
        0, rows // step_rows, some, tuple(jnp.zeros((1, 128), jnp.float32) for _ in range(blocks))
    )
    for b in range(blocks):
        row_sums[b : b + 1, :] = gains[b]


def fill_small(grid, dims, small, m_all, k_all, row_sums):
    blocks = row_sums.shape[0]
    for e in range(grid.nq):
        b = block_of(e, grid.nq, blocks)
        small[e, 0:dims] = m_all[0:dims, b, :]
        small[e, dims : 2 * dims] = k_all[:, b, :]
        small[e, 2 * dims : 2 * dims + 1] = m_all[dims, b : b + 1, :]
        small[e, 2 * dims + 1 : 2 * dims + 2] = row_sums[b : b + 1, :]


def mix_back_kernel(grid, dims, shapes, *refs):
    n = len(shapes)
    terms, refs = refs[:n], refs[n:]
    gact, x_in, mixed, carry, par, alive, spans, tok, pre, direct, small_in, *refs = refs
    sums, refs = refs[:n], refs[n:]
    (gtok_out, small_out,
     g_rows, gin_rows, before, bound, m_all, k_all, row_sums, small, seq_in, seg_in,
     sends_b, recv_b, s_send, s_recv, own_sem, send, recv, *scratch) = refs
    nq = grid.nq
    rows, width = gact.shape
    blocks = width // 128
    s = lax.axis_index("seq")
    seq_peer, seg_peer = small_peers(grid)
    meet(seq_peer + seg_peer)
    steps = scatter_steps(grid, shapes, terms, sums, scratch, own_sem, Sems(send, recv))
    little = SmallSum(grid, small, small_out, seq_in, seg_in, s_send, s_recv)

    def pump(count=1):
        for _ in range(count):
            next(steps, None)

    pump(2)
    for b in range(blocks):
        g_rows[pl.ds(b, rows, stride=blocks), :] = gact[:, b * 128 : b * 128 + 128].astype(jnp.float32)

    scan_back(
        grid, dims, g_rows, x_in, mixed, carry, par, alive, spans, gin_rows, before, bound, sends_b, recv_b,
        m_all, k_all, seq_peer, s, pump
    )
    norm_back(par, dims, tok, pre, direct, gin_rows, gtok_out, row_sums)
    for e in range(nq):
        small[e] = small_in[e]
    fill_small(grid, dims, small, m_all, k_all, row_sums)
    little.start()
    pump()
    little.middle()
    for _ in steps:
        pass
    little.end()


def mix_backward(grid, terms, cuts, gact, x_in, mixed, carry, par, alive, spans, tok, pre, direct, small, collective_id):
    rows, width = gact.shape
    nq, ng = grid.nq, grid.ng
    blocks, dims, few = width // 128, carry.shape[0], 4
    f = jnp.float32
    vm = pl.BlockSpec(memory_space=pltpu.VMEM)
    shapes, outs, scratch, count = scatter_plan(grid, terms, cuts)
    parts = [t.reshape((grid.ny, grid.nc, grid.nz, grid.nx) + v) for t, v in zip(terms, shapes)]
    n = len(parts)
    result = pl.pallas_call(
        functools.partial(mix_back_kernel, grid, dims, shapes),
        out_shape=outs
        + [jax.ShapeDtypeStruct((rows, width), jnp.bfloat16), jax.ShapeDtypeStruct(small.shape[1:], f)],
        in_specs=[ANY] * n + [vm] * 11,
        out_specs=[vm] * (n + 2),
        scratch_shapes=[
            pltpu.VMEM((rows * blocks, 128), f),
            pltpu.VMEM((rows * blocks, 128), f),
            pltpu.VMEM((rows, few, blocks, 128), f),
            pltpu.VMEM((nq, dims, blocks, 128), f),
            pltpu.VMEM((dims + 1, blocks, 128), f),
            pltpu.VMEM((dims, blocks, 128), f),
            pltpu.VMEM((blocks, 128), f),
            pltpu.VMEM(small.shape, f),
            pltpu.VMEM((nq - 1,) + small.shape[1:], f),
            pltpu.VMEM((ng - 1,) + small.shape[1:], f),
            pltpu.SemaphoreType.DMA((nq - 1,)),
            pltpu.SemaphoreType.DMA((nq - 1,)),
            pltpu.SemaphoreType.DMA((nq + ng - 2,)),
            pltpu.SemaphoreType.DMA((nq + ng - 2,)),
            pltpu.SemaphoreType.DMA((n, 2)),
            pltpu.SemaphoreType.DMA((count,)),
            pltpu.SemaphoreType.DMA((count,)),
        ]
        + scratch,
        compiler_params=pltpu.CompilerParams(
            collective_id=collective_id, has_side_effects=True, vmem_limit_bytes=62 << 20
        ),
    )(*parts, gact, x_in, mixed, carry, par, alive, spans, tok, pre, direct, small)
    return [v.reshape(-1, t.shape[-1]) for v, t in zip(result, terms)], result[n], result[n + 1]


def layer_back_kernel(grid, dims, shapes, sizes, *refs):
    n = len(shapes)
    zdim, vdim, fdim = sizes
    wholes, refs = refs[:n], refs[n:]
    (first_term, cot_hbm, ffn_hbm, two_hbm, one_hbm, hpre_hbm, proj_hbm, att_hbm, hin_hbm, value_hbm, probs, active_hbm,
     normed_hbm, tok_hbm, x_hbm, mixed_hbm, carry, par, aff, alive, spans, *refs) = refs
    sums, refs = refs[:n], refs[n:]
    gtok_out, small_out, *refs = refs
    terms, refs = [first_term, *refs[: n - 1]], refs[n - 1 :]
    (gproj, direct, pre, bound, m_all, k_all, row_sums, two_sums, aff_sums, small, seq_in, seg_in,
     sends_b, recv_b, s_send, s_recv, own_sem, load_sem, tile_sem, stage_sem, send, recv, *scratch) = refs
    nq, ng, nc, nz = grid.nq, grid.ng, grid.nc, grid.nz
    rows, width = direct.shape
    blocks = width // 128
    low, f = jnp.bfloat16, jnp.float32
    s = lax.axis_index("seq")
    seq_peer, seg_peer = small_peers(grid)
    meet(seq_peer + seg_peer)
    ready = [1]
    steps = scatter_steps(grid, shapes, terms, sums, scratch, own_sem, Sems(send, recv), lambda: ready[0])
    little = SmallSum(grid, small, small_out, seq_in, seg_in, s_send, s_recv)
    loads = [0]

    def pump(count=1):
        for _ in range(count):
            next(steps, None)

    pump(3)
    dot = functools.partial(jnp.dot, preferred_element_type=f)

    def dot_nt(a, b):
        return lax.dot_general(a, b, (((1,), (1,)), ((), ())), preferred_element_type=f)

    def dot_tn(a, b):
        return lax.dot_general(a, b, (((0,), (0,)), ((), ())), preferred_element_type=f)

    def fetch(src, dst):
        copy = pltpu.make_async_copy(src, dst, load_sem.at[loads[0]])
        loads[0] += 1
        copy.start()
        return copy.wait

    def by_rows(each=32):
        def wrap(some):
            pl.loop(0, rows // each)(lambda i: some(pl.ds(pl.multiple_of(i * each, each), each)))

        return wrap

    def wide(i):
        return shapes[i][-1]

    def tile_shape(i):
        return (2, grid.ny, nc, grid.nx) + shapes[i]

    def depth(i):
        return grid.nx * shapes[i][0] * shapes[i][1]

    def tile(i, tiles, zt):
        return pltpu.make_async_copy(wholes[i].at[:, :, zt], tiles.at[zt % 2], tile_sem.at[zt % 2])

    def begin(i, tiles):
        for zt in range(min(2, nz)):
            tile(i, tiles, zt).start()

    def against(i, tiles, part):
        for zt in range(nz):
            tile(i, tiles, zt).wait()
            total = None
            for g in range(ng):
                term = dot_nt(part(g), tiles[zt % 2, g // nc, g % nc].reshape(depth(i), wide(i)))
                total = term if total is None else total + term
            if zt + 2 < nz:
                tile(i, tiles, zt + 2).start()
            yield slice(zt * depth(i), zt * depth(i) + depth(i)), total

    def grads(i, left, stage, part):
        copies = []
        slots = stage.shape[0]
        for g in range(ng):
            right = part(g)
            for zt in range(nz):
                k = len(copies)
                if k >= slots:
                    copies[k - slots].wait()
                d = depth(i)
                term = dot(left[zt * d : zt * d + d, :], right)
                stage[k % slots] = term.astype(low).reshape(stage.shape[1:])
                copies.append(
                    pltpu.make_async_copy(stage.at[k % slots], terms[i].at[g // nc, g % nc, zt], stage_sem.at[k % slots])
                )
                copies[k].start()
        for copy in copies[-slots:]:
            copy.wait()
        ready[0] = i + 1

    def turned(src, dst):
        for a in range(0, src.shape[1], 256):
            b = min(a + 256, src.shape[1])
            dst[a:b, :] = src[:, a:b].T

    def vm(*shape, kind=low):
        return pltpu.VMEM(shape, kind)

    def stage_of(i, slots=4):
        return pltpu.VMEM((slots, grid.nx) + shapes[i], low)

    def cut(ref, i):
        return lambda g: ref[:, g * wide(i) : (g + 1) * wide(i)]

    first_gate, first_reset, first_cand = width, width + zdim, width + zdim + vdim
    out_i, in_i, att_i, value_i, mix_i = range(5)

    def ffn_back(cot, hold, norm_grad, two):
        wait_cot, wait_two = fetch(cot_hbm, cot), fetch(two_hbm, two)

        def second(pre_act, tiles):
            begin(out_i, tiles)
            each = depth(out_i)
            pre_waits = [fetch(ffn_hbm.at[:, k * each : (k + 1) * each], pre_act.at[k]) for k in range(2)]
            wait_cot()
            for k, (cols, grad) in enumerate(against(out_i, tiles, cut(cot, out_i))):
                pre_waits[k]()
                hold[:, cols] = (grad * silu_slope(pre_act[k % 2])).astype(low)
                if k + 2 < nz:
                    pre_waits.append(fetch(ffn_hbm.at[:, (k + 2) * each : (k + 3) * each], pre_act.at[k % 2]))
            pump()

        pl.run_scoped(second, vm(2, rows, depth(out_i), kind=f), pltpu.VMEM(tile_shape(out_i), low))

        def rest(one, hpre, upd, tok):
            waits = [fetch(one_hbm, one), fetch(hpre_hbm, hpre), fetch(proj_hbm.at[:, 0:width], upd), fetch(tok_hbm, tok)]

            def first(left, stage, tiles):
                begin(in_i, tiles)
                wait_two()
                turned(two, left)
                grads(in_i, left, stage, cut(hold, in_i))
                pump()
                for cols, grad in against(in_i, tiles, cut(hold, in_i)):
                    norm_grad[:, cols] = grad

            pl.run_scoped(first, vm(width, rows), stage_of(in_i), pltpu.VMEM(tile_shape(in_i), low))
            for wait in waits:
                wait()
            two_sums[...] = jnp.zeros_like(two_sums)

            @by_rows(16)
            def _(at):
                v, x, h, c = one[at, :], tok[at, :].astype(f), hpre[at, :], cot[at, :].astype(f)
                gain = jnp.concatenate([par[4 * dims + 2, b : b + 1, :] for b in range(blocks)], axis=1)
                r = lax.rsqrt(jnp.mean(v * v, axis=1, keepdims=True) + epsilon)
                gy = norm_grad[at, :]
                scaled = gy * gain
                pull = r * r * jnp.mean(scaled * v, axis=1, keepdims=True)
                grad_one = c + r * (scaled - v * pull)
                two_sums[...] += jnp.sum(gy * (v * r), axis=0, keepdims=True)
                u = jax.nn.sigmoid(upd[at, :])
                sig = jax.nn.sigmoid(h)
                direct[at, :] = grad_one * (1.0 - u)
                gproj[at, first_cand:] = (grad_one * u * (sig * (1.0 + h * (1.0 - sig)))).astype(low)
                gproj[at, 0:width] = (grad_one * (h * sig - x) * (u * (1.0 - u))).astype(low)

        pl.run_scoped(
            rest, vm(rows, width, kind=f), vm(rows, width, kind=f), vm(rows, width, kind=f), vm(rows, width)
        )

    pl.run_scoped(ffn_back, vm(rows, width), vm(rows, fdim), vm(rows, width, kind=f), vm(rows, width))
    pump()

    def attention_back(grad_hin, att, gate, shared_pre, value_pre):
        waits = [
            fetch(att_hbm, att),
            fetch(proj_hbm.at[:, first_reset:first_cand], gate),
            fetch(proj_hbm.at[:, first_gate:first_reset], shared_pre),
            fetch(value_hbm, value_pre),
        ]

        def out_back(hin, left, stage, tiles):
            wait_hin = fetch(hin_hbm, hin)
            begin(att_i, tiles)
            wait_hin()
            turned(hin, left)

            def part(g):
                return gproj[:, first_cand + g * wide(att_i) : first_cand + (g + 1) * wide(att_i)]

            grads(att_i, left, stage, part)
            pump()
            for cols, grad in against(att_i, tiles, part):
                grad_hin[:, cols] = grad

        pl.run_scoped(out_back, vm(rows, vdim), vm(vdim, rows), stage_of(att_i), pltpu.VMEM(tile_shape(att_i), low))

        def inner(grad_pre, normed, value_tiles):
            wait_normed = fetch(normed_hbm, normed)
            begin(value_i, value_tiles)

            def blocks_back(grad_att, values):
                for wait in waits:
                    wait()

                @by_rows(16)
                def _(at):
                    v, g, p = gate[at, :], grad_hin[at, :], value_pre[at, :]
                    sig = jax.nn.sigmoid(v)
                    grad_att[at, :] = (g * (v * sig)).astype(low)
                    gproj[at, first_reset:first_cand] = (g * att[at, :] * (sig * (1.0 + v * (1.0 - sig)))).astype(low)
                    values[at, :] = (p * jax.nn.sigmoid(p)).astype(low)

                aff_total = [jnp.zeros((1, zdim), f)] * 4
                scale_q = zdim**-0.5
                for r in range(rows // STRETCH):
                    at = slice(r * STRETCH, r * STRETCH + STRETCH)
                    v = shared_pre[at, :]
                    shared = v * jax.nn.sigmoid(v)
                    query = (scale_q * (shared * aff[0:1] + aff[1:2])).astype(low)
                    key = (shared * aff[2:3] + aff[3:4]).astype(low)
                    prob, ga = probs[at, :], grad_att[at, :]
                    grad_prob = dot_nt(ga, values[at, :])
                    weighted = jnp.sum(prob * grad_prob, axis=1, keepdims=True)
                    grad_score = (prob * (grad_prob - weighted)).astype(low)
                    grad_query = dot(grad_score, key) * scale_q
                    grad_key = dot_tn(grad_score, query)
                    grad_shared = grad_query * aff[0:1] + grad_key * aff[2:3]
                    gproj[at, first_gate:first_reset] = (grad_shared * silu_slope(v)).astype(low)
                    for k, t in enumerate([grad_query * shared, grad_query, grad_key * shared, grad_key]):
                        aff_total[k] = aff_total[k] + jnp.sum(t, axis=0, keepdims=True)
                    grad_hin[at, :] = dot_tn(prob.astype(low), ga)
                for k in range(4):
                    aff_sums[k : k + 1, :] = aff_total[k]

                @by_rows(16)
                def _(at):
                    grad_pre[at, :] = (grad_hin[at, :] * silu_slope(value_pre[at, :])).astype(low)

            pl.run_scoped(blocks_back, vm(rows, vdim), vm(rows, vdim))
            pump()

            def value_back(left, stage):
                wait_normed()
                turned(normed, left)
                grads(value_i, left, stage, cut(grad_pre, value_i))
                for cols, grad in against(value_i, value_tiles, cut(grad_pre, value_i)):
                    pre[:, cols] = grad

            pl.run_scoped(value_back, vm(width, rows), stage_of(value_i))

        pl.run_scoped(inner, vm(rows, vdim), vm(rows, width), pltpu.VMEM(tile_shape(value_i), low))

    pl.run_scoped(
        attention_back, vm(rows, vdim, kind=f), vm(rows, vdim, kind=f), vm(rows, vdim, kind=f), vm(rows, zdim, kind=f),
        vm(rows, vdim, kind=f)
    )
    pump()

    def mix_back(g_rows, gin_rows, x_in, mixed, tok):
        waits = [fetch(x_hbm, x_in), fetch(mixed_hbm, mixed), fetch(tok_hbm, tok)]

        def mix_weight_back(active, left, stage, tiles):
            wait_active = fetch(active_hbm, active)
            begin(mix_i, tiles)
            wait_active()
            turned(active, left)
            grads(mix_i, left, stage, cut(gproj, mix_i))
            pump()
            for cols, grad in against(mix_i, tiles, cut(gproj, mix_i)):
                grad = grad.astype(low).astype(f)
                for b in range(cols.start // 128, cols.stop // 128):
                    lane = b * 128 - cols.start
                    g_rows[pl.ds(b, rows, stride=blocks), :] = grad[:, lane : lane + 128]

        pl.run_scoped(
            mix_weight_back, vm(rows, width), vm(width, rows), stage_of(mix_i), pltpu.VMEM(tile_shape(mix_i), low)
        )

        for wait in waits:
            wait()

        def scan(before):
            scan_back(
                grid, dims, g_rows, x_in, mixed, carry, par, alive, spans, gin_rows, before, bound, sends_b, recv_b,
                m_all, k_all, seq_peer, s, pump
            )

        pl.run_scoped(scan, vm(rows, 4, blocks, 128, kind=f))
        norm_back(par, dims, tok, pre, direct, gin_rows, gtok_out, row_sums)

    pl.run_scoped(
        mix_back, vm(rows * blocks, 128, kind=f), vm(rows * blocks, 128, kind=f), vm(rows * blocks, 128, kind=f),
        vm(rows * blocks, 128, kind=f), vm(rows, width)
    )
    small[...] = jnp.zeros_like(small)
    fill_small(grid, dims, small, m_all, k_all, row_sums)
    for e in range(nq):
        b = block_of(e, nq, blocks)
        small[e, 2 * dims + 2 : 2 * dims + 3] = two_sums[:, b * 128 : b * 128 + 128]
        small[e, 2 * dims + 3 : 2 * dims + 7] = aff_sums[...]
    little.start()
    pump()
    little.middle()
    for _ in steps:
        pass
    little.end()


def layer_backward(grid, wholes, cuts, kept, probs, carry, par, aff, alive, spans, sizes, collective_id):
    nq, ng = grid.nq, grid.ng
    dims, blocks = carry.shape[0], carry.shape[1]
    zdim, vdim, fdim = sizes
    width = blocks * 128
    rows = probs.shape[0]
    f = jnp.float32
    vm = pl.BlockSpec(memory_space=pltpu.VMEM)
    n = len(wholes)
    like = [jax.ShapeDtypeStruct((ng, w.size // ng // w.shape[-1], w.shape[-1]), w.dtype) for w in wholes]
    shapes, outs, scratch, count = scatter_plan(grid, like, cuts)
    whole_shapes = [jax.ShapeDtypeStruct(w.shape[:4] + s, w.dtype) for w, s in zip(wholes, shapes)]
    low = [w.reshape(v.shape) for w, v in zip(wholes, whole_shapes)]
    small_shape = (-(-(2 * dims + 7) // 8) * 8, 128)
    result = pl.pallas_call(
        functools.partial(layer_back_kernel, grid, dims, shapes, sizes),
        out_shape=outs
        + [jax.ShapeDtypeStruct((rows, width), jnp.bfloat16), jax.ShapeDtypeStruct(small_shape, f)]
        + whole_shapes[1:],
        in_specs=[ANY] * n + [ANY] * 10 + [vm] + [ANY] * 5 + [vm] * 5,
        out_specs=[vm] * (n + 2) + [ANY] * (n - 1),
        scratch_shapes=[
            pltpu.VMEM((rows, width * 2 + zdim + vdim), jnp.bfloat16),
            pltpu.VMEM((rows, width), f),
            pltpu.VMEM((rows, width), f),
            pltpu.VMEM((nq, dims, blocks, 128), f),
            pltpu.VMEM((dims + 1, blocks, 128), f),
            pltpu.VMEM((dims, blocks, 128), f),
            pltpu.VMEM((blocks, 128), f),
            pltpu.VMEM((1, width), f),
            pltpu.VMEM((4, zdim), f),
            pltpu.VMEM((nq,) + small_shape, f),
            pltpu.VMEM((nq - 1,) + small_shape, f),
            pltpu.VMEM((ng - 1,) + small_shape, f),
            pltpu.SemaphoreType.DMA((nq - 1,)),
            pltpu.SemaphoreType.DMA((nq - 1,)),
            pltpu.SemaphoreType.DMA((nq + ng - 2,)),
            pltpu.SemaphoreType.DMA((nq + ng - 2,)),
            pltpu.SemaphoreType.DMA((n, 2)),
            pltpu.SemaphoreType.DMA((24,)),
            pltpu.SemaphoreType.DMA((2,)),
            pltpu.SemaphoreType.DMA((4,)),
            pltpu.SemaphoreType.DMA((count,)),
            pltpu.SemaphoreType.DMA((count,)),
        ]
        + scratch,
        compiler_params=pltpu.CompilerParams(
            collective_id=collective_id, has_side_effects=True, vmem_limit_bytes=63 << 20
        ),
    )(*low, *kept[:10], probs, *kept[10:], carry, par, aff, alive, spans)
    return [v.reshape(-1, t.shape[-1]) for v, t in zip(result, like)], result[n], result[n + 1]


def rms_forward(values, gain):
    inverse = lax.rsqrt(jnp.mean(values * values, axis=-1, keepdims=True) + epsilon)
    return (values * inverse * gain, inverse)


def rms_backward(grad_out, values, inverse, gain):
    scaled = grad_out * gain
    projection = jnp.mean(scaled * values, axis=-1, keepdims=True)
    grad_in = inverse * (scaled - values * inverse * inverse * projection)
    return (grad_in, jnp.sum(grad_out * values * inverse, axis=0))


def silu_slope(values):
    sigma_v = jax.nn.sigmoid(values)
    return sigma_v * (1.0 + values * (1.0 - sigma_v))


def times(left, pieces):
    return jnp.concatenate(
        [jnp.dot(left, pieces[i], preferred_element_type=jnp.float32) for i in range(pieces.shape[0])], axis=1
    )


def against(left, pieces):
    n = pieces.shape[2]
    return sum(
        lax.dot_general(
            left[:, i * n : i * n + n], pieces[i], (((1,), (1,)), ((), ())), preferred_element_type=jnp.float32
        )
        for i in range(pieces.shape[0])
    )


def over_rows(left, right, count):
    n = right.shape[1] // count
    return jnp.stack(
        [
            lax.dot_general(
                left, right[:, i * n : i * n + n], (((0,), (0,)), ((), ())), preferred_element_type=jnp.float32
            ).astype(jnp.bfloat16)
            for i in range(count)
        ]
    )


def masked_scores(query_blk, key_blk, allowed):
    raw_scores = jnp.einsum("cid,cjd->cij", query_blk, key_blk, preferred_element_type=jnp.float32)
    return jnp.where(allowed, raw_scores, -1e30)


def backward_apart(grid, cotangent, tokens_low, forward, weights, alive, spans, sizes):
    (carry, par, affine, probs, _, normed_b, active, x_rows, mixed_rows, out_one, normed_two_b,
     projected, value_pre, attended, hidden_in, hidden_pre, ffn_hidden, ffn_act) = forward
    ffn_hidden = ffn_hidden.astype(jnp.float32)
    token_count, model_width = tokens_low.shape
    nq, ng = grid.nq, grid.ng
    dims, blocks = carry.shape[0], carry.shape[1]
    zdim, vdim, _ = sizes
    block_count = token_count // STRETCH
    tokens_flat = tokens_low.astype(jnp.float32)
    mix_full, value_full, out_full, ffn_in_full, ffn_out_full = (w.reshape(ng, -1, w.shape[-1]) for w in weights)
    gain_two = par[4 * dims + 2].reshape(-1)
    update = jax.nn.sigmoid(projected[:, :model_width])
    gate_pre = projected[:, model_width : model_width + zdim + vdim]
    gate_rows = jax.nn.silu(gate_pre)
    shared = gate_rows[:, :zdim]
    reset_gate = gate_rows[:, zdim:]
    values_b = jax.nn.silu(value_pre).astype(jnp.bfloat16)
    scale_q = zdim ** (-0.5)
    query_b = (scale_q * (shared * affine[0] + affine[1])).astype(jnp.bfloat16)
    key_b = (shared * affine[2] + affine[3]).astype(jnp.bfloat16)
    query_blk = query_b.reshape(block_count, STRETCH, zdim)
    key_blk = key_b.reshape(block_count, STRETCH, zdim)
    value_blk = values_b.reshape(block_count, STRETCH, vdim)
    probs = probs.reshape(block_count, STRETCH, STRETCH)
    probs_b = probs.astype(jnp.bfloat16)
    hidden_act = jax.nn.silu(hidden_pre)
    inverse_two = lax.rsqrt(jnp.mean(out_one * out_one, axis=-1, keepdims=True) + epsilon)

    grad_y_b = cotangent
    grad_ffn_out = over_rows(ffn_act, grad_y_b, ng)
    grad_act = against(grad_y_b, ffn_out_full)
    grad_hidden_b = (grad_act * silu_slope(ffn_hidden)).astype(jnp.bfloat16)
    grad_ffn_in = over_rows(normed_two_b, grad_hidden_b, ng)
    grad_normed_two = against(grad_hidden_b, ffn_in_full)
    grad_norm_two, grad_gain_two = rms_backward(grad_normed_two, out_one, inverse_two, gain_two)
    grad_out_one = grad_y_b.astype(jnp.float32) + grad_norm_two
    grad_update = grad_out_one * (hidden_act - tokens_flat)
    grad_tokens_flat = grad_out_one * (1.0 - update)
    grad_hpre_b = (grad_out_one * update * silu_slope(hidden_pre)).astype(jnp.bfloat16)
    grad_out_weight = over_rows(hidden_in, grad_hpre_b, ng)
    grad_hidden_in = against(grad_hpre_b, out_full)
    grad_att_b = (grad_hidden_in * reset_gate).astype(jnp.bfloat16)
    grad_reset = grad_hidden_in * attended
    grad_att_blk = grad_att_b.reshape(block_count, STRETCH, vdim)
    grad_probs = jnp.einsum("civ,cjv->cij", grad_att_blk, value_blk, preferred_element_type=jnp.float32)
    weighted = jnp.sum(probs * grad_probs, axis=2, keepdims=True)
    grad_scores_b = (probs * (grad_probs - weighted)).astype(jnp.bfloat16)
    grad_query = jnp.einsum("cij,cjd->cid", grad_scores_b, key_blk, preferred_element_type=jnp.float32).reshape(
        token_count, zdim
    )
    grad_key = jnp.einsum("cij,cid->cjd", grad_scores_b, query_blk, preferred_element_type=jnp.float32).reshape(
        token_count, zdim
    )
    grad_values = jnp.einsum("cij,civ->cjv", probs_b, grad_att_blk, preferred_element_type=jnp.float32).reshape(
        token_count, vdim
    )
    grad_qs = grad_query * scale_q
    grad_shared = grad_qs * affine[0] + grad_key * affine[2]
    grad_affine = jnp.stack(
        [
            jnp.sum(grad_qs * shared, axis=0),
            jnp.sum(grad_qs, axis=0),
            jnp.sum(grad_key * shared, axis=0),
            jnp.sum(grad_key, axis=0),
        ]
    )
    grad_gate_pre = jnp.concatenate([grad_shared, grad_reset], axis=1) * silu_slope(gate_pre)
    grad_upre = grad_update * update * (1.0 - update)
    grad_proj_b = jnp.concatenate(
        [grad_upre.astype(jnp.bfloat16), grad_gate_pre.astype(jnp.bfloat16), grad_hpre_b], axis=1
    )
    grad_mix = over_rows(active, grad_proj_b, ng)
    grad_active_b = against(grad_proj_b, mix_full).astype(jnp.bfloat16)
    grad_vpre_b = (grad_values * silu_slope(value_pre)).astype(jnp.bfloat16)
    grad_value = over_rows(normed_b, grad_vpre_b, ng)
    grad_normed = against(grad_vpre_b, value_full)

    small = jnp.concatenate(
        [jnp.zeros((blocks, 2 * dims + 2, 128), jnp.float32), grad_gain_two.reshape(blocks, 1, 128)], axis=1
    )
    if nq != blocks:
        small = jnp.take(small, np.arange(nq) * blocks // nq, axis=0)
    small = jnp.concatenate([small, jnp.broadcast_to(grad_affine[None], (nq, 4, 128))], axis=1)
    small = jnp.pad(small, ((0, 0), (0, -small.shape[1] % 8), (0, 0)))
    return mix_backward(
        grid, [grad_ffn_out, grad_ffn_in, grad_out_weight, grad_value, grad_mix], SCATTER_CUTS, grad_active_b, x_rows,
        mixed_rows, carry, par, alive, spans, tokens_low, grad_normed, grad_tokens_flat, small, 1
    )


def body(
    tokens,
    starts,
    norm_gain,
    ema_delta,
    ema_alpha,
    ema_beta,
    ema_eta,
    ema_omega,
    mix_weight,
    value_weight,
    qk_affine,
    out_weight,
    ffn_gain,
    ffn_in,
    ffn_out,
    cotangent,
):
    seg_count, row_count, model_width = tokens.shape
    nq, ng = lax.axis_size("seq"), lax.axis_size("seg")
    grid = Grid(nq, ng)
    seq_index, seg_index = lax.axis_index("seq"), lax.axis_index("seg")
    seq_length = row_count * nq
    dims = ema_delta.shape[1]
    zdim = qk_affine.shape[0] * nq * ng // 4
    vdim = value_weight.shape[1] * ng
    token_count = seg_count * row_count
    blocks = model_width // 128

    index = seq_index * ng + seg_index
    mine, part = norm_gain.shape[0], qk_affine.shape[0]
    own_params = [
        ema_delta, ema_alpha, ema_beta, ema_eta, norm_gain[:, None], ema_omega[:, None], ffn_gain[:, None],
        jnp.pad(qk_affine, (0, mine - part))[:, None],
    ]
    own_params = jnp.pad(jnp.concatenate(own_params, axis=1), ((0, 0), (0, 128 - 4 * dims - 4)))
    cotangent_low = cotangent.reshape(token_count, model_width)
    shards = [mix_weight, value_weight, out_weight, ffn_in, ffn_out]
    apart = min(w.shape[1] for w in shards) < 128
    out_term = None
    if not apart:
        k, n = ffn_out.shape
        q = max(1, min(SCATTER_CUTS[0], k // 32))
        out_term = (2 * q, k // (2 * q), n)
    tokens_low = tokens.reshape(token_count, model_width)
    weights, term, forward = mix_forward(
        grid, shards, GATHER_CUTS, tokens_low, own_params, starts, cotangent_low, dims, part, out_term, 0
    )
    alive, spans, *forward = forward
    (carry, par, affine, probs, result, normed_b, active, x_rows, mixed_rows, out_one, normed_two_b,
     projected, value_pre, attended, hidden_in, hidden_pre, ffn_hidden, ffn_act) = forward
    sizes = (zdim, vdim, ffn_act.shape[1])
    if apart:
        result_back = backward_apart(grid, cotangent_low, tokens_low, forward, weights, alive, spans, sizes)
    else:
        kept = [term[0], cotangent_low, ffn_hidden, normed_two_b, out_one, hidden_pre, projected, attended, hidden_in,
                value_pre, active, normed_b, tokens_low, x_rows, mixed_rows]
        order = [weights[4], weights[3], weights[2], weights[1], weights[0]]
        result_back = layer_backward(
            grid, order, SCATTER_CUTS, kept, probs, carry, par, affine, alive, spans, sizes, 1
        )
    (g_ffn_out, g_ffn_in, g_out, g_value, g_mix), grad_tokens, sums = result_back
    return (
        result.reshape(seg_count, row_count, model_width),
        grad_tokens.reshape(seg_count, row_count, model_width),
        *small_outputs(sums, index, dims, ema_delta, ema_alpha, ema_beta, ema_eta, mine, part, g_mix, g_value, g_out, g_ffn_in, g_ffn_out),
    )


def small_outputs(sums, index, dims, ema_delta, ema_alpha, ema_beta, ema_eta, mine, part, g_mix, g_value, g_out, g_ffn_in, g_ffn_out):
    own = lax.dynamic_slice_in_dim(sums, lax.rem(index * mine, 128), mine, 1)
    m_sum, k_sum = own[:dims].T, own[dims : 2 * dims].T
    vectors = own[2 * dims : 2 * dims + 3]
    delta, alpha, beta, eta = (v.astype(jnp.float32) for v in (ema_delta, ema_alpha, ema_beta, ema_eta))
    damping, decay = jax.nn.sigmoid(delta), jax.nn.sigmoid(alpha)
    g_keep = damping * beta * eta * k_sum
    grad_eta = damping * beta * m_sum
    grad_beta = damping * eta * m_sum
    grad_alpha = -g_keep * damping * decay * (1.0 - decay)
    grad_delta = (beta * eta * m_sum - g_keep * decay) * damping * (1.0 - damping)
    grad_affine = lax.dynamic_slice(
        sums, (2 * dims + 3 + index * part // 128, lax.rem(index * part, 128)), (1, part)
    ).reshape(-1)
    return (vectors[1], grad_delta, grad_alpha, grad_beta, grad_eta, vectors[0],
            g_mix, g_value, grad_affine, g_out, vectors[2], g_ffn_in, g_ffn_out)


def solution(mesh):
    placed = (
        P("seg", "seq", None),
        P("seg", None),
        P(("seq", "seg")),
        P(("seq", "seg"), None),
        P(("seq", "seg"), None),
        P(("seq", "seg"), None),
        P(("seq", "seg"), None),
        P(("seq", "seg")),
        P("seq", "seg"),
        P("seq", "seg"),
        P(("seq", "seg")),
        P("seq", "seg"),
        P(("seq", "seg")),
        P("seq", "seg"),
        P("seq", "seg"),
        P("seg", "seq", None),
    )
    return jax.shard_map(
        body,
        mesh=mesh,
        in_specs=placed,
        out_specs=(P("seg", "seq", None),) * 2 + placed[2:15],
        check_vma=False,
    )
```

```python
import functools
import math

import jax
import jax.numpy as jnp
import numpy as np
from jax import lax
from jax.experimental import pallas as pl
from jax.experimental.pallas import tpu as pltpu
from jax.sharding import PartitionSpec as P

STRETCH = 128
epsilon = 1e-05
GATHER_LAG = (1, 1, 1, 1, 1)
SCATTER_LAG = (0, 1, 1, 1, 1)
GATHER_CUTS = (4, 2, 2, 4, 4)
SCATTER_CUTS = (4, 4, 2, 2, 4)

MESH = pl.DeviceIdType.MESH
ANY = pl.BlockSpec(memory_space=pl.ANY)


class Grid:
    def __init__(self, nq, ng):
        self.nq, self.ng = nq, ng
        self.nz = math.gcd(nq, 4)
        self.nx = nq // self.nz
        self.nc = math.gcd(ng, 2)
        self.ny = ng // self.nc

    def here(self):
        s, g = lax.axis_index("seq"), lax.axis_index("seg")
        return s // self.nx, lax.rem(s, self.nx), g // self.nc, lax.rem(g, self.nc)

    def peer(self, axis, d):
        z, x, y, c = self.here()
        if axis == "z":
            z = lax.rem(z + d, self.nz)
        if axis == "x":
            x = lax.rem(x + d, self.nx)
        if axis == "y":
            y = lax.rem(y + d, self.ny)
        if axis == "c":
            c = lax.rem(c + d, self.nc)
        return z, x, y, c

    def size(self, axis):
        return {"z": self.nz, "x": self.nx, "y": self.ny, "c": self.nc}[axis]

    def device(self, place):
        z, x, y, c = place
        return {"seq": z * self.nx + x, "seg": y * self.nc + c}

    def peers(self, axes):
        return [self.peer(a, d) for a in axes for d in range(1, self.size(a))]


def enter(grid, peers):
    barrier = pltpu.get_barrier_semaphore()
    for place in peers:
        pl.semaphore_signal(barrier, inc=1, device_id=grid.device(place), device_id_type=MESH)
    pl.semaphore_wait(barrier, len(peers))


class Sems:
    def __init__(self, send, recv):
        self.send, self.recv, self.used = send, recv, 0

    def take_index(self):
        self.used += 1
        return self.used - 1

    def take(self):
        i = self.take_index()
        return self.send.at[i], self.recv.at[i]


def gather_steps(grid, shapes, shards, wholes, own_sem, sems):
    n = len(shapes)
    z, x, y, c = grid.here()
    pending = []

    def push(src, dst, axis, d, arrives):
        s, r = sems.take()
        device = grid.device(grid.peer(axis, d))
        copy = pltpu.make_async_remote_copy(src, dst, s, r, device_id=device, device_id_type=MESH)
        copy.start()
        pending.append(copy)
        there = pltpu.make_async_remote_copy(arrives, arrives, s, r, device_id=device, device_id_type=MESH)
        return there.wait_recv

    def back(axis, d):
        return dict(zip("zxyc", grid.peer(axis, grid.size(axis) - d)))[axis]

    owns = []
    chunks = [(i, q) for i in range(n) for q in range(shapes[i][0] // 2)]
    core_waits = {}

    def core(k, view):
        core_waits.setdefault(k, []).extend(
            push(view(c), view(c), "c", d, view(back("c", d))) for d in range(1, grid.nc)
        )

    def stage_z(k, i, h):
        w = wholes[i]
        return [
            push(shards[i].at[h], w.at[y, c, z, x, h], "z", d, w.at[y, c, back("z", d), x, h])
            for d in range(1, grid.nz)
        ]

    def stage_two(k, i, h):
        w = wholes[i]
        src = w.at[y, c, :, x, h]
        if h % 2 == 0:
            waits = [push(src, src, "x", d, w.at[y, c, :, back("x", d), h]) for d in range(1, grid.nx)]
        else:
            waits = [push(src, src, "y", d, w.at[back("y", d), c, :, x, h]) for d in range(1, grid.ny)]
        core(k, lambda cc: w.at[y, cc, :, x, h])
        return waits

    def stage_three(k, i, h):
        w = wholes[i]
        if h % 2 == 0:
            src = w.at[y, c, :, :, h]
            waits = [push(src, src, "y", d, w.at[back("y", d), c, :, :, h]) for d in range(1, grid.ny)]
            for d in range(1, grid.nx):
                core(k, lambda cc: w.at[y, cc, :, back("x", d), h])
            return waits
        src = w.at[:, c, :, x, h]
        waits = [push(src, src, "x", d, w.at[:, c, :, back("x", d), h]) for d in range(1, grid.nx)]
        for d in range(1, grid.ny):
            core(k, lambda cc: w.at[back("y", d), cc, :, x, h])
        return waits

    def stage_last(k, i, h):
        w = wholes[i]
        if h % 2 == 0:
            for d in range(1, grid.ny):
                core(k, lambda cc: w.at[back("y", d), cc, :, :, h])
        else:
            for d in range(1, grid.nx):
                core(k, lambda cc: w.at[:, cc, :, back("x", d), h])

    def finish(waits):
        for wait in waits:
            wait()

    got = {}
    total = len(chunks)
    at = [0] * 5

    def advance(j):
        k = at[j]
        i, q = chunks[k]
        if j == 1 and q == 0:
            owns[i].wait()
        if j == 4:
            finish(core_waits[k])
            at[j] += 1
            return [i] if q + 1 == shapes[i][0] // 2 else []
        for h in (0, 1):
            if j:
                finish(got[k, h])
            got[k, h] = (stage_z, stage_two, stage_three, stage_last)[j](k, i, 2 * q + h)
        at[j] += 1
        return []

    advance(0)
    yield []
    for i in range(n):
        copy = pltpu.make_async_copy(shards[i], wholes[i].at[y, c, z, x], own_sem.at[i])
        copy.start()
        owns.append(copy)
    while at[4] < total:
        before = list(at)
        done = []
        for j in (1, 0, 2, 3, 4):
            if j == 0:
                go = at[0] < total and at[0] - at[1] < GATHER_LAG[0]
            else:
                go = at[j] < before[j - 1] and (before[j - 1] == total or before[j - 1] - at[j] >= GATHER_LAG[j])
            if go:
                done += advance(j)
        if at[4] == total:
            for copy in pending:
                copy.wait_send()
        yield done


def gather_plan(grid, shards, cuts):
    shapes, args, outs = [], [], []
    for w, q in zip(shards, cuts):
        k, n = w.shape
        q = max(1, min(q, k // 32))
        shapes.append((2 * q, k // (2 * q), n))
        args.append(w.reshape(shapes[-1]))
        outs.append(jax.ShapeDtypeStruct((grid.ny, grid.nc, grid.nz, grid.nx) + shapes[-1], w.dtype))
    per = (grid.nz - 1) + (grid.nx - 1) + (grid.ny - 1) + (grid.nc - 1) * (grid.nx + grid.ny)
    count = sum(s[0] for s in shapes) * per
    return shapes, args, outs, count


def scatter_steps(grid, shapes, terms, sums, scratch, own_sem, sems, ready=None):
    n = len(shapes)
    nz, nx, ny, nc = grid.nz, grid.nx, grid.ny, grid.nc
    own = [scratch[7 * i] for i in range(n)]
    one = [scratch[7 * i + 1] for i in range(n)]
    two_a = [scratch[7 * i + 2] for i in range(n)]
    two_b = [scratch[7 * i + 3] for i in range(n)]
    three_a = [scratch[7 * i + 4] for i in range(n)]
    three_b = [scratch[7 * i + 5] for i in range(n)]
    four = [scratch[7 * i + 6] for i in range(n)]
    z, x, y, c = grid.here()
    pending = []
    around = {(axis, d): grid.peer(axis, d) for axis in "zxyc" for d in range(1, grid.size(axis))}
    devices = {key: grid.device(place) for key, place in around.items()}

    def push(ends, axis, d):
        k = sems.take_index()

        def copy():
            return pltpu.make_async_remote_copy(
                *ends(), sems.send.at[k], sems.recv.at[k], device_id=devices[axis, d], device_id_type=MESH
            )

        copy().start()
        pending.append(lambda: copy().wait_send())
        return lambda: copy().wait_recv()

    def to(axis, d):
        return dict(zip("zxyc", around[axis, d]))[axis]

    def finish(waits):
        for wait in waits:
            wait()

    assert nc == 2

    def stage_one(i, q, h):
        return [push(lambda: (terms[i].at[:, to("c", 1), :, :, 2 * q + h], one[i].at[q, h]), "c", 1)]

    def load_own(i, q, h):
        def load():
            return pltpu.make_async_copy(terms[i].at[:, c, :, :, 2 * q + h], own[i].at[h], own_sem.at[i, h])

        load().start()
        return [lambda: load().wait()]

    def stage_two(i, q, h):
        mine = one[i].at[q, h]

        @pl.loop(0, ny * nz)
        def _(ab):
            a, b = ab // nz, lax.rem(ab, nz)
            for e in range(nx):
                mine[a, b, e] += own[i][h, a, b, e]

        if h == 0:
            return [
                push(lambda d=d: (one[i].at[q, h, to("y", d)], two_a[i].at[q, d - 1]), "y", d) for d in range(1, ny)
            ]
        return [
            push(lambda d=d: (one[i].at[q, h, :, :, to("x", d)], two_b[i].at[q, d - 1]), "x", d) for d in range(1, nx)
        ]

    def stage_three(i, q, h):
        mine = one[i].at[q, h]
        if h == 0:

            @pl.loop(0, nz)
            def _(b):
                for e in range(nx):
                    total = mine[y, b, e]
                    for d in range(ny - 1):
                        total += two_a[i][q, d, b, e]
                    mine[y, b, e] = total

            return [
                push(lambda d=d: (one[i].at[q, h, y, :, to("x", d)], three_a[i].at[q, d - 1]), "x", d)
                for d in range(1, nx)
            ]

        @pl.loop(0, nz)
        def _(b):
            for a in range(ny):
                total = mine[a, b, x]
                for d in range(nx - 1):
                    total += two_b[i][q, d, a, b]
                mine[a, b, x] = total

        return [
            push(lambda d=d: (one[i].at[q, h, to("y", d), :, x], three_b[i].at[q, d - 1]), "y", d)
            for d in range(1, ny)
        ]

    def stage_four(i, q, h):
        mine = one[i].at[q, h]
        came = three_a[i] if h == 0 else three_b[i]

        @pl.loop(0, nz)
        def _(b):
            total = mine[y, b, x]
            for d in range((nx if h == 0 else ny) - 1):
                total += came[q, d, b]
            mine[y, b, x] = total

        return [
            push(lambda d=d: (one[i].at[q, h, y, to("z", d), x], four[i].at[q, h, d - 1]), "z", d)
            for d in range(1, nz)
        ]

    def stage_last(i, q, h):
        total = one[i][q, h, y, z, x].astype(jnp.float32)
        for d in range(nz - 1):
            total += four[i][q, h, d].astype(jnp.float32)
        sums[i][2 * q + h] = total

    stages = [stage_one, stage_two, stage_three, stage_four, stage_last]
    chunks = [(i, q) for i in range(n) for q in range(shapes[i][0] // 2)]
    waits = {}
    total = len(chunks)
    at = [0] * len(stages)
    yield
    while at[-1] < total:
        there = total if ready is None else sum(1 for i, q in chunks if i < ready())
        before = [there] + at[:-1]
        fresh = None
        for j, stage in enumerate(stages):
            lag = SCATTER_LAG[j]
            if at[j] < before[j] and (before[j] == total or j == 0 or before[j] - at[j] >= lag):
                i, q = chunks[at[j]]
                for h in (0, 1):
                    if j:
                        finish(waits[i, q, h])
                    waits[i, q, h] = stage(i, q, h)
                if j == 0:
                    fresh = i, q
                at[j] += 1
            if j == 1 and fresh:
                for h in (0, 1):
                    waits[fresh[0], fresh[1], h] += load_own(*fresh, h)
        if at[-1] == total:
            finish(pending)
        yield


class SmallSum:
    def __init__(self, grid, small, total, seq_in, seg_in, send, recv):
        self.grid, self.small, self.total = grid, small, total
        self.seq_in, self.seg_in, self.send, self.recv = seq_in, seg_in, send, recv
        self.seq_peer, self.seg_peer = small_peers(grid)
        self.copies = []

    def push(self, src, dst, device):
        i = len(self.copies)
        copy = pltpu.make_async_remote_copy(
            src, dst, self.send.at[i], self.recv.at[i], device_id=device, device_id_type=MESH
        )
        copy.start()
        self.copies.append(copy)

    def start(self):
        nq, sq = self.grid.nq, lax.axis_index("seq")
        for d in range(1, nq):
            self.push(self.small.at[lax.rem(sq + d, nq)], self.seq_in.at[d - 1], self.seq_peer[d - 1])

    def middle(self):
        nq, ng = self.grid.nq, self.grid.ng
        total = self.small[lax.axis_index("seq")]
        for d in range(1, nq):
            self.copies[d - 1].wait_recv()
            total += self.seq_in[d - 1]
        self.total[...] = total
        for d in range(1, ng):
            self.push(self.total, self.seg_in.at[d - 1], self.seg_peer[d - 1])

    def end(self):
        nq, ng = self.grid.nq, self.grid.ng
        total = self.total[...]
        for d in range(1, ng):
            self.copies[nq + d - 2].wait_recv()
            total += self.seg_in[d - 1]
        for copy in self.copies:
            copy.wait_send()
        self.total[...] = total


def small_peers(grid):
    nq, ng = grid.nq, grid.ng
    s, g = lax.axis_index("seq"), lax.axis_index("seg")
    return (
        [{"seq": lax.rem(s + d, nq), "seg": g} for d in range(1, nq)],
        [{"seq": s, "seg": lax.rem(g + d, ng)} for d in range(1, ng)],
    )


def meet(peers):
    barrier = pltpu.get_barrier_semaphore()
    for place in peers:
        pl.semaphore_signal(barrier, inc=1, device_id=place, device_id_type=MESH)
    pl.semaphore_wait(barrier, len(peers))


def scatter_plan(grid, terms, cuts):
    nz, nx, ny = grid.nz, grid.nx, grid.ny
    shapes, outs, scratch = [], [], []
    for t, q in zip(terms, cuts):
        _, rows, n = t.shape
        if n < 128:
            rows, n = rows * n // 128, 128
        k = rows // grid.nq
        q = max(1, min(q, k // 32))
        kh = k // (2 * q)
        shapes.append((2 * q, kh, n))
        outs.append(jax.ShapeDtypeStruct((2 * q, kh, n), jnp.float32))
        b = t.dtype
        scratch += [
            pltpu.VMEM((2, ny, nz, nx, kh, n), b),
            pltpu.VMEM((q, 2, ny, nz, nx, kh, n), b),
            pltpu.VMEM((q, max(ny - 1, 1), nz, nx, kh, n), b),
            pltpu.VMEM((q, max(nx - 1, 1), ny, nz, kh, n), b),
            pltpu.VMEM((q, max(nx - 1, 1), nz, kh, n), b),
            pltpu.VMEM((q, max(ny - 1, 1), nz, kh, n), b),
            pltpu.VMEM((q, 2, max(nz - 1, 1), kh, n), b),
        ]
    per = (grid.nc - 1) + (nx - 1) + (ny - 1) + (nz - 1)
    count = per * sum(s[0] for s in shapes)
    return shapes, outs, scratch, count


def block_of(e, nq, blocks):
    return e * blocks // nq


def place_params(grid, tables, vectors, affine, tile):
    index = lax.axis_index("seq") * grid.ng + lax.axis_index("seg")

    def spread(v):
        mine = v.shape[1]
        row = lax.broadcasted_iota(jnp.int32, (mine, 128), 0)
        lane = lax.broadcasted_iota(jnp.int32, (mine, 128), 1)
        where = (lane == row + lax.rem(index * mine, 128)).astype(jnp.bfloat16)
        wide = jnp.broadcast_to(v.astype(jnp.float32), (max(v.shape[0], 8), mine)).astype(jnp.bfloat16)
        return jnp.dot(wide, where, preferred_element_type=jnp.float32)[0 : v.shape[0]]

    tile[...] = jnp.zeros_like(tile)
    first = 0
    for v in tables + vectors:
        tile[first : first + v.shape[0], :] = spread(v[...])
        first += v.shape[0]
    at = lax.broadcasted_iota(jnp.int32, (4, 128), 0) == index * affine.shape[1] // 128
    tile[first : first + 4, :] = jnp.where(at, spread(affine[...]), 0.0)


def place_documents(grid, starts, alive, spans, mask):
    rows = alive.shape[0]
    first = [starts[0, k] for k in range(starts.shape[1])]
    base = lax.axis_index("seq") * rows
    place = lax.broadcasted_iota(jnp.int32, (rows, 128), 0)
    column = lax.broadcasted_iota(jnp.int32, (rows, 128), 1)
    within = jnp.bitwise_and(place, STRETCH - 1)
    here, there = base + place, base + place - within + column
    goes_on = jnp.ones((rows, 128), jnp.float32)
    doc_here, doc_there = jnp.zeros((rows, 128), jnp.int32), jnp.zeros((rows, 128), jnp.int32)
    for f in first:
        goes_on = jnp.where(here == f, 0.0, goes_on)
        doc_here = doc_here + jnp.where(here >= f, 1, 0)
        doc_there = doc_there + jnp.where(there >= f, 1, 0)
    alive[...] = goes_on
    mask[...] = jnp.where((doc_here == doc_there) & (column <= within), 1.0, 0.0)
    low = lax.broadcasted_iota(jnp.int32, spans.shape, 0) * rows
    whole = jnp.ones(spans.shape, jnp.float32)
    for f in first:
        whole = jnp.where((low <= f) & (f < low + rows), 0.0, whole)
    spans[...] = whole


def mix_kernel(grid, width, dims, shapes, out_term, *refs):
    n = len(shapes)
    shards, refs = refs[:n], refs[n:]
    tok, starts, cot, *refs = refs
    tables, vectors, affine, refs = refs[:4], refs[4:7], refs[7], refs[8:]
    wholes, refs = refs[:n], refs[n:]
    term_hbm = None
    if out_term:
        term_hbm, *refs = refs
    (alive, spans, carry_out, par_out, aff_out, probs_out, layer_out,
     normed_hbm, active_hbm, x_hbm, mixed_hbm, one_hbm, two_hbm, proj_hbm, value_hbm, att_hbm, hin_hbm, hpre_hbm, ffn_hbm, act_hbm,
     normed_out, active_out, x_out, mixed_out, out_one_out, two_out, proj, value_pre, att, hin, hpre, ffn_pre, act, values,
     mask, tile, tiles, table, bound, sends_t, recv_t, sends_b, recv_b, own_sem, flush_sem, load_sem, send, recv,
     *slots) = refs
    if out_term:
        *slots, turned_act, stage, stage_sem = slots
    nq, ng = grid.nq, grid.ng
    rows = tok.shape[0]
    blocks = width // 128
    s = lax.axis_index("seq")
    seq_peer, seg_peer = small_peers(grid)
    meet(seq_peer + seg_peer)
    steps = gather_steps(grid, shapes, shards, wholes, own_sem, Sems(send, recv))

    done = set()

    def pump(count=1):
        for _ in range(count):
            done.update(next(steps, ()))

    flushes = []

    def flush(ref, hbm):
        copy = pltpu.make_async_copy(ref, hbm, flush_sem.at[len(flushes)])
        copy.start()
        flushes.append(copy)

    place_params(grid, tables, vectors, affine, tile)
    place_documents(grid, starts, alive, spans, mask)

    copies = []
    for d in range(1, ng):
        copies.append(pltpu.make_async_remote_copy(
            tile, tiles.at[d - 1], sends_t.at[d - 1], recv_t.at[d - 1],
            device_id=seg_peer[d - 1], device_id_type=MESH))
        copies[-1].start()
    for copy in copies:
        copy.wait_recv()
    lanes = tile[...]
    for d in range(1, ng):
        lanes += tiles[d - 1]
    table[s] = lanes
    for d in range(1, nq):
        copies.append(pltpu.make_async_remote_copy(
            table.at[s], table.at[s], sends_t.at[ng + d - 2], recv_t.at[ng + d - 2],
            device_id=seq_peer[d - 1], device_id_type=MESH))
        copies[-1].start()
    pump()
    for d in range(1, nq):
        came = table.at[lax.rem(s + nq - d, nq)]
        pltpu.make_async_remote_copy(
            came, came, sends_t.at[ng + d - 2], recv_t.at[ng + d - 2],
            device_id=seq_peer[d - 1], device_id_type=MESH).wait_recv()
    count = 4 * dims + 3
    for b in range(blocks):
        mine = [e for e in range(nq) if block_of(e, nq, blocks) == b]
        whole = table[mine[0], 0:count]
        for e in mine[1:]:
            whole += table[e, 0:count]
        par_out[:, b, :] = whole
    aff = table[0, count : count + 4]
    for e in range(1, nq):
        aff += table[e, count : count + 4]
    aff_out[...] = aff

    pump()

    gain = [par_out[4 * dims, b : b + 1, :] for b in range(blocks)]
    step_rows = 32

    @pl.loop(0, rows // step_rows)
    def _(i):
        at = pl.ds(pl.multiple_of(i * step_rows, step_rows), step_rows)
        v = tok[at, :].astype(jnp.float32)
        r = lax.rsqrt(jnp.mean(v * v, axis=1, keepdims=True) + epsilon)
        for b in range(blocks):
            lane = slice(b * 128, b * 128 + 128)
            n = (v[:, lane] * r * gain[b]).astype(jnp.bfloat16)
            normed_out[at, lane] = n
            x_out[pl.ds(i * step_rows * blocks + b, step_rows, stride=blocks), :] = n.astype(jnp.float32)

    flush(normed_out, normed_hbm)
    flush(x_out, x_hbm)
    damping = [jax.nn.sigmoid(par_out[j]) for j in range(dims)]
    keep = [1.0 - damping[j] * jax.nn.sigmoid(par_out[dims + j]) for j in range(dims)]
    weight = [damping[j] * par_out[2 * dims + j] * par_out[3 * dims + j] for j in range(dims)]
    omega = par_out[4 * dims + 1]

    def row(ref, p):
        return ref[pl.ds(pl.multiple_of(p * blocks, blocks), blocks), :]

    def first_pass(p, state):
        x, a = row(x_out, p), alive[pl.ds(p, 1), :]
        return tuple(keep[j] * (state[j] * a) + x for j in range(dims))

    zero = tuple(jnp.zeros((blocks, 128), jnp.float32) for _ in range(dims))
    pump()
    ends = zero
    for part in range(2):
        ends = lax.fori_loop(part * rows // 2, (part + 1) * rows // 2, first_pass, ends, unroll=4)
        if part == 0:
            pump()
    for j in range(dims):
        bound[s, j] = ends[j]
    out = []
    for d in range(1, nq):
        out.append(pltpu.make_async_remote_copy(
            bound.at[s], bound.at[s], sends_b.at[d - 1], recv_b.at[d - 1],
            device_id=seq_peer[d - 1], device_id_type=MESH))
        out[-1].start()
    pump(3)
    for d in range(1, nq):
        came = bound.at[lax.rem(s + nq - d, nq)]
        pltpu.make_async_remote_copy(
            came, came, sends_b.at[d - 1], recv_b.at[d - 1],
            device_id=seq_peer[d - 1], device_id_type=MESH).wait_recv()
    for j in range(dims):
        through = power(keep[j], rows)
        state = jnp.zeros((blocks, 128), jnp.float32)
        for e in range(nq - 1):
            later = through * spans[e : e + 1, :] * state + bound[e, j]
            state = jnp.where(e < s, later, state)
        carry_out[j] = state

    def second_pass(p, state):
        x, a = row(x_out, p), alive[pl.ds(p, 1), :]
        state = tuple(keep[j] * (state[j] * a) + x for j in range(dims))
        sums = [omega * x] + [weight[j] * state[j] for j in range(dims)]
        while len(sums) > 1:
            sums = [sum(sums[k : k + 2][1:], sums[k]) for k in range(0, len(sums), 2)]
        mixed_out[pl.ds(pl.multiple_of(p * blocks, blocks), blocks), :] = sums[0]
        return state

    state = tuple(carry_out[j] for j in range(dims))
    for part in range(4):
        state = lax.fori_loop(part * rows // 4, (part + 1) * rows // 4, second_pass, state, unroll=4)
        if part % 2:
            pump()
    for b in range(blocks):
        m = mixed_out[pl.ds(b, rows, stride=blocks), :]
        active_out[:, b * 128 : b * 128 + 128] = (m * jax.nn.sigmoid(m)).astype(jnp.bfloat16)
    flush(mixed_out, mixed_hbm)
    flush(active_out, active_hbm)
    for copy in copies + out:
        copy.wait_send()

    def pieces(i):
        while i not in done:
            pump()

        def fetch(g):
            return pltpu.make_async_copy(
                wholes[i].at[g // grid.nc, g % grid.nc], slots[i].at[g % 2], load_sem.at[i, g % 2]
            )

        fetch(0).start()
        for g in range(grid.ng):
            if g + 1 < grid.ng:
                fetch(g + 1).start()
            fetch(g).wait()
            piece = slots[i][g % 2]
            wide = piece.shape[-1]
            yield g, slice(g * wide, g * wide + wide), piece.reshape(-1, wide)
            if g + 1 == grid.ng:
                pump()

    block_rows = 32
    zdim = aff_out.shape[1]
    vdim = value_pre.shape[1]
    first_gate, first_reset, first_cand = width, width + zdim, width + zdim + vdim
    dot = functools.partial(jnp.dot, preferred_element_type=jnp.float32)

    def by_rows(count=rows, each=block_rows):
        def wrap(f):
            pl.loop(0, count // each)(lambda i: f(pl.ds(pl.multiple_of(i * each, each), each)))

        return wrap

    for g, cols, piece in pieces(0):
        proj[:, cols] = dot(active_out[...], piece)
    flush(proj, proj_hbm)

    scale_q = zdim**-0.5
    near = []
    for r in range(rows // STRETCH):
        at = slice(r * STRETCH, r * STRETCH + STRETCH)
        gate = proj[at, first_gate:first_reset]
        shared = gate * jax.nn.sigmoid(gate)
        query = (scale_q * (shared * aff_out[0:1] + aff_out[1:2])).astype(jnp.bfloat16)
        key = (shared * aff_out[2:3] + aff_out[3:4]).astype(jnp.bfloat16)
        scores = lax.dot_general(query, key, (((1,), (1,)), ((), ())), preferred_element_type=jnp.float32)
        scores = jnp.where(mask[at, :] > 0.0, scores, -1e30)
        expo = jnp.exp(scores - jnp.max(scores, axis=1, keepdims=True))
        probs = expo / jnp.sum(expo, axis=1, keepdims=True)
        probs_out[at, :] = probs
        near.append(probs.astype(jnp.bfloat16))

    for g, cols, piece in pieces(1):
        pre = dot(normed_out[...], piece)
        value_pre[:, cols] = pre
        values[:, cols] = (pre * jax.nn.sigmoid(pre)).astype(jnp.bfloat16)
    flush(value_pre, value_hbm)
    for r in range(rows // STRETCH):
        at = slice(r * STRETCH, r * STRETCH + STRETCH)
        att[at, :] = dot(near[r], values[at, :])

    @by_rows()
    def _(at):
        gate = proj[at, first_reset:first_cand]
        hin[at, :] = (att[at, :] * (gate * jax.nn.sigmoid(gate))).astype(jnp.bfloat16)

    flush(att, att_hbm)
    flush(hin, hin_hbm)

    for g, cols, piece in pieces(2):
        hpre[:, cols] = proj[:, first_cand + cols.start : first_cand + cols.stop] + dot(hin[...], piece)
    flush(hpre, hpre_hbm)

    gain_two = [par_out[4 * dims + 2, b : b + 1, :] for b in range(blocks)]

    @by_rows()
    def _(at):
        v = tok[at, :].astype(jnp.float32)
        h = hpre[at, :]
        one = v + jax.nn.sigmoid(proj[at, 0:width]) * (h * jax.nn.sigmoid(h) - v)
        out_one_out[at, :] = one
        r = lax.rsqrt(jnp.mean(one * one, axis=1, keepdims=True) + epsilon)
        for b in range(blocks):
            lane = slice(b * 128, b * 128 + 128)
            two_out[at, lane] = (one[:, lane] * r * gain_two[b]).astype(jnp.bfloat16)

    flush(out_one_out, one_hbm)
    flush(two_out, two_hbm)
    for g, cols, piece in pieces(3):
        pre = dot(two_out[...], piece)
        ffn_pre[:, cols] = pre
        act[:, cols] = (pre * jax.nn.sigmoid(pre)).astype(jnp.bfloat16)
    flush(ffn_pre, ffn_hbm)
    flush(act, act_hbm)

    if out_term:
        for a in range(0, act.shape[1], 256):
            turned_act[a : a + 256, :] = act[:, a : a + 256].T
        n_cols, deep = out_term[-1], act.shape[1] // grid.nz
        copies = []
        for g in range(ng):
            right = cot[:, g * n_cols : (g + 1) * n_cols]
            for zt in range(grid.nz):
                m = len(copies)
                if m >= 4:
                    copies[m - 4].wait()
                stage[m % 4] = dot(turned_act[zt * deep : (zt + 1) * deep, :], right).astype(jnp.bfloat16).reshape(stage.shape[1:])
                copies.append(
                    pltpu.make_async_copy(stage.at[m % 4], term_hbm.at[g // grid.nc, g % grid.nc, zt], stage_sem.at[m % 4])
                )
                copies[m].start()
            if g == ng // 2:
                pump()
        for copy in copies[-4:]:
            copy.wait()
    for g, cols, piece in pieces(4):
        layer_out[:, cols] = (out_one_out[:, cols] + dot(act[...], piece)).astype(jnp.bfloat16)
    for _ in steps:
        pass
    for copy in flushes:
        copy.wait()


def power(v, n):
    result = None
    while n:
        if n & 1:
            result = v if result is None else result * v
        n >>= 1
        if n:
            v = v * v
    return result


def mix_forward(grid, weights, cuts, tok, own_params, starts, cot, dims, out_term, collective_id):
    rows, width = tok.shape
    nq, ng = grid.nq, grid.ng
    blocks = width // 128
    f = jnp.float32
    vm = pl.BlockSpec(memory_space=pltpu.VMEM)
    shapes, shards, outs, count = gather_plan(grid, weights, cuts)
    n = len(shards)
    vdim, fdim, proj_dim = weights[1].shape[1] * ng, weights[3].shape[1] * ng, weights[0].shape[1] * ng
    low = jnp.bfloat16
    kept = [
        ((rows, width), low),
        ((rows, width), low),
        ((rows * blocks, 128), f),
        ((rows * blocks, 128), f),
        ((rows, width), f),
        ((rows, width), low),
        ((rows, proj_dim), f),
        ((rows, vdim), f),
        ((rows, vdim), f),
        ((rows, vdim), low),
        ((rows, width), f),
        ((rows, fdim), f),
        ((rows, fdim), low),
    ]
    count_rows = 4 * dims + 3
    tile_shape = (-(-(count_rows + 4) // 8) * 8, 128)
    local = [
        ((rows, 128), f),
        ((nq, 128), f),
        ((dims, blocks, 128), f),
        ((count_rows, blocks, 128), f),
        ((4, 128), f),
        ((rows, STRETCH), f),
        ((rows, width), low),
    ]
    term = [jax.ShapeDtypeStruct((grid.ny, grid.nc, grid.nz, grid.nx) + out_term, low)] if out_term else []
    held = len(term)
    turning = [
        pltpu.VMEM((fdim, rows), low),
        pltpu.VMEM((4, grid.nx) + out_term, low),
        pltpu.SemaphoreType.DMA((4,)),
    ] if out_term else []
    result = pl.pallas_call(
        functools.partial(mix_kernel, grid, width, dims, shapes, out_term),
        out_shape=outs + term + [jax.ShapeDtypeStruct(*v) for v in local + kept],
        in_specs=[ANY] * n + [vm, pl.BlockSpec(memory_space=pltpu.SMEM)] + [vm] * 9,
        out_specs=[ANY] * (n + held) + [vm] * len(local) + [ANY] * len(kept),
        scratch_shapes=[pltpu.VMEM(*v) for v in kept]
        + [
            pltpu.VMEM((rows, vdim), low),
            pltpu.VMEM((rows, STRETCH), f),
            pltpu.VMEM(tile_shape, f),
            pltpu.VMEM((ng - 1,) + tile_shape, f),
            pltpu.VMEM((nq,) + tile_shape, f),
            pltpu.VMEM((nq, dims, blocks, 128), f),
            pltpu.SemaphoreType.DMA((nq + ng - 2,)),
            pltpu.SemaphoreType.DMA((nq + ng - 2,)),
            pltpu.SemaphoreType.DMA((nq - 1,)),
            pltpu.SemaphoreType.DMA((nq - 1,)),
            pltpu.SemaphoreType.DMA((n,)),
            pltpu.SemaphoreType.DMA((len(kept),)),
            pltpu.SemaphoreType.DMA((n, 2)),
            pltpu.SemaphoreType.DMA((count,)),
            pltpu.SemaphoreType.DMA((count,)),
        ]
        + [pltpu.VMEM((2,) + o.shape[2:], o.dtype) for o in outs]
        + turning,
        compiler_params=pltpu.CompilerParams(
            collective_id=collective_id, has_side_effects=True, vmem_limit_bytes=60 << 20
        ),
    )(*shards, tok, starts, cot, *own_params)
    return result[:n], result[n : n + held], result[n + held :]


def scan_back(grid, dims, g_rows, x_in, mixed, carry, par, alive, spans, gin_rows, before, bound, sends_b, recv_b,
              m_all, k_all, seq_peer, s, pump):
    nq = grid.nq
    blocks = carry.shape[1]
    rows = g_rows.shape[0] // blocks

    @pl.loop(0, rows * blocks // 64)
    def _(i):
        at = pl.ds(pl.multiple_of(i * 64, 64), 64)
        g_rows[at, :] = g_rows[at, :] * silu_slope(mixed[at, :])

    damping = [jax.nn.sigmoid(par[j]) for j in range(dims)]
    keep = [1.0 - damping[j] * jax.nn.sigmoid(par[dims + j]) for j in range(dims)]
    weight = [damping[j] * par[2 * dims + j] * par[3 * dims + j] for j in range(dims)]
    omega = par[4 * dims + 1]

    def row(ref, p):
        return ref[pl.ds(pl.multiple_of(p * blocks, blocks), blocks), :]

    def first_pass(i, flow):
        p = rows - 1 - i
        gp, a = row(g_rows, p), alive[pl.ds(p, 1), :]
        return tuple(keep[j] * (a * (gp + flow[j])) for j in range(dims))

    zero = jnp.zeros((blocks, 128), jnp.float32)
    ends = lax.fori_loop(0, rows, first_pass, (zero,) * dims, unroll=4)
    for j in range(dims):
        bound[s, j] = ends[j]
    def sent(d):
        return pltpu.make_async_remote_copy(
            bound.at[s], bound.at[s], sends_b.at[d - 1], recv_b.at[d - 1],
            device_id=seq_peer[d - 1], device_id_type=MESH)

    for d in range(1, nq):
        sent(d).start()
    pump()
    for d in range(1, nq):
        came = bound.at[lax.rem(s + nq - d, nq)]
        pltpu.make_async_remote_copy(
            came, came, sends_b.at[d - 1], recv_b.at[d - 1],
            device_id=seq_peer[d - 1], device_id_type=MESH).wait_recv()
    flow_in = []
    for j in range(dims):
        through = power(keep[j], rows)
        flow = zero
        for e in range(nq - 1, 0, -1):
            later = through * spans[e : e + 1, :] * flow + bound[e, j]
            flow = jnp.where(e > s, later, flow)
        flow_in.append(flow)

    few = before.shape[1]
    for j0 in range(0, dims, few):
        js = range(j0, j0 + few)

        def ahead(p, state):
            x, a = row(x_in, p), alive[pl.ds(p, 1), :]
            for t in range(few):
                before[p, t] = state[t]
            return tuple(keep[j] * (state[t] * a) + x for t, j in enumerate(js))

        lax.fori_loop(0, rows, ahead, tuple(carry[j] for j in js), unroll=4)
        if j0:
            pump()

        def back(i, held):
            flow, m_sum, k_sum, om_sum = held
            p = rows - 1 - i
            at = pl.ds(pl.multiple_of(p * blocks, blocks), blocks)
            gp, x, a = g_rows[at, :], x_in[at, :], alive[pl.ds(p, 1), :]
            total = omega * gp if j0 == 0 else gin_rows[at, :]
            if j0 == 0:
                om_sum = om_sum + gp * x
            new_flow, new_m, new_k = [], [], []
            for t, j in enumerate(js):
                c = gp + flow[t]
                ac = a * c
                total = total + weight[j] * c
                new_flow.append(keep[j] * ac)
                new_m.append(m_sum[t] + c * x)
                new_k.append(k_sum[t] + ac * before[p, t])
            gin_rows[at, :] = total
            return tuple(new_flow), tuple(new_m), tuple(new_k), om_sum

        zeros = (zero,) * few
        _, m_sum, k_sum, om_sum = lax.fori_loop(
            0, rows, back, (tuple(flow_in[j] for j in js), zeros, zeros, zero), unroll=4
        )
        for t, j in enumerate(js):
            m_all[j] = m_sum[t]
            k_all[j] = k_sum[t]
        if j0 == 0:
            m_all[dims] = om_sum
        pump()
    for d in range(1, nq):
        sent(d).wait_send()


def norm_back(par, dims, tok, pre, direct, gin_rows, gtok_out, row_sums):
    rows, width = tok.shape
    blocks = width // 128
    gain = [par[4 * dims, b : b + 1, :] for b in range(blocks)]
    lanes = [slice(b * 128, b * 128 + 128) for b in range(blocks)]
    step_rows = 32

    def some(i, gains):
        at = pl.ds(pl.multiple_of(i * step_rows, step_rows), step_rows)
        v = tok[at, :].astype(jnp.float32)
        r = lax.rsqrt(jnp.mean(v * v, axis=1, keepdims=True) + epsilon)
        gy = []
        for b in range(blocks):
            came = gin_rows[pl.ds(i * step_rows * blocks + b, step_rows, stride=blocks), :]
            gy.append(pre[at, lanes[b]] + came.astype(jnp.bfloat16).astype(jnp.float32))
        scaled = [gy[b] * gain[b] for b in range(blocks)]
        dots = sum(jnp.sum(scaled[b] * v[:, lanes[b]], axis=1, keepdims=True) for b in range(blocks))
        pull = r * r * (dots / width)
        new = []
        for b in range(blocks):
            vb = v[:, lanes[b]]
            gx = r * (scaled[b] - vb * pull)
            gtok_out[at, lanes[b]] = (direct[at, lanes[b]] + gx).astype(jnp.bfloat16)
            new.append(gains[b] + jnp.sum(gy[b] * (vb * r), axis=0, keepdims=True))
        return tuple(new)

    gains = lax.fori_loop(
        0, rows // step_rows, some, tuple(jnp.zeros((1, 128), jnp.float32) for _ in range(blocks))
    )
    for b in range(blocks):
        row_sums[b : b + 1, :] = gains[b]


def fill_small(grid, dims, small, m_all, k_all, row_sums):
    blocks = row_sums.shape[0]
    for e in range(grid.nq):
        b = block_of(e, grid.nq, blocks)
        small[e, 0:dims] = m_all[0:dims, b, :]
        small[e, dims : 2 * dims] = k_all[:, b, :]
        small[e, 2 * dims : 2 * dims + 1] = m_all[dims, b : b + 1, :]
        small[e, 2 * dims + 1 : 2 * dims + 2] = row_sums[b : b + 1, :]


def mix_back_kernel(grid, dims, shapes, *refs):
    n = len(shapes)
    terms, refs = refs[:n], refs[n:]
    gact, x_in, mixed, carry, par, alive, spans, tok, pre, direct, small_in, *refs = refs
    sums, refs = refs[:n], refs[n:]
    (gtok_out, small_out,
     g_rows, gin_rows, before, bound, m_all, k_all, row_sums, small, seq_in, seg_in,
     sends_b, recv_b, s_send, s_recv, own_sem, send, recv, *scratch) = refs
    nq = grid.nq
    rows, width = gact.shape
    blocks = width // 128
    s = lax.axis_index("seq")
    seq_peer, seg_peer = small_peers(grid)
    meet(seq_peer + seg_peer)
    steps = scatter_steps(grid, shapes, terms, sums, scratch, own_sem, Sems(send, recv))
    little = SmallSum(grid, small, small_out, seq_in, seg_in, s_send, s_recv)

    def pump(count=1):
        for _ in range(count):
            next(steps, None)

    pump(2)
    for b in range(blocks):
        g_rows[pl.ds(b, rows, stride=blocks), :] = gact[:, b * 128 : b * 128 + 128].astype(jnp.float32)

    scan_back(
        grid, dims, g_rows, x_in, mixed, carry, par, alive, spans, gin_rows, before, bound, sends_b, recv_b,
        m_all, k_all, seq_peer, s, pump
    )
    norm_back(par, dims, tok, pre, direct, gin_rows, gtok_out, row_sums)
    for e in range(nq):
        small[e] = small_in[e]
    fill_small(grid, dims, small, m_all, k_all, row_sums)
    little.start()
    pump()
    little.middle()
    for _ in steps:
        pass
    little.end()


def mix_backward(grid, terms, cuts, gact, x_in, mixed, carry, par, alive, spans, tok, pre, direct, small, collective_id):
    rows, width = gact.shape
    nq, ng = grid.nq, grid.ng
    blocks, dims, few = width // 128, carry.shape[0], 4
    f = jnp.float32
    vm = pl.BlockSpec(memory_space=pltpu.VMEM)
    shapes, outs, scratch, count = scatter_plan(grid, terms, cuts)
    parts = [t.reshape((grid.ny, grid.nc, grid.nz, grid.nx) + v) for t, v in zip(terms, shapes)]
    n = len(parts)
    result = pl.pallas_call(
        functools.partial(mix_back_kernel, grid, dims, shapes),
        out_shape=outs
        + [jax.ShapeDtypeStruct((rows, width), jnp.bfloat16), jax.ShapeDtypeStruct(small.shape[1:], f)],
        in_specs=[ANY] * n + [vm] * 11,
        out_specs=[vm] * (n + 2),
        scratch_shapes=[
            pltpu.VMEM((rows * blocks, 128), f),
            pltpu.VMEM((rows * blocks, 128), f),
            pltpu.VMEM((rows, few, blocks, 128), f),
            pltpu.VMEM((nq, dims, blocks, 128), f),
            pltpu.VMEM((dims + 1, blocks, 128), f),
            pltpu.VMEM((dims, blocks, 128), f),
            pltpu.VMEM((blocks, 128), f),
            pltpu.VMEM(small.shape, f),
            pltpu.VMEM((nq - 1,) + small.shape[1:], f),
            pltpu.VMEM((ng - 1,) + small.shape[1:], f),
            pltpu.SemaphoreType.DMA((nq - 1,)),
            pltpu.SemaphoreType.DMA((nq - 1,)),
            pltpu.SemaphoreType.DMA((nq + ng - 2,)),
            pltpu.SemaphoreType.DMA((nq + ng - 2,)),
            pltpu.SemaphoreType.DMA((n, 2)),
            pltpu.SemaphoreType.DMA((count,)),
            pltpu.SemaphoreType.DMA((count,)),
        ]
        + scratch,
        compiler_params=pltpu.CompilerParams(
            collective_id=collective_id, has_side_effects=True, vmem_limit_bytes=62 << 20
        ),
    )(*parts, gact, x_in, mixed, carry, par, alive, spans, tok, pre, direct, small)
    return [v.reshape(-1, t.shape[-1]) for v, t in zip(result, terms)], result[n], result[n + 1]


def layer_back_kernel(grid, dims, shapes, sizes, *refs):
    n = len(shapes)
    zdim, vdim, fdim = sizes
    wholes, refs = refs[:n], refs[n:]
    (first_term, cot_hbm, ffn_hbm, two_hbm, one_hbm, hpre_hbm, proj_hbm, att_hbm, hin_hbm, value_hbm, probs, active_hbm,
     normed_hbm, tok_hbm, x_hbm, mixed_hbm, carry, par, aff, alive, spans, *refs) = refs
    sums, refs = refs[:n], refs[n:]
    gtok_out, small_out, *refs = refs
    terms, refs = [first_term, *refs[: n - 1]], refs[n - 1 :]
    (gproj, direct, pre, bound, m_all, k_all, row_sums, two_sums, aff_sums, small, seq_in, seg_in,
     sends_b, recv_b, s_send, s_recv, own_sem, load_sem, tile_sem, stage_sem, send, recv, *scratch) = refs
    nq, ng, nc, nz = grid.nq, grid.ng, grid.nc, grid.nz
    rows, width = direct.shape
    blocks = width // 128
    low, f = jnp.bfloat16, jnp.float32
    s = lax.axis_index("seq")
    seq_peer, seg_peer = small_peers(grid)
    meet(seq_peer + seg_peer)
    ready = [1]
    steps = scatter_steps(grid, shapes, terms, sums, scratch, own_sem, Sems(send, recv), lambda: ready[0])
    little = SmallSum(grid, small, small_out, seq_in, seg_in, s_send, s_recv)
    loads = [0]

    def pump(count=1):
        for _ in range(count):
            next(steps, None)

    pump(3)
    dot = functools.partial(jnp.dot, preferred_element_type=f)

    def dot_nt(a, b):
        return lax.dot_general(a, b, (((1,), (1,)), ((), ())), preferred_element_type=f)

    def dot_tn(a, b):
        return lax.dot_general(a, b, (((0,), (0,)), ((), ())), preferred_element_type=f)

    def fetch(src, dst):
        copy = pltpu.make_async_copy(src, dst, load_sem.at[loads[0]])
        loads[0] += 1
        copy.start()
        return copy.wait

    def by_rows(each=32):
        def wrap(some):
            pl.loop(0, rows // each)(lambda i: some(pl.ds(pl.multiple_of(i * each, each), each)))

        return wrap

    def wide(i):
        return shapes[i][-1]

    def tile_shape(i):
        return (2, grid.ny, nc, grid.nx) + shapes[i]

    def depth(i):
        return grid.nx * shapes[i][0] * shapes[i][1]

    def tile(i, tiles, zt):
        return pltpu.make_async_copy(wholes[i].at[:, :, zt], tiles.at[zt % 2], tile_sem.at[zt % 2])

    def begin(i, tiles):
        for zt in range(min(2, nz)):
            tile(i, tiles, zt).start()

    def against(i, tiles, part):
        for zt in range(nz):
            tile(i, tiles, zt).wait()
            total = None
            for g in range(ng):
                term = dot_nt(part(g), tiles[zt % 2, g // nc, g % nc].reshape(depth(i), wide(i)))
                total = term if total is None else total + term
            if zt + 2 < nz:
                tile(i, tiles, zt + 2).start()
            yield slice(zt * depth(i), zt * depth(i) + depth(i)), total

    def grads(i, left, stage, part):
        copies = []
        slots = stage.shape[0]
        for g in range(ng):
            right = part(g)
            for zt in range(nz):
                k = len(copies)
                if k >= slots:
                    copies[k - slots].wait()
                d = depth(i)
                term = dot(left[zt * d : zt * d + d, :], right)
                stage[k % slots] = term.astype(low).reshape(stage.shape[1:])
                copies.append(
                    pltpu.make_async_copy(stage.at[k % slots], terms[i].at[g // nc, g % nc, zt], stage_sem.at[k % slots])
                )
                copies[k].start()
        for copy in copies[-slots:]:
            copy.wait()
        ready[0] = i + 1

    def turned(src, dst):
        for a in range(0, src.shape[1], 256):
            b = min(a + 256, src.shape[1])
            dst[a:b, :] = src[:, a:b].T

    def vm(*shape, kind=low):
        return pltpu.VMEM(shape, kind)

    def stage_of(i, slots=4):
        return pltpu.VMEM((slots, grid.nx) + shapes[i], low)

    def cut(ref, i):
        return lambda g: ref[:, g * wide(i) : (g + 1) * wide(i)]

    first_gate, first_reset, first_cand = width, width + zdim, width + zdim + vdim
    out_i, in_i, att_i, value_i, mix_i = range(5)

    def ffn_back(cot, hold, norm_grad, two):
        wait_cot, wait_two = fetch(cot_hbm, cot), fetch(two_hbm, two)

        def second(pre_act, tiles):
            begin(out_i, tiles)
            each = depth(out_i)
            pre_waits = [fetch(ffn_hbm.at[:, k * each : (k + 1) * each], pre_act.at[k]) for k in range(2)]
            wait_cot()
            for k, (cols, grad) in enumerate(against(out_i, tiles, cut(cot, out_i))):
                pre_waits[k]()
                hold[:, cols] = (grad * silu_slope(pre_act[k % 2])).astype(low)
                if k + 2 < nz:
                    pre_waits.append(fetch(ffn_hbm.at[:, (k + 2) * each : (k + 3) * each], pre_act.at[k % 2]))
            pump()

        pl.run_scoped(second, vm(2, rows, depth(out_i), kind=f), pltpu.VMEM(tile_shape(out_i), low))

        def rest(one, hpre, upd, tok):
            waits = [fetch(one_hbm, one), fetch(hpre_hbm, hpre), fetch(proj_hbm.at[:, 0:width], upd), fetch(tok_hbm, tok)]

            def first(left, stage, tiles):
                begin(in_i, tiles)
                wait_two()
                turned(two, left)
                grads(in_i, left, stage, cut(hold, in_i))
                pump()
                for cols, grad in against(in_i, tiles, cut(hold, in_i)):
                    norm_grad[:, cols] = grad

            pl.run_scoped(first, vm(width, rows), stage_of(in_i), pltpu.VMEM(tile_shape(in_i), low))
            for wait in waits:
                wait()
            two_sums[...] = jnp.zeros_like(two_sums)

            @by_rows(16)
            def _(at):
                v, x, h, c = one[at, :], tok[at, :].astype(f), hpre[at, :], cot[at, :].astype(f)
                gain = jnp.concatenate([par[4 * dims + 2, b : b + 1, :] for b in range(blocks)], axis=1)
                r = lax.rsqrt(jnp.mean(v * v, axis=1, keepdims=True) + epsilon)
                gy = norm_grad[at, :]
                scaled = gy * gain
                pull = r * r * jnp.mean(scaled * v, axis=1, keepdims=True)
                grad_one = c + r * (scaled - v * pull)
                two_sums[...] += jnp.sum(gy * (v * r), axis=0, keepdims=True)
                u = jax.nn.sigmoid(upd[at, :])
                sig = jax.nn.sigmoid(h)
                direct[at, :] = grad_one * (1.0 - u)
                gproj[at, first_cand:] = (grad_one * u * (sig * (1.0 + h * (1.0 - sig)))).astype(low)
                gproj[at, 0:width] = (grad_one * (h * sig - x) * (u * (1.0 - u))).astype(low)

        pl.run_scoped(
            rest, vm(rows, width, kind=f), vm(rows, width, kind=f), vm(rows, width, kind=f), vm(rows, width)
        )

    pl.run_scoped(ffn_back, vm(rows, width), vm(rows, fdim), vm(rows, width, kind=f), vm(rows, width))
    pump()

    def attention_back(grad_hin, att, gate, shared_pre, value_pre):
        waits = [
            fetch(att_hbm, att),
            fetch(proj_hbm.at[:, first_reset:first_cand], gate),
            fetch(proj_hbm.at[:, first_gate:first_reset], shared_pre),
            fetch(value_hbm, value_pre),
        ]

        def out_back(hin, left, stage, tiles):
            wait_hin = fetch(hin_hbm, hin)
            begin(att_i, tiles)
            wait_hin()
            turned(hin, left)

            def part(g):
                return gproj[:, first_cand + g * wide(att_i) : first_cand + (g + 1) * wide(att_i)]

            grads(att_i, left, stage, part)
            pump()
            for cols, grad in against(att_i, tiles, part):
                grad_hin[:, cols] = grad

        pl.run_scoped(out_back, vm(rows, vdim), vm(vdim, rows), stage_of(att_i), pltpu.VMEM(tile_shape(att_i), low))

        def inner(grad_pre, normed, value_tiles):
            wait_normed = fetch(normed_hbm, normed)
            begin(value_i, value_tiles)

            def blocks_back(grad_att, values):
                for wait in waits:
                    wait()

                @by_rows(16)
                def _(at):
                    v, g, p = gate[at, :], grad_hin[at, :], value_pre[at, :]
                    sig = jax.nn.sigmoid(v)
                    grad_att[at, :] = (g * (v * sig)).astype(low)
                    gproj[at, first_reset:first_cand] = (g * att[at, :] * (sig * (1.0 + v * (1.0 - sig)))).astype(low)
                    values[at, :] = (p * jax.nn.sigmoid(p)).astype(low)

                aff_total = [jnp.zeros((1, zdim), f)] * 4
                scale_q = zdim**-0.5
                for r in range(rows // STRETCH):
                    at = slice(r * STRETCH, r * STRETCH + STRETCH)
                    v = shared_pre[at, :]
                    shared = v * jax.nn.sigmoid(v)
                    query = (scale_q * (shared * aff[0:1] + aff[1:2])).astype(low)
                    key = (shared * aff[2:3] + aff[3:4]).astype(low)
                    prob, ga = probs[at, :], grad_att[at, :]
                    grad_prob = dot_nt(ga, values[at, :])
                    weighted = jnp.sum(prob * grad_prob, axis=1, keepdims=True)
                    grad_score = (prob * (grad_prob - weighted)).astype(low)
                    grad_query = dot(grad_score, key) * scale_q
                    grad_key = dot_tn(grad_score, query)
                    grad_shared = grad_query * aff[0:1] + grad_key * aff[2:3]
                    gproj[at, first_gate:first_reset] = (grad_shared * silu_slope(v)).astype(low)
                    for k, t in enumerate([grad_query * shared, grad_query, grad_key * shared, grad_key]):
                        aff_total[k] = aff_total[k] + jnp.sum(t, axis=0, keepdims=True)
                    grad_hin[at, :] = dot_tn(prob.astype(low), ga)
                for k in range(4):
                    aff_sums[k : k + 1, :] = aff_total[k]

                @by_rows(16)
                def _(at):
                    grad_pre[at, :] = (grad_hin[at, :] * silu_slope(value_pre[at, :])).astype(low)

            pl.run_scoped(blocks_back, vm(rows, vdim), vm(rows, vdim))
            pump()

            def value_back(left, stage):
                wait_normed()
                turned(normed, left)
                grads(value_i, left, stage, cut(grad_pre, value_i))
                for cols, grad in against(value_i, value_tiles, cut(grad_pre, value_i)):
                    pre[:, cols] = grad

            pl.run_scoped(value_back, vm(width, rows), stage_of(value_i))

        pl.run_scoped(inner, vm(rows, vdim), vm(rows, width), pltpu.VMEM(tile_shape(value_i), low))

    pl.run_scoped(
        attention_back, vm(rows, vdim, kind=f), vm(rows, vdim, kind=f), vm(rows, vdim, kind=f), vm(rows, zdim, kind=f),
        vm(rows, vdim, kind=f)
    )
    pump()

    def mix_back(g_rows, gin_rows, x_in, mixed, tok):
        waits = [fetch(x_hbm, x_in), fetch(mixed_hbm, mixed), fetch(tok_hbm, tok)]

        def mix_weight_back(active, left, stage, tiles):
            wait_active = fetch(active_hbm, active)
            begin(mix_i, tiles)
            wait_active()
            turned(active, left)
            grads(mix_i, left, stage, cut(gproj, mix_i))
            pump()
            for cols, grad in against(mix_i, tiles, cut(gproj, mix_i)):
                grad = grad.astype(low).astype(f)
                for b in range(cols.start // 128, cols.stop // 128):
                    lane = b * 128 - cols.start
                    g_rows[pl.ds(b, rows, stride=blocks), :] = grad[:, lane : lane + 128]

        pl.run_scoped(
            mix_weight_back, vm(rows, width), vm(width, rows), stage_of(mix_i), pltpu.VMEM(tile_shape(mix_i), low)
        )

        for wait in waits:
            wait()

        def scan(before):
            scan_back(
                grid, dims, g_rows, x_in, mixed, carry, par, alive, spans, gin_rows, before, bound, sends_b, recv_b,
                m_all, k_all, seq_peer, s, pump
            )

        pl.run_scoped(scan, vm(rows, 4, blocks, 128, kind=f))
        norm_back(par, dims, tok, pre, direct, gin_rows, gtok_out, row_sums)

    pl.run_scoped(
        mix_back, vm(rows * blocks, 128, kind=f), vm(rows * blocks, 128, kind=f), vm(rows * blocks, 128, kind=f),
        vm(rows * blocks, 128, kind=f), vm(rows, width)
    )
    small[...] = jnp.zeros_like(small)
    fill_small(grid, dims, small, m_all, k_all, row_sums)
    for e in range(nq):
        b = block_of(e, nq, blocks)
        small[e, 2 * dims + 2 : 2 * dims + 3] = two_sums[:, b * 128 : b * 128 + 128]
        small[e, 2 * dims + 3 : 2 * dims + 7] = aff_sums[...]
    little.start()
    pump()
    little.middle()
    for _ in steps:
        pass
    little.end()


def layer_backward(grid, wholes, cuts, kept, probs, carry, par, aff, alive, spans, sizes, collective_id):
    nq, ng = grid.nq, grid.ng
    dims, blocks = carry.shape[0], carry.shape[1]
    zdim, vdim, fdim = sizes
    width = blocks * 128
    rows = probs.shape[0]
    f = jnp.float32
    vm = pl.BlockSpec(memory_space=pltpu.VMEM)
    n = len(wholes)
    like = [jax.ShapeDtypeStruct((ng, w.size // ng // w.shape[-1], w.shape[-1]), w.dtype) for w in wholes]
    shapes, outs, scratch, count = scatter_plan(grid, like, cuts)
    whole_shapes = [jax.ShapeDtypeStruct(w.shape[:4] + s, w.dtype) for w, s in zip(wholes, shapes)]
    low = [w.reshape(v.shape) for w, v in zip(wholes, whole_shapes)]
    small_shape = (-(-(2 * dims + 7) // 8) * 8, 128)
    result = pl.pallas_call(
        functools.partial(layer_back_kernel, grid, dims, shapes, sizes),
        out_shape=outs
        + [jax.ShapeDtypeStruct((rows, width), jnp.bfloat16), jax.ShapeDtypeStruct(small_shape, f)]
        + whole_shapes[1:],
        in_specs=[ANY] * n + [ANY] * 10 + [vm] + [ANY] * 5 + [vm] * 5,
        out_specs=[vm] * (n + 2) + [ANY] * (n - 1),
        scratch_shapes=[
            pltpu.VMEM((rows, width * 2 + zdim + vdim), jnp.bfloat16),
            pltpu.VMEM((rows, width), f),
            pltpu.VMEM((rows, width), f),
            pltpu.VMEM((nq, dims, blocks, 128), f),
            pltpu.VMEM((dims + 1, blocks, 128), f),
            pltpu.VMEM((dims, blocks, 128), f),
            pltpu.VMEM((blocks, 128), f),
            pltpu.VMEM((1, width), f),
            pltpu.VMEM((4, zdim), f),
            pltpu.VMEM((nq,) + small_shape, f),
            pltpu.VMEM((nq - 1,) + small_shape, f),
            pltpu.VMEM((ng - 1,) + small_shape, f),
            pltpu.SemaphoreType.DMA((nq - 1,)),
            pltpu.SemaphoreType.DMA((nq - 1,)),
            pltpu.SemaphoreType.DMA((nq + ng - 2,)),
            pltpu.SemaphoreType.DMA((nq + ng - 2,)),
            pltpu.SemaphoreType.DMA((n, 2)),
            pltpu.SemaphoreType.DMA((24,)),
            pltpu.SemaphoreType.DMA((2,)),
            pltpu.SemaphoreType.DMA((4,)),
            pltpu.SemaphoreType.DMA((count,)),
            pltpu.SemaphoreType.DMA((count,)),
        ]
        + scratch,
        compiler_params=pltpu.CompilerParams(
            collective_id=collective_id, has_side_effects=True, vmem_limit_bytes=63 << 20
        ),
    )(*low, *kept[:10], probs, *kept[10:], carry, par, aff, alive, spans)
    return [v.reshape(-1, t.shape[-1]) for v, t in zip(result, like)], result[n], result[n + 1]


def rms_forward(values, gain):
    inverse = lax.rsqrt(jnp.mean(values * values, axis=-1, keepdims=True) + epsilon)
    return (values * inverse * gain, inverse)


def rms_backward(grad_out, values, inverse, gain):
    scaled = grad_out * gain
    projection = jnp.mean(scaled * values, axis=-1, keepdims=True)
    grad_in = inverse * (scaled - values * inverse * inverse * projection)
    return (grad_in, jnp.sum(grad_out * values * inverse, axis=0))


def silu_slope(values):
    sigma_v = jax.nn.sigmoid(values)
    return sigma_v * (1.0 + values * (1.0 - sigma_v))


def times(left, pieces):
    return jnp.concatenate(
        [jnp.dot(left, pieces[i], preferred_element_type=jnp.float32) for i in range(pieces.shape[0])], axis=1
    )


def against(left, pieces):
    n = pieces.shape[2]
    return sum(
        lax.dot_general(
            left[:, i * n : i * n + n], pieces[i], (((1,), (1,)), ((), ())), preferred_element_type=jnp.float32
        )
        for i in range(pieces.shape[0])
    )


def over_rows(left, right, count):
    n = right.shape[1] // count
    return jnp.stack(
        [
            lax.dot_general(
                left, right[:, i * n : i * n + n], (((0,), (0,)), ((), ())), preferred_element_type=jnp.float32
            ).astype(jnp.bfloat16)
            for i in range(count)
        ]
    )


def masked_scores(query_blk, key_blk, allowed):
    raw_scores = jnp.einsum("cid,cjd->cij", query_blk, key_blk, preferred_element_type=jnp.float32)
    return jnp.where(allowed, raw_scores, -1e30)


def backward_apart(grid, cotangent, tokens_low, forward, weights, alive, spans, sizes):
    (carry, par, affine, probs, _, normed_b, active, x_rows, mixed_rows, out_one, normed_two_b,
     projected, value_pre, attended, hidden_in, hidden_pre, ffn_hidden, ffn_act) = forward
    ffn_hidden = ffn_hidden.astype(jnp.float32)
    token_count, model_width = tokens_low.shape
    nq, ng = grid.nq, grid.ng
    dims, blocks = carry.shape[0], carry.shape[1]
    zdim, vdim, _ = sizes
    block_count = token_count // STRETCH
    tokens_flat = tokens_low.astype(jnp.float32)
    mix_full, value_full, out_full, ffn_in_full, ffn_out_full = (w.reshape(ng, -1, w.shape[-1]) for w in weights)
    gain_two = par[4 * dims + 2].reshape(-1)
    update = jax.nn.sigmoid(projected[:, :model_width])
    gate_pre = projected[:, model_width : model_width + zdim + vdim]
    gate_rows = jax.nn.silu(gate_pre)
    shared = gate_rows[:, :zdim]
    reset_gate = gate_rows[:, zdim:]
    values_b = jax.nn.silu(value_pre).astype(jnp.bfloat16)
    scale_q = zdim ** (-0.5)
    query_b = (scale_q * (shared * affine[0] + affine[1])).astype(jnp.bfloat16)
    key_b = (shared * affine[2] + affine[3]).astype(jnp.bfloat16)
    query_blk = query_b.reshape(block_count, STRETCH, zdim)
    key_blk = key_b.reshape(block_count, STRETCH, zdim)
    value_blk = values_b.reshape(block_count, STRETCH, vdim)
    probs = probs.reshape(block_count, STRETCH, STRETCH)
    probs_b = probs.astype(jnp.bfloat16)
    hidden_act = jax.nn.silu(hidden_pre)
    inverse_two = lax.rsqrt(jnp.mean(out_one * out_one, axis=-1, keepdims=True) + epsilon)

    grad_y_b = cotangent
    grad_ffn_out = over_rows(ffn_act, grad_y_b, ng)
    grad_act = against(grad_y_b, ffn_out_full)
    grad_hidden_b = (grad_act * silu_slope(ffn_hidden)).astype(jnp.bfloat16)
    grad_ffn_in = over_rows(normed_two_b, grad_hidden_b, ng)
    grad_normed_two = against(grad_hidden_b, ffn_in_full)
    grad_norm_two, grad_gain_two = rms_backward(grad_normed_two, out_one, inverse_two, gain_two)
    grad_out_one = grad_y_b.astype(jnp.float32) + grad_norm_two
    grad_update = grad_out_one * (hidden_act - tokens_flat)
    grad_tokens_flat = grad_out_one * (1.0 - update)
    grad_hpre_b = (grad_out_one * update * silu_slope(hidden_pre)).astype(jnp.bfloat16)
    grad_out_weight = over_rows(hidden_in, grad_hpre_b, ng)
    grad_hidden_in = against(grad_hpre_b, out_full)
    grad_att_b = (grad_hidden_in * reset_gate).astype(jnp.bfloat16)
    grad_reset = grad_hidden_in * attended
    grad_att_blk = grad_att_b.reshape(block_count, STRETCH, vdim)
    grad_probs = jnp.einsum("civ,cjv->cij", grad_att_blk, value_blk, preferred_element_type=jnp.float32)
    weighted = jnp.sum(probs * grad_probs, axis=2, keepdims=True)
    grad_scores_b = (probs * (grad_probs - weighted)).astype(jnp.bfloat16)
    grad_query = jnp.einsum("cij,cjd->cid", grad_scores_b, key_blk, preferred_element_type=jnp.float32).reshape(
        token_count, zdim
    )
    grad_key = jnp.einsum("cij,cid->cjd", grad_scores_b, query_blk, preferred_element_type=jnp.float32).reshape(
        token_count, zdim
    )
    grad_values = jnp.einsum("cij,civ->cjv", probs_b, grad_att_blk, preferred_element_type=jnp.float32).reshape(
        token_count, vdim
    )
    grad_qs = grad_query * scale_q
    grad_shared = grad_qs * affine[0] + grad_key * affine[2]
    grad_affine = jnp.stack(
        [
            jnp.sum(grad_qs * shared, axis=0),
            jnp.sum(grad_qs, axis=0),
            jnp.sum(grad_key * shared, axis=0),
            jnp.sum(grad_key, axis=0),
        ]
    )
    grad_gate_pre = jnp.concatenate([grad_shared, grad_reset], axis=1) * silu_slope(gate_pre)
    grad_upre = grad_update * update * (1.0 - update)
    grad_proj_b = jnp.concatenate(
        [grad_upre.astype(jnp.bfloat16), grad_gate_pre.astype(jnp.bfloat16), grad_hpre_b], axis=1
    )
    grad_mix = over_rows(active, grad_proj_b, ng)
    grad_active_b = against(grad_proj_b, mix_full).astype(jnp.bfloat16)
    grad_vpre_b = (grad_values * silu_slope(value_pre)).astype(jnp.bfloat16)
    grad_value = over_rows(normed_b, grad_vpre_b, ng)
    grad_normed = against(grad_vpre_b, value_full)

    small = jnp.concatenate(
        [jnp.zeros((blocks, 2 * dims + 2, 128), jnp.float32), grad_gain_two.reshape(blocks, 1, 128)], axis=1
    )
    if nq != blocks:
        small = jnp.take(small, np.arange(nq) * blocks // nq, axis=0)
    small = jnp.concatenate([small, jnp.broadcast_to(grad_affine[None], (nq, 4, 128))], axis=1)
    small = jnp.pad(small, ((0, 0), (0, -small.shape[1] % 8), (0, 0)))
    return mix_backward(
        grid, [grad_ffn_out, grad_ffn_in, grad_out_weight, grad_value, grad_mix], SCATTER_CUTS, grad_active_b, x_rows,
        mixed_rows, carry, par, alive, spans, tokens_low, grad_normed, grad_tokens_flat, small, 1
    )


def body(
    tokens,
    starts,
    norm_gain,
    ema_delta,
    ema_alpha,
    ema_beta,
    ema_eta,
    ema_omega,
    mix_weight,
    value_weight,
    qk_affine,
    out_weight,
    ffn_gain,
    ffn_in,
    ffn_out,
    cotangent,
):
    seg_count, row_count, model_width = tokens.shape
    nq, ng = lax.axis_size("seq"), lax.axis_size("seg")
    grid = Grid(nq, ng)
    seq_index, seg_index = lax.axis_index("seq"), lax.axis_index("seg")
    seq_length = row_count * nq
    dims = ema_delta.shape[1]
    zdim = qk_affine.shape[0] * nq * ng // 4
    vdim = value_weight.shape[1] * ng
    token_count = seg_count * row_count
    blocks = model_width // 128

    index = seq_index * ng + seg_index
    mine, part = norm_gain.shape[0], qk_affine.shape[0]
    own_params = [
        ema_delta.T, ema_alpha.T, ema_beta.T, ema_eta.T, norm_gain[None], ema_omega[None], ffn_gain[None], qk_affine[None]
    ]
    cotangent_low = cotangent.reshape(token_count, model_width)
    shards = [mix_weight, value_weight, out_weight, ffn_in, ffn_out]
    apart = min(w.shape[1] for w in shards) < 128
    out_term = None
    if not apart:
        k, n = ffn_out.shape
        q = max(1, min(SCATTER_CUTS[0], k // 32))
        out_term = (2 * q, k // (2 * q), n)
    tokens_low = tokens.reshape(token_count, model_width)
    weights, term, forward = mix_forward(
        grid, shards, GATHER_CUTS, tokens_low, own_params, starts, cotangent_low, dims, out_term, 0
    )
    alive, spans, *forward = forward
    (carry, par, affine, probs, result, normed_b, active, x_rows, mixed_rows, out_one, normed_two_b,
     projected, value_pre, attended, hidden_in, hidden_pre, ffn_hidden, ffn_act) = forward
    sizes = (zdim, vdim, ffn_act.shape[1])
    if apart:
        result_back = backward_apart(grid, cotangent_low, tokens_low, forward, weights, alive, spans, sizes)
    else:
        kept = [term[0], cotangent_low, ffn_hidden, normed_two_b, out_one, hidden_pre, projected, attended, hidden_in,
                value_pre, active, normed_b, tokens_low, x_rows, mixed_rows]
        order = [weights[4], weights[3], weights[2], weights[1], weights[0]]
        result_back = layer_backward(
            grid, order, SCATTER_CUTS, kept, probs, carry, par, affine, alive, spans, sizes, 1
        )
    (g_ffn_out, g_ffn_in, g_out, g_value, g_mix), grad_tokens, sums = result_back
    return (
        result.reshape(seg_count, row_count, model_width),
        grad_tokens.reshape(seg_count, row_count, model_width),
        *small_outputs(sums, index, dims, ema_delta, ema_alpha, ema_beta, ema_eta, mine, part, g_mix, g_value, g_out, g_ffn_in, g_ffn_out),
    )


def small_outputs(sums, index, dims, ema_delta, ema_alpha, ema_beta, ema_eta, mine, part, g_mix, g_value, g_out, g_ffn_in, g_ffn_out):
    own = lax.dynamic_slice_in_dim(sums, lax.rem(index * mine, 128), mine, 1)
    m_sum, k_sum = own[:dims].T, own[dims : 2 * dims].T
    vectors = own[2 * dims : 2 * dims + 3]
    delta, alpha, beta, eta = (v.astype(jnp.float32) for v in (ema_delta, ema_alpha, ema_beta, ema_eta))
    damping, decay = jax.nn.sigmoid(delta), jax.nn.sigmoid(alpha)
    g_keep = damping * beta * eta * k_sum
    grad_eta = damping * beta * m_sum
    grad_beta = damping * eta * m_sum
    grad_alpha = -g_keep * damping * decay * (1.0 - decay)
    grad_delta = (beta * eta * m_sum - g_keep * decay) * damping * (1.0 - damping)
    grad_affine = lax.dynamic_slice(
        sums, (2 * dims + 3 + index * part // 128, lax.rem(index * part, 128)), (1, part)
    ).reshape(-1)
    return (vectors[1], grad_delta, grad_alpha, grad_beta, grad_eta, vectors[0],
            g_mix, g_value, grad_affine, g_out, vectors[2], g_ffn_in, g_ffn_out)


def solution(mesh):
    placed = (
        P("seg", "seq", None),
        P("seg", None),
        P(("seq", "seg")),
        P(("seq", "seg"), None),
        P(("seq", "seg"), None),
        P(("seq", "seg"), None),
        P(("seq", "seg"), None),
        P(("seq", "seg")),
        P("seq", "seg"),
        P("seq", "seg"),
        P(("seq", "seg")),
        P("seq", "seg"),
        P(("seq", "seg")),
        P("seq", "seg"),
        P("seq", "seg"),
        P("seg", "seq", None),
    )
    return jax.shard_map(
        body,
        mesh=mesh,
        in_specs=placed,
        out_specs=(P("seg", "seq", None),) * 2 + placed[2:15],
        check_vma=False,
    )
```

```python
import functools
import math

import jax
import jax.numpy as jnp
import numpy as np
from jax import lax
from jax.experimental import pallas as pl
from jax.experimental.pallas import tpu as pltpu
from jax.sharding import PartitionSpec as P

STRETCH = 128
epsilon = 1e-05
GATHER_LAG = (1, 1, 1, 1, 1)
SCATTER_LAG = (0, 1, 1, 1, 1)
GATHER_CUTS = (4, 2, 2, 4, 4)
SCATTER_CUTS = (4, 4, 2, 2, 4)

MESH = pl.DeviceIdType.MESH
ANY = pl.BlockSpec(memory_space=pl.ANY)


class Grid:
    def __init__(self, nq, ng):
        self.nq, self.ng = nq, ng
        self.nz = math.gcd(nq, 4)
        self.nx = nq // self.nz
        self.nc = math.gcd(ng, 2)
        self.ny = ng // self.nc

    def here(self):
        s, g = lax.axis_index("seq"), lax.axis_index("seg")
        return s // self.nx, lax.rem(s, self.nx), g // self.nc, lax.rem(g, self.nc)

    def peer(self, axis, d):
        z, x, y, c = self.here()
        if axis == "z":
            z = lax.rem(z + d, self.nz)
        if axis == "x":
            x = lax.rem(x + d, self.nx)
        if axis == "y":
            y = lax.rem(y + d, self.ny)
        if axis == "c":
            c = lax.rem(c + d, self.nc)
        return z, x, y, c

    def size(self, axis):
        return {"z": self.nz, "x": self.nx, "y": self.ny, "c": self.nc}[axis]

    def device(self, place):
        z, x, y, c = place
        return {"seq": z * self.nx + x, "seg": y * self.nc + c}

    def peers(self, axes):
        return [self.peer(a, d) for a in axes for d in range(1, self.size(a))]


def enter(grid, peers):
    barrier = pltpu.get_barrier_semaphore()
    for place in peers:
        pl.semaphore_signal(barrier, inc=1, device_id=grid.device(place), device_id_type=MESH)
    pl.semaphore_wait(barrier, len(peers))


class Sems:
    def __init__(self, send, recv):
        self.send, self.recv, self.used = send, recv, 0

    def take_index(self):
        self.used += 1
        return self.used - 1

    def take(self):
        i = self.take_index()
        return self.send.at[i], self.recv.at[i]


def gather_steps(grid, shapes, shards, wholes, own_sem, sems):
    n = len(shapes)
    z, x, y, c = grid.here()
    pending = []

    def push(src, dst, axis, d, arrives):
        s, r = sems.take()
        device = grid.device(grid.peer(axis, d))
        copy = pltpu.make_async_remote_copy(src, dst, s, r, device_id=device, device_id_type=MESH)
        copy.start()
        pending.append(copy)
        there = pltpu.make_async_remote_copy(arrives, arrives, s, r, device_id=device, device_id_type=MESH)
        return there.wait_recv

    def back(axis, d):
        return dict(zip("zxyc", grid.peer(axis, grid.size(axis) - d)))[axis]

    owns = []
    chunks = [(i, q) for i in range(n) for q in range(shapes[i][0] // 2)]
    core_waits = {}

    def core(k, view):
        core_waits.setdefault(k, []).extend(
            push(view(c), view(c), "c", d, view(back("c", d))) for d in range(1, grid.nc)
        )

    def stage_z(k, i, h):
        w = wholes[i]
        return [
            push(shards[i].at[h], w.at[y, c, z, x, h], "z", d, w.at[y, c, back("z", d), x, h])
            for d in range(1, grid.nz)
        ]

    def stage_two(k, i, h):
        w = wholes[i]
        src = w.at[y, c, :, x, h]
        if h % 2 == 0:
            waits = [push(src, src, "x", d, w.at[y, c, :, back("x", d), h]) for d in range(1, grid.nx)]
        else:
            waits = [push(src, src, "y", d, w.at[back("y", d), c, :, x, h]) for d in range(1, grid.ny)]
        core(k, lambda cc: w.at[y, cc, :, x, h])
        return waits

    def stage_three(k, i, h):
        w = wholes[i]
        if h % 2 == 0:
            src = w.at[y, c, :, :, h]
            waits = [push(src, src, "y", d, w.at[back("y", d), c, :, :, h]) for d in range(1, grid.ny)]
            for d in range(1, grid.nx):
                core(k, lambda cc: w.at[y, cc, :, back("x", d), h])
            return waits
        src = w.at[:, c, :, x, h]
        waits = [push(src, src, "x", d, w.at[:, c, :, back("x", d), h]) for d in range(1, grid.nx)]
        for d in range(1, grid.ny):
            core(k, lambda cc: w.at[back("y", d), cc, :, x, h])
        return waits

    def stage_last(k, i, h):
        w = wholes[i]
        if h % 2 == 0:
            for d in range(1, grid.ny):
                core(k, lambda cc: w.at[back("y", d), cc, :, :, h])
        else:
            for d in range(1, grid.nx):
                core(k, lambda cc: w.at[:, cc, :, back("x", d), h])

    def finish(waits):
        for wait in waits:
            wait()

    got = {}
    total = len(chunks)
    at = [0] * 5

    def advance(j):
        k = at[j]
        i, q = chunks[k]
        if j == 1 and q == 0:
            owns[i].wait()
        if j == 4:
            finish(core_waits[k])
            at[j] += 1
            return [(i, q), i] if q + 1 == shapes[i][0] // 2 else [(i, q)]
        for h in (0, 1):
            if j:
                finish(got[k, h])
            got[k, h] = (stage_z, stage_two, stage_three, stage_last)[j](k, i, 2 * q + h)
        at[j] += 1
        return []

    advance(0)
    yield []
    for i in range(n):
        copy = pltpu.make_async_copy(shards[i], wholes[i].at[y, c, z, x], own_sem.at[i])
        copy.start()
        owns.append(copy)
    while at[4] < total:
        before = list(at)
        done = []
        for j in (1, 0, 2, 3, 4):
            if j == 0:
                go = at[0] < total and at[0] - at[1] < GATHER_LAG[0]
            else:
                go = at[j] < before[j - 1] and (before[j - 1] == total or before[j - 1] - at[j] >= GATHER_LAG[j])
            if go:
                done += advance(j)
        if at[4] == total:
            for copy in pending:
                copy.wait_send()
        yield done


def gather_plan(grid, shards, cuts):
    shapes, args, outs = [], [], []
    for w, q in zip(shards, cuts):
        k, n = w.shape
        q = max(1, min(q, k // 32))
        shapes.append((2 * q, k // (2 * q), n))
        args.append(w.reshape(shapes[-1]))
        outs.append(jax.ShapeDtypeStruct((grid.ny, grid.nc, grid.nz, grid.nx) + shapes[-1], w.dtype))
    per = (grid.nz - 1) + (grid.nx - 1) + (grid.ny - 1) + (grid.nc - 1) * (grid.nx + grid.ny)
    count = sum(s[0] for s in shapes) * per
    return shapes, args, outs, count


def scatter_steps(grid, shapes, terms, sums, scratch, own_sem, sems, ready=None):
    n = len(shapes)
    nz, nx, ny, nc = grid.nz, grid.nx, grid.ny, grid.nc
    own = [scratch[7 * i] for i in range(n)]
    one = [scratch[7 * i + 1] for i in range(n)]
    two_a = [scratch[7 * i + 2] for i in range(n)]
    two_b = [scratch[7 * i + 3] for i in range(n)]
    three_a = [scratch[7 * i + 4] for i in range(n)]
    three_b = [scratch[7 * i + 5] for i in range(n)]
    four = [scratch[7 * i + 6] for i in range(n)]
    z, x, y, c = grid.here()
    pending = []
    around = {(axis, d): grid.peer(axis, d) for axis in "zxyc" for d in range(1, grid.size(axis))}
    devices = {key: grid.device(place) for key, place in around.items()}

    def push(ends, axis, d):
        k = sems.take_index()

        def copy():
            return pltpu.make_async_remote_copy(
                *ends(), sems.send.at[k], sems.recv.at[k], device_id=devices[axis, d], device_id_type=MESH
            )

        copy().start()
        pending.append(lambda: copy().wait_send())
        return lambda: copy().wait_recv()

    def to(axis, d):
        return dict(zip("zxyc", around[axis, d]))[axis]

    def finish(waits):
        for wait in waits:
            wait()

    assert nc == 2

    def stage_one(i, q, h):
        return [push(lambda: (terms[i].at[:, to("c", 1), :, :, 2 * q + h], one[i].at[q, h]), "c", 1)]

    def load_own(i, q, h):
        def load():
            return pltpu.make_async_copy(terms[i].at[:, c, :, :, 2 * q + h], own[i].at[h], own_sem.at[i, h])

        load().start()
        return [lambda: load().wait()]

    def stage_two(i, q, h):
        mine = one[i].at[q, h]

        @pl.loop(0, ny * nz)
        def _(ab):
            a, b = ab // nz, lax.rem(ab, nz)
            for e in range(nx):
                mine[a, b, e] += own[i][h, a, b, e]

        if h == 0:
            return [
                push(lambda d=d: (one[i].at[q, h, to("y", d)], two_a[i].at[q, d - 1]), "y", d) for d in range(1, ny)
            ]
        return [
            push(lambda d=d: (one[i].at[q, h, :, :, to("x", d)], two_b[i].at[q, d - 1]), "x", d) for d in range(1, nx)
        ]

    def stage_three(i, q, h):
        mine = one[i].at[q, h]
        if h == 0:

            @pl.loop(0, nz)
            def _(b):
                for e in range(nx):
                    total = mine[y, b, e]
                    for d in range(ny - 1):
                        total += two_a[i][q, d, b, e]
                    mine[y, b, e] = total

            return [
                push(lambda d=d: (one[i].at[q, h, y, :, to("x", d)], three_a[i].at[q, d - 1]), "x", d)
                for d in range(1, nx)
            ]

        @pl.loop(0, nz)
        def _(b):
            for a in range(ny):
                total = mine[a, b, x]
                for d in range(nx - 1):
                    total += two_b[i][q, d, a, b]
                mine[a, b, x] = total

        return [
            push(lambda d=d: (one[i].at[q, h, to("y", d), :, x], three_b[i].at[q, d - 1]), "y", d)
            for d in range(1, ny)
        ]

    def stage_four(i, q, h):
        mine = one[i].at[q, h]
        came = three_a[i] if h == 0 else three_b[i]

        @pl.loop(0, nz)
        def _(b):
            total = mine[y, b, x]
            for d in range((nx if h == 0 else ny) - 1):
                total += came[q, d, b]
            mine[y, b, x] = total

        return [
            push(lambda d=d: (one[i].at[q, h, y, to("z", d), x], four[i].at[q, h, d - 1]), "z", d)
            for d in range(1, nz)
        ]

    def stage_last(i, q, h):
        total = one[i][q, h, y, z, x].astype(jnp.float32)
        for d in range(nz - 1):
            total += four[i][q, h, d].astype(jnp.float32)
        sums[i][2 * q + h] = total

    stages = [stage_one, stage_two, stage_three, stage_four, stage_last]
    chunks = [(i, q) for i in range(n) for q in range(shapes[i][0] // 2)]
    waits = {}
    total = len(chunks)
    at = [0] * len(stages)
    yield
    while at[-1] < total:
        there = total if ready is None else sum(1 for i, q in chunks if i < ready())
        before = [there] + at[:-1]
        fresh = None
        for j, stage in enumerate(stages):
            lag = SCATTER_LAG[j]
            if at[j] < before[j] and (before[j] == total or j == 0 or before[j] - at[j] >= lag):
                i, q = chunks[at[j]]
                for h in (0, 1):
                    if j:
                        finish(waits[i, q, h])
                    waits[i, q, h] = stage(i, q, h)
                if j == 0:
                    fresh = i, q
                at[j] += 1
            if j == 1 and fresh:
                for h in (0, 1):
                    waits[fresh[0], fresh[1], h] += load_own(*fresh, h)
        if at[-1] == total:
            finish(pending)
        yield


class SmallSum:
    def __init__(self, grid, small, total, seq_in, seg_in, send, recv):
        self.grid, self.small, self.total = grid, small, total
        self.seq_in, self.seg_in, self.send, self.recv = seq_in, seg_in, send, recv
        self.seq_peer, self.seg_peer = small_peers(grid)
        self.copies = []

    def push(self, src, dst, device):
        i = len(self.copies)
        copy = pltpu.make_async_remote_copy(
            src, dst, self.send.at[i], self.recv.at[i], device_id=device, device_id_type=MESH
        )
        copy.start()
        self.copies.append(copy)

    def start(self):
        nq, sq = self.grid.nq, lax.axis_index("seq")
        for d in range(1, nq):
            self.push(self.small.at[lax.rem(sq + d, nq)], self.seq_in.at[d - 1], self.seq_peer[d - 1])

    def middle(self):
        nq, ng = self.grid.nq, self.grid.ng
        total = self.small[lax.axis_index("seq")]
        for d in range(1, nq):
            self.copies[d - 1].wait_recv()
            total += self.seq_in[d - 1]
        self.total[...] = total
        for d in range(1, ng):
            self.push(self.total, self.seg_in.at[d - 1], self.seg_peer[d - 1])

    def end(self):
        nq, ng = self.grid.nq, self.grid.ng
        total = self.total[...]
        for d in range(1, ng):
            self.copies[nq + d - 2].wait_recv()
            total += self.seg_in[d - 1]
        for copy in self.copies:
            copy.wait_send()
        self.total[...] = total


def small_peers(grid):
    nq, ng = grid.nq, grid.ng
    s, g = lax.axis_index("seq"), lax.axis_index("seg")
    return (
        [{"seq": lax.rem(s + d, nq), "seg": g} for d in range(1, nq)],
        [{"seq": s, "seg": lax.rem(g + d, ng)} for d in range(1, ng)],
    )


def meet(peers):
    barrier = pltpu.get_barrier_semaphore()
    for place in peers:
        pl.semaphore_signal(barrier, inc=1, device_id=place, device_id_type=MESH)
    pl.semaphore_wait(barrier, len(peers))


def scatter_plan(grid, terms, cuts):
    nz, nx, ny = grid.nz, grid.nx, grid.ny
    shapes, outs, scratch = [], [], []
    for t, q in zip(terms, cuts):
        _, rows, n = t.shape
        if n < 128:
            rows, n = rows * n // 128, 128
        k = rows // grid.nq
        q = max(1, min(q, k // 32))
        kh = k // (2 * q)
        shapes.append((2 * q, kh, n))
        outs.append(jax.ShapeDtypeStruct((2 * q, kh, n), jnp.float32))
        b = t.dtype
        scratch += [
            pltpu.VMEM((2, ny, nz, nx, kh, n), b),
            pltpu.VMEM((q, 2, ny, nz, nx, kh, n), b),
            pltpu.VMEM((q, max(ny - 1, 1), nz, nx, kh, n), b),
            pltpu.VMEM((q, max(nx - 1, 1), ny, nz, kh, n), b),
            pltpu.VMEM((q, max(nx - 1, 1), nz, kh, n), b),
            pltpu.VMEM((q, max(ny - 1, 1), nz, kh, n), b),
            pltpu.VMEM((q, 2, max(nz - 1, 1), kh, n), b),
        ]
    per = (grid.nc - 1) + (nx - 1) + (ny - 1) + (nz - 1)
    count = per * sum(s[0] for s in shapes)
    return shapes, outs, scratch, count


def block_of(e, nq, blocks):
    return e * blocks // nq


def by_cut(shape):
    return 2 * shape[1] % 128 == 0


def place_params(grid, tables, vectors, affine, tile):
    index = lax.axis_index("seq") * grid.ng + lax.axis_index("seg")

    def spread(v):
        mine = v.shape[1]
        row = lax.broadcasted_iota(jnp.int32, (mine, 128), 0)
        lane = lax.broadcasted_iota(jnp.int32, (mine, 128), 1)
        where = (lane == row + lax.rem(index * mine, 128)).astype(jnp.bfloat16)
        wide = jnp.broadcast_to(v.astype(jnp.float32), (max(v.shape[0], 8), mine)).astype(jnp.bfloat16)
        return jnp.dot(wide, where, preferred_element_type=jnp.float32)[0 : v.shape[0]]

    tile[...] = jnp.zeros_like(tile)
    first = 0
    for v in tables + vectors:
        tile[first : first + v.shape[0], :] = spread(v[...])
        first += v.shape[0]
    at = lax.broadcasted_iota(jnp.int32, (4, 128), 0) == index * affine.shape[1] // 128
    tile[first : first + 4, :] = jnp.where(at, spread(affine[...]), 0.0)


def place_documents(grid, starts, alive, spans, mask):
    rows = alive.shape[0]
    first = [starts[0, k] for k in range(starts.shape[1])]
    base = lax.axis_index("seq") * rows
    place = lax.broadcasted_iota(jnp.int32, (rows, 128), 0)
    column = lax.broadcasted_iota(jnp.int32, (rows, 128), 1)
    within = jnp.bitwise_and(place, STRETCH - 1)
    here, there = base + place, base + place - within + column
    goes_on = jnp.ones((rows, 128), jnp.float32)
    doc_here, doc_there = jnp.zeros((rows, 128), jnp.int32), jnp.zeros((rows, 128), jnp.int32)
    for f in first:
        goes_on = jnp.where(here == f, 0.0, goes_on)
        doc_here = doc_here + jnp.where(here >= f, 1, 0)
        doc_there = doc_there + jnp.where(there >= f, 1, 0)
    alive[...] = goes_on
    mask[...] = jnp.where((doc_here == doc_there) & (column <= within), 1.0, 0.0)
    low = lax.broadcasted_iota(jnp.int32, spans.shape, 0) * rows
    whole = jnp.ones(spans.shape, jnp.float32)
    for f in first:
        whole = jnp.where((low <= f) & (f < low + rows), 0.0, whole)
    spans[...] = whole


def mix_kernel(grid, width, dims, shapes, out_term, *refs):
    n = len(shapes)
    shards, refs = refs[:n], refs[n:]
    tok, starts, cot, *refs = refs
    tables, vectors, affine, refs = refs[:4], refs[4:7], refs[7], refs[8:]
    wholes, refs = refs[:n], refs[n:]
    term_hbm = None
    if out_term:
        term_hbm, *refs = refs
    (alive, spans, carry_out, par_out, aff_out, probs_out, layer_out,
     normed_hbm, active_hbm, x_hbm, mixed_hbm, one_hbm, two_hbm, proj_hbm, value_hbm, att_hbm, hin_hbm, hpre_hbm, ffn_hbm, act_hbm,
     normed_out, active_out, x_out, mixed_out, out_one_out, two_out, proj, value_pre, att, hin, hpre, ffn_pre, act, values,
     mask, tile, tiles, table, bound, sends_t, recv_t, sends_b, recv_b, own_sem, flush_sem, load_sem, send, recv,
     layer_sum, *slots) = refs
    if out_term:
        *slots, turned_act, stage, stage_sem = slots
    nq, ng = grid.nq, grid.ng
    rows = tok.shape[0]
    blocks = width // 128
    s = lax.axis_index("seq")
    seq_peer, seg_peer = small_peers(grid)
    meet(seq_peer + seg_peer)
    steps = gather_steps(grid, shapes, shards, wholes, own_sem, Sems(send, recv))

    done = set()

    def pump(count=1):
        for _ in range(count):
            done.update(next(steps, ()))

    flushes = []

    def flush(ref, hbm):
        copy = pltpu.make_async_copy(ref, hbm, flush_sem.at[len(flushes)])
        copy.start()
        flushes.append(copy)

    place_params(grid, tables, vectors, affine, tile)
    place_documents(grid, starts, alive, spans, mask)

    copies = []
    for d in range(1, ng):
        copies.append(pltpu.make_async_remote_copy(
            tile, tiles.at[d - 1], sends_t.at[d - 1], recv_t.at[d - 1],
            device_id=seg_peer[d - 1], device_id_type=MESH))
        copies[-1].start()
    for copy in copies:
        copy.wait_recv()
    lanes = tile[...]
    for d in range(1, ng):
        lanes += tiles[d - 1]
    table[s] = lanes
    for d in range(1, nq):
        copies.append(pltpu.make_async_remote_copy(
            table.at[s], table.at[s], sends_t.at[ng + d - 2], recv_t.at[ng + d - 2],
            device_id=seq_peer[d - 1], device_id_type=MESH))
        copies[-1].start()
    pump()
    for d in range(1, nq):
        came = table.at[lax.rem(s + nq - d, nq)]
        pltpu.make_async_remote_copy(
            came, came, sends_t.at[ng + d - 2], recv_t.at[ng + d - 2],
            device_id=seq_peer[d - 1], device_id_type=MESH).wait_recv()
    count = 4 * dims + 3
    for b in range(blocks):
        mine = [e for e in range(nq) if block_of(e, nq, blocks) == b]
        whole = table[mine[0], 0:count]
        for e in mine[1:]:
            whole += table[e, 0:count]
        par_out[:, b, :] = whole
    aff = table[0, count : count + 4]
    for e in range(1, nq):
        aff += table[e, count : count + 4]
    aff_out[...] = aff

    pump()

    gain = [par_out[4 * dims, b : b + 1, :] for b in range(blocks)]
    step_rows = 32

    @pl.loop(0, rows // step_rows)
    def _(i):
        at = pl.ds(pl.multiple_of(i * step_rows, step_rows), step_rows)
        v = tok[at, :].astype(jnp.float32)
        r = lax.rsqrt(jnp.mean(v * v, axis=1, keepdims=True) + epsilon)
        for b in range(blocks):
            lane = slice(b * 128, b * 128 + 128)
            n = (v[:, lane] * r * gain[b]).astype(jnp.bfloat16)
            normed_out[at, lane] = n
            x_out[pl.ds(i * step_rows * blocks + b, step_rows, stride=blocks), :] = n.astype(jnp.float32)

    flush(normed_out, normed_hbm)
    flush(x_out, x_hbm)
    damping = [jax.nn.sigmoid(par_out[j]) for j in range(dims)]
    keep = [1.0 - damping[j] * jax.nn.sigmoid(par_out[dims + j]) for j in range(dims)]
    weight = [damping[j] * par_out[2 * dims + j] * par_out[3 * dims + j] for j in range(dims)]
    omega = par_out[4 * dims + 1]

    def row(ref, p):
        return ref[pl.ds(pl.multiple_of(p * blocks, blocks), blocks), :]

    def first_pass(p, state):
        x, a = row(x_out, p), alive[pl.ds(p, 1), :]
        return tuple(keep[j] * (state[j] * a) + x for j in range(dims))

    zero = tuple(jnp.zeros((blocks, 128), jnp.float32) for _ in range(dims))
    pump()
    ends = zero
    for part in range(2):
        ends = lax.fori_loop(part * rows // 2, (part + 1) * rows // 2, first_pass, ends, unroll=4)
        if part == 0:
            pump()
    for j in range(dims):
        bound[s, j] = ends[j]
    out = []
    for d in range(1, nq):
        out.append(pltpu.make_async_remote_copy(
            bound.at[s], bound.at[s], sends_b.at[d - 1], recv_b.at[d - 1],
            device_id=seq_peer[d - 1], device_id_type=MESH))
        out[-1].start()
    pump(3)
    for d in range(1, nq):
        came = bound.at[lax.rem(s + nq - d, nq)]
        pltpu.make_async_remote_copy(
            came, came, sends_b.at[d - 1], recv_b.at[d - 1],
            device_id=seq_peer[d - 1], device_id_type=MESH).wait_recv()
    for j in range(dims):
        through = power(keep[j], rows)
        state = jnp.zeros((blocks, 128), jnp.float32)
        for e in range(nq - 1):
            later = through * spans[e : e + 1, :] * state + bound[e, j]
            state = jnp.where(e < s, later, state)
        carry_out[j] = state

    def second_pass(p, state):
        x, a = row(x_out, p), alive[pl.ds(p, 1), :]
        state = tuple(keep[j] * (state[j] * a) + x for j in range(dims))
        sums = [omega * x] + [weight[j] * state[j] for j in range(dims)]
        while len(sums) > 1:
            sums = [sum(sums[k : k + 2][1:], sums[k]) for k in range(0, len(sums), 2)]
        mixed_out[pl.ds(pl.multiple_of(p * blocks, blocks), blocks), :] = sums[0]
        return state

    state = tuple(carry_out[j] for j in range(dims))
    for part in range(4):
        state = lax.fori_loop(part * rows // 4, (part + 1) * rows // 4, second_pass, state, unroll=4)
        if part % 2:
            pump()
    for b in range(blocks):
        m = mixed_out[pl.ds(b, rows, stride=blocks), :]
        active_out[:, b * 128 : b * 128 + 128] = (m * jax.nn.sigmoid(m)).astype(jnp.bfloat16)
    flush(mixed_out, mixed_hbm)
    flush(active_out, active_hbm)
    for copy in copies + out:
        copy.wait_send()

    def pieces(i):
        while i not in done:
            pump()

        def fetch(g):
            return pltpu.make_async_copy(
                wholes[i].at[g // grid.nc, g % grid.nc], slots[i].at[g % 2], load_sem.at[i, g % 2]
            )

        fetch(0).start()
        for g in range(grid.ng):
            if g + 1 < grid.ng:
                fetch(g + 1).start()
            fetch(g).wait()
            piece = slots[i][g % 2]
            wide = piece.shape[-1]
            yield g, slice(g * wide, g * wide + wide), piece.reshape(-1, wide)
            if g + 1 == grid.ng:
                pump()

    block_rows = 32
    zdim = aff_out.shape[1]
    vdim = value_pre.shape[1]
    first_gate, first_reset, first_cand = width, width + zdim, width + zdim + vdim
    dot = functools.partial(jnp.dot, preferred_element_type=jnp.float32)

    def by_rows(count=rows, each=block_rows):
        def wrap(f):
            pl.loop(0, count // each)(lambda i: f(pl.ds(pl.multiple_of(i * each, each), each)))

        return wrap

    for g, cols, piece in pieces(0):
        proj[:, cols] = dot(active_out[...], piece)
    flush(proj, proj_hbm)

    scale_q = zdim**-0.5
    near = []
    for r in range(rows // STRETCH):
        at = slice(r * STRETCH, r * STRETCH + STRETCH)
        gate = proj[at, first_gate:first_reset]
        shared = gate * jax.nn.sigmoid(gate)
        query = (scale_q * (shared * aff_out[0:1] + aff_out[1:2])).astype(jnp.bfloat16)
        key = (shared * aff_out[2:3] + aff_out[3:4]).astype(jnp.bfloat16)
        scores = lax.dot_general(query, key, (((1,), (1,)), ((), ())), preferred_element_type=jnp.float32)
        scores = jnp.where(mask[at, :] > 0.0, scores, -1e30)
        expo = jnp.exp(scores - jnp.max(scores, axis=1, keepdims=True))
        probs = expo / jnp.sum(expo, axis=1, keepdims=True)
        probs_out[at, :] = probs
        near.append(probs.astype(jnp.bfloat16))

    for g, cols, piece in pieces(1):
        pre = dot(normed_out[...], piece)
        value_pre[:, cols] = pre
        values[:, cols] = (pre * jax.nn.sigmoid(pre)).astype(jnp.bfloat16)
    flush(value_pre, value_hbm)
    for r in range(rows // STRETCH):
        at = slice(r * STRETCH, r * STRETCH + STRETCH)
        att[at, :] = dot(near[r], values[at, :])

    @by_rows()
    def _(at):
        gate = proj[at, first_reset:first_cand]
        hin[at, :] = (att[at, :] * (gate * jax.nn.sigmoid(gate))).astype(jnp.bfloat16)

    flush(att, att_hbm)
    flush(hin, hin_hbm)

    for g, cols, piece in pieces(2):
        hpre[:, cols] = proj[:, first_cand + cols.start : first_cand + cols.stop] + dot(hin[...], piece)
    flush(hpre, hpre_hbm)

    gain_two = [par_out[4 * dims + 2, b : b + 1, :] for b in range(blocks)]

    @by_rows()
    def _(at):
        v = tok[at, :].astype(jnp.float32)
        h = hpre[at, :]
        one = v + jax.nn.sigmoid(proj[at, 0:width]) * (h * jax.nn.sigmoid(h) - v)
        out_one_out[at, :] = one
        r = lax.rsqrt(jnp.mean(one * one, axis=1, keepdims=True) + epsilon)
        for b in range(blocks):
            lane = slice(b * 128, b * 128 + 128)
            two_out[at, lane] = (one[:, lane] * r * gain_two[b]).astype(jnp.bfloat16)

    flush(out_one_out, one_hbm)
    flush(two_out, two_hbm)
    for g, cols, piece in pieces(3):
        pre = dot(two_out[...], piece)
        ffn_pre[:, cols] = pre
        act[:, cols] = (pre * jax.nn.sigmoid(pre)).astype(jnp.bfloat16)
    flush(ffn_pre, ffn_hbm)
    flush(act, act_hbm)

    if out_term:
        for a in range(0, act.shape[1], 256):
            turned_act[a : a + 256, :] = act[:, a : a + 256].T
        n_cols, deep = out_term[-1], act.shape[1] // grid.nz
        copies = []
        for g in range(ng):
            right = cot[:, g * n_cols : (g + 1) * n_cols]
            for zt in range(grid.nz):
                m = len(copies)
                if m >= 4:
                    copies[m - 4].wait()
                stage[m % 4] = dot(turned_act[zt * deep : (zt + 1) * deep, :], right).astype(jnp.bfloat16).reshape(stage.shape[1:])
                copies.append(
                    pltpu.make_async_copy(stage.at[m % 4], term_hbm.at[g // grid.nc, g % grid.nc, zt], stage_sem.at[m % 4])
                )
                copies[m].start()
            if g == ng // 2:
                pump()
        for copy in copies[-4:]:
            copy.wait()
    cuts, high, n_cols = shapes[4]
    if by_cut(shapes[4]):
        layer_sum[...] = out_one_out[...]
        deep, each = cuts * high, 2 * high
        for q in range(cuts // 2):
            while (4, q) not in done:
                pump()
            slot = slots[4].at[q % 2]
            copy = pltpu.make_async_copy(wholes[4].at[:, :, :, :, 2 * q : 2 * q + 2], slot, load_sem.at[4, q % 2])
            copy.start()
            left = jnp.concatenate([act[:, a * deep + q * each : a * deep + (q + 1) * each] for a in range(nq)], axis=1)
            copy.wait()
            for g in range(ng):
                cols = slice(g * n_cols, (g + 1) * n_cols)
                layer_sum[:, cols] += dot(left, slots[4][q % 2, g // grid.nc, g % grid.nc].reshape(-1, n_cols))
        layer_out[...] = layer_sum[...].astype(jnp.bfloat16)
    else:
        for g, cols, piece in pieces(4):
            layer_out[:, cols] = (out_one_out[:, cols] + dot(act[...], piece)).astype(jnp.bfloat16)
    for _ in steps:
        pass
    for copy in flushes:
        copy.wait()


def power(v, n):
    result = None
    while n:
        if n & 1:
            result = v if result is None else result * v
        n >>= 1
        if n:
            v = v * v
    return result


def mix_forward(grid, weights, cuts, tok, own_params, starts, cot, dims, out_term, collective_id):
    rows, width = tok.shape
    nq, ng = grid.nq, grid.ng
    blocks = width // 128
    f = jnp.float32
    vm = pl.BlockSpec(memory_space=pltpu.VMEM)
    shapes, shards, outs, count = gather_plan(grid, weights, cuts)
    n = len(shards)
    vdim, fdim, proj_dim = weights[1].shape[1] * ng, weights[3].shape[1] * ng, weights[0].shape[1] * ng
    low = jnp.bfloat16
    kept = [
        ((rows, width), low),
        ((rows, width), low),
        ((rows * blocks, 128), f),
        ((rows * blocks, 128), f),
        ((rows, width), f),
        ((rows, width), low),
        ((rows, proj_dim), f),
        ((rows, vdim), f),
        ((rows, vdim), f),
        ((rows, vdim), low),
        ((rows, width), f),
        ((rows, fdim), f),
        ((rows, fdim), low),
    ]
    count_rows = 4 * dims + 3
    tile_shape = (-(-(count_rows + 4) // 8) * 8, 128)
    local = [
        ((rows, 128), f),
        ((nq, 128), f),
        ((dims, blocks, 128), f),
        ((count_rows, blocks, 128), f),
        ((4, 128), f),
        ((rows, STRETCH), f),
        ((rows, width), low),
    ]
    term = [jax.ShapeDtypeStruct((grid.ny, grid.nc, grid.nz, grid.nx) + out_term, low)] if out_term else []
    held = len(term)
    turning = [
        pltpu.VMEM((fdim, rows), low),
        pltpu.VMEM((4, grid.nx) + out_term, low),
        pltpu.SemaphoreType.DMA((4,)),
    ] if out_term else []
    result = pl.pallas_call(
        functools.partial(mix_kernel, grid, width, dims, shapes, out_term),
        out_shape=outs + term + [jax.ShapeDtypeStruct(*v) for v in local + kept],
        in_specs=[ANY] * n + [vm, pl.BlockSpec(memory_space=pltpu.SMEM)] + [vm] * 9,
        out_specs=[ANY] * (n + held) + [vm] * len(local) + [ANY] * len(kept),
        scratch_shapes=[pltpu.VMEM(*v) for v in kept]
        + [
            pltpu.VMEM((rows, vdim), low),
            pltpu.VMEM((rows, STRETCH), f),
            pltpu.VMEM(tile_shape, f),
            pltpu.VMEM((ng - 1,) + tile_shape, f),
            pltpu.VMEM((nq,) + tile_shape, f),
            pltpu.VMEM((nq, dims, blocks, 128), f),
            pltpu.SemaphoreType.DMA((nq + ng - 2,)),
            pltpu.SemaphoreType.DMA((nq + ng - 2,)),
            pltpu.SemaphoreType.DMA((nq - 1,)),
            pltpu.SemaphoreType.DMA((nq - 1,)),
            pltpu.SemaphoreType.DMA((n,)),
            pltpu.SemaphoreType.DMA((len(kept),)),
            pltpu.SemaphoreType.DMA((n, 2)),
            pltpu.SemaphoreType.DMA((count,)),
            pltpu.SemaphoreType.DMA((count,)),
        ]
        + [pltpu.VMEM((rows, width), f)]
        + [pltpu.VMEM((2,) + o.shape[2:], o.dtype) for o in outs[:4]]
        + [pltpu.VMEM((2,) + (outs[4].shape[:4] + (2,) + outs[4].shape[5:] if by_cut(shapes[4]) else outs[4].shape[2:]), low)]
        + turning,
        compiler_params=pltpu.CompilerParams(
            collective_id=collective_id, has_side_effects=True, vmem_limit_bytes=60 << 20
        ),
    )(*shards, tok, starts, cot, *own_params)
    return result[:n], result[n : n + held], result[n + held :]


def scan_back(grid, dims, g_rows, x_in, mixed, carry, par, alive, spans, gin_rows, before, bound, sends_b, recv_b,
              m_all, k_all, seq_peer, s, pump):
    nq = grid.nq
    blocks = carry.shape[1]
    rows = g_rows.shape[0] // blocks

    @pl.loop(0, rows * blocks // 64)
    def _(i):
        at = pl.ds(pl.multiple_of(i * 64, 64), 64)
        g_rows[at, :] = g_rows[at, :] * silu_slope(mixed[at, :])

    damping = [jax.nn.sigmoid(par[j]) for j in range(dims)]
    keep = [1.0 - damping[j] * jax.nn.sigmoid(par[dims + j]) for j in range(dims)]
    weight = [damping[j] * par[2 * dims + j] * par[3 * dims + j] for j in range(dims)]
    omega = par[4 * dims + 1]

    def row(ref, p):
        return ref[pl.ds(pl.multiple_of(p * blocks, blocks), blocks), :]

    def first_pass(i, flow):
        p = rows - 1 - i
        gp, a = row(g_rows, p), alive[pl.ds(p, 1), :]
        return tuple(keep[j] * (a * (gp + flow[j])) for j in range(dims))

    zero = jnp.zeros((blocks, 128), jnp.float32)
    ends = lax.fori_loop(0, rows, first_pass, (zero,) * dims, unroll=4)
    for j in range(dims):
        bound[s, j] = ends[j]
    def sent(d):
        return pltpu.make_async_remote_copy(
            bound.at[s], bound.at[s], sends_b.at[d - 1], recv_b.at[d - 1],
            device_id=seq_peer[d - 1], device_id_type=MESH)

    for d in range(1, nq):
        sent(d).start()
    pump()
    for d in range(1, nq):
        came = bound.at[lax.rem(s + nq - d, nq)]
        pltpu.make_async_remote_copy(
            came, came, sends_b.at[d - 1], recv_b.at[d - 1],
            device_id=seq_peer[d - 1], device_id_type=MESH).wait_recv()
    flow_in = []
    for j in range(dims):
        through = power(keep[j], rows)
        flow = zero
        for e in range(nq - 1, 0, -1):
            later = through * spans[e : e + 1, :] * flow + bound[e, j]
            flow = jnp.where(e > s, later, flow)
        flow_in.append(flow)

    few = before.shape[1]
    for j0 in range(0, dims, few):
        js = range(j0, j0 + few)

        def ahead(p, state):
            x, a = row(x_in, p), alive[pl.ds(p, 1), :]
            for t in range(few):
                before[p, t] = state[t]
            return tuple(keep[j] * (state[t] * a) + x for t, j in enumerate(js))

        lax.fori_loop(0, rows, ahead, tuple(carry[j] for j in js), unroll=4)
        if j0:
            pump()

        def back(i, held):
            flow, m_sum, k_sum, om_sum = held
            p = rows - 1 - i
            at = pl.ds(pl.multiple_of(p * blocks, blocks), blocks)
            gp, x, a = g_rows[at, :], x_in[at, :], alive[pl.ds(p, 1), :]
            total = omega * gp if j0 == 0 else gin_rows[at, :]
            if j0 == 0:
                om_sum = om_sum + gp * x
            new_flow, new_m, new_k = [], [], []
            for t, j in enumerate(js):
                c = gp + flow[t]
                ac = a * c
                total = total + weight[j] * c
                new_flow.append(keep[j] * ac)
                new_m.append(m_sum[t] + c * x)
                new_k.append(k_sum[t] + ac * before[p, t])
            gin_rows[at, :] = total
            return tuple(new_flow), tuple(new_m), tuple(new_k), om_sum

        zeros = (zero,) * few
        _, m_sum, k_sum, om_sum = lax.fori_loop(
            0, rows, back, (tuple(flow_in[j] for j in js), zeros, zeros, zero), unroll=4
        )
        for t, j in enumerate(js):
            m_all[j] = m_sum[t]
            k_all[j] = k_sum[t]
        if j0 == 0:
            m_all[dims] = om_sum
        pump()
    for d in range(1, nq):
        sent(d).wait_send()


def norm_back(par, dims, tok, pre, direct, gin_rows, gtok_out, row_sums):
    rows, width = tok.shape
    blocks = width // 128
    gain = [par[4 * dims, b : b + 1, :] for b in range(blocks)]
    lanes = [slice(b * 128, b * 128 + 128) for b in range(blocks)]
    step_rows = 32

    def some(i, gains):
        at = pl.ds(pl.multiple_of(i * step_rows, step_rows), step_rows)
        v = tok[at, :].astype(jnp.float32)
        r = lax.rsqrt(jnp.mean(v * v, axis=1, keepdims=True) + epsilon)
        gy = []
        for b in range(blocks):
            came = gin_rows[pl.ds(i * step_rows * blocks + b, step_rows, stride=blocks), :]
            gy.append(pre[at, lanes[b]] + came.astype(jnp.bfloat16).astype(jnp.float32))
        scaled = [gy[b] * gain[b] for b in range(blocks)]
        dots = sum(jnp.sum(scaled[b] * v[:, lanes[b]], axis=1, keepdims=True) for b in range(blocks))
        pull = r * r * (dots / width)
        new = []
        for b in range(blocks):
            vb = v[:, lanes[b]]
            gx = r * (scaled[b] - vb * pull)
            gtok_out[at, lanes[b]] = (direct[at, lanes[b]] + gx).astype(jnp.bfloat16)
            new.append(gains[b] + jnp.sum(gy[b] * (vb * r), axis=0, keepdims=True))
        return tuple(new)

    gains = lax.fori_loop(
        0, rows // step_rows, some, tuple(jnp.zeros((1, 128), jnp.float32) for _ in range(blocks))
    )
    for b in range(blocks):
        row_sums[b : b + 1, :] = gains[b]


def fill_small(grid, dims, small, m_all, k_all, row_sums):
    blocks = row_sums.shape[0]
    for e in range(grid.nq):
        b = block_of(e, grid.nq, blocks)
        small[e, 0:dims] = m_all[0:dims, b, :]
        small[e, dims : 2 * dims] = k_all[:, b, :]
        small[e, 2 * dims : 2 * dims + 1] = m_all[dims, b : b + 1, :]
        small[e, 2 * dims + 1 : 2 * dims + 2] = row_sums[b : b + 1, :]


def mix_back_kernel(grid, dims, shapes, *refs):
    n = len(shapes)
    terms, refs = refs[:n], refs[n:]
    gact, x_in, mixed, carry, par, alive, spans, tok, pre, direct, small_in, *refs = refs
    sums, refs = refs[:n], refs[n:]
    (gtok_out, small_out,
     g_rows, gin_rows, before, bound, m_all, k_all, row_sums, small, seq_in, seg_in,
     sends_b, recv_b, s_send, s_recv, own_sem, send, recv, *scratch) = refs
    nq = grid.nq
    rows, width = gact.shape
    blocks = width // 128
    s = lax.axis_index("seq")
    seq_peer, seg_peer = small_peers(grid)
    meet(seq_peer + seg_peer)
    steps = scatter_steps(grid, shapes, terms, sums, scratch, own_sem, Sems(send, recv))
    little = SmallSum(grid, small, small_out, seq_in, seg_in, s_send, s_recv)

    def pump(count=1):
        for _ in range(count):
            next(steps, None)

    pump(2)
    for b in range(blocks):
        g_rows[pl.ds(b, rows, stride=blocks), :] = gact[:, b * 128 : b * 128 + 128].astype(jnp.float32)

    scan_back(
        grid, dims, g_rows, x_in, mixed, carry, par, alive, spans, gin_rows, before, bound, sends_b, recv_b,
        m_all, k_all, seq_peer, s, pump
    )
    norm_back(par, dims, tok, pre, direct, gin_rows, gtok_out, row_sums)
    for e in range(nq):
        small[e] = small_in[e]
    fill_small(grid, dims, small, m_all, k_all, row_sums)
    little.start()
    pump()
    little.middle()
    for _ in steps:
        pass
    little.end()


def mix_backward(grid, terms, cuts, gact, x_in, mixed, carry, par, alive, spans, tok, pre, direct, small, collective_id):
    rows, width = gact.shape
    nq, ng = grid.nq, grid.ng
    blocks, dims, few = width // 128, carry.shape[0], 4
    f = jnp.float32
    vm = pl.BlockSpec(memory_space=pltpu.VMEM)
    shapes, outs, scratch, count = scatter_plan(grid, terms, cuts)
    parts = [t.reshape((grid.ny, grid.nc, grid.nz, grid.nx) + v) for t, v in zip(terms, shapes)]
    n = len(parts)
    result = pl.pallas_call(
        functools.partial(mix_back_kernel, grid, dims, shapes),
        out_shape=outs
        + [jax.ShapeDtypeStruct((rows, width), jnp.bfloat16), jax.ShapeDtypeStruct(small.shape[1:], f)],
        in_specs=[ANY] * n + [vm] * 11,
        out_specs=[vm] * (n + 2),
        scratch_shapes=[
            pltpu.VMEM((rows * blocks, 128), f),
            pltpu.VMEM((rows * blocks, 128), f),
            pltpu.VMEM((rows, few, blocks, 128), f),
            pltpu.VMEM((nq, dims, blocks, 128), f),
            pltpu.VMEM((dims + 1, blocks, 128), f),
            pltpu.VMEM((dims, blocks, 128), f),
            pltpu.VMEM((blocks, 128), f),
            pltpu.VMEM(small.shape, f),
            pltpu.VMEM((nq - 1,) + small.shape[1:], f),
            pltpu.VMEM((ng - 1,) + small.shape[1:], f),
            pltpu.SemaphoreType.DMA((nq - 1,)),
            pltpu.SemaphoreType.DMA((nq - 1,)),
            pltpu.SemaphoreType.DMA((nq + ng - 2,)),
            pltpu.SemaphoreType.DMA((nq + ng - 2,)),
            pltpu.SemaphoreType.DMA((n, 2)),
            pltpu.SemaphoreType.DMA((count,)),
            pltpu.SemaphoreType.DMA((count,)),
        ]
        + scratch,
        compiler_params=pltpu.CompilerParams(
            collective_id=collective_id, has_side_effects=True, vmem_limit_bytes=62 << 20
        ),
    )(*parts, gact, x_in, mixed, carry, par, alive, spans, tok, pre, direct, small)
    return [v.reshape(-1, t.shape[-1]) for v, t in zip(result, terms)], result[n], result[n + 1]


def layer_back_kernel(grid, dims, shapes, sizes, *refs):
    n = len(shapes)
    zdim, vdim, fdim = sizes
    wholes, refs = refs[:n], refs[n:]
    (first_term, cot_hbm, ffn_hbm, two_hbm, one_hbm, hpre_hbm, proj_hbm, att_hbm, hin_hbm, value_hbm, probs, active_hbm,
     normed_hbm, tok_hbm, x_hbm, mixed_hbm, carry, par, aff, alive, spans, *refs) = refs
    sums, refs = refs[:n], refs[n:]
    gtok_out, small_out, *refs = refs
    terms, refs = [first_term, *refs[: n - 1]], refs[n - 1 :]
    (gproj, direct, pre, bound, m_all, k_all, row_sums, two_sums, aff_sums, small, seq_in, seg_in,
     sends_b, recv_b, s_send, s_recv, own_sem, load_sem, tile_sem, stage_sem, send, recv, *scratch) = refs
    nq, ng, nc, nz = grid.nq, grid.ng, grid.nc, grid.nz
    rows, width = direct.shape
    blocks = width // 128
    low, f = jnp.bfloat16, jnp.float32
    s = lax.axis_index("seq")
    seq_peer, seg_peer = small_peers(grid)
    meet(seq_peer + seg_peer)
    ready = [1]
    steps = scatter_steps(grid, shapes, terms, sums, scratch, own_sem, Sems(send, recv), lambda: ready[0])
    little = SmallSum(grid, small, small_out, seq_in, seg_in, s_send, s_recv)
    loads = [0]

    def pump(count=1):
        for _ in range(count):
            next(steps, None)

    pump(3)
    dot = functools.partial(jnp.dot, preferred_element_type=f)

    def dot_nt(a, b):
        return lax.dot_general(a, b, (((1,), (1,)), ((), ())), preferred_element_type=f)

    def dot_tn(a, b):
        return lax.dot_general(a, b, (((0,), (0,)), ((), ())), preferred_element_type=f)

    def fetch(src, dst):
        copy = pltpu.make_async_copy(src, dst, load_sem.at[loads[0]])
        loads[0] += 1
        copy.start()
        return copy.wait

    def by_rows(each=32):
        def wrap(some):
            pl.loop(0, rows // each)(lambda i: some(pl.ds(pl.multiple_of(i * each, each), each)))

        return wrap

    def wide(i):
        return shapes[i][-1]

    def tile_shape(i):
        return (2, grid.ny, nc, grid.nx) + shapes[i]

    def depth(i):
        return grid.nx * shapes[i][0] * shapes[i][1]

    def tile(i, tiles, zt):
        return pltpu.make_async_copy(wholes[i].at[:, :, zt], tiles.at[zt % 2], tile_sem.at[zt % 2])

    def begin(i, tiles):
        for zt in range(min(2, nz)):
            tile(i, tiles, zt).start()

    def against(i, tiles, part):
        for zt in range(nz):
            tile(i, tiles, zt).wait()
            total = None
            for g in range(ng):
                term = dot_nt(part(g), tiles[zt % 2, g // nc, g % nc].reshape(depth(i), wide(i)))
                total = term if total is None else total + term
            if zt + 2 < nz:
                tile(i, tiles, zt + 2).start()
            yield slice(zt * depth(i), zt * depth(i) + depth(i)), total

    def grads(i, left, stage, part):
        copies = []
        slots = stage.shape[0]
        for g in range(ng):
            right = part(g)
            for zt in range(nz):
                k = len(copies)
                if k >= slots:
                    copies[k - slots].wait()
                d = depth(i)
                term = dot(left[zt * d : zt * d + d, :], right)
                stage[k % slots] = term.astype(low).reshape(stage.shape[1:])
                copies.append(
                    pltpu.make_async_copy(stage.at[k % slots], terms[i].at[g // nc, g % nc, zt], stage_sem.at[k % slots])
                )
                copies[k].start()
        for copy in copies[-slots:]:
            copy.wait()
        ready[0] = i + 1

    def turned(src, dst):
        for a in range(0, src.shape[1], 256):
            b = min(a + 256, src.shape[1])
            dst[a:b, :] = src[:, a:b].T

    def vm(*shape, kind=low):
        return pltpu.VMEM(shape, kind)

    def stage_of(i, slots=4):
        return pltpu.VMEM((slots, grid.nx) + shapes[i], low)

    def cut(ref, i):
        return lambda g: ref[:, g * wide(i) : (g + 1) * wide(i)]

    first_gate, first_reset, first_cand = width, width + zdim, width + zdim + vdim
    out_i, in_i, att_i, value_i, mix_i = range(5)

    def ffn_back(cot, hold, norm_grad, two):
        wait_cot, wait_two = fetch(cot_hbm, cot), fetch(two_hbm, two)

        def second(pre_act, tiles):
            begin(out_i, tiles)
            each = depth(out_i)
            pre_waits = [fetch(ffn_hbm.at[:, k * each : (k + 1) * each], pre_act.at[k]) for k in range(2)]
            wait_cot()
            for k, (cols, grad) in enumerate(against(out_i, tiles, cut(cot, out_i))):
                pre_waits[k]()
                hold[:, cols] = (grad * silu_slope(pre_act[k % 2])).astype(low)
                if k + 2 < nz:
                    pre_waits.append(fetch(ffn_hbm.at[:, (k + 2) * each : (k + 3) * each], pre_act.at[k % 2]))
            pump()

        pl.run_scoped(second, vm(2, rows, depth(out_i), kind=f), pltpu.VMEM(tile_shape(out_i), low))

        def rest(one, hpre, upd, tok):
            waits = [fetch(one_hbm, one), fetch(hpre_hbm, hpre), fetch(proj_hbm.at[:, 0:width], upd), fetch(tok_hbm, tok)]

            def first(left, stage, tiles):
                begin(in_i, tiles)
                wait_two()
                turned(two, left)
                grads(in_i, left, stage, cut(hold, in_i))
                pump()
                for cols, grad in against(in_i, tiles, cut(hold, in_i)):
                    norm_grad[:, cols] = grad

            pl.run_scoped(first, vm(width, rows), stage_of(in_i), pltpu.VMEM(tile_shape(in_i), low))
            for wait in waits:
                wait()
            two_sums[...] = jnp.zeros_like(two_sums)

            @by_rows(16)
            def _(at):
                v, x, h, c = one[at, :], tok[at, :].astype(f), hpre[at, :], cot[at, :].astype(f)
                gain = jnp.concatenate([par[4 * dims + 2, b : b + 1, :] for b in range(blocks)], axis=1)
                r = lax.rsqrt(jnp.mean(v * v, axis=1, keepdims=True) + epsilon)
                gy = norm_grad[at, :]
                scaled = gy * gain
                pull = r * r * jnp.mean(scaled * v, axis=1, keepdims=True)
                grad_one = c + r * (scaled - v * pull)
                two_sums[...] += jnp.sum(gy * (v * r), axis=0, keepdims=True)
                u = jax.nn.sigmoid(upd[at, :])
                sig = jax.nn.sigmoid(h)
                direct[at, :] = grad_one * (1.0 - u)
                gproj[at, first_cand:] = (grad_one * u * (sig * (1.0 + h * (1.0 - sig)))).astype(low)
                gproj[at, 0:width] = (grad_one * (h * sig - x) * (u * (1.0 - u))).astype(low)

        pl.run_scoped(
            rest, vm(rows, width, kind=f), vm(rows, width, kind=f), vm(rows, width, kind=f), vm(rows, width)
        )

    pl.run_scoped(ffn_back, vm(rows, width), vm(rows, fdim), vm(rows, width, kind=f), vm(rows, width))
    pump()

    def attention_back(grad_hin, att, gate, shared_pre, value_pre):
        waits = [
            fetch(att_hbm, att),
            fetch(proj_hbm.at[:, first_reset:first_cand], gate),
            fetch(proj_hbm.at[:, first_gate:first_reset], shared_pre),
            fetch(value_hbm, value_pre),
        ]

        def out_back(hin, left, stage, tiles):
            wait_hin = fetch(hin_hbm, hin)
            begin(att_i, tiles)
            wait_hin()
            turned(hin, left)

            def part(g):
                return gproj[:, first_cand + g * wide(att_i) : first_cand + (g + 1) * wide(att_i)]

            grads(att_i, left, stage, part)
            pump()
            for cols, grad in against(att_i, tiles, part):
                grad_hin[:, cols] = grad

        pl.run_scoped(out_back, vm(rows, vdim), vm(vdim, rows), stage_of(att_i), pltpu.VMEM(tile_shape(att_i), low))

        def inner(grad_pre, normed, value_tiles):
            wait_normed = fetch(normed_hbm, normed)
            begin(value_i, value_tiles)

            def blocks_back(grad_att, values):
                for wait in waits:
                    wait()

                @by_rows(16)
                def _(at):
                    v, g, p = gate[at, :], grad_hin[at, :], value_pre[at, :]
                    sig = jax.nn.sigmoid(v)
                    grad_att[at, :] = (g * (v * sig)).astype(low)
                    gproj[at, first_reset:first_cand] = (g * att[at, :] * (sig * (1.0 + v * (1.0 - sig)))).astype(low)
                    values[at, :] = (p * jax.nn.sigmoid(p)).astype(low)

                aff_total = [jnp.zeros((1, zdim), f)] * 4
                scale_q = zdim**-0.5
                for r in range(rows // STRETCH):
                    at = slice(r * STRETCH, r * STRETCH + STRETCH)
                    v = shared_pre[at, :]
                    shared = v * jax.nn.sigmoid(v)
                    query = (scale_q * (shared * aff[0:1] + aff[1:2])).astype(low)
                    key = (shared * aff[2:3] + aff[3:4]).astype(low)
                    prob, ga = probs[at, :], grad_att[at, :]
                    grad_prob = dot_nt(ga, values[at, :])
                    weighted = jnp.sum(prob * grad_prob, axis=1, keepdims=True)
                    grad_score = (prob * (grad_prob - weighted)).astype(low)
                    grad_query = dot(grad_score, key) * scale_q
                    grad_key = dot_tn(grad_score, query)
                    grad_shared = grad_query * aff[0:1] + grad_key * aff[2:3]
                    gproj[at, first_gate:first_reset] = (grad_shared * silu_slope(v)).astype(low)
                    for k, t in enumerate([grad_query * shared, grad_query, grad_key * shared, grad_key]):
                        aff_total[k] = aff_total[k] + jnp.sum(t, axis=0, keepdims=True)
                    grad_hin[at, :] = dot_tn(prob.astype(low), ga)
                for k in range(4):
                    aff_sums[k : k + 1, :] = aff_total[k]

                @by_rows(16)
                def _(at):
                    grad_pre[at, :] = (grad_hin[at, :] * silu_slope(value_pre[at, :])).astype(low)

            pl.run_scoped(blocks_back, vm(rows, vdim), vm(rows, vdim))
            pump()

            def value_back(left, stage):
                wait_normed()
                turned(normed, left)
                grads(value_i, left, stage, cut(grad_pre, value_i))
                for cols, grad in against(value_i, value_tiles, cut(grad_pre, value_i)):
                    pre[:, cols] = grad

            pl.run_scoped(value_back, vm(width, rows), stage_of(value_i))

        pl.run_scoped(inner, vm(rows, vdim), vm(rows, width), pltpu.VMEM(tile_shape(value_i), low))

    pl.run_scoped(
        attention_back, vm(rows, vdim, kind=f), vm(rows, vdim, kind=f), vm(rows, vdim, kind=f), vm(rows, zdim, kind=f),
        vm(rows, vdim, kind=f)
    )
    pump()

    def mix_back(g_rows, gin_rows, x_in, mixed, tok):
        waits = [fetch(x_hbm, x_in), fetch(mixed_hbm, mixed), fetch(tok_hbm, tok)]

        def mix_weight_back(active, left, stage, tiles):
            wait_active = fetch(active_hbm, active)
            begin(mix_i, tiles)
            wait_active()
            turned(active, left)
            grads(mix_i, left, stage, cut(gproj, mix_i))
            pump()
            for cols, grad in against(mix_i, tiles, cut(gproj, mix_i)):
                grad = grad.astype(low).astype(f)
                for b in range(cols.start // 128, cols.stop // 128):
                    lane = b * 128 - cols.start
                    g_rows[pl.ds(b, rows, stride=blocks), :] = grad[:, lane : lane + 128]

        pl.run_scoped(
            mix_weight_back, vm(rows, width), vm(width, rows), stage_of(mix_i), pltpu.VMEM(tile_shape(mix_i), low)
        )

        for wait in waits:
            wait()

        def scan(before):
            scan_back(
                grid, dims, g_rows, x_in, mixed, carry, par, alive, spans, gin_rows, before, bound, sends_b, recv_b,
                m_all, k_all, seq_peer, s, pump
            )

        pl.run_scoped(scan, vm(rows, 4, blocks, 128, kind=f))
        norm_back(par, dims, tok, pre, direct, gin_rows, gtok_out, row_sums)

    pl.run_scoped(
        mix_back, vm(rows * blocks, 128, kind=f), vm(rows * blocks, 128, kind=f), vm(rows * blocks, 128, kind=f),
        vm(rows * blocks, 128, kind=f), vm(rows, width)
    )
    small[...] = jnp.zeros_like(small)
    fill_small(grid, dims, small, m_all, k_all, row_sums)
    for e in range(nq):
        b = block_of(e, nq, blocks)
        small[e, 2 * dims + 2 : 2 * dims + 3] = two_sums[:, b * 128 : b * 128 + 128]
        small[e, 2 * dims + 3 : 2 * dims + 7] = aff_sums[...]
    little.start()
    pump()
    little.middle()
    for _ in steps:
        pass
    little.end()


def layer_backward(grid, wholes, cuts, kept, probs, carry, par, aff, alive, spans, sizes, collective_id):
    nq, ng = grid.nq, grid.ng
    dims, blocks = carry.shape[0], carry.shape[1]
    zdim, vdim, fdim = sizes
    width = blocks * 128
    rows = probs.shape[0]
    f = jnp.float32
    vm = pl.BlockSpec(memory_space=pltpu.VMEM)
    n = len(wholes)
    like = [jax.ShapeDtypeStruct((ng, w.size // ng // w.shape[-1], w.shape[-1]), w.dtype) for w in wholes]
    shapes, outs, scratch, count = scatter_plan(grid, like, cuts)
    whole_shapes = [jax.ShapeDtypeStruct(w.shape[:4] + s, w.dtype) for w, s in zip(wholes, shapes)]
    low = [w.reshape(v.shape) for w, v in zip(wholes, whole_shapes)]
    small_shape = (-(-(2 * dims + 7) // 8) * 8, 128)
    result = pl.pallas_call(
        functools.partial(layer_back_kernel, grid, dims, shapes, sizes),
        out_shape=outs
        + [jax.ShapeDtypeStruct((rows, width), jnp.bfloat16), jax.ShapeDtypeStruct(small_shape, f)]
        + whole_shapes[1:],
        in_specs=[ANY] * n + [ANY] * 10 + [vm] + [ANY] * 5 + [vm] * 5,
        out_specs=[vm] * (n + 2) + [ANY] * (n - 1),
        scratch_shapes=[
            pltpu.VMEM((rows, width * 2 + zdim + vdim), jnp.bfloat16),
            pltpu.VMEM((rows, width), f),
            pltpu.VMEM((rows, width), f),
            pltpu.VMEM((nq, dims, blocks, 128), f),
            pltpu.VMEM((dims + 1, blocks, 128), f),
            pltpu.VMEM((dims, blocks, 128), f),
            pltpu.VMEM((blocks, 128), f),
            pltpu.VMEM((1, width), f),
            pltpu.VMEM((4, zdim), f),
            pltpu.VMEM((nq,) + small_shape, f),
            pltpu.VMEM((nq - 1,) + small_shape, f),
            pltpu.VMEM((ng - 1,) + small_shape, f),
            pltpu.SemaphoreType.DMA((nq - 1,)),
            pltpu.SemaphoreType.DMA((nq - 1,)),
            pltpu.SemaphoreType.DMA((nq + ng - 2,)),
            pltpu.SemaphoreType.DMA((nq + ng - 2,)),
            pltpu.SemaphoreType.DMA((n, 2)),
            pltpu.SemaphoreType.DMA((24,)),
            pltpu.SemaphoreType.DMA((2,)),
            pltpu.SemaphoreType.DMA((4,)),
            pltpu.SemaphoreType.DMA((count,)),
            pltpu.SemaphoreType.DMA((count,)),
        ]
        + scratch,
        compiler_params=pltpu.CompilerParams(
            collective_id=collective_id, has_side_effects=True, vmem_limit_bytes=63 << 20
        ),
    )(*low, *kept[:10], probs, *kept[10:], carry, par, aff, alive, spans)
    return [v.reshape(-1, t.shape[-1]) for v, t in zip(result, like)], result[n], result[n + 1]


def rms_forward(values, gain):
    inverse = lax.rsqrt(jnp.mean(values * values, axis=-1, keepdims=True) + epsilon)
    return (values * inverse * gain, inverse)


def rms_backward(grad_out, values, inverse, gain):
    scaled = grad_out * gain
    projection = jnp.mean(scaled * values, axis=-1, keepdims=True)
    grad_in = inverse * (scaled - values * inverse * inverse * projection)
    return (grad_in, jnp.sum(grad_out * values * inverse, axis=0))


def silu_slope(values):
    sigma_v = jax.nn.sigmoid(values)
    return sigma_v * (1.0 + values * (1.0 - sigma_v))


def times(left, pieces):
    return jnp.concatenate(
        [jnp.dot(left, pieces[i], preferred_element_type=jnp.float32) for i in range(pieces.shape[0])], axis=1
    )


def against(left, pieces):
    n = pieces.shape[2]
    return sum(
        lax.dot_general(
            left[:, i * n : i * n + n], pieces[i], (((1,), (1,)), ((), ())), preferred_element_type=jnp.float32
        )
        for i in range(pieces.shape[0])
    )


def over_rows(left, right, count):
    n = right.shape[1] // count
    return jnp.stack(
        [
            lax.dot_general(
                left, right[:, i * n : i * n + n], (((0,), (0,)), ((), ())), preferred_element_type=jnp.float32
            ).astype(jnp.bfloat16)
            for i in range(count)
        ]
    )


def masked_scores(query_blk, key_blk, allowed):
    raw_scores = jnp.einsum("cid,cjd->cij", query_blk, key_blk, preferred_element_type=jnp.float32)
    return jnp.where(allowed, raw_scores, -1e30)


def backward_apart(grid, cotangent, tokens_low, forward, weights, alive, spans, sizes):
    (carry, par, affine, probs, _, normed_b, active, x_rows, mixed_rows, out_one, normed_two_b,
     projected, value_pre, attended, hidden_in, hidden_pre, ffn_hidden, ffn_act) = forward
    ffn_hidden = ffn_hidden.astype(jnp.float32)
    token_count, model_width = tokens_low.shape
    nq, ng = grid.nq, grid.ng
    dims, blocks = carry.shape[0], carry.shape[1]
    zdim, vdim, _ = sizes
    block_count = token_count // STRETCH
    tokens_flat = tokens_low.astype(jnp.float32)
    mix_full, value_full, out_full, ffn_in_full, ffn_out_full = (w.reshape(ng, -1, w.shape[-1]) for w in weights)
    gain_two = par[4 * dims + 2].reshape(-1)
    update = jax.nn.sigmoid(projected[:, :model_width])
    gate_pre = projected[:, model_width : model_width + zdim + vdim]
    gate_rows = jax.nn.silu(gate_pre)
    shared = gate_rows[:, :zdim]
    reset_gate = gate_rows[:, zdim:]
    values_b = jax.nn.silu(value_pre).astype(jnp.bfloat16)
    scale_q = zdim ** (-0.5)
    query_b = (scale_q * (shared * affine[0] + affine[1])).astype(jnp.bfloat16)
    key_b = (shared * affine[2] + affine[3]).astype(jnp.bfloat16)
    query_blk = query_b.reshape(block_count, STRETCH, zdim)
    key_blk = key_b.reshape(block_count, STRETCH, zdim)
    value_blk = values_b.reshape(block_count, STRETCH, vdim)
    probs = probs.reshape(block_count, STRETCH, STRETCH)
    probs_b = probs.astype(jnp.bfloat16)
    hidden_act = jax.nn.silu(hidden_pre)
    inverse_two = lax.rsqrt(jnp.mean(out_one * out_one, axis=-1, keepdims=True) + epsilon)

    grad_y_b = cotangent
    grad_ffn_out = over_rows(ffn_act, grad_y_b, ng)
    grad_act = against(grad_y_b, ffn_out_full)
    grad_hidden_b = (grad_act * silu_slope(ffn_hidden)).astype(jnp.bfloat16)
    grad_ffn_in = over_rows(normed_two_b, grad_hidden_b, ng)
    grad_normed_two = against(grad_hidden_b, ffn_in_full)
    grad_norm_two, grad_gain_two = rms_backward(grad_normed_two, out_one, inverse_two, gain_two)
    grad_out_one = grad_y_b.astype(jnp.float32) + grad_norm_two
    grad_update = grad_out_one * (hidden_act - tokens_flat)
    grad_tokens_flat = grad_out_one * (1.0 - update)
    grad_hpre_b = (grad_out_one * update * silu_slope(hidden_pre)).astype(jnp.bfloat16)
    grad_out_weight = over_rows(hidden_in, grad_hpre_b, ng)
    grad_hidden_in = against(grad_hpre_b, out_full)
    grad_att_b = (grad_hidden_in * reset_gate).astype(jnp.bfloat16)
    grad_reset = grad_hidden_in * attended
    grad_att_blk = grad_att_b.reshape(block_count, STRETCH, vdim)
    grad_probs = jnp.einsum("civ,cjv->cij", grad_att_blk, value_blk, preferred_element_type=jnp.float32)
    weighted = jnp.sum(probs * grad_probs, axis=2, keepdims=True)
    grad_scores_b = (probs * (grad_probs - weighted)).astype(jnp.bfloat16)
    grad_query = jnp.einsum("cij,cjd->cid", grad_scores_b, key_blk, preferred_element_type=jnp.float32).reshape(
        token_count, zdim
    )
    grad_key = jnp.einsum("cij,cid->cjd", grad_scores_b, query_blk, preferred_element_type=jnp.float32).reshape(
        token_count, zdim
    )
    grad_values = jnp.einsum("cij,civ->cjv", probs_b, grad_att_blk, preferred_element_type=jnp.float32).reshape(
        token_count, vdim
    )
    grad_qs = grad_query * scale_q
    grad_shared = grad_qs * affine[0] + grad_key * affine[2]
    grad_affine = jnp.stack(
        [
            jnp.sum(grad_qs * shared, axis=0),
            jnp.sum(grad_qs, axis=0),
            jnp.sum(grad_key * shared, axis=0),
            jnp.sum(grad_key, axis=0),
        ]
    )
    grad_gate_pre = jnp.concatenate([grad_shared, grad_reset], axis=1) * silu_slope(gate_pre)
    grad_upre = grad_update * update * (1.0 - update)
    grad_proj_b = jnp.concatenate(
        [grad_upre.astype(jnp.bfloat16), grad_gate_pre.astype(jnp.bfloat16), grad_hpre_b], axis=1
    )
    grad_mix = over_rows(active, grad_proj_b, ng)
    grad_active_b = against(grad_proj_b, mix_full).astype(jnp.bfloat16)
    grad_vpre_b = (grad_values * silu_slope(value_pre)).astype(jnp.bfloat16)
    grad_value = over_rows(normed_b, grad_vpre_b, ng)
    grad_normed = against(grad_vpre_b, value_full)

    small = jnp.concatenate(
        [jnp.zeros((blocks, 2 * dims + 2, 128), jnp.float32), grad_gain_two.reshape(blocks, 1, 128)], axis=1
    )
    if nq != blocks:
        small = jnp.take(small, np.arange(nq) * blocks // nq, axis=0)
    small = jnp.concatenate([small, jnp.broadcast_to(grad_affine[None], (nq, 4, 128))], axis=1)
    small = jnp.pad(small, ((0, 0), (0, -small.shape[1] % 8), (0, 0)))
    return mix_backward(
        grid, [grad_ffn_out, grad_ffn_in, grad_out_weight, grad_value, grad_mix], SCATTER_CUTS, grad_active_b, x_rows,
        mixed_rows, carry, par, alive, spans, tokens_low, grad_normed, grad_tokens_flat, small, 1
    )


def body(
    tokens,
    starts,
    norm_gain,
    ema_delta,
    ema_alpha,
    ema_beta,
    ema_eta,
    ema_omega,
    mix_weight,
    value_weight,
    qk_affine,
    out_weight,
    ffn_gain,
    ffn_in,
    ffn_out,
    cotangent,
):
    seg_count, row_count, model_width = tokens.shape
    nq, ng = lax.axis_size("seq"), lax.axis_size("seg")
    grid = Grid(nq, ng)
    seq_index, seg_index = lax.axis_index("seq"), lax.axis_index("seg")
    seq_length = row_count * nq
    dims = ema_delta.shape[1]
    zdim = qk_affine.shape[0] * nq * ng // 4
    vdim = value_weight.shape[1] * ng
    token_count = seg_count * row_count
    blocks = model_width // 128

    index = seq_index * ng + seg_index
    mine, part = norm_gain.shape[0], qk_affine.shape[0]
    own_params = [
        ema_delta.T, ema_alpha.T, ema_beta.T, ema_eta.T, norm_gain[None], ema_omega[None], ffn_gain[None], qk_affine[None]
    ]
    cotangent_low = cotangent.reshape(token_count, model_width)
    shards = [mix_weight, value_weight, out_weight, ffn_in, ffn_out]
    apart = min(w.shape[1] for w in shards) < 128
    out_term = None
    if not apart:
        k, n = ffn_out.shape
        q = max(1, min(SCATTER_CUTS[0], k // 32))
        out_term = (2 * q, k // (2 * q), n)
    tokens_low = tokens.reshape(token_count, model_width)
    weights, term, forward = mix_forward(
        grid, shards, GATHER_CUTS, tokens_low, own_params, starts, cotangent_low, dims, out_term, 0
    )
    alive, spans, *forward = forward
    (carry, par, affine, probs, result, normed_b, active, x_rows, mixed_rows, out_one, normed_two_b,
     projected, value_pre, attended, hidden_in, hidden_pre, ffn_hidden, ffn_act) = forward
    sizes = (zdim, vdim, ffn_act.shape[1])
    if apart:
        result_back = backward_apart(grid, cotangent_low, tokens_low, forward, weights, alive, spans, sizes)
    else:
        kept = [term[0], cotangent_low, ffn_hidden, normed_two_b, out_one, hidden_pre, projected, attended, hidden_in,
                value_pre, active, normed_b, tokens_low, x_rows, mixed_rows]
        order = [weights[4], weights[3], weights[2], weights[1], weights[0]]
        result_back = layer_backward(
            grid, order, SCATTER_CUTS, kept, probs, carry, par, affine, alive, spans, sizes, 1
        )
    (g_ffn_out, g_ffn_in, g_out, g_value, g_mix), grad_tokens, sums = result_back
    return (
        result.reshape(seg_count, row_count, model_width),
        grad_tokens.reshape(seg_count, row_count, model_width),
        *small_outputs(sums, index, dims, ema_delta, ema_alpha, ema_beta, ema_eta, mine, part, g_mix, g_value, g_out, g_ffn_in, g_ffn_out),
    )


def small_outputs(sums, index, dims, ema_delta, ema_alpha, ema_beta, ema_eta, mine, part, g_mix, g_value, g_out, g_ffn_in, g_ffn_out):
    own = lax.dynamic_slice_in_dim(sums, lax.rem(index * mine, 128), mine, 1)
    m_sum, k_sum = own[:dims].T, own[dims : 2 * dims].T
    vectors = own[2 * dims : 2 * dims + 3]
    delta, alpha, beta, eta = (v.astype(jnp.float32) for v in (ema_delta, ema_alpha, ema_beta, ema_eta))
    damping, decay = jax.nn.sigmoid(delta), jax.nn.sigmoid(alpha)
    g_keep = damping * beta * eta * k_sum
    grad_eta = damping * beta * m_sum
    grad_beta = damping * eta * m_sum
    grad_alpha = -g_keep * damping * decay * (1.0 - decay)
    grad_delta = (beta * eta * m_sum - g_keep * decay) * damping * (1.0 - damping)
    grad_affine = lax.dynamic_slice(
        sums, (2 * dims + 3 + index * part // 128, lax.rem(index * part, 128)), (1, part)
    ).reshape(-1)
    return (vectors[1], grad_delta, grad_alpha, grad_beta, grad_eta, vectors[0],
            g_mix, g_value, grad_affine, g_out, vectors[2], g_ffn_in, g_ffn_out)


def solution(mesh):
    placed = (
        P("seg", "seq", None),
        P("seg", None),
        P(("seq", "seg")),
        P(("seq", "seg"), None),
        P(("seq", "seg"), None),
        P(("seq", "seg"), None),
        P(("seq", "seg"), None),
        P(("seq", "seg")),
        P("seq", "seg"),
        P("seq", "seg"),
        P(("seq", "seg")),
        P("seq", "seg"),
        P(("seq", "seg")),
        P("seq", "seg"),
        P("seq", "seg"),
        P("seg", "seq", None),
    )
    return jax.shard_map(
        body,
        mesh=mesh,
        in_specs=placed,
        out_specs=(P("seg", "seq", None),) * 2 + placed[2:15],
        check_vma=False,
    )
```
